32 devices in a mesh: seq: 8 (over y, x, core), head: 4 (over z).
Axes of the slice: x: 2, y: 2, z: 4, core: 2. Of those that a mesh axis runs over, the one named last changes fastest.
Arguments:
- query_state: bfloat16 [12288, 512], P('seq'), may hold values from -6 to 6
- content: bfloat16 [12288, 512], P('seq'), may hold values from -6 to 6
- encoded: bfloat16 [12288, 512], P('seq'), may hold values from -6 to 6
- sentence_lengths: int32 [217], replicated, may hold values from 4 to 1024, as said below
- key_score: int32 [12288], replicated, may hold values from 0 to 63
- query_cut: int32 [12288], replicated, may hold values from 1 to 64
- w_query: bfloat16 [512, 512], P(None, 'head'), may hold values from -0.625 to 0.625
- w_key: bfloat16 [512, 512], P(None, 'head'), may hold values from -0.25 to 0.25
- w_value: bfloat16 [512, 512], P(None, 'head'), may hold values from -0.25 to 0.25
- w_out: bfloat16 [512, 512], P('head'), may hold values from -1.5 to 1.5
- gain_self: float32 [512], replicated, may hold values from 0.5 to 1.5
- w_cross_query: bfloat16 [512, 512], P(None, 'head'), may hold values from -0.625 to 0.625
- w_cross_key: bfloat16 [512, 512], P(None, 'head'), may hold values from -0.25 to 0.25
- w_cross_value: bfloat16 [512, 512], P(None, 'head'), may hold values from -0.25 to 0.25
- w_cross_out: bfloat16 [512, 512], P('head'), may hold values from -1.5 to 1.5
- gain_cross: float32 [512], replicated, may hold values from 0.5 to 1.5
- w_inner: bfloat16 [512, 2048], P(None, 'head'), may hold values from -0.25 to 0.25
- w_outer: bfloat16 [2048, 512], P('head'), may hold values from -0.1875 to 0.1875
- gain_final: float32 [512], replicated, may hold values from 0.5 to 1.5
- out_grad: bfloat16 [12288, 512], P('seq'), may hold values from -6 to 6
Outputs:
- mixed: bfloat16 [12288, 512], P('seq')
- query_state_grad: float32 [12288, 512], P('seq')
- content_grad: float32 [12288, 512], P('seq')
- encoded_grad: float32 [12288, 512], P('seq')
- w_query_grad: float32 [512, 512], P(None, 'head')
- w_key_grad: float32 [512, 512], P(None, 'head')
- w_value_grad: float32 [512, 512], P(None, 'head')
- w_out_grad: float32 [512, 512], P('head')
- gain_self_grad: float32 [512], replicated
- w_cross_query_grad: float32 [512, 512], P(None, 'head')
- w_cross_key_grad: float32 [512, 512], P(None, 'head')
- w_cross_value_grad: float32 [512, 512], P(None, 'head')
- w_cross_out_grad: float32 [512, 512], P('head')
- gain_cross_grad: float32 [512], replicated
- w_inner_grad: float32 [512, 2048], P(None, 'head')
- w_outer_grad: float32 [2048, 512], P('head')
- gain_final_grad: float32 [512], replicated
The draws below stay inside these ranges and needn't reach their ends.
Inputs may be any that keep to these rules, and one draw needn't show every extreme that they name: `sentence_lengths`: exactly 6 entries equal 1024 (the documents); every other entry is a sentence of 4 to 56 tokens, one of them exactly 4; the entries sum to 12288; the order is drawn from the seed.
All inputs are finite; a program needn't handle non-finite values.
Results may differ from the reference program's by a relative error of at most 0.029.
The reference program's roundings to bfloat16 on the way count: a program that leaves them out, or rounds other values in their place, can miss the bound.
Values may be sent and summed in bfloat16 or wider, within the bound.
A program may use at most 384 MiB of HBM per device.

```python
import math
import jax
import jax.numpy as jnp
from jax import lax

D = 512
HEADS = 8
HEAD_SIZE = 64
FF = 2048
TOK_DEV = 1536
SENT_MIN = 4
SENT_MAX = 56
DOC_LEN = 1024
LEVELS = 64
TOKENS = 12288
DOCS = 6
SHORT_TOK = 6144
SHORTS = 211
SENTS = 217


def draw_sentence_lengths(key, part):
    key = jax.random.fold_in(key, 11)
    first_key, second_key, third_key = jax.random.split(key, 3)
    base = SHORT_TOK // SHORTS
    extra = SHORT_TOK - base * SHORTS
    index = jnp.arange(SHORTS, dtype=jnp.int32)
    shorts = (base + (index < extra).astype(jnp.int32)).astype(jnp.int32)
    pairs = SHORTS // 2
    spread = min(base - SENT_MIN, SENT_MAX - base - 1)
    moved = jax.random.randint(first_key, (pairs,), -spread, spread + 1).astype(jnp.int32)
    left_half = shorts[0:2 * pairs:2]
    right_half = shorts[1:2 * pairs:2]
    chosen = jax.random.randint(second_key, (), 0, pairs)
    moved = jnp.where(jnp.arange(pairs) == chosen, left_half - SENT_MIN, moved).astype(jnp.int32)
    left_half = left_half - moved
    right_half = right_half + moved
    paired = jnp.stack([left_half, right_half], axis=1).reshape(-1)
    shorts = jnp.concatenate([paired, shorts[2 * pairs:]]).astype(jnp.int32)
    documents = jnp.full((DOCS,), DOC_LEN, jnp.int32)
    together = jnp.concatenate([shorts, documents]).astype(jnp.int32)
    order = jax.random.permutation(third_key, SENTS)
    return together[order].astype(jnp.int32)


def place_ends(result, rng, smallest, largest):
    spot = [jax.random.randint(jax.random.fold_in(rng, axis), (), 0, length) for axis, length in enumerate(result.shape)]
    widest = result.shape.index(max(result.shape))
    beside = spot[:widest] + [(spot[widest] + 1) % result.shape[widest]] + spot[widest + 1:]
    return result.at[tuple(spot)].set(smallest).at[tuple(beside)].set(largest)


def shard_levels(key, dims, shards, low, largest):
    level, own = 1.0, jax.random.fold_in(key, 6)
    for dim, blocks in shards:
        draws = jnp.exp(jax.random.uniform(jax.random.fold_in(own, dim), (blocks,), jnp.float32, low / len(shards), largest / len(shards)))
        level = level * jnp.repeat(draws, dims[dim] // blocks).reshape([-1 if axis == dim else 1 for axis in range(len(dims))])
    return level


def noise(key, extent, width, bound, cuts=(), kind=jnp.bfloat16):
    drawn = jax.random.normal(key, extent, jnp.float32) * width
    if len(cuts) > 0:
        drawn = shard_levels(key, extent, cuts, -0.22, 0.18) * drawn
    return jnp.clip(drawn, min=-bound, max=bound).astype(kind)


def setup_inputs(seed: int = 0) -> dict:
    seeds = jax.random.split(jax.random.key(seed), 21)
    query_state = noise(seeds[0], (TOKENS, D), 1.0, 6.0, ((0, 8),))
    content = noise(seeds[1], (TOKENS, D), 1.0, 6.0, ((0, 8),))
    encoded = noise(seeds[2], (TOKENS, D), 1.0, 6.0, ((0, 8),))
    sentence_lengths = draw_sentence_lengths(jax.random.fold_in(seeds[20], 71), 0)
    key_score = place_ends(jax.random.randint(seeds[4], (TOKENS,), 0, LEVELS), jax.random.fold_in(seeds[4], 1), 0, LEVELS - 1).astype(jnp.int32)
    query_cut = place_ends(jax.random.randint(seeds[5], (TOKENS,), 1, LEVELS + 1), jax.random.fold_in(seeds[5], 1), 1, LEVELS).astype(jnp.int32)
    w_query = noise(seeds[6], (D, D), (D // 6) ** -0.5, 0.625, ((1, 4),))
    w_key = noise(seeds[7], (D, D), D ** -0.5, 0.25, ((1, 4),))
    w_value = noise(seeds[8], (D, D), D ** -0.5, 0.25, ((1, 4),))
    w_out = noise(seeds[9], (D, D), (D // 32) ** -0.5, 1.5, ((0, 4),))
    gain_self = jnp.clip(1.0 + 0.1 * jax.random.normal(seeds[10], (D,), jnp.float32), 0.5, 1.5)
    w_cross_query = noise(seeds[11], (D, D), (D // 6) ** -0.5, 0.625, ((1, 4),))
    w_cross_key = noise(seeds[12], (D, D), D ** -0.5, 0.25, ((1, 4),))
    w_cross_value = noise(seeds[13], (D, D), D ** -0.5, 0.25, ((1, 4),))
    w_cross_out = noise(seeds[14], (D, D), (D // 32) ** -0.5, 1.5, ((0, 4),))
    gain_cross = jnp.clip(1.0 + 0.1 * jax.random.normal(seeds[15], (D,), jnp.float32), 0.5, 1.5)
    w_inner = noise(seeds[16], (D, FF), D ** -0.5, 0.25, ((1, 4),))
    w_outer = noise(seeds[17], (FF, D), (FF // 2) ** -0.5, 0.1875, ((0, 4),))
    gain_final = jnp.clip(1.0 + 0.1 * jax.random.normal(seeds[18], (D,), jnp.float32), 0.5, 1.5)
    out_grad = noise(seeds[19], (TOKENS, D), 1.0, 6.0, ((0, 8),))
    return dict(query_state=query_state, content=content, encoded=encoded, sentence_lengths=sentence_lengths, key_score=key_score, query_cut=query_cut, w_query=w_query, w_key=w_key, w_value=w_value, w_out=w_out, gain_self=gain_self, w_cross_query=w_cross_query, w_cross_key=w_cross_key, w_cross_value=w_cross_value, w_cross_out=w_cross_out, gain_cross=gain_cross, w_inner=w_inner, w_outer=w_outer, gain_final=gain_final, out_grad=out_grad)


eps_norm = 1e-05
neg_big = -1e+30

@jax.custom_vjp
def reduced_precision(v):
    return lax.optimization_barrier(v.astype(jnp.bfloat16)).astype(jnp.float32)

@jax.custom_vjp
def low_back(v):
    return v

def low_keep(v):
    return (reduced_precision(v), None)

def low_pass(kept, grad):
    return (grad,)

def back_keep(v):
    return (v, None)

def back_low(kept, grad):
    return (reduced_precision(grad),)
reduced_precision.defvjp(low_keep, low_pass)
low_back.defvjp(back_keep, back_low)

def both_ways(value):
    return reduced_precision(low_back(value))

def product(left, right):
    return jnp.dot(left, right, precision=lax.Precision.HIGHEST)

def sentence_of(positions, lengths):
    ends = jnp.cumsum(lengths).astype(jnp.int32)
    passed = (positions[:, None] >= ends[None, :]).astype(jnp.int32)
    sentence = lax.optimization_barrier(jnp.sum(passed, axis=1)).astype(jnp.int32)
    first = lax.optimization_barrier(jnp.sum(passed * lengths[None, :], axis=1)).astype(jnp.int32)
    return (sentence, first)

def normalize(resid, gain):
    mean_row = lax.optimization_barrier(jnp.mean(resid, axis=1, keepdims=True))
    centred = resid - mean_row
    var_row = lax.optimization_barrier(jnp.mean(centred * centred, axis=1, keepdims=True))
    return centred * lax.rsqrt(var_row + eps_norm) * gain[None, :]

def self_visible(query_side, key_side):
    same = query_side[0][:, None] == key_side[1][None, :]
    chosen = (key_side[0][None, :] == query_side[1][:, None]) | (key_side[2][None, :] < query_side[2][:, None])
    return same & chosen

def cross_visible(query_side, key_side):
    return query_side[0][:, None] == key_side[1][None, :]

def attention(query, keys, value_matrix, query_side, key_side, visible_fn):
    rows = TOK_DEV
    span = DOC_LEN - 1
    model_width = rows + 2 * span
    count = TOKENS // rows
    keys_pad = jnp.pad(keys, ((span, span), (0, 0)))
    values_pad = jnp.pad(value_matrix, ((span, span), (0, 0)))
    side_pad = tuple((jnp.pad(x, (span, span), constant_values=-1) for x in key_side))

    def one_block(item):
        start = item[4]
        query_tile = item[0].reshape(rows, HEADS, HEAD_SIZE)
        key_cube = lax.dynamic_slice_in_dim(keys_pad, start, model_width, 0).reshape(model_width, HEADS, HEAD_SIZE)
        value_cube = lax.dynamic_slice_in_dim(values_pad, start, model_width, 0).reshape(model_width, HEADS, HEAD_SIZE)
        side = tuple((lax.dynamic_slice_in_dim(x, start, model_width, 0) for x in side_pad))
        unscaled_scores = jnp.einsum('qui,zui->uqz', query_tile, key_cube, precision=lax.Precision.HIGHEST) * (1.0 / math.sqrt(HEAD_SIZE))
        scores = jnp.where(visible_fn(item[1:4], side)[None], low_back(unscaled_scores), neg_big)
        top = lax.optimization_barrier(jnp.max(scores, axis=2, keepdims=True))
        expo = jnp.exp(scores - top)
        probabilities = expo / lax.optimization_barrier(jnp.sum(expo, axis=2, keepdims=True))
        blended_rows = jnp.einsum('xiv,vxj->ixj', reduced_precision(probabilities), value_cube, precision=lax.Precision.HIGHEST)
        return blended_rows.reshape(rows, HEADS * HEAD_SIZE)
    starts = (jnp.arange(count, dtype=jnp.int32) * rows).astype(jnp.int32)
    blocks = (query.reshape(count, rows, HEADS * HEAD_SIZE),) + tuple((x.reshape(count, rows) for x in query_side)) + (starts,)
    out = lax.map(jax.checkpoint(one_block), blocks)
    return both_ways(out.reshape(TOKENS, HEADS * HEAD_SIZE))

def reference(query_state, content, encoded, sentence_lengths, key_score, query_cut, w_query, w_key, w_value, w_out, gain_self, w_cross_query, w_cross_key, w_cross_value, w_cross_out, gain_cross, w_inner, w_outer, gain_final, out_grad):
    positions = jnp.arange(TOKENS, dtype=jnp.int32)
    sentence, first = sentence_of(positions, sentence_lengths.astype(jnp.int32))
    query_side = (sentence, first, query_cut.astype(jnp.int32))
    key_side = (positions, sentence, key_score.astype(jnp.int32))

    def forward(query_state, content, encoded, w_query, w_key, w_value, w_out, gain_self, w_cross_query, w_cross_key, w_cross_value, w_cross_out, gain_cross, w_inner, w_outer, gain_final):
        query = both_ways(product(query_state, w_query))
        keys = both_ways(product(content, w_key))
        value_matrix = both_ways(product(content, w_value))
        cross_keys = both_ways(product(encoded, w_cross_key))
        cross_values = both_ways(product(encoded, w_cross_value))
        attn = attention(query, keys, value_matrix, query_side, key_side, self_visible)
        resid_one = query_state + low_back(product(attn, w_out))
        hidden_one = normalize(resid_one, gain_self)
        cross_query = both_ways(product(reduced_precision(hidden_one), w_cross_query))
        cross_attn = attention(cross_query, cross_keys, cross_values, query_side, key_side, cross_visible)
        resid_two = hidden_one + low_back(product(cross_attn, w_cross_out))
        hidden_two = normalize(resid_two, gain_cross)
        inner = low_back(product(reduced_precision(hidden_two), w_inner))
        active = reduced_precision(jax.nn.gelu(inner, approximate=False))
        resid_three = hidden_two + low_back(product(active, w_outer))
        return normalize(resid_three, gain_final)
    floats = tuple((x.astype(jnp.float32) for x in (query_state, content, encoded, w_query, w_key, w_value, w_out, gain_self, w_cross_query, w_cross_key, w_cross_value, w_cross_out, gain_cross, w_inner, w_outer, gain_final)))
    mixed, backward = jax.vjp(forward, *floats)
    grads = backward(out_grad.astype(jnp.float32))
    return (mixed.astype(jnp.bfloat16), grads[0], grads[1], grads[2], grads[3], grads[4], grads[5], grads[6], grads[7], grads[8], grads[9], grads[10], grads[11], grads[12], grads[13], grads[14], grads[15])
```

```python
from functools import partial
import math

import jax
import jax.numpy as jnp
from jax import lax
from jax.experimental import pallas as pl
from jax.experimental.pallas import tpu as pltpu
from jax.sharding import PartitionSpec as P

HEADS = 8
HEAD_SIZE = 64
PAIR = 2 * HEAD_SIZE
PAIRS = HEADS // 2
DOC_LEN = 1024
CHUNK = 256
EPS = 1e-05
NEG_BIG = -1e30
LOG2E = 1.4426950408889634
SCALE = 1.0 / math.sqrt(HEAD_SIZE)
SCORE_SCALE = SCALE * LOG2E
CODES = 128
BF16 = jnp.bfloat16
F32 = jnp.float32
VMEM_LIMIT = 60 << 20


def dot_nn(left, right):
    return lax.dot_general(left, right, (((1,), (0,)), ((), ())), preferred_element_type=F32)


def dot_nt(left, right):
    return lax.dot_general(left, right, (((1,), (1,)), ((), ())), preferred_element_type=F32)


def dot_tn(left, right):
    return lax.dot_general(left, right, (((0,), (0,)), ((), ())), preferred_element_type=F32)


def chunk_rows(c):
    return pl.ds(pl.multiple_of(c * CHUNK, CHUNK), CHUNK)


def layer_norm(resid):
    mean_row = jnp.mean(resid, axis=1, keepdims=True)
    centred = resid - mean_row
    var_row = jnp.mean(centred * centred, axis=1, keepdims=True)
    scale_row = lax.rsqrt(var_row + EPS)
    return centred * scale_row, scale_row


def norm_back(grad, normed, scale_row, gain):
    gain_grad = jnp.sum(grad * normed, axis=0, keepdims=True)
    scaled = grad * gain
    centre = jnp.mean(scaled, axis=1, keepdims=True)
    along = jnp.mean(scaled * normed, axis=1, keepdims=True)
    return scale_row * (scaled - centre - normed * along), gain_grad


def spread_heads(source, target):
    target[...] = jnp.zeros_like(target)
    for h in range(HEADS):
        row = h * PAIR + (h % 2) * HEAD_SIZE
        target[row : row + HEAD_SIZE, :] = source[h * HEAD_SIZE : (h + 1) * HEAD_SIZE, :]


def pair_rows(source, p, target):
    rows = source.shape[0]
    both = source[:, p * PAIR : (p + 1) * PAIR]
    lane = lax.broadcasted_iota(jnp.int32, both.shape, 1)
    zero = jnp.zeros_like(both)
    target[p, 0:rows, :] = jnp.where(lane < HEAD_SIZE, both, zero)
    target[p, rows : 2 * rows, :] = jnp.where(lane < HEAD_SIZE, zero, both)


def mask_bias(code, low, high):
    return jnp.where((code >= low) & (code < high), 0.0, NEG_BIG).astype(F32)


def attend(bounds, window, code, low, high, w_key_t, w_value_t, spread, bias, top, total, out):
    top[...] = jnp.full_like(top, NEG_BIG)
    total[...] = jnp.zeros_like(total)
    out[...] = jnp.zeros_like(out)

    def step(c, carry):
        rows = window[chunk_rows(c), :]
        keys = dot_nt(rows, w_key_t[...]).astype(BF16)
        values_t = dot_nt(w_value_t[...], rows).astype(BF16)
        bias[...] = mask_bias(code[chunk_rows(c), :], low[...], high[...])
        for h in range(HEADS):
            p = h // 2
            scores = dot_nn(keys[:, p * PAIR : (p + 1) * PAIR], spread[h * PAIR : (h + 1) * PAIR, :])
            scores = scores * SCORE_SCALE + bias[...]
            before = top[h : h + 1, :]
            now = jnp.maximum(before, jnp.max(scores, axis=0, keepdims=True))
            weights = jnp.exp2(scores - now)
            shrink = jnp.exp2(before - now)
            top[h : h + 1, :] = now
            total[h : h + 1, :] = total[h : h + 1, :] * shrink + jnp.sum(weights, axis=0, keepdims=True)
            head = slice(h * HEAD_SIZE, (h + 1) * HEAD_SIZE)
            out[head, :] = out[head, :] * shrink + dot_nn(values_t[head, :], weights.astype(BF16))
        return carry

    lax.fori_loop(bounds[0], bounds[1], step, 0)
    for h in range(HEADS):
        head = slice(h * HEAD_SIZE, (h + 1) * HEAD_SIZE)
        out[head, :] = out[head, :] / total[h : h + 1, :]


def attend_back(
    bounds, window, code, low, high, w_key_t, w_value_t, spread, grad_spread, pairs, grad_pairs, lse, delta, bias,
    query_grad, window_grad, w_key_grad, w_value_grad,
):
    chunks = window.shape[0] // CHUNK
    count = spread.shape[1]
    query_grad[...] = jnp.zeros_like(query_grad)
    w_key_grad[...] = jnp.zeros_like(w_key_grad)
    w_value_grad[...] = jnp.zeros_like(w_value_grad)

    def clear(c, carry):
        window_grad[chunk_rows(c), :] = jnp.zeros((CHUNK, window_grad.shape[1]), window_grad.dtype)
        return carry

    lax.fori_loop(0, bounds[0], clear, 0)
    lax.fori_loop(bounds[1], chunks, clear, 0)

    def step(c, carry):
        rows = window[chunk_rows(c), :]
        keys = dot_nt(rows, w_key_t[...]).astype(BF16)
        keys_t = dot_nt(w_key_t[...], rows).astype(BF16)
        values = dot_nt(rows, w_value_t[...]).astype(BF16)
        bias[...] = mask_bias(code[chunk_rows(c), :], low[...], high[...])
        key_grads, value_grads = [], []
        for p in range(PAIRS):
            columns = slice(p * PAIR, (p + 1) * PAIR)
            probs, score_grads = [], []
            for h in (2 * p, 2 * p + 1):
                wide = slice(h * PAIR, (h + 1) * PAIR)
                head = slice(h * HEAD_SIZE, (h + 1) * HEAD_SIZE)
                scores = dot_nn(keys[:, columns], spread[wide, :])
                prob = jnp.exp2(scores * SCORE_SCALE + bias[...] - lse[h : h + 1, :])
                dprob = dot_nn(values[:, columns], grad_spread[wide, :])
                score_grad = (prob * (dprob - delta[h : h + 1, :])).astype(BF16)
                query_grad[head, :] += dot_nn(keys_t[head, :], score_grad)
                probs.append(prob.astype(BF16))
                score_grads.append(score_grad)
            if count % 128 == 0:
                key_grads.append(dot_nn(jnp.concatenate(score_grads, axis=1), pairs[p]))
                value_grads.append(dot_nn(jnp.concatenate(probs, axis=1), grad_pairs[p]))
            else:
                key_grads.append(dot_nn(score_grads[0], pairs[p, 0:count]) + dot_nn(score_grads[1], pairs[p, count:]))
                value_grads.append(dot_nn(probs[0], grad_pairs[p, 0:count]) + dot_nn(probs[1], grad_pairs[p, count:]))
        keys_low = (jnp.concatenate(key_grads, axis=1) * SCALE).astype(BF16)
        values_low = jnp.concatenate(value_grads, axis=1).astype(BF16)
        window_grad[chunk_rows(c), :] = (
            dot_nn(keys_low, w_key_t[...]) + dot_nn(values_low, w_value_t[...])
        ).astype(window_grad.dtype)
        w_key_grad[...] += dot_tn(rows, keys_low)
        w_value_grad[...] += dot_tn(rows, values_low)
        return carry

    lax.fori_loop(bounds[0], bounds[1], step, 0)


def self_kernel(bounds, own, window, code, low, high, w_query_t, w_key_t, w_value_t, out, lse, spread, bias, top, total, low_t):
    low_t[...] = dot_nt(w_query_t[...], own[...]).astype(BF16)
    spread_heads(low_t, spread)
    attend(bounds, window, code, low, high, w_key_t, w_value_t, spread, bias, top, total, out)
    lse[...] = top[...] + jnp.log2(total[...])


def cross_kernel(
    bounds, own, attn_t, w_out, gain, window, code, low, high, w_query_t, w_key_t, w_value_t,
    hidden, out, lse, spread, bias, top, total, low_t,
):
    branch = dot_tn(attn_t[...].astype(BF16), w_out[...])
    normed, _ = layer_norm(own[...].astype(F32) + branch)
    hidden[...] = normed * gain[...]
    low_t[...] = dot_nt(w_query_t[...], hidden[...].astype(BF16)).astype(BF16)
    spread_heads(low_t, spread)
    attend(bounds, window, code, low, high, w_key_t, w_value_t, spread, bias, top, total, out)
    lse[...] = top[...] + jnp.log2(total[...])


def ffn_kernel(
    hidden_one, cross_t, w_out, gain_cross, w_inner, w_outer, gain_final, out_grad,
    mixed, resid_grad, w_out_grad, w_inner_grad, w_outer_grad, gain_cross_grad, gain_final_grad,
    normed_two, hidden_two_low, slope, active, sum_ffn,
):
    slices = w_inner.shape[0]
    cross_low = cross_t[...].astype(BF16)
    normed, scale_two = layer_norm(hidden_one[...] + dot_tn(cross_low, w_out[...]))
    normed_two[...] = normed
    hidden_two = normed * gain_cross[...]
    hidden_two_low[...] = hidden_two.astype(BF16)
    sum_ffn[...] = hidden_two
    for z in range(slices):
        inner = dot_nn(hidden_two_low[...], w_inner[z])
        below = 0.5 * (1.0 + lax.erf(inner * math.sqrt(0.5)))
        slope[z] = below + inner * (jnp.exp2(inner * inner * (-0.5 * LOG2E)) * (1.0 / math.sqrt(2.0 * math.pi)))
        active[z] = (inner * below).astype(BF16)
        sum_ffn[...] += dot_nn(active[z], w_outer[z])
    normed_three, scale_three = layer_norm(sum_ffn[...])
    mixed[...] = (normed_three * gain_final[...]).astype(BF16)
    grad_three, gain_grad = norm_back(out_grad[...].astype(F32), normed_three, scale_three, gain_final[...])
    gain_final_grad[...] = gain_grad
    ffn_low = grad_three.astype(BF16)
    sum_ffn[...] = grad_three
    for z in range(slices):
        w_outer_grad[z] = dot_tn(active[z], ffn_low).astype(BF16)
        inner_low = (dot_nt(ffn_low, w_outer[z]) * slope[z]).astype(BF16)
        w_inner_grad[z] = dot_tn(hidden_two_low[...], inner_low).astype(BF16)
        sum_ffn[...] += dot_nt(inner_low, w_inner[z])
    grad, gain_grad = norm_back(sum_ffn[...], normed_two[...], scale_two, gain_cross[...])
    gain_cross_grad[...] = gain_grad
    resid_grad[...] = grad
    w_out_grad[...] = dot_nn(cross_low, grad.astype(BF16)).astype(BF16)


def prepare_back(query, query_t, grad, grad_t, out, spread, grad_spread, pairs, grad_pairs, delta, low_t):
    low_t[...] = query_t.astype(BF16)
    spread_heads(low_t, spread)
    for p in range(PAIRS):
        pair_rows(query.astype(BF16), p, pairs)
        pair_rows(grad.astype(BF16), p, grad_pairs)
    low_t[...] = grad_t.astype(BF16)
    spread_heads(low_t, grad_spread)
    for h in range(HEADS):
        head = slice(h * HEAD_SIZE, (h + 1) * HEAD_SIZE)
        delta[h : h + 1, :] = jnp.sum(low_t[head, :].astype(F32) * out[head, :], axis=0, keepdims=True)


def cross_back_kernel(
    bounds, own, self_t, w_out, gain, resid_two_grad, w_cross_out, cross_t, lse, window, code, low, high,
    w_query_t, w_key_t, w_value_t,
    resid_one_grad, window_grad, w_query_grad, w_key_grad, w_value_grad, w_out_grad, gain_grad,
    spread, grad_spread, pairs, grad_pairs, delta, bias, low_t, query_grad, key_sum, value_sum, normed_one, scale_one,
):
    self_low = self_t[...].astype(BF16)
    normed, scale = layer_norm(own[...].astype(F32) + dot_tn(self_low, w_out[...]))
    normed_one[...] = normed
    scale_one[...] = scale
    hidden_low = (normed * gain[...]).astype(BF16)
    branch_low = resid_two_grad[...].astype(BF16)
    prepare_back(
        dot_nt(hidden_low, w_query_t[...]), dot_nt(w_query_t[...], hidden_low),
        dot_nt(branch_low, w_cross_out[...]), dot_nt(w_cross_out[...], branch_low),
        cross_t, spread, grad_spread, pairs, grad_pairs, delta, low_t,
    )
    attend_back(
        bounds, window, code, low, high, w_key_t, w_value_t, spread, grad_spread, pairs, grad_pairs, lse, delta, bias,
        query_grad, window_grad, key_sum, value_sum,
    )
    w_key_grad[...] = key_sum[...].astype(BF16)
    w_value_grad[...] = value_sum[...].astype(BF16)
    query_low = (query_grad[...] * SCALE).astype(BF16)
    hidden_low = (normed_one[...] * gain[...]).astype(BF16)
    w_query_grad[...] = dot_nn(query_low, hidden_low).astype(BF16)
    grad_one = resid_two_grad[...] + dot_tn(query_low, w_query_t[...])
    grad, gain_sum = norm_back(grad_one, normed_one[...], scale_one[...], gain[...])
    gain_grad[...] = gain_sum
    resid_one_grad[...] = grad
    w_out_grad[...] = dot_nn(self_t[...].astype(BF16), grad.astype(BF16)).astype(BF16)


def self_back_kernel(
    bounds, own, resid_one_grad, w_out, self_t, lse, window, code, low, high, w_query_t, w_key_t, w_value_t,
    own_grad, window_grad, w_query_grad, w_key_grad, w_value_grad,
    spread, grad_spread, pairs, grad_pairs, delta, bias, low_t, query_grad, key_sum, value_sum,
):
    branch_low = resid_one_grad[...].astype(BF16)
    prepare_back(
        dot_nt(own[...], w_query_t[...]), dot_nt(w_query_t[...], own[...]),
        dot_nt(branch_low, w_out[...]), dot_nt(w_out[...], branch_low),
        self_t, spread, grad_spread, pairs, grad_pairs, delta, low_t,
    )
    attend_back(
        bounds, window, code, low, high, w_key_t, w_value_t, spread, grad_spread, pairs, grad_pairs, lse, delta, bias,
        query_grad, window_grad, key_sum, value_sum,
    )
    w_key_grad[...] = key_sum[...].astype(BF16)
    w_value_grad[...] = value_sum[...].astype(BF16)
    query_low = (query_grad[...] * SCALE).astype(BF16)
    w_query_grad[...] = dot_nn(query_low, own[...]).astype(BF16)
    own_grad[...] = (resid_one_grad[...] + dot_tn(query_low, w_query_t[...])).astype(BF16)


def call(kernel, outs, scratch, smem, *args):
    place = [pl.BlockSpec(memory_space=pltpu.SMEM)] * smem
    place += [pl.BlockSpec(memory_space=pltpu.VMEM)] * (len(args) - smem)
    return pl.pallas_call(
        kernel,
        out_shape=[jax.ShapeDtypeStruct(shape, kind) for shape, kind in outs],
        in_specs=place,
        out_specs=[pl.BlockSpec(memory_space=pltpu.VMEM)] * len(outs),
        scratch_shapes=[pltpu.VMEM(shape, kind) for shape, kind in scratch],
        compiler_params=pltpu.CompilerParams(vmem_limit_bytes=VMEM_LIMIT),
    )(*args)


def shifted(value, by):
    peers = lax.axis_size("seq")
    return lax.ppermute(value, "seq", [(i, i + by) for i in range(peers) if 0 <= i + by < peers])


def body(
    query_state, content, encoded, sentence_lengths, key_score, query_cut, w_query, w_key, w_value, w_out, gain_self,
    w_cross_query, w_cross_key, w_cross_value, w_cross_out, gain_cross, w_inner, w_outer, gain_final, out_grad,
):
    rows, width = query_state.shape
    slices = lax.axis_size("head")
    count = rows // slices
    wide = -(-(count + 2 * DOC_LEN) // CHUNK) * CHUNK
    spare = wide - count - 2 * DOC_LEN
    total_rows = rows * lax.axis_size("seq")
    seq, part = lax.axis_index("seq"), lax.axis_index("head")
    begin = seq * rows + part * count
    window_pos = begin - DOC_LEN + jnp.arange(wide, dtype=jnp.int32)

    ends = jnp.cumsum(sentence_lengths)
    passed = (window_pos[:, None] >= ends[None, :]).astype(jnp.int32)
    sentence = jnp.sum(passed, axis=1)
    first = jnp.sum(passed * sentence_lengths[None, :], axis=1)
    inside = (window_pos >= 0) & (window_pos < total_rows)
    score = lax.dynamic_slice_in_dim(jnp.pad(key_score, (DOC_LEN, DOC_LEN + spare)), begin, wide, 0)
    score = jnp.where(window_pos == first, -1, score)
    code = jnp.where(inside, sentence * CODES + score, -CODES).reshape(wide, 1)
    own_sentence = lax.slice_in_dim(sentence, DOC_LEN, DOC_LEN + count)
    own_cut = lax.dynamic_slice_in_dim(query_cut, begin, count, 0)
    low = (own_sentence * CODES - 1).reshape(1, count)
    high_self = (own_sentence * CODES + own_cut).reshape(1, count)
    high_cross = (own_sentence * CODES + CODES // 2).reshape(1, count)
    first_row = first[DOC_LEN]
    last_row = jnp.sum(jnp.where(jnp.arange(sentence_lengths.shape[0]) <= own_sentence[-1], sentence_lengths, 0))
    origin = begin - DOC_LEN
    bounds = jnp.stack([(first_row - origin) // CHUNK, (last_row - origin + CHUNK - 1) // CHUNK]).astype(jnp.int32)

    def gathered(weight):
        return lax.all_gather(weight, "head", axis=0, tiled=True)

    def window_of(value):
        below = shifted(value[rows - DOC_LEN :], 1)
        above = shifted(value[:DOC_LEN], -1)
        whole = jnp.concatenate([below, value, above, jnp.zeros((spare, width), value.dtype)], axis=0)
        return lax.dynamic_slice_in_dim(whole, part * count, wide, 0)

    own = lax.dynamic_slice_in_dim(query_state, part * count, count, 0)
    own_out_grad = lax.dynamic_slice_in_dim(out_grad, part * count, count, 0)
    w_query_t, w_key_t, w_value_t = gathered(w_query.T), gathered(w_key.T), gathered(w_value.T)
    content_window = window_of(content)
    w_out_all = gathered(w_out)
    w_cross_query_t = gathered(w_cross_query.T)
    w_cross_key_t, w_cross_value_t = gathered(w_cross_key.T), gathered(w_cross_value.T)
    encoded_window = window_of(encoded)
    w_cross_out_all = gathered(w_cross_out)
    w_inner_all = lax.all_gather(w_inner, "head", axis=0)
    w_outer_all = lax.all_gather(w_outer, "head", axis=0)
    gain_self, gain_cross, gain_final = (g.reshape(1, width) for g in (gain_self, gain_cross, gain_final))

    stats = [((HEADS * PAIR, count), BF16), ((CHUNK, count), F32), ((HEADS, count), F32), ((HEADS, count), F32), ((width, count), BF16)]
    self_t, lse_self = call(
        self_kernel, [((width, count), F32), ((HEADS, count), F32)], stats, 1,
        bounds, own, content_window, code, low, high_self, w_query_t, w_key_t, w_value_t,
    )
    hidden_one, cross_t, lse_cross = call(
        cross_kernel, [((count, width), F32), ((width, count), F32), ((HEADS, count), F32)], stats, 1,
        bounds, own, self_t, w_out_all, gain_self, encoded_window, code, low, high_cross,
        w_cross_query_t, w_cross_key_t, w_cross_value_t,
    )
    hidden_units = w_inner.shape[1]
    mixed, resid_two_grad, w_cross_out_grad, w_inner_grad, w_outer_grad, gain_cross_grad, gain_final_grad = call(
        ffn_kernel,
        [
            ((count, width), BF16), ((count, width), F32), ((width, width), BF16), ((slices, width, hidden_units), BF16),
            ((slices, hidden_units, width), BF16), ((1, width), F32), ((1, width), F32),
        ],
        [
            ((count, width), F32), ((count, width), BF16), ((slices, count, hidden_units), F32),
            ((slices, count, hidden_units), BF16), ((count, width), F32),
        ], 0,
        hidden_one, cross_t, w_cross_out_all, gain_cross, w_inner_all, w_outer_all, gain_final, own_out_grad,
    )
    back = [
        ((HEADS * PAIR, count), BF16), ((HEADS * PAIR, count), BF16), ((PAIRS, 2 * count, PAIR), BF16),
        ((PAIRS, 2 * count, PAIR), BF16), ((HEADS, count), F32), ((CHUNK, count), F32), ((width, count), BF16),
        ((width, count), F32), ((width, width), F32), ((width, width), F32),
    ]
    square = ((width, width), BF16)
    resid_one_grad, encoded_part, w_cross_query_grad, w_cross_key_grad, w_cross_value_grad, w_out_grad, gain_self_grad = call(
        cross_back_kernel,
        [((count, width), F32), ((wide, width), BF16), square, square, square, square, ((1, width), F32)],
        back + [((count, width), F32), ((count, 1), F32)], 1,
        bounds, own, self_t, w_out_all, gain_self, resid_two_grad, w_cross_out_all, cross_t, lse_cross,
        encoded_window, code, low, high_cross, w_cross_query_t, w_cross_key_t, w_cross_value_t,
    )
    own_grad, content_part, w_query_grad, w_key_grad, w_value_grad = call(
        self_back_kernel, [((count, width), BF16), ((wide, width), BF16), square, square, square], back, 1,
        bounds, own, resid_one_grad, w_out_all, self_t, lse_self,
        content_window, code, low, high_self, w_query_t, w_key_t, w_value_t,
    )

    def returned(grad):
        place = jnp.zeros((2 * DOC_LEN + rows + spare, width), BF16)
        place = lax.dynamic_update_slice_in_dim(place, grad, part * count, 0)
        below = shifted(place[:DOC_LEN], -1).astype(F32)
        above = shifted(place[DOC_LEN + rows : 2 * DOC_LEN + rows], 1).astype(F32)
        whole = place[DOC_LEN : DOC_LEN + rows].astype(F32)
        whole = whole + jnp.pad(below, ((rows - DOC_LEN, 0), (0, 0))) + jnp.pad(above, ((0, rows - DOC_LEN), (0, 0)))
        return lax.psum(whole.astype(BF16), "head").astype(F32)

    def summed(grad):
        return lax.psum(lax.psum_scatter(grad, "head", scatter_dimension=0, tiled=True), "seq").astype(F32)

    def summed_t(grad):
        return summed(grad).T

    def summed_columns(grad):
        return lax.psum(lax.psum_scatter(grad, "head", scatter_dimension=1, tiled=True), "seq").astype(F32)

    def summed_gain(grad):
        return lax.psum(grad.reshape(width), ("seq", "head"))

    return (
        lax.all_gather(mixed, "head", axis=0, tiled=True),
        lax.all_gather(own_grad, "head", axis=0, tiled=True).astype(F32),
        returned(content_part),
        returned(encoded_part),
        summed_t(w_query_grad),
        summed_columns(w_key_grad),
        summed_columns(w_value_grad),
        summed(w_out_grad),
        summed_gain(gain_self_grad),
        summed_t(w_cross_query_grad),
        summed_columns(w_cross_key_grad),
        summed_columns(w_cross_value_grad),
        summed(w_cross_out_grad),
        summed_gain(gain_cross_grad),
        lax.psum(lax.psum_scatter(w_inner_grad, "head", scatter_dimension=0, tiled=False), "seq").astype(F32),
        lax.psum(lax.psum_scatter(w_outer_grad, "head", scatter_dimension=0, tiled=False), "seq").astype(F32),
        summed_gain(gain_final_grad),
    )


def solution(mesh):
    rows, whole, columns, split = P("seq", None), P(), P(None, "head"), P("head", None)
    in_specs = (
        rows, rows, rows, whole, whole, whole, columns, columns, columns, split, whole,
        columns, columns, columns, split, whole, columns, split, whole, rows,
    )
    out_specs = (
        rows, rows, rows, rows, columns, columns, columns, split, whole,
        columns, columns, columns, split, whole, columns, split, whole,
    )
    return jax.shard_map(body, mesh=mesh, in_specs=in_specs, out_specs=out_specs, check_vma=False)
```

```python
from functools import partial
import math

import jax
import jax.numpy as jnp
from jax import lax
from jax.experimental import pallas as pl
from jax.experimental.pallas import tpu as pltpu
from jax.sharding import PartitionSpec as P

HEADS = 8
HEAD_SIZE = 64
PAIR = 2 * HEAD_SIZE
PAIRS = HEADS // 2
DOC_LEN = 1024
CHUNK = 256
EPS = 1e-05
NEG_BIG = -1e30
LOG2E = 1.4426950408889634
SCALE = 1.0 / math.sqrt(HEAD_SIZE)
SCORE_SCALE = SCALE * LOG2E
CODES = 128
BF16 = jnp.bfloat16
F32 = jnp.float32
VMEM_LIMIT = 60 << 20


def dot_nn(left, right):
    return lax.dot_general(left, right, (((1,), (0,)), ((), ())), preferred_element_type=F32)


def dot_nt(left, right):
    return lax.dot_general(left, right, (((1,), (1,)), ((), ())), preferred_element_type=F32)


def dot_tn(left, right):
    return lax.dot_general(left, right, (((0,), (0,)), ((), ())), preferred_element_type=F32)


def chunk_rows(c):
    return pl.ds(pl.multiple_of(c * CHUNK, CHUNK), CHUNK)


def layer_norm(resid):
    mean_row = jnp.mean(resid, axis=1, keepdims=True)
    centred = resid - mean_row
    var_row = jnp.mean(centred * centred, axis=1, keepdims=True)
    scale_row = lax.rsqrt(var_row + EPS)
    return centred * scale_row, scale_row


def norm_back(grad, normed, scale_row, gain):
    gain_grad = jnp.sum(grad * normed, axis=0, keepdims=True)
    scaled = grad * gain
    centre = jnp.mean(scaled, axis=1, keepdims=True)
    along = jnp.mean(scaled * normed, axis=1, keepdims=True)
    return scale_row * (scaled - centre - normed * along), gain_grad


def spread_heads(source, target):
    target[...] = jnp.zeros_like(target)
    for h in range(HEADS):
        row = h * PAIR + (h % 2) * HEAD_SIZE
        target[row : row + HEAD_SIZE, :] = source[h * HEAD_SIZE : (h + 1) * HEAD_SIZE, :]


def pair_rows(source, p, target):
    rows = source.shape[0]
    both = source[:, p * PAIR : (p + 1) * PAIR]
    lane = lax.broadcasted_iota(jnp.int32, both.shape, 1)
    zero = jnp.zeros_like(both)
    target[p, 0:rows, :] = jnp.where(lane < HEAD_SIZE, both, zero)
    target[p, rows : 2 * rows, :] = jnp.where(lane < HEAD_SIZE, zero, both)


MESH = pl.DeviceIdType.MESH


class Copies:
    def __init__(self, send, recv, local):
        self.send, self.recv, self.local = send, recv, local
        self.remotes, self.locals = 0, 0

    def remote(self, source, target, seq, part):
        k = self.remotes
        self.remotes += 1
        return pltpu.make_async_remote_copy(
            src_ref=source, dst_ref=target, send_sem=self.send.at[k], recv_sem=self.recv.at[k],
            device_id=(seq, part), device_id_type=MESH,
        )

    def own(self, source, target):
        k = self.locals
        self.locals += 1
        return pltpu.make_async_copy(source, target, self.local.at[k])


def greet(seq, part, peers, slices):
    barrier = pltpu.get_barrier_semaphore()
    for d in range(1, peers):
        pl.semaphore_signal(barrier, inc=1, device_id=(lax.rem(seq + d, peers), part), device_id_type=MESH)
    for d in range(1, slices):
        pl.semaphore_signal(barrier, inc=1, device_id=(seq, lax.rem(part + d, slices)), device_id_type=MESH)
    pl.semaphore_wait(barrier, peers - 1 + slices - 1)


def halo_sizes(part, count, rows):
    return max(0, DOC_LEN - part * count), max(0, (part + 1) * count + DOC_LEN - rows)


def start_kernel(
    peers, slices, count, content, encoded, pack_one, pack_two, pack_three,
    content_window, encoded_window, all_one, all_two, all_three, send, recv, local, zeros,
):
    seq, part = lax.axis_index("seq"), lax.axis_index("head")
    chip, core = seq // 2, lax.rem(seq, 2)
    chips = peers // 2
    sibling = chip * 2 + 1 - core
    rows = content.shape[0]
    span = count + 2 * DOC_LEN
    spare = content_window.shape[0] - span
    copies = Copies(send, recv, local)
    zeros[...] = jnp.zeros_like(zeros)
    greet(seq, part, peers, slices)
    waits = []

    def halo(source, window):
        for k in range(slices):
            below, above = halo_sizes(k, count, rows)
            low = max(0, k * count - DOC_LEN)
            inner = span - below - above
            mine = copies.own(source.at[pl.ds(low, inner)], window.at[pl.ds(below, inner)])
            tail = copies.own(zeros.at[pl.ds(0, spare)], window.at[pl.ds(span, spare)])
            up = down = fill_low = fill_high = None
            if below:
                up = copies.remote(source.at[pl.ds(rows - below, below)], window.at[pl.ds(0, below)], seq + 1, part)
                fill_low = copies.own(zeros.at[pl.ds(0, below)], window.at[pl.ds(0, below)])
            if above:
                down = copies.remote(source.at[pl.ds(0, above)], window.at[pl.ds(span - above, above)], seq - 1, part)
                fill_high = copies.own(zeros.at[pl.ds(0, above)], window.at[pl.ds(span - above, above)])
            here, first, last = part == k, seq == 0, seq == peers - 1

            def start(mine=mine, tail=tail, up=up, down=down, fill_low=fill_low, fill_high=fill_high, here=here):
                @pl.when(here)
                def _():
                    if up is not None:
                        pl.when(jnp.logical_not(last))(up.start)
                        pl.when(first)(fill_low.start)
                    if down is not None:
                        pl.when(jnp.logical_not(first))(down.start)
                        pl.when(last)(fill_high.start)
                    mine.start()
                    tail.start()

            def finish(mine=mine, tail=tail, up=up, down=down, fill_low=fill_low, fill_high=fill_high, here=here):
                @pl.when(here)
                def _():
                    if up is not None:
                        pl.when(jnp.logical_not(last))(up.wait_send)
                        pl.when(jnp.logical_not(first))(up.wait_recv)
                        pl.when(first)(fill_low.wait)
                    if down is not None:
                        pl.when(jnp.logical_not(first))(down.wait_send)
                        pl.when(jnp.logical_not(last))(down.wait_recv)
                        pl.when(last)(fill_high.wait)
                    mine.wait()
                    tail.wait()

            start()
            waits.append(finish)

    packs = ((pack_one, all_one), (pack_two, all_two), (pack_three, all_three))

    def piece(ref, owner, index, size):
        return ref.at[owner, pl.ds(pl.multiple_of(index * size, 16), size)]

    across = {}
    for n, (pack, whole) in enumerate(packs):
        size = pack.shape[0] // peers
        for d in range(1, slices):
            to = lax.rem(part + d, slices)
            source = pack.at[pl.ds(pl.multiple_of(seq * size, 16), size)]
            across[n, d] = copies.remote(source, piece(whole, part, seq, size), seq, to)
            across[n, d].start()
        mine = copies.own(pack, whole.at[part])
        mine.start()
        waits.append(mine.wait)
        if n == 0:
            halo(content, content_window)
    round_plane, to_sibling = {}, {}
    for n, (pack, whole) in enumerate(packs):
        size = pack.shape[0] // peers
        for d in range(1, slices):
            across[n, d].wait_recv()
            owner = lax.rem(part + slices - d, slices)
            got = piece(whole, owner, seq, size)
            for e in range(1, chips):
                round_plane[n, d, e] = copies.remote(got, got, lax.rem(chip + e, chips) * 2 + core, part)
                round_plane[n, d, e].start()
            to_sibling[n, d, 0] = copies.remote(got, got, sibling, part)
            to_sibling[n, d, 0].start()
    halo(encoded, encoded_window)
    for n, (pack, whole) in enumerate(packs):
        size = pack.shape[0] // peers
        for d in range(1, slices):
            owner = lax.rem(part + slices - d, slices)
            for e in range(1, chips):
                round_plane[n, d, e].wait_recv()
                got = piece(whole, owner, lax.rem(chip + chips - e, chips) * 2 + core, size)
                to_sibling[n, d, e] = copies.remote(got, got, sibling, part)
                to_sibling[n, d, e].start()
    for copy in to_sibling.values():
        copy.wait_recv()
    for copy in (*across.values(), *round_plane.values(), *to_sibling.values()):
        copy.wait_send()
    for wait in waits:
        wait()


def add_rows(target, source, target_at, source_at, size):
    step = 64 if size % 64 == 0 else 16

    def one(i, carry):
        to = pl.ds(pl.multiple_of(target_at + i * step, 16), step)
        by = pl.ds(pl.multiple_of(source_at + i * step, 16), step)
        target[to, :] = (target[to, :].astype(F32) + source[by, :].astype(F32)).astype(BF16)
        return carry

    lax.fori_loop(0, size // step, one, 0)


def end_kernel(
    peers, slices, count, blocks, parts, packs, plane_sums, outs, part_outs, pack_outs, scratch,
):
    seq, part = lax.axis_index("seq"), lax.axis_index("head")
    chip, core = seq // 2, lax.rem(seq, 2)
    chips = peers // 2
    sibling = chip * 2 + 1 - core
    rows = slices * count
    span = count + 2 * DOC_LEN
    send, recv, local = scratch[:3]
    copies = Copies(send, recv, local)
    first, last = seq == 0, seq == peers - 1
    start_line, end_line = part == 0, part == slices - 1
    greet(seq, part, peers, slices)
    sent = []

    def block(ref, index):
        return ref.at[pl.ds(pl.multiple_of(index * count, 16), count)]

    weight_scratch = scratch[3 : 3 + 5 * len(packs)]
    to_core, held = [], []
    for n, pack in enumerate(packs):
        half = pack.shape[1] // 2
        sibling_sum, mine = weight_scratch[5 * n : 5 * n + 2]
        copy = copies.remote(pack.at[:, pl.ds(pl.multiple_of((1 - core) * half, 16), half)], sibling_sum, sibling, part)
        copy.start()
        to_core.append(copy)
        keep = copies.own(pack.at[:, pl.ds(pl.multiple_of(core * half, 16), half)], mine)
        keep.start()
        held.append(keep)
        sent.append(copy)

    part_scratch = scratch[3 + 5 * len(packs) :]
    halos = []
    for n, grad in enumerate(parts):
        total, from_above, from_below = part_scratch[5 * n : 5 * n + 3]
        for k in range(slices):
            below, above = halo_sizes(k, count, rows)
            low = max(0, k * count - DOC_LEN)
            inner = span - below - above
            mine = copies.own(grad.at[pl.ds(below, inner)], total.at[pl.ds(low, inner)])
            down = up = None
            if below:
                down = copies.remote(grad.at[pl.ds(0, below)], from_above.at[pl.ds(0, below)], seq - 1, part)
            if above:
                up = copies.remote(grad.at[pl.ds(span - above, above)], from_below.at[pl.ds(0, above)], seq + 1, part)
            halos.append((n, k, below, above, low, inner, mine, down, up))

            @pl.when(part == k)
            def _(low=low, inner=inner, mine=mine, down=down, up=up, total=total):
                if down is not None:
                    pl.when(jnp.logical_not(first))(down.start)
                if up is not None:
                    pl.when(jnp.logical_not(last))(up.start)
                mine.start()
                if low:
                    total[0:low, :] = jnp.zeros((low, total.shape[1]), BF16)
                if low + inner < rows:
                    total[low + inner : rows, :] = jnp.zeros((rows - low - inner, total.shape[1]), BF16)

    def finish_halo(which):
        for n, k, below, above, low, inner, mine, down, up in halos:
            if n != which:
                continue
            total, from_above, from_below = part_scratch[5 * n : 5 * n + 3]

            @pl.when(part == k)
            def _(below=below, above=above, mine=mine, down=down, up=up, total=total, from_above=from_above, from_below=from_below):
                mine.wait()
                if down is not None:
                    pl.when(jnp.logical_not(first))(down.wait_send)

                    @pl.when(jnp.logical_not(last))
                    def _():
                        down.wait_recv()
                        add_rows(total, from_above, rows - below, 0, below)

                if up is not None:
                    pl.when(jnp.logical_not(last))(up.wait_send)

                    @pl.when(jnp.logical_not(first))
                    def _():
                        up.wait_recv()
                        add_rows(total, from_below, 0, 0, above)

    halves = 2 if slices <= 4 else 1
    sub = count // halves

    def unit_rows(ref, index, h):
        return ref.at[pl.ds(index * count + h * sub, sub)]

    def gather_rounds(out, me):
        rounds, flows = {}, ((1, slices - 1 - me), (-1, me))
        for sign, onward in flows:
            behind = me if sign > 0 else slices - 1 - me
            sends, waits = {}, {}
            for k in range(behind + 1):
                for h in range(halves):
                    ref = unit_rows(out, me - sign * k, h)
                    if onward:
                        sends[k * halves + h] = ref
                    if k:
                        waits[k * halves + h] = ref
            rounds[sign] = (sends, waits)
        return rounds

    def line_gather(out, me, sems):
        steps, ends = [], []
        ring = gather_rounds(out, me)
        copies_of = {}
        for sign in (1, -1):
            sends, waits = ring[sign]
            for i, ref in sends.items():
                copies_of[sign, i] = sems(sign, i, ref, ref, me + sign)

        def step(i):
            for sign in (1, -1):
                sends, waits = ring[sign]
                if i in waits:
                    sems(sign, i - halves, waits[i], waits[i], me).wait_recv()
                if i in sends:
                    if i:
                        copies_of[sign, i - 1].wait_send()
                    copies_of[sign, i].start()

        def finish():
            for sign in (1, -1):
                sends, _ = ring[sign]
                if sends:
                    copies_of[sign, max(sends)].wait_send()

        return [partial(step, i) for i in range(slices * halves)], finish

    def line_sum(total, ins, out, me, sems):
        units = (slices - 1) * halves
        copies_of, before = {}, {1: None, -1: None}

        def place(sign, i):
            b = slices - 1 - i // halves if sign > 0 else i // halves
            return b, unit_rows(total, b, i % halves)

        def step(r):
            for sign in (1, -1):
                depth = me if sign > 0 else slices - 1 - me
                i = r - depth
                if not 0 <= i < units:
                    continue
                b, ref = place(sign, i)
                passes = b > me if sign > 0 else b < me
                slot = ins[0 if sign > 0 else 1].at[i]
                if (passes or b == me) and depth:
                    sems(sign, i, slot, slot, me).wait_recv()
                    add_rows(total, slot, b * count + (i % halves) * sub, 0, sub)
                if passes:
                    if before[sign] is not None:
                        before[sign].wait_send()
                    before[sign] = sems(sign, i, ref, slot, me + sign)
                    before[sign].start()

        def finish():
            for sign in (1, -1):
                if before[sign] is not None:
                    before[sign].wait_send()

        def place_own():
            out[pl.ds(me * count, count), :] = total[pl.ds(me * count, count), :]

        return [partial(step, r) for r in range(units + slices - 1)], place_own, finish

    def semaphores(units):
        base = copies.remotes
        copies.remotes += 2 * units

        def make(sign, i, source, target, to):
            k = base + i + (0 if sign > 0 else units)
            return pltpu.make_async_remote_copy(
                src_ref=source, dst_ref=target, send_sem=send.at[k], recv_sem=recv.at[k],
                device_id=(seq, to), device_id_type=MESH,
            )

        return make

    def interleave(*lists):
        for k in range(max((len(steps) for steps in lists), default=0)):
            for steps in lists:
                if k < len(steps):
                    steps[k]()

    def at_place(run):
        for me in range(slices):
            pl.when(part == me)(partial(run, me))

    own_copies = []
    for own, out in zip(blocks, outs):
        mine = copies.own(own, block(out, part))
        mine.start()
        own_copies.append(mine)
    block_sems = [semaphores(slices * halves) for _ in outs]
    sum_sems = [semaphores(slices * halves) for _ in part_outs]
    after_sems = [semaphores(slices * halves) for _ in part_outs]

    to_chips = []
    for n, pack in enumerate(packs):
        half = pack.shape[1] // 2
        size = half // chips
        sibling_sum, mine, by_chip = weight_scratch[5 * n : 5 * n + 3]
        held[n].wait()
        to_core[n].wait_recv()

        def add_half(z, carry, sibling_sum=sibling_sum, mine=mine, half=half):
            add_rows(mine.at[z], sibling_sum.at[z], 0, 0, half)
            return carry

        lax.fori_loop(0, slices, add_half, 0)
        for e in range(1, chips):
            to = lax.rem(chip + e, chips)
            copy = copies.remote(mine.at[:, pl.ds(pl.multiple_of(to * size, 16), size)], by_chip.at[e - 1], to * 2 + core, part)
            copy.start()
            to_chips.append((n, e, copy))
            sent.append(copy)
    for mine in own_copies:
        mine.wait()
    for n in range(len(parts)):
        finish_halo(n)

    def first_section(me):
        lists, ends = [], []
        for out, sems in zip(outs, block_sems):
            steps, finish = line_gather(out, me, sems)
            lists.append(steps)
            ends.append(finish)
        for n, out in enumerate(part_outs):
            total, _, _, right_in, left_in = part_scratch[5 * n : 5 * n + 5]
            steps, place_own, finish = line_sum(total, (right_in, left_in), out, me, sum_sems[n])
            lists.append(steps)
            ends += [finish, place_own]
        interleave(*lists)
        for finish in ends:
            finish()

    at_place(first_section)

    to_slices = []

    def share(n, plane_sum, by_slice):
        for d in range(1, slices):
            to = lax.rem(part + d, slices)
            copy = copies.remote(plane_sum.at[to], by_slice.at[d - 1], seq, to)
            copy.start()
            to_slices.append((n, copy))
            sent.append(copy)

    for n, pack in enumerate(packs):
        half = pack.shape[1] // 2
        size = half // chips
        mine, by_chip, plane_sum, by_slice = weight_scratch[5 * n + 1 : 5 * n + 5]
        for m, e, copy in to_chips:
            if m == n:
                copy.wait_recv()

        def add_plane(i, carry, mine=mine, by_chip=by_chip, plane_sum=plane_sum, size=size):
            z, r = i // (size // 16), lax.rem(i, size // 16)
            at = pl.ds(pl.multiple_of(r * 16, 16), 16)
            value = mine[z, pl.ds(pl.multiple_of(chip * size + r * 16, 16), 16), :].astype(F32)
            for e in range(chips - 1):
                value = value + by_chip[e, z, at, :].astype(F32)
            plane_sum[z, at, :] = value.astype(BF16)
            return carry

        lax.fori_loop(0, slices * (size // 16), add_plane, 0)
        share(n, plane_sum, by_slice)
    plane_scratch = part_scratch[5 * len(parts) :]
    for n, summed in enumerate(plane_sums):
        plane_sum, by_slice = plane_scratch[2 * n : 2 * n + 2]
        keep = copies.own(summed, plane_sum)
        keep.start()
        keep.wait()
        share(len(packs) + n, plane_sum, by_slice)

    def piece_at(n, of_chip, of_core):
        size = pack_outs[n].shape[0] // peers
        index = of_core * chips + of_chip if n < len(packs) else of_chip * 2 + of_core
        return pl.multiple_of(index * size, 16), size

    round_plane, to_sibling = [], []

    def back_to_plane():
        for n, out in enumerate(pack_outs):
            if n < len(packs):
                plane_sum, by_slice = weight_scratch[5 * n + 3 : 5 * n + 5]
            else:
                plane_sum, by_slice = plane_scratch[2 * (n - len(packs)) : 2 * (n - len(packs)) + 2]
            start, size = piece_at(n, chip, core)
            for m, copy in to_slices:
                if m == n:
                    copy.wait_recv()

            def add_slices(r, carry, plane_sum=plane_sum, by_slice=by_slice, out=out, start=start):
                at = pl.ds(pl.multiple_of(r * 16, 16), 16)
                value = plane_sum[part, at, :].astype(F32)
                for d in range(slices - 1):
                    value = value + by_slice[d, at, :].astype(F32)
                out[pl.ds(pl.multiple_of(start + r * 16, 16), 16), :] = value.astype(BF16)
                return carry

            lax.fori_loop(0, size // 16, add_slices, 0)
            piece = out.at[pl.ds(start, size)]
            for e in range(1, chips):
                copy = copies.remote(piece, piece, lax.rem(chip + e, chips) * 2 + core, part)
                copy.start()
                round_plane.append((n, e, copy))
                sent.append(copy)
            copy = copies.remote(piece, piece, sibling, part)
            copy.start()
            round_plane.append((n, 0, copy))
            sent.append(copy)

    def second_section(me, low, high):
        lists, ends = [], []
        for out, sems in zip(part_outs, after_sems):
            steps, finish = line_gather(out, me, sems)
            lists.append(steps[low:high])
            if high >= len(steps):
                ends.append(finish)
        interleave(*lists)
        for finish in ends:
            finish()

    middle = slices * halves // 2 + 1
    at_place(lambda me: second_section(me, 0, middle))
    back_to_plane()
    at_place(lambda me: second_section(me, middle, slices * halves))
    for n, e, copy in round_plane:
        copy.wait_recv()
        if e:
            start, size = piece_at(n, lax.rem(chip + chips - e, chips), core)
            piece = pack_outs[n].at[pl.ds(start, size)]
            copy = copies.remote(piece, piece, sibling, part)
            copy.start()
            to_sibling.append(copy)
            sent.append(copy)
    for copy in to_sibling:
        copy.wait_recv()
    for copy in sent:
        copy.wait_send()


class Rows:
    def __init__(self, pack, index, size):
        self.pack, self.at = pack, slice(index * size, (index + 1) * size)

    def __getitem__(self, _):
        value = self.pack[:, self.at, :]
        return value.reshape(value.shape[0] * value.shape[1], value.shape[2])


def write_rows(pack, index, size, value):
    slices = pack.shape[0]
    pack[:, index * size : (index + 1) * size, :] = value.astype(BF16).reshape(slices, size, value.shape[1])


def write_pieces(pack, z, row, value):
    size = pack.shape[2]
    for i in range(value.shape[0] // size):
        pack[row // size + i, z] = value[i * size : (i + 1) * size, :].astype(BF16)


def mask_bias(code, low, high):
    return jnp.where((code >= low) & (code < high), 0.0, NEG_BIG).astype(F32)


def attend(bounds, window, code, low, high, w_key_t, w_value_t, spread, bias, top, total, out):
    top[...] = jnp.full_like(top, NEG_BIG)
    total[...] = jnp.zeros_like(total)
    out[...] = jnp.zeros_like(out)

    def step(c, carry):
        rows = window[chunk_rows(c), :]
        keys = dot_nt(rows, w_key_t[...]).astype(BF16)
        values_t = dot_nt(w_value_t[...], rows).astype(BF16)
        bias[...] = mask_bias(code[chunk_rows(c), :], low[...], high[...])
        for h in range(HEADS):
            p = h // 2
            scores = dot_nn(keys[:, p * PAIR : (p + 1) * PAIR], spread[h * PAIR : (h + 1) * PAIR, :])
            scores = scores * SCORE_SCALE + bias[...]
            before = top[h : h + 1, :]
            now = jnp.maximum(before, jnp.max(scores, axis=0, keepdims=True))
            weights = jnp.exp2(scores - now)
            shrink = jnp.exp2(before - now)
            top[h : h + 1, :] = now
            total[h : h + 1, :] = total[h : h + 1, :] * shrink + jnp.sum(weights, axis=0, keepdims=True)
            head = slice(h * HEAD_SIZE, (h + 1) * HEAD_SIZE)
            out[head, :] = out[head, :] * shrink + dot_nn(values_t[head, :], weights.astype(BF16))
        return carry

    lax.fori_loop(bounds[0], bounds[1], step, 0)
    for h in range(HEADS):
        head = slice(h * HEAD_SIZE, (h + 1) * HEAD_SIZE)
        out[head, :] = out[head, :] / total[h : h + 1, :]


def attend_back(
    bounds, window, code, low, high, w_key_t, w_value_t, spread, grad_spread, pairs, grad_pairs, lse, delta, bias,
    query_grad, window_grad, w_key_grad, w_value_grad,
):
    chunks = window.shape[0] // CHUNK
    count = spread.shape[1]
    query_grad[...] = jnp.zeros_like(query_grad)
    w_key_grad[...] = jnp.zeros_like(w_key_grad)
    w_value_grad[...] = jnp.zeros_like(w_value_grad)

    def clear(c, carry):
        window_grad[chunk_rows(c), :] = jnp.zeros((CHUNK, window_grad.shape[1]), window_grad.dtype)
        return carry

    lax.fori_loop(0, bounds[0], clear, 0)
    lax.fori_loop(bounds[1], chunks, clear, 0)

    def step(c, carry):
        rows = window[chunk_rows(c), :]
        keys = dot_nt(rows, w_key_t[...]).astype(BF16)
        keys_t = dot_nt(w_key_t[...], rows).astype(BF16)
        values = dot_nt(rows, w_value_t[...]).astype(BF16)
        bias[...] = mask_bias(code[chunk_rows(c), :], low[...], high[...])
        key_grads, value_grads = [], []
        for p in range(PAIRS):
            columns = slice(p * PAIR, (p + 1) * PAIR)
            probs, score_grads = [], []
            for h in (2 * p, 2 * p + 1):
                wide = slice(h * PAIR, (h + 1) * PAIR)
                head = slice(h * HEAD_SIZE, (h + 1) * HEAD_SIZE)
                scores = dot_nn(keys[:, columns], spread[wide, :])
                prob = jnp.exp2(scores * SCORE_SCALE + bias[...] - lse[h : h + 1, :])
                dprob = dot_nn(values[:, columns], grad_spread[wide, :])
                score_grad = (prob * (dprob - delta[h : h + 1, :])).astype(BF16)
                query_grad[head, :] += dot_nn(keys_t[head, :], score_grad)
                probs.append(prob.astype(BF16))
                score_grads.append(score_grad)
            if count % 128 == 0:
                key_grads.append(dot_nn(jnp.concatenate(score_grads, axis=1), pairs[p]))
                value_grads.append(dot_nn(jnp.concatenate(probs, axis=1), grad_pairs[p]))
            else:
                key_grads.append(dot_nn(score_grads[0], pairs[p, 0:count]) + dot_nn(score_grads[1], pairs[p, count:]))
                value_grads.append(dot_nn(probs[0], grad_pairs[p, 0:count]) + dot_nn(probs[1], grad_pairs[p, count:]))
        keys_low = (jnp.concatenate(key_grads, axis=1) * SCALE).astype(BF16)
        values_low = jnp.concatenate(value_grads, axis=1).astype(BF16)
        window_grad[chunk_rows(c), :] = (
            dot_nn(keys_low, w_key_t[...]) + dot_nn(values_low, w_value_t[...])
        ).astype(window_grad.dtype)
        w_key_grad[...] += dot_tn(rows, keys_low)
        w_value_grad[...] += dot_tn(rows, values_low)
        return carry

    lax.fori_loop(bounds[0], bounds[1], step, 0)


def self_kernel(cols, bounds, own, window, code, low, high, pack_one, out, lse, spread, bias, top, total, low_t):
    w_query_t, w_key_t, w_value_t = (Rows(pack_one, k, cols) for k in range(3))
    low_t[...] = dot_nt(w_query_t[...], own[...]).astype(BF16)
    spread_heads(low_t, spread)
    attend(bounds, window, code, low, high, w_key_t, w_value_t, spread, bias, top, total, out)
    lse[...] = top[...] + jnp.log2(total[...])


def cross_kernel(
    cols, bounds, own, attn_t, gain, window, code, low, high, pack_two, hidden, out, lse, spread, bias, top, total, low_t,
):
    w_out, w_query_t, w_key_t, w_value_t = (Rows(pack_two, k, cols) for k in range(4))
    branch = dot_tn(attn_t[...].astype(BF16), w_out[...])
    normed, _ = layer_norm(own[...].astype(F32) + branch)
    hidden[...] = normed * gain[...]
    low_t[...] = dot_nt(w_query_t[...], hidden[...].astype(BF16)).astype(BF16)
    spread_heads(low_t, spread)
    attend(bounds, window, code, low, high, w_key_t, w_value_t, spread, bias, top, total, out)
    lse[...] = top[...] + jnp.log2(total[...])


def ffn_kernel(
    cols, hidden_one, cross_t, pack_two, gain_cross, pack_three, gain_final, out_grad,
    mixed, resid_grad, w_out_grad, grad_three_pack, gain_cross_grad, gain_final_grad,
    normed_two, hidden_two_low, slope, active, sum_ffn,
):
    slices, units = pack_three.shape[0], pack_three.shape[1] // 2
    w_out = Rows(pack_two, 4, cols)
    cross_low = cross_t[...].astype(BF16)
    normed, scale_two = layer_norm(hidden_one[...] + dot_tn(cross_low, w_out[...]))
    normed_two[...] = normed
    hidden_two = normed * gain_cross[...]
    hidden_two_low[...] = hidden_two.astype(BF16)
    sum_ffn[...] = hidden_two
    for z in range(slices):
        inner = dot_nt(hidden_two_low[...], pack_three[z, 0:units, :])
        below = 0.5 * (1.0 + lax.erf(inner * math.sqrt(0.5)))
        slope[z] = below + inner * (jnp.exp2(inner * inner * (-0.5 * LOG2E)) * (1.0 / math.sqrt(2.0 * math.pi)))
        active[z] = (inner * below).astype(BF16)
        sum_ffn[...] += dot_nn(active[z], pack_three[z, units:, :])
    normed_three, scale_three = layer_norm(sum_ffn[...])
    mixed[...] = (normed_three * gain_final[...]).astype(BF16)
    grad_three, gain_grad = norm_back(out_grad[...].astype(F32), normed_three, scale_three, gain_final[...])
    gain_final_grad[...] = gain_grad
    ffn_low = grad_three.astype(BF16)
    sum_ffn[...] = grad_three
    for z in range(slices):
        write_pieces(grad_three_pack, z, units, dot_tn(active[z], ffn_low))
        inner_low = (dot_nt(ffn_low, pack_three[z, units:, :]) * slope[z]).astype(BF16)
        write_pieces(grad_three_pack, z, 0, dot_tn(inner_low, hidden_two_low[...]))
        sum_ffn[...] += dot_nn(inner_low, pack_three[z, 0:units, :])
    grad, gain_grad = norm_back(sum_ffn[...], normed_two[...], scale_two, gain_cross[...])
    gain_cross_grad[...] = gain_grad
    resid_grad[...] = grad
    w_out_grad[...] = dot_nn(cross_low, grad.astype(BF16)).astype(BF16)


def prepare_back(query, query_t, grad, grad_t, out, spread, grad_spread, pairs, grad_pairs, delta, low_t):
    low_t[...] = query_t.astype(BF16)
    spread_heads(low_t, spread)
    for p in range(PAIRS):
        pair_rows(query.astype(BF16), p, pairs)
        pair_rows(grad.astype(BF16), p, grad_pairs)
    low_t[...] = grad_t.astype(BF16)
    spread_heads(low_t, grad_spread)
    for h in range(HEADS):
        head = slice(h * HEAD_SIZE, (h + 1) * HEAD_SIZE)
        delta[h : h + 1, :] = jnp.sum(low_t[head, :].astype(F32) * out[head, :], axis=0, keepdims=True)


def cross_back_kernel(
    cols, bounds, own, self_t, gain, resid_two_grad, cross_t, lse, window, code, low, high, pack_two,
    w_cross_out_grad, gain_cross_grad, gain_final_grad, resid_one_grad, window_grad, grad_two_pack,
    spread, grad_spread, pairs, grad_pairs, delta, bias, low_t, query_grad, key_sum, value_sum, normed_one, scale_one,
):
    w_out, w_query_t, w_key_t, w_value_t, w_cross_out = (Rows(pack_two, k, cols) for k in range(5))
    self_low = self_t[...].astype(BF16)
    normed, scale = layer_norm(own[...].astype(F32) + dot_tn(self_low, w_out[...]))
    normed_one[...] = normed
    scale_one[...] = scale
    hidden_low = (normed * gain[...]).astype(BF16)
    branch_low = resid_two_grad[...].astype(BF16)
    prepare_back(
        dot_nt(hidden_low, w_query_t[...]), dot_nt(w_query_t[...], hidden_low),
        dot_nt(branch_low, w_cross_out[...]), dot_nt(w_cross_out[...], branch_low),
        cross_t, spread, grad_spread, pairs, grad_pairs, delta, low_t,
    )
    attend_back(
        bounds, window, code, low, high, w_key_t, w_value_t, spread, grad_spread, pairs, grad_pairs, lse, delta, bias,
        query_grad, window_grad, key_sum, value_sum,
    )
    query_low = (query_grad[...] * SCALE).astype(BF16)
    hidden_low = (normed_one[...] * gain[...]).astype(BF16)
    grad_one = resid_two_grad[...] + dot_tn(query_low, w_query_t[...])
    grad, gain_sum = norm_back(grad_one, normed_one[...], scale_one[...], gain[...])
    resid_one_grad[...] = grad
    write_rows(grad_two_pack, 0, cols, dot_nn(self_t[...].astype(BF16), grad.astype(BF16)))
    write_rows(grad_two_pack, 1, cols, dot_nn(query_low, hidden_low))
    write_rows(grad_two_pack, 2, cols, key_sum[...].T)
    write_rows(grad_two_pack, 3, cols, value_sum[...].T)
    write_rows(grad_two_pack, 4, cols, w_cross_out_grad[...])
    slices, rows, width = grad_two_pack.shape
    gains = jnp.concatenate([gain_sum, gain_cross_grad[...], gain_final_grad[...], jnp.zeros((13, width), F32)], axis=0)
    for z in range(slices):
        grad_two_pack[z, 5 * cols : 5 * cols + 16, :] = gains.astype(BF16)
        if rows > 5 * cols + 16:
            grad_two_pack[z, 5 * cols + 16 :, :] = jnp.zeros((rows - 5 * cols - 16, width), BF16)


def self_back_kernel(
    cols, bounds, own, resid_one_grad, pack_two, self_t, lse, window, code, low, high, pack_one,
    own_grad, window_grad, grad_one_pack,
    spread, grad_spread, pairs, grad_pairs, delta, bias, low_t, query_grad, key_sum, value_sum,
):
    w_query_t, w_key_t, w_value_t = (Rows(pack_one, k, cols) for k in range(3))
    w_out = Rows(pack_two, 0, cols)
    branch_low = resid_one_grad[...].astype(BF16)
    prepare_back(
        dot_nt(own[...], w_query_t[...]), dot_nt(w_query_t[...], own[...]),
        dot_nt(branch_low, w_out[...]), dot_nt(w_out[...], branch_low),
        self_t, spread, grad_spread, pairs, grad_pairs, delta, low_t,
    )
    attend_back(
        bounds, window, code, low, high, w_key_t, w_value_t, spread, grad_spread, pairs, grad_pairs, lse, delta, bias,
        query_grad, window_grad, key_sum, value_sum,
    )
    query_low = (query_grad[...] * SCALE).astype(BF16)
    write_rows(grad_one_pack, 0, cols, dot_nn(query_low, own[...]))
    write_rows(grad_one_pack, 1, cols, key_sum[...].T)
    write_rows(grad_one_pack, 2, cols, value_sum[...].T)
    slices, rows, width = grad_one_pack.shape
    if rows > 3 * cols:
        grad_one_pack[:, 3 * cols :, :] = jnp.zeros((slices, rows - 3 * cols, width), BF16)
    own_grad[...] = (resid_one_grad[...] + dot_tn(query_low, w_query_t[...])).astype(BF16)


def call(kernel, outs, scratch, smem, *args, micros=20):
    place = [pl.BlockSpec(memory_space=pltpu.SMEM)] * smem
    place += [pl.BlockSpec(memory_space=pltpu.VMEM)] * (len(args) - smem)
    return pl.pallas_call(
        kernel,
        out_shape=[jax.ShapeDtypeStruct(shape, kind) for shape, kind in outs],
        in_specs=place,
        out_specs=[pl.BlockSpec(memory_space=pltpu.VMEM)] * len(outs),
        scratch_shapes=[pltpu.VMEM(shape, kind) for shape, kind in scratch],
        compiler_params=pltpu.CompilerParams(vmem_limit_bytes=VMEM_LIMIT),
        cost_estimate=pl.CostEstimate(flops=micros * 10**9, bytes_accessed=micros * 10**6, transcendentals=0),
    )(*args)


def padded(size, unit):
    return -(-size // unit) * unit


def talk(kernel, outs, out_space, scratch, copies, number, *args):
    return pl.pallas_call(
        kernel,
        out_shape=[jax.ShapeDtypeStruct(shape, kind) for shape, kind in outs],
        in_specs=[pl.BlockSpec(memory_space=pl.ANY)] * len(args),
        out_specs=[pl.BlockSpec(memory_space=out_space)] * len(outs),
        scratch_shapes=[pltpu.SemaphoreType.DMA((n,)) for n in (copies[0], copies[0], copies[1])] + [pltpu.VMEM(shape, kind) for shape, kind in scratch],
        compiler_params=pltpu.CompilerParams(vmem_limit_bytes=VMEM_LIMIT, collective_id=number, has_side_effects=True),
        cost_estimate=pl.CostEstimate(flops=80 * 10**9, bytes_accessed=80 * 10**6, transcendentals=0),
    )(*args)


def body(
    query_state, content, encoded, sentence_lengths, key_score, query_cut, w_query, w_key, w_value, w_out, gain_self,
    w_cross_query, w_cross_key, w_cross_value, w_cross_out, gain_cross, w_inner, w_outer, gain_final, out_grad,
):
    rows, width = query_state.shape
    slices = lax.axis_size("head")
    count = rows // slices
    wide = -(-(count + 2 * DOC_LEN) // CHUNK) * CHUNK
    spare = wide - count - 2 * DOC_LEN
    total_rows = rows * lax.axis_size("seq")
    seq, part = lax.axis_index("seq"), lax.axis_index("head")
    begin = seq * rows + part * count
    window_pos = begin - DOC_LEN + jnp.arange(wide, dtype=jnp.int32)

    ends = jnp.cumsum(sentence_lengths)
    passed = (window_pos[:, None] >= ends[None, :]).astype(jnp.int32)
    sentence = jnp.sum(passed, axis=1)
    first = jnp.sum(passed * sentence_lengths[None, :], axis=1)
    inside = (window_pos >= 0) & (window_pos < total_rows)
    score = lax.dynamic_slice_in_dim(jnp.pad(key_score, (DOC_LEN, DOC_LEN + spare)), begin, wide, 0)
    score = jnp.where(window_pos == first, -1, score)
    code = jnp.where(inside, sentence * CODES + score, -CODES).reshape(wide, 1)
    own_sentence = lax.slice_in_dim(sentence, DOC_LEN, DOC_LEN + count)
    own_cut = lax.dynamic_slice_in_dim(query_cut, begin, count, 0)
    low = (own_sentence * CODES - 1).reshape(1, count)
    high_self = (own_sentence * CODES + own_cut).reshape(1, count)
    high_cross = (own_sentence * CODES + CODES // 2).reshape(1, count)
    first_row = first[DOC_LEN]
    last_row = jnp.sum(jnp.where(jnp.arange(sentence_lengths.shape[0]) <= own_sentence[-1], sentence_lengths, 0))
    origin = begin - DOC_LEN
    bounds = jnp.stack([(first_row - origin) // CHUNK, (last_row - origin + CHUNK - 1) // CHUNK]).astype(jnp.int32)

    own = lax.dynamic_slice_in_dim(query_state, part * count, count, 0)
    own_out_grad = lax.dynamic_slice_in_dim(out_grad, part * count, count, 0)
    gain_self, gain_cross, gain_final = (g.reshape(1, width) for g in (gain_self, gain_cross, gain_final))

    peers = lax.axis_size("seq")
    chips = peers // 2
    cols, units = w_query.shape[1], w_inner.shape[1]
    unit = 16 * peers
    sizes = [padded(n, unit) for n in (3 * cols, 5 * cols, 2 * units)]
    grad_sizes = [sizes[0], padded(5 * cols + 16, unit), sizes[2]]

    def packed(size, *weights):
        used = sum(w.shape[0] for w in weights)
        return jnp.concatenate(list(weights) + [jnp.zeros((size - used, width), BF16)] * (size > used), axis=0)

    packs = (
        packed(sizes[0], w_query.T, w_key.T, w_value.T),
        packed(sizes[1], w_out, w_cross_query.T, w_cross_key.T, w_cross_value.T, w_cross_out),
        packed(sizes[2], w_inner.T, w_outer),
    )
    start_copies = 3 * (slices - 1) * (2 * chips) + 4 * slices
    content_window, encoded_window, pack_one, pack_two, pack_three = talk(
        partial(start_kernel, peers, slices, count),
        [((wide, width), BF16)] * 2 + [((slices, n, width), BF16) for n in sizes], pltpu.VMEM,
        [((DOC_LEN, width), BF16)], (start_copies, 8 * slices + 8), 0, content, encoded, *packs,
    )

    def split_refs(kernel, ins, outs):
        def run(*refs):
            return kernel(refs[:ins], refs[ins : ins + outs], refs[ins + outs :])
        return run

    stats = [((HEADS * PAIR, count), BF16), ((CHUNK, count), F32), ((HEADS, count), F32), ((HEADS, count), F32), ((width, count), BF16)]
    self_t, lse_self = call(
        partial(self_kernel, cols), [((width, count), F32), ((HEADS, count), F32)], stats, 1,
        bounds, own, content_window, code, low, high_self, pack_one,
    )
    hidden_one, cross_t, lse_cross = call(
        partial(cross_kernel, cols), [((count, width), F32), ((width, count), F32), ((HEADS, count), F32)], stats, 1,
        bounds, own, self_t, gain_self, encoded_window, code, low, high_cross, pack_two,
    )
    mixed, resid_two_grad, w_cross_out_grad, grads_three, gain_cross_grad, gain_final_grad = call(
        partial(ffn_kernel, cols),
        [
            ((count, width), BF16), ((count, width), F32), ((width, width), BF16), ((peers, slices, grad_sizes[2] // peers, width), BF16),
            ((1, width), F32), ((1, width), F32),
        ],
        [
            ((count, width), F32), ((count, width), BF16), ((slices, count, units), F32),
            ((slices, count, units), BF16), ((count, width), F32),
        ], 0,
        hidden_one, cross_t, pack_two, gain_cross, pack_three, gain_final, own_out_grad,
    )
    back = [
        ((HEADS * PAIR, count), BF16), ((HEADS * PAIR, count), BF16), ((PAIRS, 2 * count, PAIR), BF16),
        ((PAIRS, 2 * count, PAIR), BF16), ((HEADS, count), F32), ((CHUNK, count), F32), ((width, count), BF16),
        ((width, count), F32), ((width, width), F32), ((width, width), F32),
    ]
    resid_one_grad, encoded_part, grads_two = call(
        partial(cross_back_kernel, cols),
        [((count, width), F32), ((wide, width), BF16), ((slices, grad_sizes[1], width), BF16)],
        back + [((count, width), F32), ((count, 1), F32)], 1,
        bounds, own, self_t, gain_self, resid_two_grad, cross_t, lse_cross, encoded_window, code, low, high_cross, pack_two,
        w_cross_out_grad, gain_cross_grad, gain_final_grad, micros=35,
    )
    own_grad, content_part, grads_one = call(
        partial(self_back_kernel, cols),
        [((count, width), BF16), ((wide, width), BF16), ((slices, grad_sizes[0], width), BF16)], back, 1,
        bounds, own, resid_one_grad, pack_two, self_t, lse_self, content_window, code, low, high_self, pack_one, micros=35,
    )

    mixed = lax.all_gather(mixed, "head", axis=0, tiled=True)
    plane_three = lax.psum_scatter(grads_three, "seq", scatter_dimension=0, tiled=True).reshape(grads_three.shape[1:])
    blocks, parts, grads, planes = [own_grad], [content_part, encoded_part], [grads_one, grads_two], [plane_three]
    weight_scratch = []
    for n in grad_sizes[: len(grads)]:
        half, size = n // 2, n // 2 // chips
        weight_scratch += [
            ((slices, half, width), BF16), ((slices, half, width), BF16), ((chips - 1, slices, size, width), BF16),
            ((slices, size, width), BF16), ((slices - 1, size, width), BF16),
        ]
    halves = 2 if slices <= 4 else 1
    units_in = (slices - 1) * halves
    part_scratch = [
        ((rows, width), BF16), ((DOC_LEN, width), BF16), ((DOC_LEN, width), BF16),
        ((units_in, count // halves, width), BF16), ((units_in, count // halves, width), BF16),
    ] * len(parts)
    plane_scratch = []
    for n in grad_sizes[len(grads) :]:
        plane_scratch += [((slices, n // peers, width), BF16), ((slices - 1, n // peers, width), BF16)]
    ins, outs = (len(blocks), len(parts), len(grads), len(planes)), (len(blocks), len(parts), len(grad_sizes))

    def end(refs, out_refs, scratch):
        a, b, c = ins[0], ins[0] + ins[1], sum(ins[:3])
        end_kernel(
            peers, slices, count, refs[:a], refs[a:b], refs[b:c], refs[c:], out_refs[: outs[0]],
            out_refs[outs[0] : outs[0] + outs[1]], out_refs[outs[0] + outs[1] :], scratch,
        )

    end_copies = len(grad_sizes) * (1 + 3 * (chips - 1) + slices) + len(parts) * 2 * slices + (len(blocks) + 2 * len(parts)) * 2 * slices * halves
    results = talk(
        split_refs(end, sum(ins), sum(outs)),
        [((rows, width), BF16)] * (len(blocks) + len(parts)) + [((n, width), BF16) for n in grad_sizes], pltpu.VMEM,
        weight_scratch + part_scratch + plane_scratch, (end_copies, 8 * slices + 8), 1, *blocks, *parts, *grads, *planes,
    )
    query_state_grad, content_grad, encoded_grad, sum_one, sum_two, sum_three = results

    def rows_of(pack, k):
        return pack[k * cols : (k + 1) * cols].astype(F32)

    gains = sum_two[5 * cols : 5 * cols + 16].astype(F32)
    return (
        mixed,
        query_state_grad.astype(F32),
        content_grad.astype(F32),
        encoded_grad.astype(F32),
        rows_of(sum_one, 0).T,
        rows_of(sum_one, 1).T,
        rows_of(sum_one, 2).T,
        rows_of(sum_two, 0),
        gains[0],
        rows_of(sum_two, 1).T,
        rows_of(sum_two, 2).T,
        rows_of(sum_two, 3).T,
        rows_of(sum_two, 4),
        gains[1],
        sum_three[:units].astype(F32).T,
        sum_three[units : 2 * units].astype(F32),
        gains[2],
    )


def solution(mesh):
    rows, whole, columns, split = P("seq", None), P(), P(None, "head"), P("head", None)
    in_specs = (
        rows, rows, rows, whole, whole, whole, columns, columns, columns, split, whole,
        columns, columns, columns, split, whole, columns, split, whole, rows,
    )
    out_specs = (
        rows, rows, rows, rows, columns, columns, columns, split, whole,
        columns, columns, columns, split, whole, columns, split, whole,
    )
    return jax.shard_map(body, mesh=mesh, in_specs=in_specs, out_specs=out_specs, check_vma=False)
```

```python
from functools import partial
import math

import jax
import jax.numpy as jnp
from jax import lax
from jax.experimental import pallas as pl
from jax.experimental.pallas import tpu as pltpu
from jax.sharding import PartitionSpec as P

HEADS = 8
HEAD_SIZE = 64
PAIR = 2 * HEAD_SIZE
PAIRS = HEADS // 2
DOC_LEN = 1024
CHUNK = 528
LANES = 128
EPS = 1e-05
NEG_BIG = -1e30
LOG2E = 1.4426950408889634
SCALE = 1.0 / math.sqrt(HEAD_SIZE)
SCORE_SCALE = SCALE * LOG2E
CODES = 128
BF16 = jnp.bfloat16
F32 = jnp.float32
VMEM_LIMIT = 60 << 20


def dot_nn(left, right):
    return lax.dot_general(left, right, (((1,), (0,)), ((), ())), preferred_element_type=F32)


def dot_nt(left, right):
    return lax.dot_general(left, right, (((1,), (1,)), ((), ())), preferred_element_type=F32)


def dot_tn(left, right):
    return lax.dot_general(left, right, (((0,), (0,)), ((), ())), preferred_element_type=F32)


def chunk_loops(bounds, count, step):
    start = bounds[0, 0] // 16 * 16
    chunks = (bounds[0, 1] - start + CHUNK - 1) // CHUNK

    def loop(low, high, lanes):
        def one(c, carry):
            step(pl.ds(pl.multiple_of(start + c * CHUNK, 16), CHUNK), lanes)
            return carry

        lax.fori_loop(low, high, one, 0)

    if count != 3 * LANES:
        return loop(0, chunks, (0, count))
    left = jnp.clip((bounds[0, 2] - start) // CHUNK, 0, chunks)
    right = jnp.clip((bounds[0, 3] - start + CHUNK - 1) // CHUNK, left, chunks)
    loop(0, left, (0, 2 * LANES))
    loop(left, right, (0, count))
    loop(right, chunks, (LANES, count))


def layer_norm(resid):
    mean_row = jnp.mean(resid, axis=1, keepdims=True)
    centred = resid - mean_row
    var_row = jnp.mean(centred * centred, axis=1, keepdims=True)
    scale_row = lax.rsqrt(var_row + EPS)
    return centred * scale_row, scale_row


def norm_back(grad, normed, scale_row, gain):
    gain_grad = jnp.sum(grad * normed, axis=0, keepdims=True)
    scaled = grad * gain
    centre = jnp.mean(scaled, axis=1, keepdims=True)
    along = jnp.mean(scaled * normed, axis=1, keepdims=True)
    return scale_row * (scaled - centre - normed * along), gain_grad


def spread_heads(source, target):
    target[...] = jnp.zeros_like(target)
    for h in range(HEADS):
        row = h * PAIR + (h % 2) * HEAD_SIZE
        target[row : row + HEAD_SIZE, :] = source[h * HEAD_SIZE : (h + 1) * HEAD_SIZE, :]


def pair_rows(source, p, target):
    rows = source.shape[0]
    both = source[:, p * PAIR : (p + 1) * PAIR]
    lane = lax.broadcasted_iota(jnp.int32, both.shape, 1)
    zero = jnp.zeros_like(both)
    target[p, 0:rows, :] = jnp.where(lane < HEAD_SIZE, both, zero)
    target[p, rows : 2 * rows, :] = jnp.where(lane < HEAD_SIZE, zero, both)


MESH = pl.DeviceIdType.MESH


class Copies:
    def __init__(self, send, recv, local):
        self.send, self.recv, self.local = send, recv, local
        self.remotes, self.locals = 0, 0

    def remote(self, source, target, seq, part):
        k = self.remotes
        self.remotes += 1
        return pltpu.make_async_remote_copy(
            src_ref=source, dst_ref=target, send_sem=self.send.at[k], recv_sem=self.recv.at[k],
            device_id=(seq, part), device_id_type=MESH,
        )

    def own(self, source, target):
        k = self.locals
        self.locals += 1
        return pltpu.make_async_copy(source, target, self.local.at[k])


def greet(seq, part, peers, slices):
    barrier = pltpu.get_barrier_semaphore()
    for d in range(1, peers):
        pl.semaphore_signal(barrier, inc=1, device_id=(lax.rem(seq + d, peers), part), device_id_type=MESH)
    for d in range(1, slices):
        pl.semaphore_signal(barrier, inc=1, device_id=(seq, lax.rem(part + d, slices)), device_id_type=MESH)
    pl.semaphore_wait(barrier, peers - 1 + slices - 1)


def halo_sizes(part, count, rows):
    return max(0, DOC_LEN - part * count), max(0, (part + 1) * count + DOC_LEN - rows)


def put_rows(whole, part, row, ref, flip):
    value = ref[...]
    if flip:
        value = value.astype(F32).T.astype(BF16)
    whole[part, row : row + value.shape[0], :] = value


def pad_rows(whole, part, row):
    if row < whole.shape[1]:
        whole[part, row:, :] = jnp.zeros((whole.shape[1] - row, whole.shape[2]), BF16)


def find_sentences(begin, count, total_rows, lengths, score, cut, code, low, high_self, high_cross, bounds, blocks_code):
    blocks, lanes = score.shape
    pos = lax.broadcasted_iota(jnp.int32, (blocks, lanes), 0) * lanes + lax.broadcasted_iota(jnp.int32, (blocks, lanes), 1)
    pos = pos + (begin - DOC_LEN)
    own_pos = lax.broadcasted_iota(jnp.int32, (1, count), 1) + begin
    zero = jnp.zeros((blocks, lanes), jnp.int32)
    last_pos = begin + count - 1

    def one(s, carry):
        start, sentence, first, own_sentence, first_row, last_row, late_first, early_last = carry
        size = lengths[0, s]
        end = start + size
        passed = pos >= end
        sentence = sentence + jnp.where(passed, 1, 0)
        first = first + jnp.where(passed, size, 0)
        own_sentence = own_sentence + jnp.where(own_pos >= end, 1, 0)
        first_row = first_row + jnp.where(begin >= end, size, 0)
        last_row = last_row + jnp.where(last_pos >= start, size, 0)
        late_first = late_first + jnp.where(begin + late >= end, size, 0)
        early_last = early_last + jnp.where(begin + early >= start, size, 0)
        return end, sentence, first, own_sentence, first_row, last_row, late_first, early_last

    none = lengths[0, 0] * 0
    late, early = 2 * LANES, LANES - 1
    carry = (none, zero, zero, jnp.zeros((1, count), jnp.int32), none, none, none, none)
    _, sentence, first, own_sentence, first_row, last_row, late_first, early_last = lax.fori_loop(0, lengths.shape[1], one, carry)
    shown = jnp.where(pos == first, -1, score[...])
    inside = jnp.logical_and(pos >= 0, pos < total_rows)
    blocks_code[0:blocks, :] = jnp.where(inside, sentence * CODES + shown, -CODES).astype(F32)
    for b in range(0, blocks, 8):
        turned = blocks_code[b : b + 8, :].T
        for j in range(min(8, blocks - b)):
            code[(b + j) * lanes : (b + j + 1) * lanes, :] = turned[:, j : j + 1]
    low[...] = (own_sentence * CODES - 1).astype(F32)
    high_self[...] = (own_sentence * CODES + cut[...]).astype(F32)
    high_cross[...] = (own_sentence * CODES + CODES // 2).astype(F32)
    origin = begin - DOC_LEN
    bounds[0, 0] = first_row - origin
    bounds[0, 1] = last_row - origin
    bounds[0, 2] = late_first - origin
    bounds[0, 3] = early_last - origin


def start_kernel(
    peers, slices, count, content, encoded, query_state, out_grad, w_query, w_key, w_value, w_out,
    w_cross_query, w_cross_key, w_cross_value, w_cross_out, lengths, score, cut,
    content_window, encoded_window, all_one, all_two, own, own_out_grad, code, low, high_self, high_cross, bounds,
    send, recv, local, zeros, blocks_code,
):
    seq, part = lax.axis_index("seq"), lax.axis_index("head")
    chip, core = seq // 2, lax.rem(seq, 2)
    chips = peers // 2
    sibling = chip * 2 + 1 - core
    rows = content.shape[0]
    span = count + 2 * DOC_LEN
    spare = content_window.shape[0] - span
    copies = Copies(send, recv, local)
    cols = w_query.shape[1]
    for k, (ref, flip) in enumerate(((w_query, True), (w_key, True), (w_value, True))):
        put_rows(all_one, part, k * cols, ref, flip)
    pad_rows(all_one, part, 3 * cols)
    greet(seq, part, peers, slices)
    waits = []
    for source, target in ((query_state, own), (out_grad, own_out_grad)):
        mine = copies.own(source.at[pl.ds(pl.multiple_of(part * count, 16), count)], target)
        mine.start()
        waits.append(mine.wait)

    def halo(source, window):
        for k in range(slices):
            below, above = halo_sizes(k, count, rows)
            low = max(0, k * count - DOC_LEN)
            inner = span - below - above
            mine = copies.own(source.at[pl.ds(low, inner)], window.at[pl.ds(below, inner)])
            tail = copies.own(zeros.at[pl.ds(0, spare)], window.at[pl.ds(span, spare)])
            up = down = fill_low = fill_high = None
            if below:
                up = copies.remote(source.at[pl.ds(rows - below, below)], window.at[pl.ds(0, below)], seq + 1, part)
                fill_low = copies.own(zeros.at[pl.ds(0, below)], window.at[pl.ds(0, below)])
            if above:
                down = copies.remote(source.at[pl.ds(0, above)], window.at[pl.ds(span - above, above)], seq - 1, part)
                fill_high = copies.own(zeros.at[pl.ds(0, above)], window.at[pl.ds(span - above, above)])
            here, first, last = part == k, seq == 0, seq == peers - 1

            def start(mine=mine, tail=tail, up=up, down=down, fill_low=fill_low, fill_high=fill_high, here=here):
                @pl.when(here)
                def _():
                    if up is not None:
                        pl.when(jnp.logical_not(last))(up.start)
                        pl.when(first)(fill_low.start)
                    if down is not None:
                        pl.when(jnp.logical_not(first))(down.start)
                        pl.when(last)(fill_high.start)
                    mine.start()
                    tail.start()

            def finish(mine=mine, tail=tail, up=up, down=down, fill_low=fill_low, fill_high=fill_high, here=here):
                @pl.when(here)
                def _():
                    if up is not None:
                        pl.when(jnp.logical_not(last))(up.wait_send)
                        pl.when(jnp.logical_not(first))(up.wait_recv)
                        pl.when(first)(fill_low.wait)
                    if down is not None:
                        pl.when(jnp.logical_not(first))(down.wait_send)
                        pl.when(jnp.logical_not(last))(down.wait_recv)
                        pl.when(last)(fill_high.wait)
                    mine.wait()
                    tail.wait()

            start()
            waits.append(finish)

    packs = (all_one, all_two)

    def piece(ref, owner, index, size):
        return ref.at[owner, pl.ds(pl.multiple_of(index * size, 16), size)]

    across = {}
    for n, whole in enumerate(packs):
        size = whole.shape[1] // peers
        for d in range(1, slices):
            to = lax.rem(part + d, slices)
            across[n, d] = copies.remote(piece(whole, part, seq, size), piece(whole, part, seq, size), seq, to)
            across[n, d].start()
        if n == 0:
            zeros[...] = jnp.zeros_like(zeros)
            halo(content, content_window)
            put_rows(all_two, part, 0, w_out, False)
            for k, ref in enumerate((w_cross_query, w_cross_key, w_cross_value)):
                put_rows(all_two, part, (1 + k) * cols, ref, True)
            put_rows(all_two, part, 4 * cols, w_cross_out, False)
            pad_rows(all_two, part, 5 * cols)
    find_sentences(seq * rows + part * count, count, peers * rows, lengths, score, cut, code, low, high_self, high_cross, bounds, blocks_code)
    round_plane, to_sibling = {}, {}
    for n, whole in enumerate(packs):
        size = whole.shape[1] // peers
        for d in range(1, slices):
            across[n, d].wait_recv()
            owner = lax.rem(part + slices - d, slices)
            got = piece(whole, owner, seq, size)
            for e in range(1, chips):
                round_plane[n, d, e] = copies.remote(got, got, lax.rem(chip + e, chips) * 2 + core, part)
                round_plane[n, d, e].start()
            to_sibling[n, d, 0] = copies.remote(got, got, sibling, part)
            to_sibling[n, d, 0].start()
    halo(encoded, encoded_window)
    for n, whole in enumerate(packs):
        size = whole.shape[1] // peers
        for d in range(1, slices):
            owner = lax.rem(part + slices - d, slices)
            for e in range(1, chips):
                round_plane[n, d, e].wait_recv()
                got = piece(whole, owner, lax.rem(chip + chips - e, chips) * 2 + core, size)
                to_sibling[n, d, e] = copies.remote(got, got, sibling, part)
                to_sibling[n, d, e].start()
    for copy in to_sibling.values():
        copy.wait_recv()
    for copy in (*across.values(), *round_plane.values(), *to_sibling.values()):
        copy.wait_send()
    for wait in waits:
        wait()


def add_rows(target, source, target_at, source_at, size):
    step = 64 if size % 64 == 0 else 16

    def one(i, carry):
        to = pl.ds(pl.multiple_of(target_at + i * step, 16), step)
        by = pl.ds(pl.multiple_of(source_at + i * step, 16), step)
        target[to, :] = (target[to, :].astype(F32) + source[by, :].astype(F32)).astype(BF16)
        return carry

    lax.fori_loop(0, size // step, one, 0)


def end_kernel(
    peers, slices, count, blocks, parts, packs, plane_sums, outs, part_outs, pack_outs, scratch,
):
    seq, part = lax.axis_index("seq"), lax.axis_index("head")
    chip, core = seq // 2, lax.rem(seq, 2)
    chips = peers // 2
    sibling = chip * 2 + 1 - core
    rows = slices * count
    span = count + 2 * DOC_LEN
    send, recv, local = scratch[:3]
    copies = Copies(send, recv, local)
    first, last = seq == 0, seq == peers - 1
    start_line, end_line = part == 0, part == slices - 1
    greet(seq, part, peers, slices)
    sent = []

    def block(ref, index):
        return ref.at[pl.ds(pl.multiple_of(index * count, 16), count)]

    weight_scratch = scratch[3 : 3 + 5 * len(packs)]
    to_core, held = [], []
    for n, pack in enumerate(packs):
        half = pack.shape[1] // 2
        sibling_sum, mine = weight_scratch[5 * n : 5 * n + 2]
        copy = copies.remote(pack.at[:, pl.ds(pl.multiple_of((1 - core) * half, 16), half)], sibling_sum, sibling, part)
        copy.start()
        to_core.append(copy)
        keep = copies.own(pack.at[:, pl.ds(pl.multiple_of(core * half, 16), half)], mine)
        keep.start()
        held.append(keep)
        sent.append(copy)

    part_scratch = scratch[3 + 5 * len(packs) :]
    halos = []
    for n, grad in enumerate(parts):
        total, from_above, from_below = part_scratch[5 * n : 5 * n + 3]
        for k in range(slices):
            below, above = halo_sizes(k, count, rows)
            low = max(0, k * count - DOC_LEN)
            inner = span - below - above
            mine = copies.own(grad.at[pl.ds(below, inner)], total.at[pl.ds(low, inner)])
            down = up = None
            if below:
                down = copies.remote(grad.at[pl.ds(0, below)], from_above.at[pl.ds(0, below)], seq - 1, part)
            if above:
                up = copies.remote(grad.at[pl.ds(span - above, above)], from_below.at[pl.ds(0, above)], seq + 1, part)
            halos.append((n, k, below, above, low, inner, mine, down, up))

            @pl.when(part == k)
            def _(low=low, inner=inner, mine=mine, down=down, up=up, total=total):
                if down is not None:
                    pl.when(jnp.logical_not(first))(down.start)
                if up is not None:
                    pl.when(jnp.logical_not(last))(up.start)
                mine.start()
                if low:
                    total[0:low, :] = jnp.zeros((low, total.shape[1]), BF16)
                if low + inner < rows:
                    total[low + inner : rows, :] = jnp.zeros((rows - low - inner, total.shape[1]), BF16)

    def finish_halo(which):
        for n, k, below, above, low, inner, mine, down, up in halos:
            if n != which:
                continue
            total, from_above, from_below = part_scratch[5 * n : 5 * n + 3]

            @pl.when(part == k)
            def _(below=below, above=above, mine=mine, down=down, up=up, total=total, from_above=from_above, from_below=from_below):
                mine.wait()
                if down is not None:
                    pl.when(jnp.logical_not(first))(down.wait_send)

                    @pl.when(jnp.logical_not(last))
                    def _():
                        down.wait_recv()
                        add_rows(total, from_above, rows - below, 0, below)

                if up is not None:
                    pl.when(jnp.logical_not(last))(up.wait_send)

                    @pl.when(jnp.logical_not(first))
                    def _():
                        up.wait_recv()
                        add_rows(total, from_below, 0, 0, above)

    halves = 2 if slices <= 4 else 1
    sub = count // halves

    def unit_rows(ref, index, h):
        return ref.at[pl.ds(index * count + h * sub, sub)]

    def gather_rounds(out, me):
        rounds, flows = {}, ((1, slices - 1 - me), (-1, me))
        for sign, onward in flows:
            behind = me if sign > 0 else slices - 1 - me
            sends, waits = {}, {}
            for k in range(behind + 1):
                for h in range(halves):
                    ref = (me - sign * k, h)
                    if onward:
                        sends[k * halves + h] = ref
                    if k:
                        waits[k * halves + h] = ref
            rounds[sign] = (sends, waits)
        return rounds

    def line_gather(out, me, sems):
        steps, ends = [], []
        ring = gather_rounds(out, me)

        def onward(sign, i):
            ref = unit_rows(out, *ring[sign][0][i])
            return sems(sign, i, ref, ref, sign)

        def step(i):
            for sign in (1, -1):
                sends, waits = ring[sign]
                if i in waits:
                    sems(sign, i - halves, unit_rows(out, *waits[i]), unit_rows(out, *waits[i]), 0).wait_recv()
                if i in sends:
                    if i:
                        onward(sign, i - 1).wait_send()
                    onward(sign, i).start()

        def finish():
            for sign in (1, -1):
                sends, _ = ring[sign]
                if sends:
                    onward(sign, max(sends)).wait_send()

        return [partial(step, i) for i in range(slices * halves)], finish

    def line_sum(total, ins, out, me, sems):
        units = (slices - 1) * halves
        before = {1: None, -1: None}

        def place(sign, i):
            return slices - 1 - i // halves if sign > 0 else i // halves

        def slot(sign, i):
            return ins[0 if sign > 0 else 1].at[i]

        def onward(sign, i):
            return sems(sign, i, unit_rows(total, place(sign, i), i % halves), slot(sign, i), sign)

        def step(r):
            for sign in (1, -1):
                depth = me if sign > 0 else slices - 1 - me
                i = r - depth
                if not 0 <= i < units:
                    continue
                b = place(sign, i)
                passes = b > me if sign > 0 else b < me
                if (passes or b == me) and depth:
                    sems(sign, i, slot(sign, i), slot(sign, i), 0).wait_recv()
                    add_rows(total, slot(sign, i), b * count + (i % halves) * sub, 0, sub)
                if passes:
                    if before[sign] is not None:
                        onward(sign, before[sign]).wait_send()
                    before[sign] = i
                    onward(sign, i).start()

        def finish():
            for sign in (1, -1):
                if before[sign] is not None:
                    onward(sign, before[sign]).wait_send()

        def place_own():
            out[pl.ds(me * count, count), :] = total[pl.ds(me * count, count), :]

        return [partial(step, r) for r in range(units + slices - 1)], place_own, finish

    def semaphores(units):
        base = copies.remotes
        copies.remotes += 2 * units

        def make(sign, i, source, target, to):
            k = base + i + (0 if sign > 0 else units)
            return pltpu.make_async_remote_copy(
                src_ref=source, dst_ref=target, send_sem=send.at[k], recv_sem=recv.at[k],
                device_id=(seq, part + to), device_id_type=MESH,
            )

        return make

    def interleave(*lists):
        for k in range(max((len(steps) for steps in lists), default=0)):
            for steps in lists:
                if k < len(steps):
                    steps[k]()

    def at_place(run):
        for me in range(slices):
            pl.when(part == me)(partial(run, me))

    own_copies = []
    for own, out in zip(blocks, outs):
        mine = copies.own(own, block(out, part))
        mine.start()
        own_copies.append(mine)
    block_sems = [semaphores(slices * halves) for _ in outs]
    sum_sems = [semaphores(slices * halves) for _ in part_outs]
    after_sems = [semaphores(slices * halves) for _ in part_outs]

    to_chips = []

    def to_plane():
        for n, pack in enumerate(packs):
            half = pack.shape[1] // 2
            size = half // chips
            sibling_sum, mine, by_chip = weight_scratch[5 * n : 5 * n + 3]
            held[n].wait()
            to_core[n].wait_recv()

            def add_half(z, carry, sibling_sum=sibling_sum, mine=mine, half=half):
                add_rows(mine.at[z], sibling_sum.at[z], 0, 0, half)
                return carry

            lax.fori_loop(0, slices, add_half, 0)
            for e in range(1, chips):
                to = lax.rem(chip + e, chips)
                copy = copies.remote(mine.at[:, pl.ds(pl.multiple_of(to * size, 16), size)], by_chip.at[e - 1], to * 2 + core, part)
                copy.start()
                to_chips.append((n, e, copy))
                sent.append(copy)

    length = slices * halves
    plans = []
    for me in range(slices):
        gathers = [line_gather(out, me, sems) for out, sems in zip(outs, block_sems)]
        sums, afters = [], []
        for n, out in enumerate(part_outs):
            total, _, _, right_in, left_in = part_scratch[5 * n : 5 * n + 5]
            sums.append(line_sum(total, (right_in, left_in), out, me, sum_sems[n]))
            afters.append(line_gather(out, me, after_sems[n]))
        plans.append((gathers, sums, afters))

    def rounds(me, *which):
        lists, ends = [], []
        for kind, n, low, high in which:
            entry = plans[me][kind][n]
            steps = entry[0]
            lists.append(steps[low:high])
            if low < len(steps) <= high:
                ends += list(entry[1:])
        interleave(*lists)
        for finish in ends:
            finish()

    def run(*which):
        at_place(lambda me: rounds(me, *which))

    to_slices = []

    def share(n, plane_sum, by_slice):
        for d in range(1, slices):
            to = lax.rem(part + d, slices)
            copy = copies.remote(plane_sum.at[to], by_slice.at[d - 1], seq, to)
            copy.start()
            to_slices.append((n, copy))
            sent.append(copy)

    plane_scratch = part_scratch[5 * len(parts) :]

    def to_owners():
        for n, pack in enumerate(packs):
            half = pack.shape[1] // 2
            size = half // chips
            mine, by_chip, plane_sum, by_slice = weight_scratch[5 * n + 1 : 5 * n + 5]
            for m, e, copy in to_chips:
                if m == n:
                    copy.wait_recv()

            def add_plane(i, carry, mine=mine, by_chip=by_chip, plane_sum=plane_sum, size=size):
                z, r = i // (size // 16), lax.rem(i, size // 16)
                at = pl.ds(pl.multiple_of(r * 16, 16), 16)
                value = mine[z, pl.ds(pl.multiple_of(chip * size + r * 16, 16), 16), :].astype(F32)
                for e in range(chips - 1):
                    value = value + by_chip[e, z, at, :].astype(F32)
                plane_sum[z, at, :] = value.astype(BF16)
                return carry

            lax.fori_loop(0, slices * (size // 16), add_plane, 0)
            share(n, plane_sum, by_slice)
    def piece_at(n, of_chip, of_core):
        size = pack_outs[n].shape[0] // peers
        index = of_core * chips + of_chip if n < len(packs) else of_chip * 2 + of_core
        return pl.multiple_of(index * size, 16), size

    round_plane, to_sibling = [], []

    def back_to_plane():
        for n, out in enumerate(pack_outs):
            if n < len(packs):
                plane_sum, by_slice = weight_scratch[5 * n + 3 : 5 * n + 5]
            else:
                plane_sum, by_slice = plane_scratch[2 * (n - len(packs)) : 2 * (n - len(packs)) + 2]
            start, size = piece_at(n, chip, core)
            for m, copy in to_slices:
                if m == n:
                    copy.wait_recv()

            def add_slices(r, carry, plane_sum=plane_sum, by_slice=by_slice, out=out, start=start):
                at = pl.ds(pl.multiple_of(r * 16, 16), 16)
                value = plane_sum[part, at, :].astype(F32)
                for d in range(slices - 1):
                    value = value + by_slice[d, at, :].astype(F32)
                out[pl.ds(pl.multiple_of(start + r * 16, 16), 16), :] = value.astype(BF16)
                return carry

            lax.fori_loop(0, size // 16, add_slices, 0)
            piece = out.at[pl.ds(start, size)]
            for e in range(1, chips):
                copy = copies.remote(piece, piece, lax.rem(chip + e, chips) * 2 + core, part)
                copy.start()
                round_plane.append((n, e, copy))
                sent.append(copy)
            copy = copies.remote(piece, piece, sibling, part)
            copy.start()
            round_plane.append((n, 0, copy))
            sent.append(copy)

    sum_length = (slices - 1) * halves + slices - 1
    plane_copies = [copies.own(summed, plane_scratch[2 * n]) for n, summed in enumerate(plane_sums)]
    for keep in plane_copies:
        keep.start()
    for mine in own_copies:
        mine.wait()
    run((0, 0, 0, 2))
    for n, keep in enumerate(plane_copies):
        keep.wait()
        share(len(packs) + n, *plane_scratch[2 * n : 2 * n + 2])
    to_plane()
    run((0, 0, 2, 3))
    finish_halo(0)
    run((0, 0, 3, length), (1, 0, 0, sum_length))
    if len(parts) > 1:
        finish_halo(1)
        run((1, 1, 0, sum_length // 2), (2, 0, 0, sum_length // 2))
        to_owners()
        run((1, 1, sum_length // 2, sum_length), (2, 0, sum_length // 2, length))
        back_to_plane()
        run((2, 1, 0, length))
    else:
        to_owners()
        run((2, 0, 0, length // 2))
        back_to_plane()
        run((2, 0, length // 2, length))
    for n, e, copy in round_plane:
        copy.wait_recv()
        if e:
            start, size = piece_at(n, lax.rem(chip + chips - e, chips), core)
            piece = pack_outs[n].at[pl.ds(start, size)]
            copy = copies.remote(piece, piece, sibling, part)
            copy.start()
            to_sibling.append(copy)
            sent.append(copy)
    for copy in to_sibling:
        copy.wait_recv()
    for copy in sent:
        copy.wait_send()


class Rows:
    def __init__(self, pack, index, size):
        self.pack, self.at = pack, slice(index * size, (index + 1) * size)

    def __getitem__(self, _):
        value = self.pack[:, self.at, :]
        return value.reshape(value.shape[0] * value.shape[1], value.shape[2])


def write_rows(pack, index, size, value):
    slices = pack.shape[0]
    pack[:, index * size : (index + 1) * size, :] = value.astype(BF16).reshape(slices, size, value.shape[1])


def write_pieces(pack, z, row, value):
    size = pack.shape[2]
    for i in range(value.shape[0] // size):
        pack[row // size + i, z] = value[i * size : (i + 1) * size, :].astype(BF16)


def mask_bias(code, low, high):
    return jnp.where((code >= low) & (code < high), 0.0, NEG_BIG).astype(F32)


def attend(bounds, window, code, low, high, w_key_t, w_value_t, spread, bias, top, total, out):
    top[...] = jnp.full_like(top, NEG_BIG)
    total[...] = jnp.zeros_like(total)
    out[...] = jnp.zeros_like(out)

    def step(at, lanes):
        see = slice(*lanes)
        rows = window[at, :]
        keys = dot_nt(rows, w_key_t[...]).astype(BF16)
        values_t = dot_nt(w_value_t[...], rows).astype(BF16)
        bias[:, see] = mask_bias(code[at, :], low[:, see], high[:, see])
        for h in range(HEADS):
            p = h // 2
            scores = dot_nn(keys[:, p * PAIR : (p + 1) * PAIR], spread[h * PAIR : (h + 1) * PAIR, see])
            scores = scores * SCORE_SCALE + bias[:, see]
            before = top[h : h + 1, see]
            now = jnp.maximum(before, jnp.max(scores, axis=0, keepdims=True))
            weights = jnp.exp2(scores - now)
            shrink = jnp.exp2(before - now)
            top[h : h + 1, see] = now
            total[h : h + 1, see] = total[h : h + 1, see] * shrink + jnp.sum(weights, axis=0, keepdims=True)
            head = slice(h * HEAD_SIZE, (h + 1) * HEAD_SIZE)
            out[head, see] = out[head, see] * shrink + dot_nn(values_t[head, :], weights.astype(BF16))

    chunk_loops(bounds, out.shape[1], step)
    for h in range(HEADS):
        head = slice(h * HEAD_SIZE, (h + 1) * HEAD_SIZE)
        out[head, :] = out[head, :] / total[h : h + 1, :]


def attend_back(
    bounds, window, code, low, high, w_key_t, w_value_t, spread, grad_spread, pairs, grad_pairs, lse, delta, bias,
    query_grad, window_grad, w_key_grad, w_value_grad,
):
    count = spread.shape[1]
    query_grad[...] = jnp.zeros_like(query_grad)
    w_key_grad[...] = jnp.zeros_like(w_key_grad)
    w_value_grad[...] = jnp.zeros_like(w_value_grad)
    window_grad[...] = jnp.zeros_like(window_grad)

    def step(at, lanes):
        see = slice(*lanes)
        seen = (slice(*lanes), slice(count + lanes[0], count + lanes[1]))
        rows = window[at, :]
        keys = dot_nt(rows, w_key_t[...]).astype(BF16)
        keys_t = dot_nt(w_key_t[...], rows).astype(BF16)
        values = dot_nt(rows, w_value_t[...]).astype(BF16)
        bias[:, see] = mask_bias(code[at, :], low[:, see], high[:, see])
        key_grads, value_grads = [], []
        for p in range(PAIRS):
            columns = slice(p * PAIR, (p + 1) * PAIR)
            probs, score_grads = [], []
            for h in (2 * p, 2 * p + 1):
                wide = slice(h * PAIR, (h + 1) * PAIR)
                head = slice(h * HEAD_SIZE, (h + 1) * HEAD_SIZE)
                scores = dot_nn(keys[:, columns], spread[wide, see])
                prob = jnp.exp2(scores * SCORE_SCALE + bias[:, see] - lse[h : h + 1, see])
                dprob = dot_nn(values[:, columns], grad_spread[wide, see])
                score_grad = (prob * (dprob - delta[h : h + 1, see])).astype(BF16)
                query_grad[head, see] += dot_nn(keys_t[head, :], score_grad)
                probs.append(prob.astype(BF16))
                score_grads.append(score_grad)
            if count % LANES == 0:
                both = jnp.concatenate([pairs[p, r, :] for r in seen], axis=0)
                grad_both = jnp.concatenate([grad_pairs[p, r, :] for r in seen], axis=0)
                key_grads.append(dot_nn(jnp.concatenate(score_grads, axis=1), both))
                value_grads.append(dot_nn(jnp.concatenate(probs, axis=1), grad_both))
            else:
                key_grads.append(sum(dot_nn(x, pairs[p, r, :]) for x, r in zip(score_grads, seen)))
                value_grads.append(sum(dot_nn(x, grad_pairs[p, r, :]) for x, r in zip(probs, seen)))
        keys_low = (jnp.concatenate(key_grads, axis=1) * SCALE).astype(BF16)
        values_low = jnp.concatenate(value_grads, axis=1).astype(BF16)
        window_grad[at, :] = (dot_nn(keys_low, w_key_t[...]) + dot_nn(values_low, w_value_t[...])).astype(window_grad.dtype)
        w_key_grad[...] += dot_tn(rows, keys_low)
        w_value_grad[...] += dot_tn(rows, values_low)

    chunk_loops(bounds, count, step)


def self_kernel(cols, bounds, own, window, code, low, high, pack_one, out, lse, spread, bias, top, total, low_t):
    w_query_t, w_key_t, w_value_t = (Rows(pack_one, k, cols) for k in range(3))
    low_t[...] = dot_nt(w_query_t[...], own[...]).astype(BF16)
    spread_heads(low_t, spread)
    attend(bounds, window, code, low, high, w_key_t, w_value_t, spread, bias, top, total, out)
    lse[...] = top[...] + jnp.log2(total[...])


def cross_kernel(
    cols, bounds, own, attn_t, gain, window, code, low, high, pack_two, hidden, out, lse, spread, bias, top, total, low_t,
):
    w_out, w_query_t, w_key_t, w_value_t = (Rows(pack_two, k, cols) for k in range(4))
    branch = dot_tn(attn_t[...].astype(BF16), w_out[...])
    normed, _ = layer_norm(own[...].astype(F32) + branch)
    hidden[...] = normed * gain[...]
    low_t[...] = dot_nt(w_query_t[...], hidden[...].astype(BF16)).astype(BF16)
    spread_heads(low_t, spread)
    attend(bounds, window, code, low, high, w_key_t, w_value_t, spread, bias, top, total, out)
    lse[...] = top[...] + jnp.log2(total[...])


def ffn_kernel(
    cols, hidden_one, cross_t, pack_two, gain_cross, pack_three, gain_final, out_grad,
    mixed, resid_grad, w_out_grad, grad_three_pack, gain_cross_grad, gain_final_grad,
    normed_two, hidden_two_low, slope, active, sum_ffn,
):
    slices, units = pack_three.shape[0], pack_three.shape[1] // 2
    w_out = Rows(pack_two, 4, cols)
    cross_low = cross_t[...].astype(BF16)
    normed, scale_two = layer_norm(hidden_one[...] + dot_tn(cross_low, w_out[...]))
    normed_two[...] = normed
    hidden_two = normed * gain_cross[...]
    hidden_two_low[...] = hidden_two.astype(BF16)
    sum_ffn[...] = hidden_two
    for z in range(slices):
        inner = dot_nt(hidden_two_low[...], pack_three[z, 0:units, :])
        below = 0.5 * (1.0 + lax.erf(inner * math.sqrt(0.5)))
        slope[z] = below + inner * (jnp.exp2(inner * inner * (-0.5 * LOG2E)) * (1.0 / math.sqrt(2.0 * math.pi)))
        active[z] = (inner * below).astype(BF16)
        sum_ffn[...] += dot_nn(active[z], pack_three[z, units:, :])
    normed_three, scale_three = layer_norm(sum_ffn[...])
    mixed[...] = (normed_three * gain_final[...]).astype(BF16)
    grad_three, gain_grad = norm_back(out_grad[...].astype(F32), normed_three, scale_three, gain_final[...])
    gain_final_grad[...] = gain_grad
    ffn_low = grad_three.astype(BF16)
    sum_ffn[...] = grad_three
    for z in range(slices):
        write_pieces(grad_three_pack, z, units, dot_tn(active[z], ffn_low))
        inner_low = (dot_nt(ffn_low, pack_three[z, units:, :]) * slope[z]).astype(BF16)
        write_pieces(grad_three_pack, z, 0, dot_tn(inner_low, hidden_two_low[...]))
        sum_ffn[...] += dot_nn(inner_low, pack_three[z, 0:units, :])
    grad, gain_grad = norm_back(sum_ffn[...], normed_two[...], scale_two, gain_cross[...])
    gain_cross_grad[...] = gain_grad
    resid_grad[...] = grad
    w_out_grad[...] = dot_nn(cross_low, grad.astype(BF16)).astype(BF16)


def prepare_back(query, query_t, grad, grad_t, out, spread, grad_spread, pairs, grad_pairs, delta, low_t):
    low_t[...] = query_t.astype(BF16)
    spread_heads(low_t, spread)
    for p in range(PAIRS):
        pair_rows(query.astype(BF16), p, pairs)
        pair_rows(grad.astype(BF16), p, grad_pairs)
    low_t[...] = grad_t.astype(BF16)
    spread_heads(low_t, grad_spread)
    for h in range(HEADS):
        head = slice(h * HEAD_SIZE, (h + 1) * HEAD_SIZE)
        delta[h : h + 1, :] = jnp.sum(low_t[head, :].astype(F32) * out[head, :], axis=0, keepdims=True)


def cross_back_kernel(
    cols, bounds, own, self_t, gain, resid_two_grad, cross_t, lse, window, code, low, high, pack_two,
    w_cross_out_grad, gain_cross_grad, gain_final_grad, resid_one_grad, window_grad, grad_two_pack,
    spread, grad_spread, pairs, grad_pairs, delta, bias, low_t, query_grad, key_sum, value_sum, normed_one, scale_one,
):
    w_out, w_query_t, w_key_t, w_value_t, w_cross_out = (Rows(pack_two, k, cols) for k in range(5))
    self_low = self_t[...].astype(BF16)
    normed, scale = layer_norm(own[...].astype(F32) + dot_tn(self_low, w_out[...]))
    normed_one[...] = normed
    scale_one[...] = scale
    hidden_low = (normed * gain[...]).astype(BF16)
    branch_low = resid_two_grad[...].astype(BF16)
    prepare_back(
        dot_nt(hidden_low, w_query_t[...]), dot_nt(w_query_t[...], hidden_low),
        dot_nt(branch_low, w_cross_out[...]), dot_nt(w_cross_out[...], branch_low),
        cross_t, spread, grad_spread, pairs, grad_pairs, delta, low_t,
    )
    attend_back(
        bounds, window, code, low, high, w_key_t, w_value_t, spread, grad_spread, pairs, grad_pairs, lse, delta, bias,
        query_grad, window_grad, key_sum, value_sum,
    )
    query_low = (query_grad[...] * SCALE).astype(BF16)
    hidden_low = (normed_one[...] * gain[...]).astype(BF16)
    grad_one = resid_two_grad[...] + dot_tn(query_low, w_query_t[...])
    grad, gain_sum = norm_back(grad_one, normed_one[...], scale_one[...], gain[...])
    resid_one_grad[...] = grad
    write_rows(grad_two_pack, 0, cols, dot_nn(self_t[...].astype(BF16), grad.astype(BF16)))
    write_rows(grad_two_pack, 1, cols, dot_nn(query_low, hidden_low))
    write_rows(grad_two_pack, 2, cols, key_sum[...].T)
    write_rows(grad_two_pack, 3, cols, value_sum[...].T)
    write_rows(grad_two_pack, 4, cols, w_cross_out_grad[...])
    slices, rows, width = grad_two_pack.shape
    gains = jnp.concatenate([gain_sum, gain_cross_grad[...], gain_final_grad[...], jnp.zeros((13, width), F32)], axis=0)
    for z in range(slices):
        grad_two_pack[z, 5 * cols : 5 * cols + 16, :] = gains.astype(BF16)
        if rows > 5 * cols + 16:
            grad_two_pack[z, 5 * cols + 16 :, :] = jnp.zeros((rows - 5 * cols - 16, width), BF16)


def self_back_kernel(
    cols, bounds, own, resid_one_grad, pack_two, self_t, lse, window, code, low, high, pack_one,
    own_grad, window_grad, grad_one_pack,
    spread, grad_spread, pairs, grad_pairs, delta, bias, low_t, query_grad, key_sum, value_sum,
):
    w_query_t, w_key_t, w_value_t = (Rows(pack_one, k, cols) for k in range(3))
    w_out = Rows(pack_two, 0, cols)
    branch_low = resid_one_grad[...].astype(BF16)
    prepare_back(
        dot_nt(own[...], w_query_t[...]), dot_nt(w_query_t[...], own[...]),
        dot_nt(branch_low, w_out[...]), dot_nt(w_out[...], branch_low),
        self_t, spread, grad_spread, pairs, grad_pairs, delta, low_t,
    )
    attend_back(
        bounds, window, code, low, high, w_key_t, w_value_t, spread, grad_spread, pairs, grad_pairs, lse, delta, bias,
        query_grad, window_grad, key_sum, value_sum,
    )
    query_low = (query_grad[...] * SCALE).astype(BF16)
    write_rows(grad_one_pack, 0, cols, dot_nn(query_low, own[...]))
    write_rows(grad_one_pack, 1, cols, key_sum[...].T)
    write_rows(grad_one_pack, 2, cols, value_sum[...].T)
    slices, rows, width = grad_one_pack.shape
    if rows > 3 * cols:
        grad_one_pack[:, 3 * cols :, :] = jnp.zeros((slices, rows - 3 * cols, width), BF16)
    own_grad[...] = (resid_one_grad[...] + dot_tn(query_low, w_query_t[...])).astype(BF16)


def finish_kernel(cols, units, slices, part, *refs):
    blocks, (rows_in, (sum_one, sum_two, sum_three), outs) = refs[:slices], (refs[slices : slices + 3], refs[slices + 3 : slices + 6], refs[slices + 6 :])
    count = blocks[0].shape[0]
    for d, ref in enumerate(blocks):
        owner = lax.rem(part[0, 0] + slices - d, slices)
        outs[0][pl.ds(pl.multiple_of(owner * count, 16), count), :] = ref[...]
    for source, target in zip(rows_in, outs[1:4]):
        target[...] = source[...].astype(F32)
    w_query, w_key, w_value, w_out, w_cross_query, w_cross_key, w_cross_value, w_cross_out, w_inner, w_outer = outs[4:14]
    for k, target in enumerate((w_query, w_key, w_value)):
        target[...] = sum_one[k * cols : (k + 1) * cols, :].astype(F32).T
    w_out[...] = sum_two[0:cols, :].astype(F32)
    for k, target in enumerate((w_cross_query, w_cross_key, w_cross_value)):
        target[...] = sum_two[(1 + k) * cols : (2 + k) * cols, :].astype(F32).T
    w_cross_out[...] = sum_two[4 * cols : 5 * cols, :].astype(F32)
    w_inner[...] = sum_three[0:units, :].astype(F32).T
    w_outer[...] = sum_three[units : 2 * units, :].astype(F32)
    gains = sum_two[5 * cols : 5 * cols + 16, :].astype(F32)
    for k, target in enumerate(outs[14:17]):
        target[...] = gains[k : k + 1, :]


def call(kernel, outs, scratch, smem, *args, micros=20):
    place = [pl.BlockSpec(memory_space=pltpu.SMEM)] * smem
    place += [pl.BlockSpec(memory_space=pltpu.VMEM)] * (len(args) - smem)
    return pl.pallas_call(
        kernel,
        out_shape=[jax.ShapeDtypeStruct(shape, kind) for shape, kind in outs],
        in_specs=place,
        out_specs=[pl.BlockSpec(memory_space=pltpu.VMEM)] * len(outs),
        scratch_shapes=[pltpu.VMEM(shape, kind) for shape, kind in scratch],
        compiler_params=pltpu.CompilerParams(vmem_limit_bytes=VMEM_LIMIT),
        cost_estimate=pl.CostEstimate(flops=micros * 10**9, bytes_accessed=micros * 10**6, transcendentals=0),
    )(*args)


def padded(size, unit):
    return -(-size // unit) * unit


def talk(kernel, outs, out_spaces, scratch, copies, number, spaces, *args):
    return pl.pallas_call(
        kernel,
        out_shape=[jax.ShapeDtypeStruct(shape, kind) for shape, kind in outs],
        in_specs=[pl.BlockSpec(memory_space=space) for space in spaces],
        out_specs=[pl.BlockSpec(memory_space=space) for space in out_spaces],
        scratch_shapes=[pltpu.SemaphoreType.DMA((n,)) for n in (copies[0], copies[0], copies[1])] + [pltpu.VMEM(shape, kind) for shape, kind in scratch],
        compiler_params=pltpu.CompilerParams(vmem_limit_bytes=VMEM_LIMIT, collective_id=number, has_side_effects=True),
        cost_estimate=pl.CostEstimate(flops=80 * 10**9, bytes_accessed=80 * 10**6, transcendentals=0),
    )(*args)


def body(
    query_state, content, encoded, sentence_lengths, key_score, query_cut, w_query, w_key, w_value, w_out, gain_self,
    w_cross_query, w_cross_key, w_cross_value, w_cross_out, gain_cross, w_inner, w_outer, gain_final, out_grad,
):
    rows, width = query_state.shape
    slices = lax.axis_size("head")
    count = rows // slices
    lanes = math.gcd(count, LANES)
    wide = padded(count + 2 * DOC_LEN + CHUNK, lanes)
    spare = wide - count - 2 * DOC_LEN
    seq, part = lax.axis_index("seq"), lax.axis_index("head")
    begin = seq * rows + part * count
    score = lax.dynamic_slice_in_dim(jnp.pad(key_score, (DOC_LEN, DOC_LEN + spare)), begin, wide, 0).reshape(wide // lanes, lanes)
    cut = lax.dynamic_slice_in_dim(query_cut, begin, count, 0).reshape(1, count)
    gain_self, gain_cross, gain_final = (g.reshape(1, width) for g in (gain_self, gain_cross, gain_final))

    peers = lax.axis_size("seq")
    chips = peers // 2
    cols, units = w_query.shape[1], w_inner.shape[1]
    unit = 16 * peers
    sizes = [padded(n, unit) for n in (3 * cols, 5 * cols, 2 * units)]
    grad_sizes = [sizes[0], padded(5 * cols + 16, unit), sizes[2]]

    share = sizes[2] // peers
    slice_three = jnp.concatenate([w_inner.T, w_outer, jnp.zeros((sizes[2] - 2 * units, width), BF16)], axis=0)
    share_three = lax.dynamic_slice_in_dim(slice_three, seq * share, share, 0)
    pack_three = lax.all_gather(share_three, ("head", "seq"), axis=0, tiled=True).reshape(slices, sizes[2], width)
    start_copies = 2 * (slices - 1) * (2 * chips) + 4 * slices
    hbm, vmem, smem = pl.ANY, pltpu.VMEM, pltpu.SMEM
    (
        content_window, encoded_window, pack_one, pack_two, own, own_out_grad, code, low, high_self, high_cross, bounds,
    ) = talk(
        partial(start_kernel, peers, slices, count),
        [((wide, width), BF16)] * 2 + [((slices, n, width), BF16) for n in sizes[:2]] + [((count, width), BF16)] * 2
        + [((wide, 1), F32)] + [((1, count), F32)] * 3 + [((1, 4), jnp.int32)],
        [vmem] * 10 + [smem],
        [((DOC_LEN, width), BF16), ((padded(wide // lanes, 8), lanes), F32)], (start_copies, 8 * slices + 16), 0,
        [hbm] * 4 + [vmem] * 8 + [smem] + [vmem] * 2,
        content, encoded, query_state, out_grad, w_query, w_key, w_value, w_out,
        w_cross_query, w_cross_key, w_cross_value, w_cross_out, sentence_lengths.reshape(1, -1), score, cut,
    )

    def split_refs(kernel, ins, outs):
        def run(*refs):
            return kernel(refs[:ins], refs[ins : ins + outs], refs[ins + outs :])
        return run

    stats = [((HEADS * PAIR, count), BF16), ((CHUNK, count), F32), ((HEADS, count), F32), ((HEADS, count), F32), ((width, count), BF16)]
    self_t, lse_self = call(
        partial(self_kernel, cols), [((width, count), F32), ((HEADS, count), F32)], stats, 1,
        bounds, own, content_window, code, low, high_self, pack_one,
    )
    hidden_one, cross_t, lse_cross = call(
        partial(cross_kernel, cols), [((count, width), F32), ((width, count), F32), ((HEADS, count), F32)], stats, 1,
        bounds, own, self_t, gain_self, encoded_window, code, low, high_cross, pack_two,
    )
    mixed, resid_two_grad, w_cross_out_grad, grads_three, gain_cross_grad, gain_final_grad = call(
        partial(ffn_kernel, cols),
        [
            ((count, width), BF16), ((count, width), F32), ((width, width), BF16), ((peers, slices, grad_sizes[2] // peers, width), BF16),
            ((1, width), F32), ((1, width), F32),
        ],
        [
            ((count, width), F32), ((count, width), BF16), ((slices, count, units), F32),
            ((slices, count, units), BF16), ((count, width), F32),
        ], 0,
        hidden_one, cross_t, pack_two, gain_cross, pack_three, gain_final, own_out_grad,
    )
    back = [
        ((HEADS * PAIR, count), BF16), ((HEADS * PAIR, count), BF16), ((PAIRS, 2 * count, PAIR), BF16),
        ((PAIRS, 2 * count, PAIR), BF16), ((HEADS, count), F32), ((CHUNK, count), F32), ((width, count), BF16),
        ((width, count), F32), ((width, width), F32), ((width, width), F32),
    ]
    resid_one_grad, encoded_part, grads_two = call(
        partial(cross_back_kernel, cols),
        [((count, width), F32), ((wide, width), BF16), ((slices, grad_sizes[1], width), BF16)],
        back + [((count, width), F32), ((count, 1), F32)], 1,
        bounds, own, self_t, gain_self, resid_two_grad, cross_t, lse_cross, encoded_window, code, low, high_cross, pack_two,
        w_cross_out_grad, gain_cross_grad, gain_final_grad, micros=4,
    )
    own_grad, content_part, grads_one = call(
        partial(self_back_kernel, cols),
        [((count, width), BF16), ((wide, width), BF16), ((slices, grad_sizes[0], width), BF16)], back, 1,
        bounds, own, resid_one_grad, pack_two, self_t, lse_self, content_window, code, low, high_self, pack_one, micros=4,
    )

    mixed_blocks = [mixed] + [lax.ppermute(mixed, "head", [(i, (i + d) % slices) for i in range(slices)]) for d in range(1, slices)]
    plane_three = lax.psum_scatter(grads_three, "seq", scatter_dimension=0, tiled=True).reshape(grads_three.shape[1:])
    blocks, parts, grads, planes = [own_grad], [content_part, encoded_part], [grads_one, grads_two], [plane_three]
    weight_scratch = []
    for n in grad_sizes[: len(grads)]:
        half, size = n // 2, n // 2 // chips
        weight_scratch += [
            ((slices, half, width), BF16), ((slices, half, width), BF16), ((chips - 1, slices, size, width), BF16),
            ((slices, size, width), BF16), ((slices - 1, size, width), BF16),
        ]
    halves = 2 if slices <= 4 else 1
    units_in = (slices - 1) * halves
    part_scratch = [
        ((rows, width), BF16), ((DOC_LEN, width), BF16), ((DOC_LEN, width), BF16),
        ((units_in, count // halves, width), BF16), ((units_in, count // halves, width), BF16),
    ] * len(parts)
    plane_scratch = []
    for n in grad_sizes[len(grads) :]:
        plane_scratch += [((slices, n // peers, width), BF16), ((slices - 1, n // peers, width), BF16)]
    ins, outs = (len(blocks), len(parts), len(grads), len(planes)), (len(blocks), len(parts), len(grad_sizes))

    def end(refs, out_refs, scratch):
        a, b, c = ins[0], ins[0] + ins[1], sum(ins[:3])
        end_kernel(
            peers, slices, count, refs[:a], refs[a:b], refs[b:c], refs[c:], out_refs[: outs[0]],
            out_refs[outs[0] : outs[0] + outs[1]], out_refs[outs[0] + outs[1] :], scratch,
        )

    end_copies = len(grad_sizes) * (1 + 3 * (chips - 1) + slices) + len(parts) * 2 * slices + (len(blocks) + 2 * len(parts)) * 2 * slices * halves
    results = talk(
        split_refs(end, sum(ins), sum(outs)),
        [((rows, width), BF16)] * (len(blocks) + len(parts)) + [((n, width), BF16) for n in grad_sizes], [vmem] * sum(outs),
        weight_scratch + part_scratch + plane_scratch, (end_copies, 8 * slices + 8), 1, [hbm] * sum(ins), *blocks, *parts, *grads, *planes,
    )
    query_state_grad, content_grad, encoded_grad, sum_one, sum_two, sum_three = results

    square, tall = ((width, cols), F32), ((cols, width), F32)
    results = call(
        partial(finish_kernel, cols, units, slices),
        [((rows, width), BF16)] + [((rows, width), F32)] * 3 + [square] * 3 + [tall, square, square, square, tall]
        + [((width, units), F32), ((units, width), F32)] + [((1, width), F32)] * 3,
        [], 1, part.reshape(1, 1).astype(jnp.int32), *mixed_blocks, query_state_grad, content_grad, encoded_grad, sum_one, sum_two, sum_three,
    )
    (
        mixed, query_state_grad, content_grad, encoded_grad, w_query_grad, w_key_grad, w_value_grad, w_out_grad,
        w_cross_query_grad, w_cross_key_grad, w_cross_value_grad, w_cross_out_grad, w_inner_grad, w_outer_grad, *gains,
    ) = results
    gains = [g.reshape(width) for g in gains]
    return (
        mixed, query_state_grad, content_grad, encoded_grad, w_query_grad, w_key_grad, w_value_grad, w_out_grad, gains[0],
        w_cross_query_grad, w_cross_key_grad, w_cross_value_grad, w_cross_out_grad, gains[1], w_inner_grad, w_outer_grad, gains[2],
    )


def solution(mesh):
    rows, whole, columns, split = P("seq", None), P(), P(None, "head"), P("head", None)
    in_specs = (
        rows, rows, rows, whole, whole, whole, columns, columns, columns, split, whole,
        columns, columns, columns, split, whole, columns, split, whole, rows,
    )
    out_specs = (
        rows, rows, rows, rows, columns, columns, columns, split, whole,
        columns, columns, columns, split, whole, columns, split, whole,
    )
    return jax.shard_map(body, mesh=mesh, in_specs=in_specs, out_specs=out_specs, check_vma=False)
```

```python
from functools import partial
import math

import jax
import jax.numpy as jnp
from jax import lax
from jax.experimental import pallas as pl
from jax.experimental.pallas import tpu as pltpu
from jax.sharding import PartitionSpec as P

HEADS = 8
HEAD_SIZE = 64
PAIR = 2 * HEAD_SIZE
PAIRS = HEADS // 2
DOC_LEN = 1024
CHUNK = 528
LANES = 128
EPS = 1e-05
NEG_BIG = -1e30
LOG2E = 1.4426950408889634
SCALE = 1.0 / math.sqrt(HEAD_SIZE)
SCORE_SCALE = SCALE * LOG2E
CODES = 128
BF16 = jnp.bfloat16
F32 = jnp.float32
VMEM_LIMIT = 60 << 20


def dot_nn(left, right):
    return lax.dot_general(left, right, (((1,), (0,)), ((), ())), preferred_element_type=F32)


def dot_nt(left, right):
    return lax.dot_general(left, right, (((1,), (1,)), ((), ())), preferred_element_type=F32)


def dot_tn(left, right):
    return lax.dot_general(left, right, (((0,), (0,)), ((), ())), preferred_element_type=F32)


def chunk_range(bounds):
    start = bounds[0, 0] // 16 * 16
    return start, (bounds[0, 1] - start + CHUNK - 1) // CHUNK


def chunk_rows(start, c):
    return pl.ds(pl.multiple_of(start + c * CHUNK, 16), CHUNK)


class Window:
    def __init__(self, bounds, source, held, sems):
        self.bounds, self.source, self.held, self.sems = bounds, source, held, sems
        self.start, self.chunks = chunk_range(bounds)

    def copy(self, c):
        rows = chunk_rows(self.start, c)
        return pltpu.make_async_copy(self.source.at[rows], self.held.at[rows], self.sems.at[c])

    def fetch(self):
        def one(c, carry):
            self.copy(c).start()
            return carry

        lax.fori_loop(0, self.chunks, one, 0)

    def loops(self, count, step):
        bounds, start, chunks = self.bounds, self.start, self.chunks

        def loop(low, high, lanes):
            def one(c, carry):
                self.copy(c).wait()
                step(chunk_rows(start, c), lanes)
                return carry

            lax.fori_loop(low, high, one, 0)

        if count != 3 * LANES:
            return loop(0, chunks, (0, count))
        left = jnp.clip((bounds[0, 2] - start) // CHUNK, 0, chunks)
        right = jnp.clip((bounds[0, 3] - start + CHUNK - 1) // CHUNK, left, chunks)
        loop(0, left, (0, 2 * LANES))
        loop(left, right, (0, count))
        loop(right, chunks, (LANES, count))


def layer_norm(resid):
    mean_row = jnp.mean(resid, axis=1, keepdims=True)
    centred = resid - mean_row
    var_row = jnp.mean(centred * centred, axis=1, keepdims=True)
    scale_row = lax.rsqrt(var_row + EPS)
    return centred * scale_row, scale_row


def norm_back(grad, normed, scale_row, gain):
    gain_grad = jnp.sum(grad * normed, axis=0, keepdims=True)
    scaled = grad * gain
    centre = jnp.mean(scaled, axis=1, keepdims=True)
    along = jnp.mean(scaled * normed, axis=1, keepdims=True)
    return scale_row * (scaled - centre - normed * along), gain_grad


def spread_heads(source, target):
    target[...] = jnp.zeros_like(target)
    for h in range(HEADS):
        row = h * PAIR + (h % 2) * HEAD_SIZE
        target[row : row + HEAD_SIZE, :] = source[h * HEAD_SIZE : (h + 1) * HEAD_SIZE, :]


def pair_rows(source, p, target):
    rows = source.shape[0]
    both = source[:, p * PAIR : (p + 1) * PAIR]
    lane = lax.broadcasted_iota(jnp.int32, both.shape, 1)
    zero = jnp.zeros_like(both)
    target[p, 0:rows, :] = jnp.where(lane < HEAD_SIZE, both, zero)
    target[p, rows : 2 * rows, :] = jnp.where(lane < HEAD_SIZE, zero, both)


MESH = pl.DeviceIdType.MESH


class Copies:
    def __init__(self, send, recv, local):
        self.send, self.recv, self.local = send, recv, local
        self.remotes, self.locals = 0, 0

    def remote(self, source, target, seq, part):
        k = self.remotes
        self.remotes += 1
        return pltpu.make_async_remote_copy(
            src_ref=source, dst_ref=target, send_sem=self.send.at[k], recv_sem=self.recv.at[k],
            device_id=(seq, part), device_id_type=MESH,
        )

    def own(self, source, target):
        k = self.locals
        self.locals += 1
        return pltpu.make_async_copy(source, target, self.local.at[k])


def greet(seq, part, peers, slices):
    barrier = pltpu.get_barrier_semaphore()
    for d in range(1, peers):
        pl.semaphore_signal(barrier, inc=1, device_id=(lax.rem(seq + d, peers), part), device_id_type=MESH)
    for d in range(1, slices):
        pl.semaphore_signal(barrier, inc=1, device_id=(seq, lax.rem(part + d, slices)), device_id_type=MESH)
    pl.semaphore_wait(barrier, peers - 1 + slices - 1)


def halo_sizes(part, count, rows):
    return max(0, DOC_LEN - part * count), max(0, (part + 1) * count + DOC_LEN - rows)


def put_rows(whole, part, row, ref, flip):
    value = ref[...]
    if flip:
        value = value.astype(F32).T.astype(BF16)
    whole[part, row : row + value.shape[0], :] = value


def pad_rows(whole, part, row):
    if row < whole.shape[1]:
        whole[part, row:, :] = jnp.zeros((whole.shape[1] - row, whole.shape[2]), BF16)


def find_sentences(begin, count, total_rows, lengths, score, cut, code, low, high_self, high_cross, bounds, blocks_code):
    blocks, lanes = score.shape
    pos = lax.broadcasted_iota(jnp.int32, (blocks, lanes), 0) * lanes + lax.broadcasted_iota(jnp.int32, (blocks, lanes), 1)
    pos = pos + (begin - DOC_LEN)
    own_pos = lax.broadcasted_iota(jnp.int32, (1, count), 1) + begin
    zero = jnp.zeros((blocks, lanes), jnp.int32)
    last_pos = begin + count - 1

    def one(s, carry):
        start, sentence, first, own_sentence, first_row, last_row, late_first, early_last = carry
        size = lengths[0, s]
        end = start + size
        passed = pos >= end
        sentence = sentence + jnp.where(passed, 1, 0)
        first = first + jnp.where(passed, size, 0)
        own_sentence = own_sentence + jnp.where(own_pos >= end, 1, 0)
        first_row = first_row + jnp.where(begin >= end, size, 0)
        last_row = last_row + jnp.where(last_pos >= start, size, 0)
        late_first = late_first + jnp.where(begin + late >= end, size, 0)
        early_last = early_last + jnp.where(begin + early >= start, size, 0)
        return end, sentence, first, own_sentence, first_row, last_row, late_first, early_last

    none = lengths[0, 0] * 0
    late, early = 2 * LANES, LANES - 1
    carry = (none, zero, zero, jnp.zeros((1, count), jnp.int32), none, none, none, none)
    _, sentence, first, own_sentence, first_row, last_row, late_first, early_last = lax.fori_loop(0, lengths.shape[1], one, carry)
    shown = jnp.where(pos == first, -1, score[...])
    inside = jnp.logical_and(pos >= 0, pos < total_rows)
    blocks_code[0:blocks, :] = jnp.where(inside, sentence * CODES + shown, -CODES).astype(F32)
    for b in range(0, blocks, 8):
        turned = blocks_code[b : b + 8, :].T
        for j in range(min(8, blocks - b)):
            code[(b + j) * lanes : (b + j + 1) * lanes, :] = turned[:, j : j + 1]
    low[...] = (own_sentence * CODES - 1).astype(F32)
    high_self[...] = (own_sentence * CODES + cut[...]).astype(F32)
    high_cross[...] = (own_sentence * CODES + CODES // 2).astype(F32)
    origin = begin - DOC_LEN
    bounds[0, 0] = first_row - origin
    bounds[0, 1] = last_row - origin
    bounds[0, 2] = late_first - origin
    bounds[0, 3] = early_last - origin


def start_kernel(
    peers, slices, count, content, encoded, query_state, out_grad, w_query, w_key, w_value, w_out,
    w_cross_query, w_cross_key, w_cross_value, w_cross_out, lengths, score, cut,
    content_window, encoded_window, all_one, all_two, own, own_out_grad, code, low, high_self, high_cross, bounds,
    send, recv, local, zeros, blocks_code,
):
    seq, part = lax.axis_index("seq"), lax.axis_index("head")
    chip, core = seq // 2, lax.rem(seq, 2)
    chips = peers // 2
    sibling = chip * 2 + 1 - core
    rows = content.shape[0]
    span = count + 2 * DOC_LEN
    spare = content_window.shape[0] - span
    copies = Copies(send, recv, local)
    cols = w_query.shape[1]
    for k, (ref, flip) in enumerate(((w_query, True), (w_key, True), (w_value, True))):
        put_rows(all_one, part, k * cols, ref, flip)
    pad_rows(all_one, part, 3 * cols)
    greet(seq, part, peers, slices)
    waits = []
    for source, target in ((query_state, own), (out_grad, own_out_grad)):
        mine = copies.own(source.at[pl.ds(pl.multiple_of(part * count, 16), count)], target)
        mine.start()
        waits.append(mine.wait)

    def halo(source, window):
        for k in range(slices):
            below, above = halo_sizes(k, count, rows)
            low = max(0, k * count - DOC_LEN)
            inner = span - below - above
            mine = copies.own(source.at[pl.ds(low, inner)], window.at[pl.ds(below, inner)])
            tail = copies.own(zeros.at[pl.ds(0, spare)], window.at[pl.ds(span, spare)])
            up = down = fill_low = fill_high = None
            if below:
                up = copies.remote(source.at[pl.ds(rows - below, below)], window.at[pl.ds(0, below)], seq + 1, part)
                fill_low = copies.own(zeros.at[pl.ds(0, below)], window.at[pl.ds(0, below)])
            if above:
                down = copies.remote(source.at[pl.ds(0, above)], window.at[pl.ds(span - above, above)], seq - 1, part)
                fill_high = copies.own(zeros.at[pl.ds(0, above)], window.at[pl.ds(span - above, above)])
            here, first, last = part == k, seq == 0, seq == peers - 1

            def start(mine=mine, tail=tail, up=up, down=down, fill_low=fill_low, fill_high=fill_high, here=here):
                @pl.when(here)
                def _():
                    if up is not None:
                        pl.when(jnp.logical_not(last))(up.start)
                        pl.when(first)(fill_low.start)
                    if down is not None:
                        pl.when(jnp.logical_not(first))(down.start)
                        pl.when(last)(fill_high.start)
                    mine.start()
                    tail.start()

            def finish(mine=mine, tail=tail, up=up, down=down, fill_low=fill_low, fill_high=fill_high, here=here):
                @pl.when(here)
                def _():
                    if up is not None:
                        pl.when(jnp.logical_not(last))(up.wait_send)
                        pl.when(jnp.logical_not(first))(up.wait_recv)
                        pl.when(first)(fill_low.wait)
                    if down is not None:
                        pl.when(jnp.logical_not(first))(down.wait_send)
                        pl.when(jnp.logical_not(last))(down.wait_recv)
                        pl.when(last)(fill_high.wait)
                    mine.wait()
                    tail.wait()

            start()
            waits.append(finish)

    packs = (all_one, all_two)

    def piece(ref, owner, index, size):
        return ref.at[owner, pl.ds(pl.multiple_of(index * size, 16), size)]

    across = {}
    for n, whole in enumerate(packs):
        size = whole.shape[1] // peers
        for d in range(1, slices):
            to = lax.rem(part + d, slices)
            across[n, d] = copies.remote(piece(whole, part, seq, size), piece(whole, part, seq, size), seq, to)
            across[n, d].start()
        if n == 0:
            zeros[...] = jnp.zeros_like(zeros)
            halo(content, content_window)
            put_rows(all_two, part, 0, w_out, False)
            for k, ref in enumerate((w_cross_query, w_cross_key, w_cross_value)):
                put_rows(all_two, part, (1 + k) * cols, ref, True)
            put_rows(all_two, part, 4 * cols, w_cross_out, False)
            pad_rows(all_two, part, 5 * cols)
    find_sentences(seq * rows + part * count, count, peers * rows, lengths, score, cut, code, low, high_self, high_cross, bounds, blocks_code)
    round_plane, to_sibling = {}, {}
    for n, whole in enumerate(packs):
        size = whole.shape[1] // peers
        for d in range(1, slices):
            across[n, d].wait_recv()
            owner = lax.rem(part + slices - d, slices)
            got = piece(whole, owner, seq, size)
            for e in range(1, chips):
                round_plane[n, d, e] = copies.remote(got, got, lax.rem(chip + e, chips) * 2 + core, part)
                round_plane[n, d, e].start()
            to_sibling[n, d, 0] = copies.remote(got, got, sibling, part)
            to_sibling[n, d, 0].start()
    halo(encoded, encoded_window)
    for n, whole in enumerate(packs):
        size = whole.shape[1] // peers
        for d in range(1, slices):
            owner = lax.rem(part + slices - d, slices)
            for e in range(1, chips):
                round_plane[n, d, e].wait_recv()
                got = piece(whole, owner, lax.rem(chip + chips - e, chips) * 2 + core, size)
                to_sibling[n, d, e] = copies.remote(got, got, sibling, part)
                to_sibling[n, d, e].start()
    for copy in to_sibling.values():
        copy.wait_recv()
    for copy in (*across.values(), *round_plane.values(), *to_sibling.values()):
        copy.wait_send()
    for wait in waits:
        wait()


def add_rows(target, source, target_at, source_at, size):
    step = 64 if size % 64 == 0 else 16

    def one(i, carry):
        to = pl.ds(pl.multiple_of(target_at + i * step, 16), step)
        by = pl.ds(pl.multiple_of(source_at + i * step, 16), step)
        target[to, :] = (target[to, :].astype(F32) + source[by, :].astype(F32)).astype(BF16)
        return carry

    lax.fori_loop(0, size // step, one, 0)


def end_kernel(
    peers, slices, count, blocks, parts, packs, plane_sums, outs, part_outs, pack_outs, scratch,
):
    seq, part = lax.axis_index("seq"), lax.axis_index("head")
    chip, core = seq // 2, lax.rem(seq, 2)
    chips = peers // 2
    sibling = chip * 2 + 1 - core
    rows = slices * count
    span = count + 2 * DOC_LEN
    send, recv, local = scratch[:3]
    copies = Copies(send, recv, local)
    first, last = seq == 0, seq == peers - 1
    start_line, end_line = part == 0, part == slices - 1
    greet(seq, part, peers, slices)
    sent = []

    def block(ref, index):
        return ref.at[pl.ds(pl.multiple_of(index * count, 16), count)]

    weight_scratch = scratch[3 : 3 + 5 * len(packs)]
    to_core, held = [], []
    for n, pack in enumerate(packs):
        half = pack.shape[1] // 2
        sibling_sum, mine = weight_scratch[5 * n : 5 * n + 2]
        copy = copies.remote(pack.at[:, pl.ds(pl.multiple_of((1 - core) * half, 16), half)], sibling_sum, sibling, part)
        copy.start()
        to_core.append(copy)
        keep = copies.own(pack.at[:, pl.ds(pl.multiple_of(core * half, 16), half)], mine)
        keep.start()
        held.append(keep)
        sent.append(copy)

    part_scratch = scratch[3 + 5 * len(packs) :]
    halos = []
    for n, grad in enumerate(parts):
        total, from_above, from_below = part_scratch[5 * n : 5 * n + 3]
        for k in range(slices):
            below, above = halo_sizes(k, count, rows)
            low = max(0, k * count - DOC_LEN)
            inner = span - below - above
            mine = copies.own(grad.at[pl.ds(below, inner)], total.at[pl.ds(low, inner)])
            down = up = None
            if below:
                down = copies.remote(grad.at[pl.ds(0, below)], from_above.at[pl.ds(0, below)], seq - 1, part)
            if above:
                up = copies.remote(grad.at[pl.ds(span - above, above)], from_below.at[pl.ds(0, above)], seq + 1, part)
            halos.append((n, k, below, above, low, inner, mine, down, up))

            @pl.when(part == k)
            def _(low=low, inner=inner, mine=mine, down=down, up=up, total=total):
                if down is not None:
                    pl.when(jnp.logical_not(first))(down.start)
                if up is not None:
                    pl.when(jnp.logical_not(last))(up.start)
                mine.start()
                if low:
                    total[0:low, :] = jnp.zeros((low, total.shape[1]), BF16)
                if low + inner < rows:
                    total[low + inner : rows, :] = jnp.zeros((rows - low - inner, total.shape[1]), BF16)

    def finish_halo(which):
        for n, k, below, above, low, inner, mine, down, up in halos:
            if n != which:
                continue
            total, from_above, from_below = part_scratch[5 * n : 5 * n + 3]

            @pl.when(part == k)
            def _(below=below, above=above, mine=mine, down=down, up=up, total=total, from_above=from_above, from_below=from_below):
                mine.wait()
                if down is not None:
                    pl.when(jnp.logical_not(first))(down.wait_send)

                    @pl.when(jnp.logical_not(last))
                    def _():
                        down.wait_recv()
                        add_rows(total, from_above, rows - below, 0, below)

                if up is not None:
                    pl.when(jnp.logical_not(last))(up.wait_send)

                    @pl.when(jnp.logical_not(first))
                    def _():
                        up.wait_recv()
                        add_rows(total, from_below, 0, 0, above)

    halves = 2 if slices <= 4 else 1
    sub = count // halves

    def unit_rows(ref, index, h):
        return ref.at[pl.ds(index * count + h * sub, sub)]

    def gather_rounds(out, me):
        rounds, flows = {}, ((1, slices - 1 - me), (-1, me))
        for sign, onward in flows:
            behind = me if sign > 0 else slices - 1 - me
            sends, waits = {}, {}
            for k in range(behind + 1):
                for h in range(halves):
                    ref = (me - sign * k, h)
                    if onward:
                        sends[k * halves + h] = ref
                    if k:
                        waits[k * halves + h] = ref
            rounds[sign] = (sends, waits)
        return rounds

    def line_gather(out, me, sems):
        steps, ends = [], []
        ring = gather_rounds(out, me)

        def onward(sign, i):
            ref = unit_rows(out, *ring[sign][0][i])
            return sems(sign, i, ref, ref, sign)

        def step(i):
            for sign in (1, -1):
                sends, waits = ring[sign]
                if i in waits:
                    sems(sign, i - halves, unit_rows(out, *waits[i]), unit_rows(out, *waits[i]), 0).wait_recv()
                if i in sends:
                    if i:
                        onward(sign, i - 1).wait_send()
                    onward(sign, i).start()

        def finish():
            for sign in (1, -1):
                sends, _ = ring[sign]
                if sends:
                    onward(sign, max(sends)).wait_send()

        return [partial(step, i) for i in range(slices * halves)], finish

    def line_sum(total, ins, out, me, sems):
        units = (slices - 1) * halves
        before = {1: None, -1: None}

        def place(sign, i):
            return slices - 1 - i // halves if sign > 0 else i // halves

        def slot(sign, i):
            return ins[0 if sign > 0 else 1].at[i]

        def onward(sign, i):
            return sems(sign, i, unit_rows(total, place(sign, i), i % halves), slot(sign, i), sign)

        def step(r):
            for sign in (1, -1):
                depth = me if sign > 0 else slices - 1 - me
                i = r - depth
                if not 0 <= i < units:
                    continue
                b = place(sign, i)
                passes = b > me if sign > 0 else b < me
                if (passes or b == me) and depth:
                    sems(sign, i, slot(sign, i), slot(sign, i), 0).wait_recv()
                    add_rows(total, slot(sign, i), b * count + (i % halves) * sub, 0, sub)
                if passes:
                    if before[sign] is not None:
                        onward(sign, before[sign]).wait_send()
                    before[sign] = i
                    onward(sign, i).start()

        def finish():
            for sign in (1, -1):
                if before[sign] is not None:
                    onward(sign, before[sign]).wait_send()

        def place_own():
            out[pl.ds(me * count, count), :] = total[pl.ds(me * count, count), :]

        return [partial(step, r) for r in range(units + slices - 1)], place_own, finish

    def semaphores(units):
        base = copies.remotes
        copies.remotes += 2 * units

        def make(sign, i, source, target, to):
            k = base + i + (0 if sign > 0 else units)
            return pltpu.make_async_remote_copy(
                src_ref=source, dst_ref=target, send_sem=send.at[k], recv_sem=recv.at[k],
                device_id=(seq, part + to), device_id_type=MESH,
            )

        return make

    def interleave(*lists):
        for k in range(max((len(steps) for steps in lists), default=0)):
            for steps in lists:
                if k < len(steps):
                    steps[k]()

    def at_place(run):
        for me in range(slices):
            pl.when(part == me)(partial(run, me))

    own_copies = []
    for own, out in zip(blocks, outs):
        mine = copies.own(own, block(out, part))
        mine.start()
        own_copies.append(mine)
    block_sems = [semaphores(slices * halves) for _ in outs]
    sum_sems = [semaphores(slices * halves) for _ in part_outs]
    after_sems = [semaphores(slices * halves) for _ in part_outs]

    to_chips = []

    def to_plane():
        for n, pack in enumerate(packs):
            half = pack.shape[1] // 2
            size = half // chips
            sibling_sum, mine, by_chip = weight_scratch[5 * n : 5 * n + 3]
            held[n].wait()
            to_core[n].wait_recv()

            def add_half(z, carry, sibling_sum=sibling_sum, mine=mine, half=half):
                add_rows(mine.at[z], sibling_sum.at[z], 0, 0, half)
                return carry

            lax.fori_loop(0, slices, add_half, 0)
            for e in range(1, chips):
                to = lax.rem(chip + e, chips)
                copy = copies.remote(mine.at[:, pl.ds(pl.multiple_of(to * size, 16), size)], by_chip.at[e - 1], to * 2 + core, part)
                copy.start()
                to_chips.append((n, e, copy))
                sent.append(copy)

    length = slices * halves
    plans = []
    for me in range(slices):
        gathers = [line_gather(out, me, sems) for out, sems in zip(outs, block_sems)]
        sums, afters = [], []
        for n, out in enumerate(part_outs):
            total, _, _, right_in, left_in = part_scratch[5 * n : 5 * n + 5]
            sums.append(line_sum(total, (right_in, left_in), out, me, sum_sems[n]))
            afters.append(line_gather(out, me, after_sems[n]))
        plans.append((gathers, sums, afters))

    def rounds(me, *which):
        lists, ends = [], []
        for kind, n, low, high in which:
            entry = plans[me][kind][n]
            steps = entry[0]
            lists.append(steps[low:high])
            if low < len(steps) <= high:
                ends += list(entry[1:])
        interleave(*lists)
        for finish in ends:
            finish()

    def run(*which):
        at_place(lambda me: rounds(me, *which))

    to_slices = []

    def share(n, plane_sum, by_slice):
        for d in range(1, slices):
            to = lax.rem(part + d, slices)
            copy = copies.remote(plane_sum.at[to], by_slice.at[d - 1], seq, to)
            copy.start()
            to_slices.append((n, copy))
            sent.append(copy)

    plane_scratch = part_scratch[5 * len(parts) :]

    def to_owners():
        for n, pack in enumerate(packs):
            half = pack.shape[1] // 2
            size = half // chips
            mine, by_chip, plane_sum, by_slice = weight_scratch[5 * n + 1 : 5 * n + 5]
            for m, e, copy in to_chips:
                if m == n:
                    copy.wait_recv()

            def add_plane(i, carry, mine=mine, by_chip=by_chip, plane_sum=plane_sum, size=size):
                z, r = i // (size // 16), lax.rem(i, size // 16)
                at = pl.ds(pl.multiple_of(r * 16, 16), 16)
                value = mine[z, pl.ds(pl.multiple_of(chip * size + r * 16, 16), 16), :].astype(F32)
                for e in range(chips - 1):
                    value = value + by_chip[e, z, at, :].astype(F32)
                plane_sum[z, at, :] = value.astype(BF16)
                return carry

            lax.fori_loop(0, slices * (size // 16), add_plane, 0)
            share(n, plane_sum, by_slice)
    def piece_at(n, of_chip, of_core):
        size = pack_outs[n].shape[0] // peers
        index = of_core * chips + of_chip if n < len(packs) else of_chip * 2 + of_core
        return pl.multiple_of(index * size, 16), size

    round_plane, to_sibling = [], []

    def back_to_plane():
        for n, out in enumerate(pack_outs):
            if n < len(packs):
                plane_sum, by_slice = weight_scratch[5 * n + 3 : 5 * n + 5]
            else:
                plane_sum, by_slice = plane_scratch[2 * (n - len(packs)) : 2 * (n - len(packs)) + 2]
            start, size = piece_at(n, chip, core)
            for m, copy in to_slices:
                if m == n:
                    copy.wait_recv()

            def add_slices(r, carry, plane_sum=plane_sum, by_slice=by_slice, out=out, start=start):
                at = pl.ds(pl.multiple_of(r * 16, 16), 16)
                value = plane_sum[part, at, :].astype(F32)
                for d in range(slices - 1):
                    value = value + by_slice[d, at, :].astype(F32)
                out[pl.ds(pl.multiple_of(start + r * 16, 16), 16), :] = value.astype(BF16)
                return carry

            lax.fori_loop(0, size // 16, add_slices, 0)
            piece = out.at[pl.ds(start, size)]
            for e in range(1, chips):
                copy = copies.remote(piece, piece, lax.rem(chip + e, chips) * 2 + core, part)
                copy.start()
                round_plane.append((n, e, copy))
                sent.append(copy)
            copy = copies.remote(piece, piece, sibling, part)
            copy.start()
            round_plane.append((n, 0, copy))
            sent.append(copy)

    sum_length = (slices - 1) * halves + slices - 1
    plane_copies = [copies.own(summed, plane_scratch[2 * n]) for n, summed in enumerate(plane_sums)]
    for keep in plane_copies:
        keep.start()
    for mine in own_copies:
        mine.wait()
    run((0, 0, 0, 2))
    for n, keep in enumerate(plane_copies):
        keep.wait()
        share(len(packs) + n, *plane_scratch[2 * n : 2 * n + 2])
    to_plane()
    run((0, 0, 2, 3))
    finish_halo(0)
    run((0, 0, 3, length), (1, 0, 0, sum_length))
    if len(parts) > 1:
        finish_halo(1)
        run((1, 1, 0, sum_length // 2), (2, 0, 0, sum_length // 2))
        to_owners()
        run((1, 1, sum_length // 2, sum_length), (2, 0, sum_length // 2, length))
        back_to_plane()
        run((2, 1, 0, length))
    else:
        to_owners()
        run((2, 0, 0, length // 2))
        back_to_plane()
        run((2, 0, length // 2, length))
    for n, e, copy in round_plane:
        copy.wait_recv()
        if e:
            start, size = piece_at(n, lax.rem(chip + chips - e, chips), core)
            piece = pack_outs[n].at[pl.ds(start, size)]
            copy = copies.remote(piece, piece, sibling, part)
            copy.start()
            to_sibling.append(copy)
            sent.append(copy)
    for copy in to_sibling:
        copy.wait_recv()
    for copy in sent:
        copy.wait_send()


class Rows:
    def __init__(self, pack, index, size):
        self.pack, self.at = pack, slice(index * size, (index + 1) * size)

    def __getitem__(self, _):
        value = self.pack[:, self.at, :]
        return value.reshape(value.shape[0] * value.shape[1], value.shape[2])


def write_rows(pack, index, size, value):
    slices = pack.shape[0]
    pack[:, index * size : (index + 1) * size, :] = value.astype(BF16).reshape(slices, size, value.shape[1])


def write_pieces(pack, z, row, value):
    size = pack.shape[2]
    for i in range(value.shape[0] // size):
        pack[row // size + i, z] = value[i * size : (i + 1) * size, :].astype(BF16)


def mask_bias(code, low, high):
    return jnp.where((code >= low) & (code < high), 0.0, NEG_BIG).astype(F32)


def pair_product(left, spread, p, lanes):
    count = lanes[1] - lanes[0]
    blocks = [spread[h * PAIR : (h + 1) * PAIR, lanes[0] : lanes[1]] for h in (2 * p, 2 * p + 1)]
    if count % LANES:
        return [dot_nn(left, block) for block in blocks]
    both = dot_nn(left, jnp.concatenate(blocks, axis=1))
    return both[:, :count], both[:, count:]


def attend(window, code, low, high, w_key_t, w_value_t, spread, bias, top, total, out):
    top[...] = jnp.full_like(top, NEG_BIG)
    total[...] = jnp.zeros_like(total)
    out[...] = jnp.zeros_like(out)

    def step(at, lanes):
        see = slice(*lanes)
        rows = window.held[at, :]
        keys = dot_nt(rows, w_key_t[...]).astype(BF16)
        values_t = dot_nt(w_value_t[...], rows).astype(BF16)
        bias[:, see] = mask_bias(code[at, :], low[:, see], high[:, see])
        for h in range(HEADS):
            p = h // 2
            if h % 2 == 0:
                both = pair_product(keys[:, p * PAIR : (p + 1) * PAIR], spread, p, lanes)
            scores = both[h % 2] * SCORE_SCALE + bias[:, see]
            before = top[h : h + 1, see]
            now = jnp.maximum(before, jnp.max(scores, axis=0, keepdims=True))
            weights = jnp.exp2(scores - now)
            shrink = jnp.exp2(before - now)
            top[h : h + 1, see] = now
            total[h : h + 1, see] = total[h : h + 1, see] * shrink + jnp.sum(weights, axis=0, keepdims=True)
            head = slice(h * HEAD_SIZE, (h + 1) * HEAD_SIZE)
            out[head, see] = out[head, see] * shrink + dot_nn(values_t[head, :], weights.astype(BF16))

    window.loops(out.shape[1], step)
    for h in range(HEADS):
        head = slice(h * HEAD_SIZE, (h + 1) * HEAD_SIZE)
        out[head, :] = out[head, :] / total[h : h + 1, :]


def attend_back(
    window, code, low, high, w_key_t, w_value_t, spread, grad_spread, pairs, grad_pairs, lse, delta, bias,
    query_grad, window_grad, w_key_grad, w_value_grad,
):
    count = spread.shape[1]
    query_grad[...] = jnp.zeros_like(query_grad)
    w_key_grad[...] = jnp.zeros_like(w_key_grad)
    w_value_grad[...] = jnp.zeros_like(w_value_grad)
    window_grad[...] = jnp.zeros_like(window_grad)

    def step(at, lanes):
        see = slice(*lanes)
        seen = (slice(*lanes), slice(count + lanes[0], count + lanes[1]))
        rows = window.held[at, :]
        keys = dot_nt(rows, w_key_t[...]).astype(BF16)
        keys_t = dot_nt(w_key_t[...], rows).astype(BF16)
        values = dot_nt(rows, w_value_t[...]).astype(BF16)
        bias[:, see] = mask_bias(code[at, :], low[:, see], high[:, see])
        key_grads, value_grads = [], []
        for p in range(PAIRS):
            columns = slice(p * PAIR, (p + 1) * PAIR)
            probs, score_grads = [], []
            both_scores = pair_product(keys[:, columns], spread, p, lanes)
            both_dprobs = pair_product(values[:, columns], grad_spread, p, lanes)
            for h in (2 * p, 2 * p + 1):
                head = slice(h * HEAD_SIZE, (h + 1) * HEAD_SIZE)
                prob = jnp.exp2(both_scores[h % 2] * SCORE_SCALE + bias[:, see] - lse[h : h + 1, see])
                score_grad = (prob * (both_dprobs[h % 2] - delta[h : h + 1, see])).astype(BF16)
                query_grad[head, see] += dot_nn(keys_t[head, :], score_grad)
                probs.append(prob.astype(BF16))
                score_grads.append(score_grad)
            if count % LANES == 0:
                both = jnp.concatenate([pairs[p, r, :] for r in seen], axis=0)
                grad_both = jnp.concatenate([grad_pairs[p, r, :] for r in seen], axis=0)
                key_grads.append(dot_nn(jnp.concatenate(score_grads, axis=1), both))
                value_grads.append(dot_nn(jnp.concatenate(probs, axis=1), grad_both))
            else:
                key_grads.append(sum(dot_nn(x, pairs[p, r, :]) for x, r in zip(score_grads, seen)))
                value_grads.append(sum(dot_nn(x, grad_pairs[p, r, :]) for x, r in zip(probs, seen)))
        keys_low = (jnp.concatenate(key_grads, axis=1) * SCALE).astype(BF16)
        values_low = jnp.concatenate(value_grads, axis=1).astype(BF16)
        window_grad[at, :] = (dot_nn(keys_low, w_key_t[...]) + dot_nn(values_low, w_value_t[...])).astype(window_grad.dtype)
        w_key_grad[...] += dot_tn(rows, keys_low)
        w_value_grad[...] += dot_tn(rows, values_low)

    window.loops(count, step)


def forward_kernel(
    cols, bounds, own, content_window, encoded_window, gain, code, low, high_self, high_cross, pack_one, pack_two_in,
    self_t, lse_self, hidden, cross_t, lse_cross,
    spread, bias, top, total, low_t, content_held, encoded_held, pack_two, content_sems, encoded_sems, pack_sem,
):
    content = Window(bounds, content_window, content_held, content_sems)
    encoded = Window(bounds, encoded_window, encoded_held, encoded_sems)
    content.fetch()
    whole_pack = pltpu.make_async_copy(pack_two_in, pack_two, pack_sem.at[0])
    whole_pack.start()
    encoded.fetch()
    w_query_t, w_key_t, w_value_t = (Rows(pack_one, k, cols) for k in range(3))
    low_t[...] = dot_nt(w_query_t[...], own[...]).astype(BF16)
    spread_heads(low_t, spread)
    attend(content, code, low, high_self, w_key_t, w_value_t, spread, bias, top, total, self_t)
    lse_self[...] = top[...] + jnp.log2(total[...])
    whole_pack.wait()
    w_out, w_query_t, w_key_t, w_value_t = (Rows(pack_two, k, cols) for k in range(4))
    branch = dot_tn(self_t[...].astype(BF16), w_out[...])
    normed, _ = layer_norm(own[...].astype(F32) + branch)
    hidden[...] = normed * gain[...]
    low_t[...] = dot_nt(w_query_t[...], hidden[...].astype(BF16)).astype(BF16)
    spread_heads(low_t, spread)
    attend(encoded, code, low, high_cross, w_key_t, w_value_t, spread, bias, top, total, cross_t)
    lse_cross[...] = top[...] + jnp.log2(total[...])


def ffn_kernel(
    cols, hidden_one, cross_t, pack_two, gain_cross, pack_three_in, gain_final, out_grad,
    mixed, resid_grad, w_out_grad, grad_three_out, gain_cross_grad, gain_final_grad,
    normed_two, hidden_two_low, slope, active, sum_ffn, pack_out, pack_three, grad_three_pack, sems, out_sems,
):
    slices, units = pack_three.shape[0], pack_three.shape[1] // 2
    out_copy = pltpu.make_async_copy(pack_two.at[:, pl.ds(4 * cols, cols)], pack_out, sems.at[slices])
    out_copy.start()
    slice_copies = [pltpu.make_async_copy(pack_three_in.at[z], pack_three.at[z], sems.at[z]) for z in range(slices)]
    for copy in slice_copies:
        copy.start()
    out_copy.wait()
    w_out = Rows(pack_out, 0, cols)
    cross_low = cross_t[...].astype(BF16)
    normed, scale_two = layer_norm(hidden_one[...] + dot_tn(cross_low, w_out[...]))
    normed_two[...] = normed
    hidden_two = normed * gain_cross[...]
    hidden_two_low[...] = hidden_two.astype(BF16)
    sum_ffn[...] = hidden_two
    for z in range(slices):
        slice_copies[z].wait()
        inner = dot_nt(hidden_two_low[...], pack_three[z, 0:units, :])
        below = 0.5 * (1.0 + lax.erf(inner * math.sqrt(0.5)))
        slope[z] = below + inner * (jnp.exp2(inner * inner * (-0.5 * LOG2E)) * (1.0 / math.sqrt(2.0 * math.pi)))
        active[z] = (inner * below).astype(BF16)
        sum_ffn[...] += dot_nn(active[z], pack_three[z, units:, :])
    normed_three, scale_three = layer_norm(sum_ffn[...])
    mixed[...] = (normed_three * gain_final[...]).astype(BF16)
    grad_three, gain_grad = norm_back(out_grad[...].astype(F32), normed_three, scale_three, gain_final[...])
    gain_final_grad[...] = gain_grad
    ffn_low = grad_three.astype(BF16)
    result_copies = [pltpu.make_async_copy(grad_three_pack.at[:, z], grad_three_out.at[:, z], out_sems.at[z]) for z in range(slices)]
    sum_ffn[...] = grad_three
    for z in range(slices):
        write_pieces(grad_three_pack, z, units, dot_tn(active[z], ffn_low))
        inner_low = (dot_nt(ffn_low, pack_three[z, units:, :]) * slope[z]).astype(BF16)
        write_pieces(grad_three_pack, z, 0, dot_tn(inner_low, hidden_two_low[...]))
        sum_ffn[...] += dot_nn(inner_low, pack_three[z, 0:units, :])
        result_copies[z].start()
    grad, gain_grad = norm_back(sum_ffn[...], normed_two[...], scale_two, gain_cross[...])
    gain_cross_grad[...] = gain_grad
    resid_grad[...] = grad
    w_out_grad[...] = dot_nn(cross_low, grad.astype(BF16)).astype(BF16)
    for copy in result_copies:
        copy.wait()


def prepare_back(query, query_t, grad, grad_t, out, spread, grad_spread, pairs, grad_pairs, delta, low_t):
    low_t[...] = query_t.astype(BF16)
    spread_heads(low_t, spread)
    for p in range(PAIRS):
        pair_rows(query.astype(BF16), p, pairs)
        pair_rows(grad.astype(BF16), p, grad_pairs)
    low_t[...] = grad_t.astype(BF16)
    spread_heads(low_t, grad_spread)
    for h in range(HEADS):
        head = slice(h * HEAD_SIZE, (h + 1) * HEAD_SIZE)
        delta[h : h + 1, :] = jnp.sum(low_t[head, :].astype(F32) * out[head, :], axis=0, keepdims=True)


def cross_back_kernel(
    cols, bounds, own, self_t, gain, resid_two_grad, cross_t, lse, window_in, code, low, high, pack_two,
    w_cross_out_grad, gain_cross_grad, gain_final_grad, resid_one_grad, window_out, grad_two_pack,
    spread, grad_spread, pairs, grad_pairs, delta, bias, low_t, query_grad, key_sum, value_sum, held, window_grad, sems, out_sem,
    normed_one, scale_one,
):
    window = Window(bounds, window_in, held, sems)
    window.fetch()
    w_out, w_query_t, w_key_t, w_value_t, w_cross_out = (Rows(pack_two, k, cols) for k in range(5))
    self_low = self_t[...].astype(BF16)
    normed, scale = layer_norm(own[...].astype(F32) + dot_tn(self_low, w_out[...]))
    normed_one[...] = normed
    scale_one[...] = scale
    hidden_low = (normed * gain[...]).astype(BF16)
    branch_low = resid_two_grad[...].astype(BF16)
    prepare_back(
        dot_nt(hidden_low, w_query_t[...]), dot_nt(w_query_t[...], hidden_low),
        dot_nt(branch_low, w_cross_out[...]), dot_nt(w_cross_out[...], branch_low),
        cross_t, spread, grad_spread, pairs, grad_pairs, delta, low_t,
    )
    attend_back(
        window, code, low, high, w_key_t, w_value_t, spread, grad_spread, pairs, grad_pairs, lse, delta, bias,
        query_grad, window_grad, key_sum, value_sum,
    )
    result = pltpu.make_async_copy(window_grad, window_out, out_sem.at[0])
    result.start()
    query_low = (query_grad[...] * SCALE).astype(BF16)
    hidden_low = (normed_one[...] * gain[...]).astype(BF16)
    grad_one = resid_two_grad[...] + dot_tn(query_low, w_query_t[...])
    grad, gain_sum = norm_back(grad_one, normed_one[...], scale_one[...], gain[...])
    resid_one_grad[...] = grad
    write_rows(grad_two_pack, 0, cols, dot_nn(self_t[...].astype(BF16), grad.astype(BF16)))
    write_rows(grad_two_pack, 1, cols, dot_nn(query_low, hidden_low))
    write_rows(grad_two_pack, 2, cols, key_sum[...].T)
    write_rows(grad_two_pack, 3, cols, value_sum[...].T)
    write_rows(grad_two_pack, 4, cols, w_cross_out_grad[...])
    slices, rows, width = grad_two_pack.shape
    gains = jnp.concatenate([gain_sum, gain_cross_grad[...], gain_final_grad[...], jnp.zeros((13, width), F32)], axis=0)
    for z in range(slices):
        grad_two_pack[z, 5 * cols : 5 * cols + 16, :] = gains.astype(BF16)
        if rows > 5 * cols + 16:
            grad_two_pack[z, 5 * cols + 16 :, :] = jnp.zeros((rows - 5 * cols - 16, width), BF16)
    result.wait()


def self_back_kernel(
    cols, bounds, own, resid_one_grad, pack_two, self_t, lse, window_in, code, low, high, pack_one,
    own_grad, window_out, grad_one_pack,
    spread, grad_spread, pairs, grad_pairs, delta, bias, low_t, query_grad, key_sum, value_sum, held, window_grad, sems, out_sem,
    pack_out, pack_sem,
):
    out_copy = pltpu.make_async_copy(pack_two.at[:, pl.ds(0, cols)], pack_out, pack_sem.at[0])
    out_copy.start()
    window = Window(bounds, window_in, held, sems)
    window.fetch()
    out_copy.wait()
    w_query_t, w_key_t, w_value_t = (Rows(pack_one, k, cols) for k in range(3))
    w_out = Rows(pack_out, 0, cols)
    branch_low = resid_one_grad[...].astype(BF16)
    prepare_back(
        dot_nt(own[...], w_query_t[...]), dot_nt(w_query_t[...], own[...]),
        dot_nt(branch_low, w_out[...]), dot_nt(w_out[...], branch_low),
        self_t, spread, grad_spread, pairs, grad_pairs, delta, low_t,
    )
    attend_back(
        window, code, low, high, w_key_t, w_value_t, spread, grad_spread, pairs, grad_pairs, lse, delta, bias,
        query_grad, window_grad, key_sum, value_sum,
    )
    result = pltpu.make_async_copy(window_grad, window_out, out_sem.at[0])
    result.start()
    query_low = (query_grad[...] * SCALE).astype(BF16)
    write_rows(grad_one_pack, 0, cols, dot_nn(query_low, own[...]))
    write_rows(grad_one_pack, 1, cols, key_sum[...].T)
    write_rows(grad_one_pack, 2, cols, value_sum[...].T)
    slices, rows, width = grad_one_pack.shape
    if rows > 3 * cols:
        grad_one_pack[:, 3 * cols :, :] = jnp.zeros((slices, rows - 3 * cols, width), BF16)
    own_grad[...] = (resid_one_grad[...] + dot_tn(query_low, w_query_t[...])).astype(BF16)
    result.wait()


def finish_kernel(cols, units, slices, part, *refs):
    blocks, rows_in, (sum_one, sum_two, sum_three) = refs[:slices], refs[slices : slices + 3], refs[slices + 3 : slices + 6]
    outs = refs[slices + 6 :]
    step = pl.program_id(0)
    came = lax.rem(part[0, 0] + slices - step, slices)
    for d, ref in enumerate(blocks):

        @pl.when(came == d)
        def _(ref=ref):
            outs[0][...] = ref[...]

    for source, target in zip(rows_in, outs[1:4]):
        target[...] = source[...].astype(F32)

    @pl.when(step == 0)
    def _():
        w_query, w_key, w_value, w_out, w_cross_query, w_cross_key, w_cross_value, w_cross_out, w_inner, w_outer = outs[4:14]
        for k, target in enumerate((w_query, w_key, w_value)):
            target[...] = sum_one[k * cols : (k + 1) * cols, :].astype(F32).T
        w_out[...] = sum_two[0:cols, :].astype(F32)
        for k, target in enumerate((w_cross_query, w_cross_key, w_cross_value)):
            target[...] = sum_two[(1 + k) * cols : (2 + k) * cols, :].astype(F32).T
        w_cross_out[...] = sum_two[4 * cols : 5 * cols, :].astype(F32)
        w_inner[...] = sum_three[0:units, :].astype(F32).T
        w_outer[...] = sum_three[units : 2 * units, :].astype(F32)
        gains = sum_two[5 * cols : 5 * cols + 16, :].astype(F32)
        for k, target in enumerate(outs[14:17]):
            target[...] = gains[k : k + 1, :]


def call(kernel, outs, scratch, smem, *args, far=(), far_outs=(), micros=20):
    def space(k, left, scalars):
        return pl.ANY if k in left else pltpu.SMEM if k < scalars else pltpu.VMEM

    return pl.pallas_call(
        kernel,
        out_shape=[jax.ShapeDtypeStruct(shape, kind) for shape, kind in outs],
        in_specs=[pl.BlockSpec(memory_space=space(k, far, smem)) for k in range(len(args))],
        out_specs=[pl.BlockSpec(memory_space=space(k, far_outs, 0)) for k in range(len(outs))],
        scratch_shapes=[pltpu.SemaphoreType.DMA((shape,)) if kind is None else pltpu.VMEM(shape, kind) for shape, kind in scratch],
        compiler_params=pltpu.CompilerParams(vmem_limit_bytes=VMEM_LIMIT),
        cost_estimate=pl.CostEstimate(flops=micros * 10**9, bytes_accessed=micros * 10**6, transcendentals=0),
    )(*args)


def padded(size, unit):
    return -(-size // unit) * unit


def talk(kernel, outs, out_spaces, scratch, copies, number, spaces, *args):
    return pl.pallas_call(
        kernel,
        out_shape=[jax.ShapeDtypeStruct(shape, kind) for shape, kind in outs],
        in_specs=[pl.BlockSpec(memory_space=space) for space in spaces],
        out_specs=[pl.BlockSpec(memory_space=space) for space in out_spaces],
        scratch_shapes=[pltpu.SemaphoreType.DMA((n,)) for n in (copies[0], copies[0], copies[1])] + [pltpu.VMEM(shape, kind) for shape, kind in scratch],
        compiler_params=pltpu.CompilerParams(vmem_limit_bytes=VMEM_LIMIT, collective_id=number, has_side_effects=True),
        cost_estimate=pl.CostEstimate(flops=80 * 10**9, bytes_accessed=80 * 10**6, transcendentals=0),
    )(*args)


def body(
    query_state, content, encoded, sentence_lengths, key_score, query_cut, w_query, w_key, w_value, w_out, gain_self,
    w_cross_query, w_cross_key, w_cross_value, w_cross_out, gain_cross, w_inner, w_outer, gain_final, out_grad,
):
    rows, width = query_state.shape
    slices = lax.axis_size("head")
    count = rows // slices
    lanes = math.gcd(count, LANES)
    wide = padded(count + 2 * DOC_LEN + CHUNK, lanes)
    spare = wide - count - 2 * DOC_LEN
    seq, part = lax.axis_index("seq"), lax.axis_index("head")
    begin = seq * rows + part * count
    score = lax.dynamic_slice_in_dim(jnp.pad(key_score, (DOC_LEN, DOC_LEN + spare)), begin, wide, 0).reshape(wide // lanes, lanes)
    cut = lax.dynamic_slice_in_dim(query_cut, begin, count, 0).reshape(1, count)
    gain_self, gain_cross, gain_final = (g.reshape(1, width) for g in (gain_self, gain_cross, gain_final))

    peers = lax.axis_size("seq")
    chips = peers // 2
    cols, units = w_query.shape[1], w_inner.shape[1]
    unit = 16 * peers
    sizes = [padded(n, unit) for n in (3 * cols, 5 * cols, 2 * units)]
    grad_sizes = [sizes[0], padded(5 * cols + 16, unit), sizes[2]]

    share = sizes[2] // peers
    slice_three = jnp.concatenate([w_inner.T, w_outer, jnp.zeros((sizes[2] - 2 * units, width), BF16)], axis=0)
    share_three = lax.dynamic_slice_in_dim(slice_three, seq * share, share, 0)
    pack_three = lax.all_gather(share_three, ("head", "seq"), axis=0, tiled=True).reshape(slices, sizes[2], width)
    start_copies = 2 * (slices - 1) * (2 * chips) + 4 * slices
    hbm, vmem, smem = pl.ANY, pltpu.VMEM, pltpu.SMEM
    (
        content_window, encoded_window, pack_one, pack_two, own, own_out_grad, code, low, high_self, high_cross, bounds,
    ) = talk(
        partial(start_kernel, peers, slices, count),
        [((wide, width), BF16)] * 2 + [((slices, n, width), BF16) for n in sizes[:2]] + [((count, width), BF16)] * 2
        + [((wide, 1), F32)] + [((1, count), F32)] * 3 + [((1, 4), jnp.int32)],
        [vmem] * 10 + [smem],
        [((DOC_LEN, width), BF16), ((padded(wide // lanes, 8), lanes), F32)], (start_copies, 8 * slices + 16), 0,
        [hbm] * 4 + [vmem] * 8 + [smem] + [vmem] * 2,
        content, encoded, query_state, out_grad, w_query, w_key, w_value, w_out,
        w_cross_query, w_cross_key, w_cross_value, w_cross_out, sentence_lengths.reshape(1, -1), score, cut,
    )

    def split_refs(kernel, ins, outs):
        def run(*refs):
            return kernel(refs[:ins], refs[ins : ins + outs], refs[ins + outs :])
        return run

    touched = -(-wide // CHUNK)
    window_held = [((wide, width), BF16)]
    self_t, lse_self, hidden_one, cross_t, lse_cross = call(
        partial(forward_kernel, cols),
        [((width, count), F32), ((HEADS, count), F32), ((count, width), F32), ((width, count), F32), ((HEADS, count), F32)],
        [((HEADS * PAIR, count), BF16), ((CHUNK, count), F32), ((HEADS, count), F32), ((HEADS, count), F32), ((width, count), BF16)]
        + window_held * 2 + [((slices, sizes[1], width), BF16), (touched, None), (touched, None), (1, None)], 1,
        bounds, own, content_window, encoded_window, gain_self, code, low, high_self, high_cross, pack_one, pack_two, far=(2, 3, 10),
    )
    mixed, resid_two_grad, w_cross_out_grad, grads_three, gain_cross_grad, gain_final_grad = call(
        partial(ffn_kernel, cols),
        [
            ((count, width), BF16), ((count, width), F32), ((width, width), BF16), ((peers, slices, grad_sizes[2] // peers, width), BF16),
            ((1, width), F32), ((1, width), F32),
        ],
        [
            ((count, width), F32), ((count, width), BF16), ((slices, count, units), F32),
            ((slices, count, units), BF16), ((count, width), F32), ((slices, cols, width), BF16), ((slices, sizes[2], width), BF16),
            ((peers, slices, grad_sizes[2] // peers, width), BF16), (slices + 1, None), (slices, None),
        ], 0,
        hidden_one, cross_t, pack_two, gain_cross, pack_three, gain_final, own_out_grad, far=(2, 4), far_outs=(3,),
    )
    back = [
        ((HEADS * PAIR, count), BF16), ((HEADS * PAIR, count), BF16), ((PAIRS, 2 * count, PAIR), BF16),
        ((PAIRS, 2 * count, PAIR), BF16), ((HEADS, count), F32), ((CHUNK, count), F32), ((width, count), BF16),
        ((width, count), F32), ((width, width), F32), ((width, width), F32),
    ] + window_held * 2 + [(touched, None), (1, None)]
    resid_one_grad, encoded_part, grads_two = call(
        partial(cross_back_kernel, cols),
        [((count, width), F32), ((wide, width), BF16), ((slices, grad_sizes[1], width), BF16)],
        back + [((count, width), F32), ((count, 1), F32)], 1,
        bounds, own, self_t, gain_self, resid_two_grad, cross_t, lse_cross, encoded_window, code, low, high_cross, pack_two,
        w_cross_out_grad, gain_cross_grad, gain_final_grad, far=(7,), far_outs=(1,), micros=4,
    )
    own_grad, content_part, grads_one = call(
        partial(self_back_kernel, cols),
        [((count, width), BF16), ((wide, width), BF16), ((slices, grad_sizes[0], width), BF16)],
        back + [((slices, cols, width), BF16), (1, None)], 1,
        bounds, own, resid_one_grad, pack_two, self_t, lse_self, content_window, code, low, high_self, pack_one,
        far=(3, 6), far_outs=(1,), micros=4,
    )

    mixed_blocks = [mixed] + [lax.ppermute(mixed, "head", [(i, (i + d) % slices) for i in range(slices)]) for d in range(1, slices)]
    plane_three = lax.psum_scatter(grads_three, "seq", scatter_dimension=0, tiled=True).reshape(grads_three.shape[1:])
    blocks, parts, grads, planes = [own_grad], [content_part, encoded_part], [grads_one, grads_two], [plane_three]
    weight_scratch = []
    for n in grad_sizes[: len(grads)]:
        half, size = n // 2, n // 2 // chips
        weight_scratch += [
            ((slices, half, width), BF16), ((slices, half, width), BF16), ((chips - 1, slices, size, width), BF16),
            ((slices, size, width), BF16), ((slices - 1, size, width), BF16),
        ]
    halves = 2 if slices <= 4 else 1
    units_in = (slices - 1) * halves
    part_scratch = [
        ((rows, width), BF16), ((DOC_LEN, width), BF16), ((DOC_LEN, width), BF16),
        ((units_in, count // halves, width), BF16), ((units_in, count // halves, width), BF16),
    ] * len(parts)
    plane_scratch = []
    for n in grad_sizes[len(grads) :]:
        plane_scratch += [((slices, n // peers, width), BF16), ((slices - 1, n // peers, width), BF16)]
    ins, outs = (len(blocks), len(parts), len(grads), len(planes)), (len(blocks), len(parts), len(grad_sizes))

    def end(refs, out_refs, scratch):
        a, b, c = ins[0], ins[0] + ins[1], sum(ins[:3])
        end_kernel(
            peers, slices, count, refs[:a], refs[a:b], refs[b:c], refs[c:], out_refs[: outs[0]],
            out_refs[outs[0] : outs[0] + outs[1]], out_refs[outs[0] + outs[1] :], scratch,
        )

    end_copies = len(grad_sizes) * (1 + 3 * (chips - 1) + slices) + len(parts) * 2 * slices + (len(blocks) + 2 * len(parts)) * 2 * slices * halves
    results = talk(
        split_refs(end, sum(ins), sum(outs)),
        [((rows, width), BF16)] * (len(blocks) + len(parts)) + [((n, width), BF16) for n in grad_sizes], [vmem] * sum(outs),
        weight_scratch + part_scratch + plane_scratch, (end_copies, 8 * slices + 8), 1, [hbm] * sum(ins), *blocks, *parts, *grads, *planes,
    )
    query_state_grad, content_grad, encoded_grad, sum_one, sum_two, sum_three = results

    square, tall = ((width, cols), F32), ((cols, width), F32)
    finals = [((rows, width), BF16)] + [((rows, width), F32)] * 3 + [square] * 3 + [tall, square, square, square, tall]
    finals += [((width, units), F32), ((units, width), F32)] + [((1, width), F32)] * 3
    by_rows = pl.BlockSpec((count, width), lambda i: (i, 0))

    def whole(shape):
        return pl.BlockSpec(shape, lambda i: (0,) * len(shape))

    sums = [sum_one, sum_two, sum_three]
    results = pl.pallas_call(
        partial(finish_kernel, cols, units, slices),
        grid=(slices,),
        out_shape=[jax.ShapeDtypeStruct(shape, kind) for shape, kind in finals],
        in_specs=[pl.BlockSpec(memory_space=smem)] + [whole((count, width))] * slices + [by_rows] * 3 + [whole(x.shape) for x in sums],
        out_specs=[by_rows] * 4 + [whole(shape) for shape, _ in finals[4:]],
        compiler_params=pltpu.CompilerParams(vmem_limit_bytes=VMEM_LIMIT),
    )(part.reshape(1, 1).astype(jnp.int32), *mixed_blocks, query_state_grad, content_grad, encoded_grad, *sums)
    (
        mixed, query_state_grad, content_grad, encoded_grad, w_query_grad, w_key_grad, w_value_grad, w_out_grad,
        w_cross_query_grad, w_cross_key_grad, w_cross_value_grad, w_cross_out_grad, w_inner_grad, w_outer_grad, *gains,
    ) = results
    gains = [g.reshape(width) for g in gains]
    return (
        mixed, query_state_grad, content_grad, encoded_grad, w_query_grad, w_key_grad, w_value_grad, w_out_grad, gains[0],
        w_cross_query_grad, w_cross_key_grad, w_cross_value_grad, w_cross_out_grad, gains[1], w_inner_grad, w_outer_grad, gains[2],
    )


def solution(mesh):
    rows, whole, columns, split = P("seq", None), P(), P(None, "head"), P("head", None)
    in_specs = (
        rows, rows, rows, whole, whole, whole, columns, columns, columns, split, whole,
        columns, columns, columns, split, whole, columns, split, whole, rows,
    )
    out_specs = (
        rows, rows, rows, rows, columns, columns, columns, split, whole,
        columns, columns, columns, split, whole, columns, split, whole,
    )
    return jax.shard_map(body, mesh=mesh, in_specs=in_specs, out_specs=out_specs, check_vma=False)
```

```python
from functools import partial
import math

import jax
import jax.numpy as jnp
from jax import lax
from jax.experimental import pallas as pl
from jax.experimental.pallas import tpu as pltpu
from jax.sharding import PartitionSpec as P

HEADS = 8
HEAD_SIZE = 64
PAIR = 2 * HEAD_SIZE
PAIRS = HEADS // 2
DOC_LEN = 1024
CHUNK = 528
LANES = 128
IN_FLIGHT = 2
EPS = 1e-05
NEG_BIG = -1e30
LOG2E = 1.4426950408889634
SCALE = 1.0 / math.sqrt(HEAD_SIZE)
SCORE_SCALE = SCALE * LOG2E
CODES = 128
BF16 = jnp.bfloat16
F32 = jnp.float32
VMEM_LIMIT = 60 << 20


def dot_nn(left, right):
    return lax.dot_general(left, right, (((1,), (0,)), ((), ())), preferred_element_type=F32)


def dot_nt(left, right):
    return lax.dot_general(left, right, (((1,), (1,)), ((), ())), preferred_element_type=F32)


def dot_tn(left, right):
    return lax.dot_general(left, right, (((0,), (0,)), ((), ())), preferred_element_type=F32)


def chunk_range(bounds):
    start = bounds[0, 0] // 16 * 16
    return start, (bounds[0, 1] - start + CHUNK - 1) // CHUNK


def chunk_rows(start, c):
    return pl.ds(pl.multiple_of(start + c * CHUNK, 16), CHUNK)


class Window:
    def __init__(self, bounds, source, held, sems):
        self.bounds, self.source, self.held, self.sems = bounds, source, held, sems
        self.start, self.chunks = chunk_range(bounds)

    def copy(self, c):
        rows = chunk_rows(self.start, c)
        return pltpu.make_async_copy(self.source.at[rows], self.held.at[rows], self.sems.at[c])

    def fetch(self):
        def one(c, carry):
            self.copy(c).start()
            return carry

        lax.fori_loop(0, self.chunks, one, 0)

    def loops(self, count, step):
        bounds, start, chunks = self.bounds, self.start, self.chunks

        def loop(number, size, where):
            def one(i, carry):
                c, lane = where(i)
                self.copy(c).wait()
                step(c, pl.ds(lane, size) if isinstance(lane, int) else pl.ds(pl.multiple_of(lane, LANES), size))
                return carry

            lax.fori_loop(0, number, one, 0)

        if count != 3 * LANES:
            return loop(chunks, count, lambda i: (i, 0))
        thirds = [(bounds[0, k] - start) // CHUNK for k in (2, 3)] + [(bounds[0, k] - start + CHUNK - 1) // CHUNK for k in (4, 5)]
        edges = [chunks * 0]
        for edge in thirds:
            edges.append(jnp.clip(edge, edges[-1], chunks))
        edges.append(chunks)

        def two(first, second, second_lane):
            number = edges[first + 1] - edges[first]

            def where(i):
                early = i < number
                return jnp.where(early, edges[first] + i, edges[second] + i - number), jnp.where(early, 0, second_lane)

            return number + edges[second + 1] - edges[second], where

        loop(edges[3] - edges[2], count, lambda i: (edges[2] + i, 0))
        number, where = two(1, 3, LANES)
        loop(number, 2 * LANES, where)
        number, where = two(0, 4, 2 * LANES)
        loop(number, LANES, where)


def layer_norm(resid):
    mean_row = jnp.mean(resid, axis=1, keepdims=True)
    centred = resid - mean_row
    var_row = jnp.mean(centred * centred, axis=1, keepdims=True)
    scale_row = lax.rsqrt(var_row + EPS)
    return centred * scale_row, scale_row


def norm_back(grad, normed, scale_row, gain):
    gain_grad = jnp.sum(grad * normed, axis=0, keepdims=True)
    scaled = grad * gain
    centre = jnp.mean(scaled, axis=1, keepdims=True)
    along = jnp.mean(scaled * normed, axis=1, keepdims=True)
    return scale_row * (scaled - centre - normed * along), gain_grad


def spread_heads(source, target):
    target[...] = jnp.zeros_like(target)
    for h in range(HEADS):
        row = h * PAIR + (h % 2) * HEAD_SIZE
        target[row : row + HEAD_SIZE, :] = source[h * HEAD_SIZE : (h + 1) * HEAD_SIZE, :]


def pair_rows(source, p, target):
    rows = source.shape[0]
    both = source[:, p * PAIR : (p + 1) * PAIR]
    lane = lax.broadcasted_iota(jnp.int32, both.shape, 1)
    zero = jnp.zeros_like(both)
    target[p, 0:rows, :] = jnp.where(lane < HEAD_SIZE, both, zero)
    target[p, rows : 2 * rows, :] = jnp.where(lane < HEAD_SIZE, zero, both)


MESH = pl.DeviceIdType.MESH


class Copies:
    def __init__(self, send, recv, local):
        self.send, self.recv, self.local = send, recv, local
        self.remotes, self.locals = 0, 0

    def remote(self, source, target, seq, part):
        k = self.remotes
        self.remotes += 1
        return pltpu.make_async_remote_copy(
            src_ref=source, dst_ref=target, send_sem=self.send.at[k], recv_sem=self.recv.at[k],
            device_id=(seq, part), device_id_type=MESH,
        )

    def own(self, source, target):
        k = self.locals
        self.locals += 1
        return pltpu.make_async_copy(source, target, self.local.at[k])


def greet(seq, part, peers, slices):
    barrier = pltpu.get_barrier_semaphore()
    for d in range(1, peers):
        pl.semaphore_signal(barrier, inc=1, device_id=(lax.rem(seq + d, peers), part), device_id_type=MESH)
    for d in range(1, slices):
        pl.semaphore_signal(barrier, inc=1, device_id=(seq, lax.rem(part + d, slices)), device_id_type=MESH)
    pl.semaphore_wait(barrier, peers - 1 + slices - 1)


def halo_sizes(part, count, rows):
    return max(0, DOC_LEN - part * count), max(0, (part + 1) * count + DOC_LEN - rows)


def put_rows(whole, part, row, ref, flip):
    value = ref[...]
    if flip:
        value = value.astype(F32).T.astype(BF16)
    whole[part, row : row + value.shape[0], :] = value


def pad_rows(whole, part, row):
    if row < whole.shape[1]:
        whole[part, row:, :] = jnp.zeros((whole.shape[1] - row, whole.shape[2]), BF16)


def find_sentences(begin, count, total_rows, lengths, score, cut, code, low, high_self, high_cross, bounds, blocks_code):
    blocks, lanes = score.shape
    pos = lax.broadcasted_iota(jnp.int32, (blocks, lanes), 0) * lanes + lax.broadcasted_iota(jnp.int32, (blocks, lanes), 1)
    pos = pos + (begin - DOC_LEN)
    own_pos = lax.broadcasted_iota(jnp.int32, (1, count), 1) + begin
    zero = jnp.zeros((blocks, lanes), jnp.int32)
    last_pos = begin + count - 1

    def one(s, carry):
        start, sentence, first, own_sentence, first_row, last_row, thirds = carry
        size = lengths[0, s]
        end = start + size
        passed = pos >= end
        sentence = sentence + jnp.where(passed, 1, 0)
        first = first + jnp.where(passed, size, 0)
        own_sentence = own_sentence + jnp.where(own_pos >= end, 1, 0)
        first_row = first_row + jnp.where(begin >= end, size, 0)
        last_row = last_row + jnp.where(last_pos >= start, size, 0)
        thirds = tuple(t + jnp.where(begin + LANES * (1 + k) >= end, size, 0) for k, t in enumerate(thirds[:2])) + tuple(
            t + jnp.where(begin + LANES * (1 + k) - 1 >= start, size, 0) for k, t in enumerate(thirds[2:])
        )
        return end, sentence, first, own_sentence, first_row, last_row, thirds

    none = lengths[0, 0] * 0
    carry = (none, zero, zero, jnp.zeros((1, count), jnp.int32), none, none, (none,) * 4)
    _, sentence, first, own_sentence, first_row, last_row, thirds = lax.fori_loop(0, lengths.shape[1], one, carry)
    shown = jnp.where(pos == first, -1, score[...])
    inside = jnp.logical_and(pos >= 0, pos < total_rows)
    blocks_code[0:blocks, :] = jnp.where(inside, sentence * CODES + shown, -CODES).astype(F32)
    for b in range(0, blocks, 8):
        turned = blocks_code[b : b + 8, :].T
        for j in range(min(8, blocks - b)):
            code[(b + j) * lanes : (b + j + 1) * lanes, :] = turned[:, j : j + 1]
    low[...] = (own_sentence * CODES - 1).astype(F32)
    high_self[...] = (own_sentence * CODES + cut[...]).astype(F32)
    high_cross[...] = (own_sentence * CODES + CODES // 2).astype(F32)
    origin = begin - DOC_LEN
    bounds[0, 0] = first_row - origin
    bounds[0, 1] = last_row - origin
    for k, row in enumerate(thirds):
        bounds[0, 2 + k] = row - origin


def start_kernel(
    peers, slices, count, content, encoded, query_state, out_grad, w_query, w_key, w_value, w_out,
    w_cross_query, w_cross_key, w_cross_value, w_cross_out, lengths, score, cut,
    content_window, encoded_window, all_one, all_two, own, own_out_grad, code, low, high_self, high_cross, bounds,
    send, recv, local, zeros, blocks_code,
):
    seq, part = lax.axis_index("seq"), lax.axis_index("head")
    chip, core = seq // 2, lax.rem(seq, 2)
    chips = peers // 2
    sibling = chip * 2 + 1 - core
    rows = content.shape[0]
    span = count + 2 * DOC_LEN
    spare = content_window.shape[0] - span
    copies = Copies(send, recv, local)
    cols = w_query.shape[1]
    for k, (ref, flip) in enumerate(((w_query, True), (w_key, True), (w_value, True))):
        put_rows(all_one, part, k * cols, ref, flip)
    pad_rows(all_one, part, 3 * cols)
    greet(seq, part, peers, slices)
    waits = []
    for source, target in ((query_state, own), (out_grad, own_out_grad)):
        mine = copies.own(source.at[pl.ds(pl.multiple_of(part * count, 16), count)], target)
        mine.start()
        waits.append(mine.wait)

    def halo(source, window):
        for k in range(slices):
            below, above = halo_sizes(k, count, rows)
            low = max(0, k * count - DOC_LEN)
            inner = span - below - above
            mine = copies.own(source.at[pl.ds(low, inner)], window.at[pl.ds(below, inner)])
            tail = copies.own(zeros.at[pl.ds(0, spare)], window.at[pl.ds(span, spare)])
            up = down = fill_low = fill_high = None
            if below:
                up = copies.remote(source.at[pl.ds(rows - below, below)], window.at[pl.ds(0, below)], seq + 1, part)
                fill_low = copies.own(zeros.at[pl.ds(0, below)], window.at[pl.ds(0, below)])
            if above:
                down = copies.remote(source.at[pl.ds(0, above)], window.at[pl.ds(span - above, above)], seq - 1, part)
                fill_high = copies.own(zeros.at[pl.ds(0, above)], window.at[pl.ds(span - above, above)])
            here, first, last = part == k, seq == 0, seq == peers - 1

            def start(mine=mine, tail=tail, up=up, down=down, fill_low=fill_low, fill_high=fill_high, here=here):
                @pl.when(here)
                def _():
                    if up is not None:
                        pl.when(jnp.logical_not(last))(up.start)
                        pl.when(first)(fill_low.start)
                    if down is not None:
                        pl.when(jnp.logical_not(first))(down.start)
                        pl.when(last)(fill_high.start)
                    mine.start()
                    tail.start()

            def finish(mine=mine, tail=tail, up=up, down=down, fill_low=fill_low, fill_high=fill_high, here=here):
                @pl.when(here)
                def _():
                    if up is not None:
                        pl.when(jnp.logical_not(last))(up.wait_send)
                        pl.when(jnp.logical_not(first))(up.wait_recv)
                        pl.when(first)(fill_low.wait)
                    if down is not None:
                        pl.when(jnp.logical_not(first))(down.wait_send)
                        pl.when(jnp.logical_not(last))(down.wait_recv)
                        pl.when(last)(fill_high.wait)
                    mine.wait()
                    tail.wait()

            start()
            waits.append(finish)

    packs = (all_one, all_two)

    def piece(ref, owner, index, size):
        return ref.at[owner, pl.ds(pl.multiple_of(index * size, 16), size)]

    across = {}
    for n, whole in enumerate(packs):
        size = whole.shape[1] // peers
        for d in range(1, slices):
            to = lax.rem(part + d, slices)
            across[n, d] = copies.remote(piece(whole, part, seq, size), piece(whole, part, seq, size), seq, to)
            across[n, d].start()
        if n == 0:
            zeros[...] = jnp.zeros_like(zeros)
            halo(content, content_window)
            put_rows(all_two, part, 0, w_out, False)
            for k, ref in enumerate((w_cross_query, w_cross_key, w_cross_value)):
                put_rows(all_two, part, (1 + k) * cols, ref, True)
            put_rows(all_two, part, 4 * cols, w_cross_out, False)
            pad_rows(all_two, part, 5 * cols)
    find_sentences(seq * rows + part * count, count, peers * rows, lengths, score, cut, code, low, high_self, high_cross, bounds, blocks_code)
    round_plane, to_sibling = {}, {}
    for n, whole in enumerate(packs):
        size = whole.shape[1] // peers
        for d in range(1, slices):
            across[n, d].wait_recv()
            owner = lax.rem(part + slices - d, slices)
            got = piece(whole, owner, seq, size)
            for e in range(1, chips):
                round_plane[n, d, e] = copies.remote(got, got, lax.rem(chip + e, chips) * 2 + core, part)
                round_plane[n, d, e].start()
            to_sibling[n, d, 0] = copies.remote(got, got, sibling, part)
            to_sibling[n, d, 0].start()
    halo(encoded, encoded_window)
    for n, whole in enumerate(packs):
        size = whole.shape[1] // peers
        for d in range(1, slices):
            owner = lax.rem(part + slices - d, slices)
            for e in range(1, chips):
                round_plane[n, d, e].wait_recv()
                got = piece(whole, owner, lax.rem(chip + chips - e, chips) * 2 + core, size)
                to_sibling[n, d, e] = copies.remote(got, got, sibling, part)
                to_sibling[n, d, e].start()
    for copy in to_sibling.values():
        copy.wait_recv()
    for copy in (*across.values(), *round_plane.values(), *to_sibling.values()):
        copy.wait_send()
    for wait in waits:
        wait()


def add_rows(target, source, target_at, source_at, size):
    step = 64 if size % 64 == 0 else 16

    def one(i, carry):
        to = pl.ds(pl.multiple_of(target_at + i * step, 16), step)
        by = pl.ds(pl.multiple_of(source_at + i * step, 16), step)
        target[to, :] = (target[to, :].astype(F32) + source[by, :].astype(F32)).astype(BF16)
        return carry

    lax.fori_loop(0, size // step, one, 0)


def end_kernel(
    peers, slices, count, blocks, parts, packs, plane_sums, outs, part_outs, pack_outs, scratch,
):
    seq, part = lax.axis_index("seq"), lax.axis_index("head")
    chip, core = seq // 2, lax.rem(seq, 2)
    chips = peers // 2
    sibling = chip * 2 + 1 - core
    rows = slices * count
    span = count + 2 * DOC_LEN
    send, recv, local = scratch[:3]
    copies = Copies(send, recv, local)
    first, last = seq == 0, seq == peers - 1
    start_line, end_line = part == 0, part == slices - 1
    greet(seq, part, peers, slices)
    sent = []

    def block(ref, index):
        return ref.at[pl.ds(pl.multiple_of(index * count, 16), count)]

    weight_scratch = scratch[3 : 3 + 3 * len(packs)]
    to_core, held = [], []
    for n, pack in enumerate(packs):
        half = pack.shape[1] // 2
        sibling_sum, mine = weight_scratch[3 * n : 3 * n + 2]
        copy = copies.remote(pack.at[:, pl.ds(pl.multiple_of((1 - core) * half, 16), half)], sibling_sum, sibling, part)
        copy.start()
        to_core.append(copy)
        keep = copies.own(pack.at[:, pl.ds(pl.multiple_of(core * half, 16), half)], mine)
        keep.start()
        held.append(keep)
        sent.append(copy)

    part_scratch = scratch[3 + 3 * len(packs) :]
    halos = []
    for n, grad in enumerate(parts):
        total, from_above, from_below = part_scratch[5 * n : 5 * n + 3]
        for k in range(slices):
            below, above = halo_sizes(k, count, rows)
            low = max(0, k * count - DOC_LEN)
            inner = span - below - above
            mine = copies.own(grad.at[pl.ds(below, inner)], total.at[pl.ds(low, inner)])
            down = up = None
            if below:
                down = copies.remote(grad.at[pl.ds(0, below)], from_above.at[pl.ds(0, below)], seq - 1, part)
            if above:
                up = copies.remote(grad.at[pl.ds(span - above, above)], from_below.at[pl.ds(0, above)], seq + 1, part)
            halos.append((n, k, below, above, low, inner, mine, down, up))

            @pl.when(part == k)
            def _(low=low, inner=inner, mine=mine, down=down, up=up, total=total):
                if down is not None:
                    pl.when(jnp.logical_not(first))(down.start)
                if up is not None:
                    pl.when(jnp.logical_not(last))(up.start)
                mine.start()
                if low:
                    total[0:low, :] = jnp.zeros((low, total.shape[1]), BF16)
                if low + inner < rows:
                    total[low + inner : rows, :] = jnp.zeros((rows - low - inner, total.shape[1]), BF16)

    def finish_halo(which):
        for n, k, below, above, low, inner, mine, down, up in halos:
            if n != which:
                continue
            total, from_above, from_below = part_scratch[5 * n : 5 * n + 3]

            @pl.when(part == k)
            def _(below=below, above=above, mine=mine, down=down, up=up, total=total, from_above=from_above, from_below=from_below):
                mine.wait()
                if down is not None:
                    pl.when(jnp.logical_not(first))(down.wait_send)

                    @pl.when(jnp.logical_not(last))
                    def _():
                        down.wait_recv()
                        add_rows(total, from_above, rows - below, 0, below)

                if up is not None:
                    pl.when(jnp.logical_not(last))(up.wait_send)

                    @pl.when(jnp.logical_not(first))
                    def _():
                        up.wait_recv()
                        add_rows(total, from_below, 0, 0, above)

    halves = 2 if slices <= 4 else 1
    sub = count // halves

    def unit_rows(ref, index, h, size=count, sub=sub):
        return ref.at[pl.ds(index * size + h * sub, sub)]

    def gather_rounds(out, me):
        rounds, flows = {}, ((1, slices - 1 - me), (-1, me))
        for sign, onward in flows:
            behind = me if sign > 0 else slices - 1 - me
            sends, waits = {}, {}
            for k in range(behind + 1):
                for h in range(halves):
                    ref = (me - sign * k, h)
                    if onward:
                        sends[k * halves + h] = ref
                    if k:
                        waits[k * halves + h] = ref
            rounds[sign] = (sends, waits)
        return rounds

    def line_gather(out, me, sems):
        steps, ends = [], []
        ring = gather_rounds(out, me)

        def onward(sign, i):
            ref = unit_rows(out, *ring[sign][0][i])
            return sems(sign, i, ref, ref, sign)

        def step(i):
            for sign in (1, -1):
                sends, waits = ring[sign]
                if i in waits:
                    sems(sign, i - halves, unit_rows(out, *waits[i]), unit_rows(out, *waits[i]), 0).wait_recv()
                if i in sends:
                    if i >= IN_FLIGHT:
                        onward(sign, i - IN_FLIGHT).wait_send()
                    onward(sign, i).start()

        def finish():
            for sign in (1, -1):
                sends, _ = ring[sign]
                for i in sorted(sends)[-IN_FLIGHT:]:
                    onward(sign, i).wait_send()

        return [partial(step, i) for i in range(slices * halves)], finish

    def line_sum(total, ins, out, me, sems, size=count, halves=halves):
        units, sub = (slices - 1) * halves, size // halves
        before = {1: [], -1: []}

        def place(sign, i):
            return slices - 1 - i // halves if sign > 0 else i // halves

        def slot(sign, i):
            return ins[0 if sign > 0 else 1].at[i]

        def onward(sign, i):
            return sems(sign, i, unit_rows(total, place(sign, i), i % halves, size, sub), slot(sign, i), sign)

        def step(r):
            for sign in (1, -1):
                depth = me if sign > 0 else slices - 1 - me
                i = r - depth
                if not 0 <= i < units:
                    continue
                b = place(sign, i)
                passes = b > me if sign > 0 else b < me
                if (passes or b == me) and depth:
                    sems(sign, i, slot(sign, i), slot(sign, i), 0).wait_recv()
                    add_rows(total, slot(sign, i), b * size + (i % halves) * sub, 0, sub)
                if passes:
                    if len(before[sign]) == IN_FLIGHT:
                        onward(sign, before[sign].pop(0)).wait_send()
                    before[sign].append(i)
                    onward(sign, i).start()

        def finish():
            for sign in (1, -1):
                for i in before[sign]:
                    onward(sign, i).wait_send()

        def place_own():
            if out is not None:
                out[pl.ds(me * size, size), :] = total[pl.ds(me * size, size), :]

        return [partial(step, r) for r in range(units + slices - 1)], place_own, finish

    def semaphores(units):
        base = copies.remotes
        copies.remotes += 2 * units

        def make(sign, i, source, target, to):
            k = base + i + (0 if sign > 0 else units)
            return pltpu.make_async_remote_copy(
                src_ref=source, dst_ref=target, send_sem=send.at[k], recv_sem=recv.at[k],
                device_id=(seq, part + to), device_id_type=MESH,
            )

        return make

    def interleave(*lists):
        for k in range(max((len(steps) for steps in lists), default=0)):
            for steps in lists:
                if k < len(steps):
                    steps[k]()

    def at_place(run):
        for me in range(slices):
            pl.when(part == me)(partial(run, me))

    own_copies = []
    for own, out in zip(blocks, outs):
        mine = copies.own(own, block(out, part))
        mine.start()
        own_copies.append(mine)
    plane_total, *plane_ins = part_scratch[5 * len(parts) :]
    pieces = [out.shape[0] // peers for out in pack_outs]
    piece_rows = sum(pieces)
    plane_sems = semaphores(slices)
    block_sems = [semaphores(slices * halves) for _ in outs]
    sum_sems = [semaphores(slices * halves) for _ in part_outs]
    after_sems = [semaphores(slices * halves) for _ in part_outs]

    to_chips = []

    def to_plane():
        for n, pack in enumerate(packs):
            half = pack.shape[1] // 2
            size = half // chips
            sibling_sum, mine, by_chip = weight_scratch[3 * n : 3 * n + 3]
            held[n].wait()
            to_core[n].wait_recv()

            def add_half(z, carry, sibling_sum=sibling_sum, mine=mine, half=half):
                add_rows(mine.at[z], sibling_sum.at[z], 0, 0, half)
                return carry

            lax.fori_loop(0, slices, add_half, 0)
            for e in range(1, chips):
                to = lax.rem(chip + e, chips)
                copy = copies.remote(mine.at[:, pl.ds(pl.multiple_of(to * size, 16), size)], by_chip.at[e - 1], to * 2 + core, part)
                copy.start()
                to_chips.append((n, e, copy))
                sent.append(copy)

    length = slices * halves
    plans = []
    for me in range(slices):
        gathers = [line_gather(out, me, sems) for out, sems in zip(outs, block_sems)]
        sums, afters = [], []
        for n, out in enumerate(part_outs):
            total, _, _, right_in, left_in = part_scratch[5 * n : 5 * n + 5]
            sums.append(line_sum(total, (right_in, left_in), out, me, sum_sems[n]))
            afters.append(line_gather(out, me, after_sems[n]))
        owned = [line_sum(plane_total, plane_ins, None, me, plane_sems, piece_rows, 1)]
        plans.append((gathers, sums, afters, owned))

    def rounds(me, *which):
        lists, ends = [], []
        for kind, n, low, high in which:
            entry = plans[me][kind][n]
            steps = entry[0]
            lists.append(steps[low:high])
            if low < len(steps) <= high:
                ends += list(entry[1:])
        interleave(*lists)
        for finish in ends:
            finish()

    def run(*which):
        at_place(lambda me: rounds(me, *which))

    def to_owners():
        for n, pack in enumerate(packs):
            half = pack.shape[1] // 2
            size, first_row = half // chips, sum(pieces[:n])
            mine, by_chip = weight_scratch[3 * n + 1 : 3 * n + 3]
            for m, e, copy in to_chips:
                if m == n:
                    copy.wait_recv()

            def add_plane(i, carry, mine=mine, by_chip=by_chip, size=size, first_row=first_row):
                z, r = i // (size // 16), lax.rem(i, size // 16)
                at = pl.ds(pl.multiple_of(r * 16, 16), 16)
                value = mine[z, pl.ds(pl.multiple_of(chip * size + r * 16, 16), 16), :].astype(F32)
                for e in range(chips - 1):
                    value = value + by_chip[e, z, at, :].astype(F32)
                plane_total[pl.ds(pl.multiple_of(z * piece_rows + first_row + r * 16, 16), 16), :] = value.astype(BF16)
                return carry

            lax.fori_loop(0, slices * (size // 16), add_plane, 0)

    def piece_at(n, of_chip, of_core):
        size = pack_outs[n].shape[0] // peers
        index = of_core * chips + of_chip if n < len(packs) else of_chip * 2 + of_core
        return pl.multiple_of(index * size, 16), size

    round_plane, to_sibling = [], []

    def back_to_plane():
        for n, out in enumerate(pack_outs):
            start, size = piece_at(n, chip, core)

            def keep(r, carry, out=out, start=start, first_row=sum(pieces[:n])):
                at = pl.ds(pl.multiple_of(part * piece_rows + first_row + r * 16, 16), 16)
                out[pl.ds(pl.multiple_of(start + r * 16, 16), 16), :] = plane_total[at, :]
                return carry

            lax.fori_loop(0, size // 16, keep, 0)
            piece = out.at[pl.ds(start, size)]
            for e in range(1, chips):
                copy = copies.remote(piece, piece, lax.rem(chip + e, chips) * 2 + core, part)
                copy.start()
                round_plane.append((n, e, copy))
                sent.append(copy)
            copy = copies.remote(piece, piece, sibling, part)
            copy.start()
            round_plane.append((n, 0, copy))
            sent.append(copy)

    sum_length = (slices - 1) * halves + slices - 1
    plane_copies = []
    for n, summed in enumerate(plane_sums):
        first_row, size = sum(pieces[: len(packs) + n]), pieces[len(packs) + n]
        for z in range(slices):
            plane_copies.append(copies.own(summed.at[z], plane_total.at[pl.ds(z * piece_rows + first_row, size)]))
    for keep in plane_copies:
        keep.start()
    for mine in own_copies:
        mine.wait()
    run((0, 0, 0, 2))
    to_plane()
    run((0, 0, 2, 3))
    finish_halo(0)
    run((0, 0, 3, length), (1, 0, 0, sum_length))
    for keep in plane_copies:
        keep.wait()
    if len(parts) > 1:
        finish_halo(1)
        run((1, 1, 0, sum_length // 2), (2, 0, 0, sum_length // 2))
        to_owners()
        run((1, 1, sum_length // 2, sum_length), (2, 0, sum_length // 2, length))
    else:
        to_owners()
    last = len(parts) - 1
    run((3, 0, 0, 2 * (slices - 1)), (2, last, 0, length // 2))
    back_to_plane()
    run((2, last, length // 2, length))
    for n, e, copy in round_plane:
        copy.wait_recv()
        if e:
            start, size = piece_at(n, lax.rem(chip + chips - e, chips), core)
            piece = pack_outs[n].at[pl.ds(start, size)]
            copy = copies.remote(piece, piece, sibling, part)
            copy.start()
            to_sibling.append(copy)
            sent.append(copy)
    for copy in to_sibling:
        copy.wait_recv()
    for copy in sent:
        copy.wait_send()


class Rows:
    def __init__(self, pack, index, size):
        self.pack, self.at = pack, slice(index * size, (index + 1) * size)

    def __getitem__(self, _):
        value = self.pack[:, self.at, :]
        return value.reshape(value.shape[0] * value.shape[1], value.shape[2])


def write_rows(pack, index, size, value):
    slices = pack.shape[0]
    pack[:, index * size : (index + 1) * size, :] = value.astype(BF16).reshape(slices, size, value.shape[1])


def write_pieces(pack, z, row, value):
    size = pack.shape[2]
    for i in range(value.shape[0] // size):
        pack[row // size + i, z] = value[i * size : (i + 1) * size, :].astype(BF16)


def mask_bias(code, low, high):
    return jnp.where((code >= low) & (code < high), 0.0, NEG_BIG).astype(F32)


def pair_product(left, spread, p, see):
    count = see.size
    blocks = [spread[h * PAIR : (h + 1) * PAIR, see] for h in (2 * p, 2 * p + 1)]
    if count % LANES:
        return [dot_nn(left, block) for block in blocks]
    both = dot_nn(left, jnp.concatenate(blocks, axis=1))
    return both[:, :count], both[:, count:]


def attend(window, code, low, high, w_key_t, w_value_t, spread, bias, top, total, out):
    top[...] = jnp.full_like(top, NEG_BIG)
    total[...] = jnp.zeros_like(total)
    out[...] = jnp.zeros_like(out)

    def step(c, see):
        at = chunk_rows(window.start, c)
        rows = window.held[at, :]
        keys = dot_nt(rows, w_key_t[...]).astype(BF16)
        values_t = dot_nt(rows, w_value_t[...]).astype(BF16).T
        bias[:, see] = mask_bias(code[at, :], low[:, see], high[:, see])
        for h in range(HEADS):
            p = h // 2
            if h % 2 == 0:
                both = pair_product(keys[:, p * PAIR : (p + 1) * PAIR], spread, p, see)
            scores = both[h % 2] * SCORE_SCALE + bias[:, see]
            before = top[h : h + 1, see]
            now = jnp.maximum(before, jnp.max(scores, axis=0, keepdims=True))
            weights = jnp.exp2(scores - now)
            shrink = jnp.exp2(before - now)
            top[h : h + 1, see] = now
            total[h : h + 1, see] = total[h : h + 1, see] * shrink + jnp.sum(weights, axis=0, keepdims=True)
            head = slice(h * HEAD_SIZE, (h + 1) * HEAD_SIZE)
            out[head, see] = out[head, see] * shrink + dot_nn(values_t[head, :], weights.astype(BF16))

    window.loops(out.shape[1], step)
    for h in range(HEADS):
        head = slice(h * HEAD_SIZE, (h + 1) * HEAD_SIZE)
        out[head, :] = out[head, :] / total[h : h + 1, :]


def attend_back(
    window, code, low, high, w_key_t, w_value_t, spread, grad_spread, pairs, grad_pairs, lse, delta, bias,
    query_grad, window_grad, w_key_grad, w_value_grad,
):
    count = spread.shape[1]
    query_grad[...] = jnp.zeros_like(query_grad)
    w_key_grad[...] = jnp.zeros_like(w_key_grad)
    w_value_grad[...] = jnp.zeros_like(w_value_grad)
    window_grad[...] = jnp.zeros_like(window_grad)

    def step(c, see):
        at = chunk_rows(window.start, c)
        seen = (see, pl.ds(count + see.start, see.size) if isinstance(see.start, int) else pl.ds(pl.multiple_of(count + see.start, LANES), see.size))
        rows = window.held[at, :]
        keys = dot_nt(rows, w_key_t[...]).astype(BF16)
        keys_t = keys.T
        values = dot_nt(rows, w_value_t[...]).astype(BF16)
        bias[:, see] = mask_bias(code[at, :], low[:, see], high[:, see])
        key_grads, value_grads = [], []
        for p in range(PAIRS):
            columns = slice(p * PAIR, (p + 1) * PAIR)
            probs, score_grads = [], []
            both_scores = pair_product(keys[:, columns], spread, p, see)
            both_dprobs = pair_product(values[:, columns], grad_spread, p, see)
            for h in (2 * p, 2 * p + 1):
                head = slice(h * HEAD_SIZE, (h + 1) * HEAD_SIZE)
                prob = jnp.exp2(both_scores[h % 2] * SCORE_SCALE + bias[:, see] - lse[h : h + 1, see])
                score_grad = (prob * (both_dprobs[h % 2] - delta[h : h + 1, see])).astype(BF16)
                query_grad[head, see] += dot_nn(keys_t[head, :], score_grad)
                probs.append(prob.astype(BF16))
                score_grads.append(score_grad)
            if count % LANES == 0:
                both = jnp.concatenate([pairs[p, r, :] for r in seen], axis=0)
                grad_both = jnp.concatenate([grad_pairs[p, r, :] for r in seen], axis=0)
                key_grads.append(dot_nn(jnp.concatenate(score_grads, axis=1), both))
                value_grads.append(dot_nn(jnp.concatenate(probs, axis=1), grad_both))
            else:
                key_grads.append(sum(dot_nn(x, pairs[p, r, :]) for x, r in zip(score_grads, seen)))
                value_grads.append(sum(dot_nn(x, grad_pairs[p, r, :]) for x, r in zip(probs, seen)))
        keys_low = (jnp.concatenate(key_grads, axis=1) * SCALE).astype(BF16)
        values_low = jnp.concatenate(value_grads, axis=1).astype(BF16)
        window_grad[at, :] = (dot_nn(keys_low, w_key_t[...]) + dot_nn(values_low, w_value_t[...])).astype(window_grad.dtype)
        w_key_grad[...] += dot_tn(rows, keys_low)
        w_value_grad[...] += dot_tn(rows, values_low)

    window.loops(count, step)


def forward_kernel(
    cols, bounds, own, content_window, encoded_window, gain, code, low, high_self, high_cross, pack_one, pack_two_in,
    self_t, lse_self, hidden, cross_t, lse_cross,
    spread, bias, top, total, low_t, content_held, encoded_held, pack_two, content_sems, encoded_sems, pack_sem,
):
    content = Window(bounds, content_window, content_held, content_sems)
    encoded = Window(bounds, encoded_window, encoded_held, encoded_sems)
    content.fetch()
    whole_pack = pltpu.make_async_copy(pack_two_in, pack_two, pack_sem.at[0])
    whole_pack.start()
    encoded.fetch()
    w_query_t, w_key_t, w_value_t = (Rows(pack_one, k, cols) for k in range(3))
    low_t[...] = dot_nt(w_query_t[...], own[...]).astype(BF16)
    spread_heads(low_t, spread)
    attend(content, code, low, high_self, w_key_t, w_value_t, spread, bias, top, total, self_t)
    lse_self[...] = top[...] + jnp.log2(total[...])
    whole_pack.wait()
    w_out, w_query_t, w_key_t, w_value_t = (Rows(pack_two, k, cols) for k in range(4))
    branch = dot_tn(self_t[...].astype(BF16), w_out[...])
    normed, _ = layer_norm(own[...].astype(F32) + branch)
    hidden[...] = normed * gain[...]
    low_t[...] = dot_nt(w_query_t[...], hidden[...].astype(BF16)).astype(BF16)
    spread_heads(low_t, spread)
    attend(encoded, code, low, high_cross, w_key_t, w_value_t, spread, bias, top, total, cross_t)
    lse_cross[...] = top[...] + jnp.log2(total[...])


def ffn_kernel(
    cols, hidden_one, cross_t, pack_two, gain_cross, pack_three_in, gain_final, out_grad,
    mixed, resid_grad, w_out_grad, grad_three_out, gain_cross_grad, gain_final_grad,
    normed_two, hidden_two_low, slope, active, sum_ffn, pack_out, pack_three, grad_three_pack, sems, out_sems,
):
    slices, units = pack_three.shape[0], pack_three.shape[1] // 2
    out_copy = pltpu.make_async_copy(pack_two.at[:, pl.ds(4 * cols, cols)], pack_out, sems.at[slices])
    out_copy.start()
    slice_copies = [pltpu.make_async_copy(pack_three_in.at[z], pack_three.at[z], sems.at[z]) for z in range(slices)]
    for copy in slice_copies:
        copy.start()
    out_copy.wait()
    w_out = Rows(pack_out, 0, cols)
    cross_low = cross_t[...].astype(BF16)
    normed, scale_two = layer_norm(hidden_one[...] + dot_tn(cross_low, w_out[...]))
    normed_two[...] = normed
    hidden_two = normed * gain_cross[...]
    hidden_two_low[...] = hidden_two.astype(BF16)
    sum_ffn[...] = hidden_two
    for z in range(slices):
        slice_copies[z].wait()
        inner = dot_nt(hidden_two_low[...], pack_three[z, 0:units, :])
        below = 0.5 * (1.0 + lax.erf(inner * math.sqrt(0.5)))
        slope[z] = below + inner * (jnp.exp2(inner * inner * (-0.5 * LOG2E)) * (1.0 / math.sqrt(2.0 * math.pi)))
        active[z] = (inner * below).astype(BF16)
        sum_ffn[...] += dot_nn(active[z], pack_three[z, units:, :])
    normed_three, scale_three = layer_norm(sum_ffn[...])
    mixed[...] = (normed_three * gain_final[...]).astype(BF16)
    grad_three, gain_grad = norm_back(out_grad[...].astype(F32), normed_three, scale_three, gain_final[...])
    gain_final_grad[...] = gain_grad
    ffn_low = grad_three.astype(BF16)
    result_copies = [pltpu.make_async_copy(grad_three_pack.at[:, z], grad_three_out.at[:, z], out_sems.at[z]) for z in range(slices)]
    sum_ffn[...] = grad_three
    for z in range(slices):
        write_pieces(grad_three_pack, z, units, dot_tn(active[z], ffn_low))
        inner_low = (dot_nt(ffn_low, pack_three[z, units:, :]) * slope[z]).astype(BF16)
        write_pieces(grad_three_pack, z, 0, dot_tn(inner_low, hidden_two_low[...]))
        sum_ffn[...] += dot_nn(inner_low, pack_three[z, 0:units, :])
        result_copies[z].start()
    grad, gain_grad = norm_back(sum_ffn[...], normed_two[...], scale_two, gain_cross[...])
    gain_cross_grad[...] = gain_grad
    resid_grad[...] = grad
    w_out_grad[...] = dot_nn(cross_low, grad.astype(BF16)).astype(BF16)
    for copy in result_copies:
        copy.wait()


def prepare_back(query, query_t, grad, grad_t, out, spread, grad_spread, pairs, grad_pairs, delta, low_t):
    low_t[...] = query_t.astype(BF16)
    spread_heads(low_t, spread)
    for p in range(PAIRS):
        pair_rows(query.astype(BF16), p, pairs)
        pair_rows(grad.astype(BF16), p, grad_pairs)
    low_t[...] = grad_t.astype(BF16)
    spread_heads(low_t, grad_spread)
    for h in range(HEADS):
        head = slice(h * HEAD_SIZE, (h + 1) * HEAD_SIZE)
        delta[h : h + 1, :] = jnp.sum(low_t[head, :].astype(F32) * out[head, :], axis=0, keepdims=True)


def cross_back_kernel(
    cols, bounds, own, self_t, gain, resid_two_grad, cross_t, lse, window_in, code, low, high, pack_two,
    w_cross_out_grad, gain_cross_grad, gain_final_grad, resid_one_grad, window_out, grad_two_pack,
    spread, grad_spread, pairs, grad_pairs, delta, bias, low_t, query_grad, key_sum, value_sum, held, window_grad, sems, out_sem,
    normed_one, scale_one,
):
    window = Window(bounds, window_in, held, sems)
    window.fetch()
    w_out, w_query_t, w_key_t, w_value_t, w_cross_out = (Rows(pack_two, k, cols) for k in range(5))
    self_low = self_t[...].astype(BF16)
    normed, scale = layer_norm(own[...].astype(F32) + dot_tn(self_low, w_out[...]))
    normed_one[...] = normed
    scale_one[...] = scale
    hidden_low = (normed * gain[...]).astype(BF16)
    branch_low = resid_two_grad[...].astype(BF16)
    prepare_back(
        dot_nt(hidden_low, w_query_t[...]), dot_nt(w_query_t[...], hidden_low),
        dot_nt(branch_low, w_cross_out[...]), dot_nt(w_cross_out[...], branch_low),
        cross_t, spread, grad_spread, pairs, grad_pairs, delta, low_t,
    )
    attend_back(
        window, code, low, high, w_key_t, w_value_t, spread, grad_spread, pairs, grad_pairs, lse, delta, bias,
        query_grad, window_grad, key_sum, value_sum,
    )
    result = pltpu.make_async_copy(window_grad, window_out, out_sem.at[0])
    result.start()
    query_low = (query_grad[...] * SCALE).astype(BF16)
    hidden_low = (normed_one[...] * gain[...]).astype(BF16)
    grad_one = resid_two_grad[...] + dot_tn(query_low, w_query_t[...])
    grad, gain_sum = norm_back(grad_one, normed_one[...], scale_one[...], gain[...])
    resid_one_grad[...] = grad
    write_rows(grad_two_pack, 0, cols, dot_nn(self_t[...].astype(BF16), grad.astype(BF16)))
    write_rows(grad_two_pack, 1, cols, dot_nn(query_low, hidden_low))
    write_rows(grad_two_pack, 2, cols, key_sum[...].T)
    write_rows(grad_two_pack, 3, cols, value_sum[...].T)
    write_rows(grad_two_pack, 4, cols, w_cross_out_grad[...])
    slices, rows, width = grad_two_pack.shape
    gains = jnp.concatenate([gain_sum, gain_cross_grad[...], gain_final_grad[...], jnp.zeros((13, width), F32)], axis=0)
    for z in range(slices):
        grad_two_pack[z, 5 * cols : 5 * cols + 16, :] = gains.astype(BF16)
        if rows > 5 * cols + 16:
            grad_two_pack[z, 5 * cols + 16 :, :] = jnp.zeros((rows - 5 * cols - 16, width), BF16)
    result.wait()


def self_back_kernel(
    cols, bounds, own, resid_one_grad, pack_two, self_t, lse, window_in, code, low, high, pack_one,
    own_grad, window_out, grad_one_pack,
    spread, grad_spread, pairs, grad_pairs, delta, bias, low_t, query_grad, key_sum, value_sum, held, window_grad, sems, out_sem,
    pack_out, pack_sem,
):
    out_copy = pltpu.make_async_copy(pack_two.at[:, pl.ds(0, cols)], pack_out, pack_sem.at[0])
    out_copy.start()
    window = Window(bounds, window_in, held, sems)
    window.fetch()
    out_copy.wait()
    w_query_t, w_key_t, w_value_t = (Rows(pack_one, k, cols) for k in range(3))
    w_out = Rows(pack_out, 0, cols)
    branch_low = resid_one_grad[...].astype(BF16)
    prepare_back(
        dot_nt(own[...], w_query_t[...]), dot_nt(w_query_t[...], own[...]),
        dot_nt(branch_low, w_out[...]), dot_nt(w_out[...], branch_low),
        self_t, spread, grad_spread, pairs, grad_pairs, delta, low_t,
    )
    attend_back(
        window, code, low, high, w_key_t, w_value_t, spread, grad_spread, pairs, grad_pairs, lse, delta, bias,
        query_grad, window_grad, key_sum, value_sum,
    )
    result = pltpu.make_async_copy(window_grad, window_out, out_sem.at[0])
    result.start()
    query_low = (query_grad[...] * SCALE).astype(BF16)
    write_rows(grad_one_pack, 0, cols, dot_nn(query_low, own[...]))
    write_rows(grad_one_pack, 1, cols, key_sum[...].T)
    write_rows(grad_one_pack, 2, cols, value_sum[...].T)
    slices, rows, width = grad_one_pack.shape
    if rows > 3 * cols:
        grad_one_pack[:, 3 * cols :, :] = jnp.zeros((slices, rows - 3 * cols, width), BF16)
    own_grad[...] = (resid_one_grad[...] + dot_tn(query_low, w_query_t[...])).astype(BF16)
    result.wait()


def finish_kernel(cols, units, slices, part, *refs):
    blocks, rows_in, (sum_one, sum_two, sum_three) = refs[:slices], refs[slices : slices + 3], refs[slices + 3 : slices + 6]
    outs = refs[slices + 6 :]
    step = pl.program_id(0)
    came = lax.rem(part[0, 0] + slices - step, slices)
    for d, ref in enumerate(blocks):

        @pl.when(came == d)
        def _(ref=ref):
            outs[0][...] = ref[...]

    for source, target in zip(rows_in, outs[1:4]):
        target[...] = source[...].astype(F32)

    def weights(k):
        w_query, w_key, w_value, w_out, w_cross_query, w_cross_key, w_cross_value, w_cross_out, w_inner, w_outer = outs[4:14]
        width = sum_one.shape[1]
        wide, tall, unit_rows = width // slices, cols // slices, units // slices
        some = slice(k * wide, (k + 1) * wide)
        for n, target in enumerate((w_query, w_key, w_value)):
            target[...] = sum_one[n * cols : (n + 1) * cols, some].astype(F32).T
        for n, target in enumerate((w_cross_query, w_cross_key, w_cross_value)):
            target[...] = sum_two[(1 + n) * cols : (2 + n) * cols, some].astype(F32).T
        w_out[...] = sum_two[k * tall : (k + 1) * tall, :].astype(F32)
        w_cross_out[...] = sum_two[4 * cols + k * tall : 4 * cols + (k + 1) * tall, :].astype(F32)
        w_inner[...] = sum_three[0:units, some].astype(F32).T
        w_outer[...] = sum_three[units + k * unit_rows : units + (k + 1) * unit_rows, :].astype(F32)

    for k in range(slices):
        pl.when(step == k)(partial(weights, k))

    @pl.when(step == 0)
    def _():
        gains = sum_two[5 * cols : 5 * cols + 16, :].astype(F32)
        for k, target in enumerate(outs[14:17]):
            target[...] = gains[k : k + 1, :]


def call(kernel, outs, scratch, smem, *args, far=(), far_outs=(), micros=20):
    def space(k, left, scalars):
        return pl.ANY if k in left else pltpu.SMEM if k < scalars else pltpu.VMEM

    return pl.pallas_call(
        kernel,
        out_shape=[jax.ShapeDtypeStruct(shape, kind) for shape, kind in outs],
        in_specs=[pl.BlockSpec(memory_space=space(k, far, smem)) for k in range(len(args))],
        out_specs=[pl.BlockSpec(memory_space=space(k, far_outs, 0)) for k in range(len(outs))],
        scratch_shapes=[pltpu.SemaphoreType.DMA((shape,)) if kind is None else pltpu.VMEM(shape, kind) for shape, kind in scratch],
        compiler_params=pltpu.CompilerParams(vmem_limit_bytes=VMEM_LIMIT),
        cost_estimate=pl.CostEstimate(flops=micros * 10**9, bytes_accessed=micros * 10**6, transcendentals=0),
    )(*args)


def padded(size, unit):
    return -(-size // unit) * unit


def talk(kernel, outs, out_spaces, scratch, copies, number, spaces, *args):
    return pl.pallas_call(
        kernel,
        out_shape=[jax.ShapeDtypeStruct(shape, kind) for shape, kind in outs],
        in_specs=[pl.BlockSpec(memory_space=space) for space in spaces],
        out_specs=[pl.BlockSpec(memory_space=space) for space in out_spaces],
        scratch_shapes=[pltpu.SemaphoreType.DMA((n,)) for n in (copies[0], copies[0], copies[1])] + [pltpu.VMEM(shape, kind) for shape, kind in scratch],
        compiler_params=pltpu.CompilerParams(vmem_limit_bytes=VMEM_LIMIT, collective_id=number, has_side_effects=True),
        cost_estimate=pl.CostEstimate(flops=80 * 10**9, bytes_accessed=80 * 10**6, transcendentals=0),
    )(*args)


def body(
    query_state, content, encoded, sentence_lengths, key_score, query_cut, w_query, w_key, w_value, w_out, gain_self,
    w_cross_query, w_cross_key, w_cross_value, w_cross_out, gain_cross, w_inner, w_outer, gain_final, out_grad,
):
    rows, width = query_state.shape
    slices = lax.axis_size("head")
    count = rows // slices
    lanes = math.gcd(count, LANES)
    wide = padded(count + 2 * DOC_LEN + CHUNK, lanes)
    spare = wide - count - 2 * DOC_LEN
    seq, part = lax.axis_index("seq"), lax.axis_index("head")
    begin = seq * rows + part * count
    score = lax.dynamic_slice_in_dim(jnp.pad(key_score, (DOC_LEN, DOC_LEN + spare)), begin, wide, 0).reshape(wide // lanes, lanes)
    cut = lax.dynamic_slice_in_dim(query_cut, begin, count, 0).reshape(1, count)
    gain_self, gain_cross, gain_final = (g.reshape(1, width) for g in (gain_self, gain_cross, gain_final))

    peers = lax.axis_size("seq")
    chips = peers // 2
    cols, units = w_query.shape[1], w_inner.shape[1]
    unit = 16 * peers
    sizes = [padded(n, unit) for n in (3 * cols, 5 * cols, 2 * units)]
    grad_sizes = [sizes[0], padded(5 * cols + 16, unit), sizes[2]]

    share = sizes[2] // peers
    slice_three = jnp.concatenate([w_inner.T, w_outer, jnp.zeros((sizes[2] - 2 * units, width), BF16)], axis=0)
    share_three = lax.dynamic_slice_in_dim(slice_three, seq * share, share, 0)
    pack_three = lax.all_gather(share_three, ("head", "seq"), axis=0, tiled=True).reshape(slices, sizes[2], width)
    start_copies = 2 * (slices - 1) * (2 * chips) + 4 * slices
    hbm, vmem, smem = pl.ANY, pltpu.VMEM, pltpu.SMEM
    (
        content_window, encoded_window, pack_one, pack_two, own, own_out_grad, code, low, high_self, high_cross, bounds,
    ) = talk(
        partial(start_kernel, peers, slices, count),
        [((wide, width), BF16)] * 2 + [((slices, n, width), BF16) for n in sizes[:2]] + [((count, width), BF16)] * 2
        + [((wide, 1), F32)] + [((1, count), F32)] * 3 + [((1, 6), jnp.int32)],
        [vmem] * 10 + [smem],
        [((DOC_LEN, width), BF16), ((padded(wide // lanes, 8), lanes), F32)], (start_copies, 8 * slices + 16), 0,
        [hbm] * 4 + [vmem] * 8 + [smem] + [vmem] * 2,
        content, encoded, query_state, out_grad, w_query, w_key, w_value, w_out,
        w_cross_query, w_cross_key, w_cross_value, w_cross_out, sentence_lengths.reshape(1, -1), score, cut,
    )

    def split_refs(kernel, ins, outs):
        def run(*refs):
            return kernel(refs[:ins], refs[ins : ins + outs], refs[ins + outs :])
        return run

    touched = -(-wide // CHUNK)
    window_held = [((wide, width), BF16)]
    self_t, lse_self, hidden_one, cross_t, lse_cross = call(
        partial(forward_kernel, cols),
        [((width, count), F32), ((HEADS, count), F32), ((count, width), F32), ((width, count), F32), ((HEADS, count), F32)],
        [((HEADS * PAIR, count), BF16), ((CHUNK, count), F32), ((HEADS, count), F32), ((HEADS, count), F32), ((width, count), BF16)]
        + window_held * 2 + [((slices, sizes[1], width), BF16), (touched, None), (touched, None), (1, None)], 1,
        bounds, own, content_window, encoded_window, gain_self, code, low, high_self, high_cross, pack_one, pack_two, far=(2, 3, 10),
    )
    mixed, resid_two_grad, w_cross_out_grad, grads_three, gain_cross_grad, gain_final_grad = call(
        partial(ffn_kernel, cols),
        [
            ((count, width), BF16), ((count, width), F32), ((width, width), BF16), ((peers, slices, grad_sizes[2] // peers, width), BF16),
            ((1, width), F32), ((1, width), F32),
        ],
        [
            ((count, width), F32), ((count, width), BF16), ((slices, count, units), F32),
            ((slices, count, units), BF16), ((count, width), F32), ((slices, cols, width), BF16), ((slices, sizes[2], width), BF16),
            ((peers, slices, grad_sizes[2] // peers, width), BF16), (slices + 1, None), (slices, None),
        ], 0,
        hidden_one, cross_t, pack_two, gain_cross, pack_three, gain_final, own_out_grad, far=(2, 4), far_outs=(3,),
    )
    back = [
        ((HEADS * PAIR, count), BF16), ((HEADS * PAIR, count), BF16), ((PAIRS, 2 * count, PAIR), BF16),
        ((PAIRS, 2 * count, PAIR), BF16), ((HEADS, count), F32), ((CHUNK, count), F32), ((width, count), BF16),
        ((width, count), F32), ((width, width), F32), ((width, width), F32),
    ] + window_held * 2 + [(touched, None), (1, None)]
    resid_one_grad, encoded_part, grads_two = call(
        partial(cross_back_kernel, cols),
        [((count, width), F32), ((wide, width), BF16), ((slices, grad_sizes[1], width), BF16)],
        back + [((count, width), F32), ((count, 1), F32)], 1,
        bounds, own, self_t, gain_self, resid_two_grad, cross_t, lse_cross, encoded_window, code, low, high_cross, pack_two,
        w_cross_out_grad, gain_cross_grad, gain_final_grad, far=(7,), far_outs=(1,), micros=4,
    )
    own_grad, content_part, grads_one = call(
        partial(self_back_kernel, cols),
        [((count, width), BF16), ((wide, width), BF16), ((slices, grad_sizes[0], width), BF16)],
        back + [((slices, cols, width), BF16), (1, None)], 1,
        bounds, own, resid_one_grad, pack_two, self_t, lse_self, content_window, code, low, high_self, pack_one,
        far=(3, 6), far_outs=(1,), micros=4,
    )

    mixed_blocks = [mixed] + [lax.ppermute(mixed, "head", [(i, (i + d) % slices) for i in range(slices)]) for d in range(1, slices)]
    plane_three = lax.psum_scatter(grads_three, "seq", scatter_dimension=0, tiled=True).reshape(grads_three.shape[1:])
    blocks, parts, grads, planes = [own_grad], [content_part, encoded_part], [grads_one, grads_two], [plane_three]
    weight_scratch = []
    for n in grad_sizes[: len(grads)]:
        half, size = n // 2, n // 2 // chips
        weight_scratch += [
            ((slices, half, width), BF16), ((slices, half, width), BF16), ((chips - 1, slices, size, width), BF16),
        ]
    halves = 2 if slices <= 4 else 1
    units_in = (slices - 1) * halves
    part_scratch = [
        ((rows, width), BF16), ((DOC_LEN, width), BF16), ((DOC_LEN, width), BF16),
        ((units_in, count // halves, width), BF16), ((units_in, count // halves, width), BF16),
    ] * len(parts)
    piece_rows = sum(grad_sizes) // peers
    plane_scratch = [((slices * piece_rows, width), BF16)] + [((slices - 1, piece_rows, width), BF16)] * 2
    ins, outs = (len(blocks), len(parts), len(grads), len(planes)), (len(blocks), len(parts), len(grad_sizes))

    def end(refs, out_refs, scratch):
        a, b, c = ins[0], ins[0] + ins[1], sum(ins[:3])
        end_kernel(
            peers, slices, count, refs[:a], refs[a:b], refs[b:c], refs[c:], out_refs[: outs[0]],
            out_refs[outs[0] : outs[0] + outs[1]], out_refs[outs[0] + outs[1] :], scratch,
        )

    end_copies = len(grad_sizes) * (1 + 3 * (chips - 1) + slices) + 2 * slices + len(parts) * 2 * slices + (len(blocks) + 2 * len(parts)) * 2 * slices * halves
    results = talk(
        split_refs(end, sum(ins), sum(outs)),
        [((rows, width), BF16)] * (len(blocks) + len(parts)) + [((n, width), BF16) for n in grad_sizes], [vmem] * sum(outs),
        weight_scratch + part_scratch + plane_scratch, (end_copies, 8 * slices + 8), 1, [hbm] * sum(ins), *blocks, *parts, *grads, *planes,
    )
    query_state_grad, content_grad, encoded_grad, sum_one, sum_two, sum_three = results

    square, tall = ((width, cols), F32), ((cols, width), F32)
    finals = [((rows, width), BF16)] + [((rows, width), F32)] * 3 + [square] * 3 + [tall, square, square, square, tall]
    finals += [((width, units), F32), ((units, width), F32)] + [((1, width), F32)] * 3
    by_rows = pl.BlockSpec((count, width), lambda i: (i, 0))

    def whole(shape):
        return pl.BlockSpec(shape, lambda i: (0,) * len(shape))

    def by_step(shape):
        return pl.BlockSpec((shape[0] // slices, shape[1]), lambda i: (i, 0))

    sums = [sum_one, sum_two, sum_three]
    results = pl.pallas_call(
        partial(finish_kernel, cols, units, slices),
        grid=(slices,),
        out_shape=[jax.ShapeDtypeStruct(shape, kind) for shape, kind in finals],
        in_specs=[pl.BlockSpec(memory_space=smem)] + [whole((count, width))] * slices + [by_rows] * 3 + [whole(x.shape) for x in sums],
        out_specs=[by_rows] * 4 + [by_step(shape) for shape, _ in finals[4:14]] + [whole(shape) for shape, _ in finals[14:]],
        compiler_params=pltpu.CompilerParams(vmem_limit_bytes=VMEM_LIMIT),
    )(part.reshape(1, 1).astype(jnp.int32), *mixed_blocks, query_state_grad, content_grad, encoded_grad, *sums)
    (
        mixed, query_state_grad, content_grad, encoded_grad, w_query_grad, w_key_grad, w_value_grad, w_out_grad,
        w_cross_query_grad, w_cross_key_grad, w_cross_value_grad, w_cross_out_grad, w_inner_grad, w_outer_grad, *gains,
    ) = results
    gains = [g.reshape(width) for g in gains]
    return (
        mixed, query_state_grad, content_grad, encoded_grad, w_query_grad, w_key_grad, w_value_grad, w_out_grad, gains[0],
        w_cross_query_grad, w_cross_key_grad, w_cross_value_grad, w_cross_out_grad, gains[1], w_inner_grad, w_outer_grad, gains[2],
    )


def solution(mesh):
    rows, whole, columns, split = P("seq", None), P(), P(None, "head"), P("head", None)
    in_specs = (
        rows, rows, rows, whole, whole, whole, columns, columns, columns, split, whole,
        columns, columns, columns, split, whole, columns, split, whole, rows,
    )
    out_specs = (
        rows, rows, rows, rows, columns, columns, columns, split, whole,
        columns, columns, columns, split, whole, columns, split, whole,
    )
    return jax.shard_map(body, mesh=mesh, in_specs=in_specs, out_specs=out_specs, check_vma=False)
```

```python
from functools import partial
import math

import jax
import jax.numpy as jnp
from jax import lax
from jax.experimental import pallas as pl
from jax.experimental.pallas import tpu as pltpu
from jax.sharding import PartitionSpec as P

HEADS = 8
HEAD_SIZE = 64
PAIR = 2 * HEAD_SIZE
PAIRS = HEADS // 2
DOC_LEN = 1024
CHUNK = 528
LANES = 128
IN_FLIGHT = 2
EPS = 1e-05
NEG_BIG = -1e30
LOG2E = 1.4426950408889634
SCALE = 1.0 / math.sqrt(HEAD_SIZE)
SCORE_SCALE = SCALE * LOG2E
CODES = 128
BF16 = jnp.bfloat16
F32 = jnp.float32
VMEM_LIMIT = 60 << 20


def dot_nn(left, right):
    return lax.dot_general(left, right, (((1,), (0,)), ((), ())), preferred_element_type=F32)


def dot_nt(left, right):
    return lax.dot_general(left, right, (((1,), (1,)), ((), ())), preferred_element_type=F32)


def dot_tn(left, right):
    return lax.dot_general(left, right, (((0,), (0,)), ((), ())), preferred_element_type=F32)


def chunk_range(bounds):
    start = bounds[0, 0] // 16 * 16
    return start, (bounds[0, 1] - start + CHUNK - 1) // CHUNK


def chunk_rows(start, c):
    return pl.ds(pl.multiple_of(start + c * CHUNK, 16), CHUNK)


class Window:
    def __init__(self, bounds, source, held, sems):
        self.bounds, self.source, self.held, self.sems = bounds, source, held, sems
        self.start, self.chunks = chunk_range(bounds)

    def copy(self, c):
        rows = chunk_rows(self.start, c)
        return pltpu.make_async_copy(self.source.at[rows], self.held.at[rows], self.sems.at[c])

    def fetch(self):
        def one(c, carry):
            self.copy(c).start()
            return carry

        lax.fori_loop(0, self.chunks, one, 0)

    def loops(self, count, step):
        bounds, start, chunks = self.bounds, self.start, self.chunks

        def loop(number, size, where):
            def one(i, carry):
                c, lane = where(i)
                self.copy(c).wait()
                step(c, pl.ds(lane, size) if isinstance(lane, int) else pl.ds(pl.multiple_of(lane, LANES), size))
                return carry

            lax.fori_loop(0, number, one, 0)

        if count != 3 * LANES:
            return loop(chunks, count, lambda i: (i, 0))
        thirds = [(bounds[0, k] - start) // CHUNK for k in (2, 3)] + [(bounds[0, k] - start + CHUNK - 1) // CHUNK for k in (4, 5)]
        edges = [chunks * 0]
        for edge in thirds:
            edges.append(jnp.clip(edge, edges[-1], chunks))
        edges.append(chunks)

        def two(first, second, second_lane):
            number = edges[first + 1] - edges[first]

            def where(i):
                early = i < number
                return jnp.where(early, edges[first] + i, edges[second] + i - number), jnp.where(early, 0, second_lane)

            return number + edges[second + 1] - edges[second], where

        loop(edges[3] - edges[2], count, lambda i: (edges[2] + i, 0))
        number, where = two(1, 3, LANES)
        loop(number, 2 * LANES, where)
        number, where = two(0, 4, 2 * LANES)
        loop(number, LANES, where)


def layer_norm(resid):
    mean_row = jnp.mean(resid, axis=1, keepdims=True)
    centred = resid - mean_row
    var_row = jnp.mean(centred * centred, axis=1, keepdims=True)
    scale_row = lax.rsqrt(var_row + EPS)
    return centred * scale_row, scale_row


def norm_back(grad, normed, scale_row, gain):
    gain_grad = jnp.sum(grad * normed, axis=0, keepdims=True)
    scaled = grad * gain
    centre = jnp.mean(scaled, axis=1, keepdims=True)
    along = jnp.mean(scaled * normed, axis=1, keepdims=True)
    return scale_row * (scaled - centre - normed * along), gain_grad


def spread_heads(source, target):
    target[...] = jnp.zeros_like(target)
    for h in range(HEADS):
        row = h * PAIR + (h % 2) * HEAD_SIZE
        target[row : row + HEAD_SIZE, :] = source[h * HEAD_SIZE : (h + 1) * HEAD_SIZE, :]


def pair_rows(source, p, target):
    rows = source.shape[0]
    both = source[:, p * PAIR : (p + 1) * PAIR]
    lane = lax.broadcasted_iota(jnp.int32, both.shape, 1)
    zero = jnp.zeros_like(both)
    target[p, 0:rows, :] = jnp.where(lane < HEAD_SIZE, both, zero)
    target[p, rows : 2 * rows, :] = jnp.where(lane < HEAD_SIZE, zero, both)


MESH = pl.DeviceIdType.MESH


class Copies:
    def __init__(self, send, recv, local):
        self.send, self.recv, self.local = send, recv, local
        self.remotes, self.locals = 0, 0

    def remote(self, source, target, seq, part):
        k = self.remotes
        self.remotes += 1
        return pltpu.make_async_remote_copy(
            src_ref=source, dst_ref=target, send_sem=self.send.at[k], recv_sem=self.recv.at[k],
            device_id=(seq, part), device_id_type=MESH,
        )

    def own(self, source, target):
        k = self.locals
        self.locals += 1
        return pltpu.make_async_copy(source, target, self.local.at[k])


def greet(seq, part, peers, slices):
    barrier = pltpu.get_barrier_semaphore()
    for d in range(1, peers):
        pl.semaphore_signal(barrier, inc=1, device_id=(lax.rem(seq + d, peers), part), device_id_type=MESH)
    for d in range(1, slices):
        pl.semaphore_signal(barrier, inc=1, device_id=(seq, lax.rem(part + d, slices)), device_id_type=MESH)
    pl.semaphore_wait(barrier, peers - 1 + slices - 1)


def halo_sizes(part, count, rows):
    return max(0, DOC_LEN - part * count), max(0, (part + 1) * count + DOC_LEN - rows)


def put_rows(whole, part, row, ref, flip):
    value = ref[...]
    if flip:
        value = value.astype(F32).T.astype(BF16)
    whole[part, row : row + value.shape[0], :] = value


def pad_rows(whole, part, row):
    if row < whole.shape[1]:
        whole[part, row:, :] = jnp.zeros((whole.shape[1] - row, whole.shape[2]), BF16)


def find_sentences(begin, count, total_rows, lengths, score, cut, code, low, high_self, high_cross, bounds, blocks_code):
    lanes, blocks = score.shape[1], code.shape[0] // score.shape[1]
    first_block = (begin - DOC_LEN) // lanes
    for j in range(blocks):
        at = jnp.clip(first_block + j, 0, score.shape[0] - 1)
        blocks_code[j : j + 1, :] = score[pl.ds(at, 1), :].astype(F32)
    pos = lax.broadcasted_iota(jnp.int32, (blocks, lanes), 0) * lanes + lax.broadcasted_iota(jnp.int32, (blocks, lanes), 1)
    pos = pos + (begin - DOC_LEN)
    own_pos = lax.broadcasted_iota(jnp.int32, (1, count), 1) + begin
    zero = jnp.zeros((blocks, lanes), jnp.int32)
    last_pos = begin + count - 1

    def one(s, carry):
        start, sentence, first, own_sentence, first_row, last_row, thirds = carry
        size = lengths[0, s]
        end = start + size
        passed = pos >= end
        sentence = sentence + jnp.where(passed, 1, 0)
        first = first + jnp.where(passed, size, 0)
        own_sentence = own_sentence + jnp.where(own_pos >= end, 1, 0)
        first_row = first_row + jnp.where(begin >= end, size, 0)
        last_row = last_row + jnp.where(last_pos >= start, size, 0)
        thirds = tuple(t + jnp.where(begin + LANES * (1 + k) >= end, size, 0) for k, t in enumerate(thirds[:2])) + tuple(
            t + jnp.where(begin + LANES * (1 + k) - 1 >= start, size, 0) for k, t in enumerate(thirds[2:])
        )
        return end, sentence, first, own_sentence, first_row, last_row, thirds

    none = lengths[0, 0] * 0
    carry = (none, zero, zero, jnp.zeros((1, count), jnp.int32), none, none, (none,) * 4)
    _, sentence, first, own_sentence, first_row, last_row, thirds = lax.fori_loop(0, lengths.shape[1], one, carry)
    shown = jnp.where(pos == first, -1.0, blocks_code[0:blocks, :])
    inside = jnp.logical_and(pos >= 0, pos < total_rows)
    blocks_code[0:blocks, :] = jnp.where(inside, (sentence * CODES).astype(F32) + shown, -float(CODES))
    for b in range(0, blocks, 8):
        turned = blocks_code[b : b + 8, :].T
        for j in range(min(8, blocks - b)):
            code[(b + j) * lanes : (b + j + 1) * lanes, :] = turned[:, j : j + 1]
    low[...] = (own_sentence * CODES - 1).astype(F32)
    for j in range(count // lanes):
        some = slice(j * lanes, (j + 1) * lanes)
        high_self[:, some] = (own_sentence[:, some] * CODES + cut[pl.ds(begin // lanes + j, 1), :]).astype(F32)
    high_cross[...] = (own_sentence * CODES + CODES // 2).astype(F32)
    origin = begin - DOC_LEN
    bounds[0, 0] = first_row - origin
    bounds[0, 1] = last_row - origin
    for k, row in enumerate(thirds):
        bounds[0, 2 + k] = row - origin


def start_kernel(
    peers, slices, count, content, encoded, query_state, out_grad, w_query, w_key, w_value, w_out,
    w_cross_query, w_cross_key, w_cross_value, w_cross_out, lengths, score, cut,
    content_window, encoded_window, all_one, all_two, own, own_out_grad, code, low, high_self, high_cross, bounds,
    send, recv, local, zeros, blocks_code,
):
    seq, part = lax.axis_index("seq"), lax.axis_index("head")
    chip, core = seq // 2, lax.rem(seq, 2)
    chips = peers // 2
    sibling = chip * 2 + 1 - core
    rows = content.shape[0]
    span = count + 2 * DOC_LEN
    spare = content_window.shape[0] - span
    copies = Copies(send, recv, local)
    cols = w_query.shape[1]
    for k, (ref, flip) in enumerate(((w_query, True), (w_key, True), (w_value, True))):
        put_rows(all_one, part, k * cols, ref, flip)
    pad_rows(all_one, part, 3 * cols)
    greet(seq, part, peers, slices)
    waits = []
    for source, target in ((query_state, own), (out_grad, own_out_grad)):
        mine = copies.own(source.at[pl.ds(pl.multiple_of(part * count, 16), count)], target)
        mine.start()
        waits.append(mine.wait)

    def halo(source, window):
        for k in range(slices):
            below, above = halo_sizes(k, count, rows)
            low = max(0, k * count - DOC_LEN)
            inner = span - below - above
            mine = copies.own(source.at[pl.ds(low, inner)], window.at[pl.ds(below, inner)])
            tail = copies.own(zeros.at[pl.ds(0, spare)], window.at[pl.ds(span, spare)])
            up = down = fill_low = fill_high = None
            if below:
                up = copies.remote(source.at[pl.ds(rows - below, below)], window.at[pl.ds(0, below)], seq + 1, part)
                fill_low = copies.own(zeros.at[pl.ds(0, below)], window.at[pl.ds(0, below)])
            if above:
                down = copies.remote(source.at[pl.ds(0, above)], window.at[pl.ds(span - above, above)], seq - 1, part)
                fill_high = copies.own(zeros.at[pl.ds(0, above)], window.at[pl.ds(span - above, above)])
            here, first, last = part == k, seq == 0, seq == peers - 1

            def start(mine=mine, tail=tail, up=up, down=down, fill_low=fill_low, fill_high=fill_high, here=here):
                @pl.when(here)
                def _():
                    if up is not None:
                        pl.when(jnp.logical_not(last))(up.start)
                        pl.when(first)(fill_low.start)
                    if down is not None:
                        pl.when(jnp.logical_not(first))(down.start)
                        pl.when(last)(fill_high.start)
                    mine.start()
                    tail.start()

            def finish(mine=mine, tail=tail, up=up, down=down, fill_low=fill_low, fill_high=fill_high, here=here):
                @pl.when(here)
                def _():
                    if up is not None:
                        pl.when(jnp.logical_not(last))(up.wait_send)
                        pl.when(jnp.logical_not(first))(up.wait_recv)
                        pl.when(first)(fill_low.wait)
                    if down is not None:
                        pl.when(jnp.logical_not(first))(down.wait_send)
                        pl.when(jnp.logical_not(last))(down.wait_recv)
                        pl.when(last)(fill_high.wait)
                    mine.wait()
                    tail.wait()

            start()
            waits.append(finish)

    packs = (all_one, all_two)

    def piece(ref, owner, index, size):
        return ref.at[owner, pl.ds(pl.multiple_of(index * size, 16), size)]

    across = {}
    for n, whole in enumerate(packs):
        size = whole.shape[1] // peers
        for d in range(1, slices):
            to = lax.rem(part + d, slices)
            across[n, d] = copies.remote(piece(whole, part, seq, size), piece(whole, part, seq, size), seq, to)
            across[n, d].start()
        if n == 0:
            zeros[...] = jnp.zeros_like(zeros)
            halo(content, content_window)
            put_rows(all_two, part, 0, w_out, False)
            for k, ref in enumerate((w_cross_query, w_cross_key, w_cross_value)):
                put_rows(all_two, part, (1 + k) * cols, ref, True)
            put_rows(all_two, part, 4 * cols, w_cross_out, False)
            pad_rows(all_two, part, 5 * cols)
    find_sentences(seq * rows + part * count, count, peers * rows, lengths, score, cut, code, low, high_self, high_cross, bounds, blocks_code)
    round_plane, to_sibling = {}, {}
    for n, whole in enumerate(packs):
        size = whole.shape[1] // peers
        for d in range(1, slices):
            across[n, d].wait_recv()
            owner = lax.rem(part + slices - d, slices)
            got = piece(whole, owner, seq, size)
            for e in range(1, chips):
                round_plane[n, d, e] = copies.remote(got, got, lax.rem(chip + e, chips) * 2 + core, part)
                round_plane[n, d, e].start()
            to_sibling[n, d, 0] = copies.remote(got, got, sibling, part)
            to_sibling[n, d, 0].start()
    halo(encoded, encoded_window)
    for n, whole in enumerate(packs):
        size = whole.shape[1] // peers
        for d in range(1, slices):
            owner = lax.rem(part + slices - d, slices)
            for e in range(1, chips):
                round_plane[n, d, e].wait_recv()
                got = piece(whole, owner, lax.rem(chip + chips - e, chips) * 2 + core, size)
                to_sibling[n, d, e] = copies.remote(got, got, sibling, part)
                to_sibling[n, d, e].start()
    for copy in to_sibling.values():
        copy.wait_recv()
    for copy in (*across.values(), *round_plane.values(), *to_sibling.values()):
        copy.wait_send()
    for wait in waits:
        wait()


def add_rows(target, source, target_at, source_at, size):
    step = 64 if size % 64 == 0 else 16

    def one(i, carry):
        to = pl.ds(pl.multiple_of(target_at + i * step, 16), step)
        by = pl.ds(pl.multiple_of(source_at + i * step, 16), step)
        target[to, :] = (target[to, :].astype(F32) + source[by, :].astype(F32)).astype(BF16)
        return carry

    lax.fori_loop(0, size // step, one, 0)


def end_kernel(
    peers, slices, count, blocks, parts, packs, plane_sums, outs, part_outs, pack_outs, scratch,
):
    seq, part = lax.axis_index("seq"), lax.axis_index("head")
    chip, core = seq // 2, lax.rem(seq, 2)
    chips = peers // 2
    sibling = chip * 2 + 1 - core
    rows = slices * count
    span = count + 2 * DOC_LEN
    send, recv, local = scratch[:3]
    copies = Copies(send, recv, local)
    first, last = seq == 0, seq == peers - 1
    start_line, end_line = part == 0, part == slices - 1
    greet(seq, part, peers, slices)
    sent = []

    def block(ref, index):
        return ref.at[pl.ds(pl.multiple_of(index * count, 16), count)]

    weight_scratch = scratch[3 : 3 + 3 * len(packs)]
    to_core, held = [], []
    for n, pack in enumerate(packs):
        half = pack.shape[1] // 2
        sibling_sum, mine = weight_scratch[3 * n : 3 * n + 2]
        copy = copies.remote(pack.at[:, pl.ds(pl.multiple_of((1 - core) * half, 16), half)], sibling_sum, sibling, part)
        copy.start()
        to_core.append(copy)
        keep = copies.own(pack.at[:, pl.ds(pl.multiple_of(core * half, 16), half)], mine)
        keep.start()
        held.append(keep)
        sent.append(copy)

    part_scratch = scratch[3 + 3 * len(packs) :]
    halos = []
    for n, grad in enumerate(parts):
        total, from_above, from_below = part_scratch[5 * n : 5 * n + 3]
        for k in range(slices):
            below, above = halo_sizes(k, count, rows)
            low = max(0, k * count - DOC_LEN)
            inner = span - below - above
            mine = copies.own(grad.at[pl.ds(below, inner)], total.at[pl.ds(low, inner)])
            down = up = None
            if below:
                down = copies.remote(grad.at[pl.ds(0, below)], from_above.at[pl.ds(0, below)], seq - 1, part)
            if above:
                up = copies.remote(grad.at[pl.ds(span - above, above)], from_below.at[pl.ds(0, above)], seq + 1, part)
            halos.append((n, k, below, above, low, inner, mine, down, up))

            @pl.when(part == k)
            def _(low=low, inner=inner, mine=mine, down=down, up=up, total=total):
                if down is not None:
                    pl.when(jnp.logical_not(first))(down.start)
                if up is not None:
                    pl.when(jnp.logical_not(last))(up.start)
                mine.start()
                if low:
                    total[0:low, :] = jnp.zeros((low, total.shape[1]), BF16)
                if low + inner < rows:
                    total[low + inner : rows, :] = jnp.zeros((rows - low - inner, total.shape[1]), BF16)

    def finish_halo(which):
        for n, k, below, above, low, inner, mine, down, up in halos:
            if n != which:
                continue
            total, from_above, from_below = part_scratch[5 * n : 5 * n + 3]

            @pl.when(part == k)
            def _(below=below, above=above, mine=mine, down=down, up=up, total=total, from_above=from_above, from_below=from_below):
                mine.wait()
                if down is not None:
                    pl.when(jnp.logical_not(first))(down.wait_send)

                    @pl.when(jnp.logical_not(last))
                    def _():
                        down.wait_recv()
                        add_rows(total, from_above, rows - below, 0, below)

                if up is not None:
                    pl.when(jnp.logical_not(last))(up.wait_send)

                    @pl.when(jnp.logical_not(first))
                    def _():
                        up.wait_recv()
                        add_rows(total, from_below, 0, 0, above)

    halves = 2 if slices <= 4 else 1
    sub = count // halves

    def unit_rows(ref, index, h, size=count, sub=sub):
        return ref.at[pl.ds(index * size + h * sub, sub)]

    def gather_rounds(out, me):
        rounds, flows = {}, ((1, slices - 1 - me), (-1, me))
        for sign, onward in flows:
            behind = me if sign > 0 else slices - 1 - me
            sends, waits = {}, {}
            for k in range(behind + 1):
                for h in range(halves):
                    ref = (me - sign * k, h)
                    if onward:
                        sends[k * halves + h] = ref
                    if k:
                        waits[k * halves + h] = ref
            rounds[sign] = (sends, waits)
        return rounds

    def line_gather(out, me, sems):
        steps, ends = [], []
        ring = gather_rounds(out, me)

        def onward(sign, i):
            ref = unit_rows(out, *ring[sign][0][i])
            return sems(sign, i, ref, ref, sign)

        def step(i):
            for sign in (1, -1):
                sends, waits = ring[sign]
                if i in waits:
                    sems(sign, i - halves, unit_rows(out, *waits[i]), unit_rows(out, *waits[i]), 0).wait_recv()
                if i in sends:
                    if i >= IN_FLIGHT:
                        onward(sign, i - IN_FLIGHT).wait_send()
                    onward(sign, i).start()

        def finish():
            for sign in (1, -1):
                sends, _ = ring[sign]
                for i in sorted(sends)[-IN_FLIGHT:]:
                    onward(sign, i).wait_send()

        return [partial(step, i) for i in range(slices * halves)], finish

    def line_sum(total, ins, out, me, sems, size=count, halves=halves):
        units, sub = (slices - 1) * halves, size // halves
        before = {1: [], -1: []}

        def place(sign, i):
            return slices - 1 - i // halves if sign > 0 else i // halves

        def slot(sign, i):
            return ins[0 if sign > 0 else 1].at[i]

        def onward(sign, i):
            return sems(sign, i, unit_rows(total, place(sign, i), i % halves, size, sub), slot(sign, i), sign)

        def step(r):
            for sign in (1, -1):
                depth = me if sign > 0 else slices - 1 - me
                i = r - depth
                if not 0 <= i < units:
                    continue
                b = place(sign, i)
                passes = b > me if sign > 0 else b < me
                if (passes or b == me) and depth:
                    sems(sign, i, slot(sign, i), slot(sign, i), 0).wait_recv()
                    add_rows(total, slot(sign, i), b * size + (i % halves) * sub, 0, sub)
                if passes:
                    if len(before[sign]) == IN_FLIGHT:
                        onward(sign, before[sign].pop(0)).wait_send()
                    before[sign].append(i)
                    onward(sign, i).start()

        def finish():
            for sign in (1, -1):
                for i in before[sign]:
                    onward(sign, i).wait_send()

        def place_own():
            if out is not None:
                out[pl.ds(me * size, size), :] = total[pl.ds(me * size, size), :]

        return [partial(step, r) for r in range(units + slices - 1)], place_own, finish

    def semaphores(units):
        base = copies.remotes
        copies.remotes += 2 * units

        def make(sign, i, source, target, to):
            k = base + i + (0 if sign > 0 else units)
            return pltpu.make_async_remote_copy(
                src_ref=source, dst_ref=target, send_sem=send.at[k], recv_sem=recv.at[k],
                device_id=(seq, part + to), device_id_type=MESH,
            )

        return make

    def interleave(*lists):
        for k in range(max((len(steps) for steps in lists), default=0)):
            for steps in lists:
                if k < len(steps):
                    steps[k]()

    def at_place(run):
        for me in range(slices):
            pl.when(part == me)(partial(run, me))

    own_copies = []
    for own, out in zip(blocks, outs):
        mine = copies.own(own, block(out, part))
        mine.start()
        own_copies.append(mine)
    plane_total, *plane_ins = part_scratch[5 * len(parts) :]
    pieces = [out.shape[0] // peers for out in pack_outs]
    piece_rows = sum(pieces)
    plane_sems = semaphores(slices)
    block_sems = [semaphores(slices * halves) for _ in outs]
    sum_sems = [semaphores(slices * halves) for _ in part_outs]
    after_sems = [semaphores(slices * halves) for _ in part_outs]

    to_chips = []

    def to_plane():
        for n, pack in enumerate(packs):
            half = pack.shape[1] // 2
            size = half // chips
            sibling_sum, mine, by_chip = weight_scratch[3 * n : 3 * n + 3]
            held[n].wait()
            to_core[n].wait_recv()

            def add_half(z, carry, sibling_sum=sibling_sum, mine=mine, half=half):
                add_rows(mine.at[z], sibling_sum.at[z], 0, 0, half)
                return carry

            lax.fori_loop(0, slices, add_half, 0)
            for e in range(1, chips):
                to = lax.rem(chip + e, chips)
                copy = copies.remote(mine.at[:, pl.ds(pl.multiple_of(to * size, 16), size)], by_chip.at[e - 1], to * 2 + core, part)
                copy.start()
                to_chips.append((n, e, copy))
                sent.append(copy)

    length = slices * halves
    plans = []
    for me in range(slices):
        gathers = [line_gather(out, me, sems) for out, sems in zip(outs, block_sems)]
        sums, afters = [], []
        for n, out in enumerate(part_outs):
            total, _, _, right_in, left_in = part_scratch[5 * n : 5 * n + 5]
            sums.append(line_sum(total, (right_in, left_in), out, me, sum_sems[n]))
            afters.append(line_gather(out, me, after_sems[n]))
        owned = [line_sum(plane_total, plane_ins, None, me, plane_sems, piece_rows, 1)]
        plans.append((gathers, sums, afters, owned))

    def rounds(me, *which):
        lists, ends = [], []
        for kind, n, low, high in which:
            entry = plans[me][kind][n]
            steps = entry[0]
            lists.append(steps[low:high])
            if low < len(steps) <= high:
                ends += list(entry[1:])
        interleave(*lists)
        for finish in ends:
            finish()

    def run(*which):
        at_place(lambda me: rounds(me, *which))

    def to_owners():
        for n, pack in enumerate(packs):
            half = pack.shape[1] // 2
            size, first_row = half // chips, sum(pieces[:n])
            mine, by_chip = weight_scratch[3 * n + 1 : 3 * n + 3]
            for m, e, copy in to_chips:
                if m == n:
                    copy.wait_recv()

            def add_plane(i, carry, mine=mine, by_chip=by_chip, size=size, first_row=first_row):
                z, r = i // (size // 16), lax.rem(i, size // 16)
                at = pl.ds(pl.multiple_of(r * 16, 16), 16)
                value = mine[z, pl.ds(pl.multiple_of(chip * size + r * 16, 16), 16), :].astype(F32)
                for e in range(chips - 1):
                    value = value + by_chip[e, z, at, :].astype(F32)
                plane_total[pl.ds(pl.multiple_of(z * piece_rows + first_row + r * 16, 16), 16), :] = value.astype(BF16)
                return carry

            lax.fori_loop(0, slices * (size // 16), add_plane, 0)

    def piece_at(n, of_chip, of_core):
        size = pack_outs[n].shape[0] // peers
        index = of_core * chips + of_chip if n < len(packs) else of_chip * 2 + of_core
        return pl.multiple_of(index * size, 16), size

    round_plane, to_sibling = [], []

    def back_to_plane():
        for n, out in enumerate(pack_outs):
            start, size = piece_at(n, chip, core)

            def keep(r, carry, out=out, start=start, first_row=sum(pieces[:n])):
                at = pl.ds(pl.multiple_of(part * piece_rows + first_row + r * 16, 16), 16)
                out[pl.ds(pl.multiple_of(start + r * 16, 16), 16), :] = plane_total[at, :]
                return carry

            lax.fori_loop(0, size // 16, keep, 0)
            piece = out.at[pl.ds(start, size)]
            for e in range(1, chips):
                copy = copies.remote(piece, piece, lax.rem(chip + e, chips) * 2 + core, part)
                copy.start()
                round_plane.append((n, e, copy))
                sent.append(copy)
            copy = copies.remote(piece, piece, sibling, part)
            copy.start()
            round_plane.append((n, 0, copy))
            sent.append(copy)

    sum_length = (slices - 1) * halves + slices - 1
    plane_copies = []
    for n, summed in enumerate(plane_sums):
        first_row, size = sum(pieces[: len(packs) + n]), pieces[len(packs) + n]
        for z in range(slices):
            plane_copies.append(copies.own(summed.at[z], plane_total.at[pl.ds(z * piece_rows + first_row, size)]))
    for keep in plane_copies:
        keep.start()
    for mine in own_copies:
        mine.wait()
    run((0, 0, 0, 2))
    to_plane()
    run((0, 0, 2, 3))
    finish_halo(0)
    run((0, 0, 3, length), (1, 0, 0, sum_length))
    for keep in plane_copies:
        keep.wait()
    if len(parts) > 1:
        finish_halo(1)
        run((1, 1, 0, sum_length // 2), (2, 0, 0, sum_length // 2))
        to_owners()
        run((1, 1, sum_length // 2, sum_length), (2, 0, sum_length // 2, length))
    else:
        to_owners()
    last = len(parts) - 1
    run((3, 0, 0, 2 * (slices - 1)), (2, last, 0, length // 2))
    back_to_plane()
    run((2, last, length // 2, length))
    for n, e, copy in round_plane:
        copy.wait_recv()
        if e:
            start, size = piece_at(n, lax.rem(chip + chips - e, chips), core)
            piece = pack_outs[n].at[pl.ds(start, size)]
            copy = copies.remote(piece, piece, sibling, part)
            copy.start()
            to_sibling.append(copy)
            sent.append(copy)
    for copy in to_sibling:
        copy.wait_recv()
    for copy in sent:
        copy.wait_send()


class Rows:
    def __init__(self, pack, index, size):
        self.pack, self.at = pack, slice(index * size, (index + 1) * size)

    def __getitem__(self, _):
        value = self.pack[:, self.at, :]
        return value.reshape(value.shape[0] * value.shape[1], value.shape[2])


def write_rows(pack, index, size, value):
    slices = pack.shape[0]
    pack[:, index * size : (index + 1) * size, :] = value.astype(BF16).reshape(slices, size, value.shape[1])


def mask_bias(code, low, high):
    return jnp.where((code >= low) & (code < high), 0.0, NEG_BIG).astype(F32)


def pair_product(left, spread, p, see):
    count = see.size
    blocks = [spread[h * PAIR : (h + 1) * PAIR, see] for h in (2 * p, 2 * p + 1)]
    if count % LANES:
        return [dot_nn(left, block) for block in blocks]
    both = dot_nn(left, jnp.concatenate(blocks, axis=1))
    return both[:, :count], both[:, count:]


def attend(window, code, low, high, w_key_t, w_value_t, spread, bias, top, total, out):
    top[...] = jnp.full_like(top, NEG_BIG)
    total[...] = jnp.zeros_like(total)
    out[...] = jnp.zeros_like(out)

    def step(c, see):
        at = chunk_rows(window.start, c)
        rows = window.held[at, :]
        keys = dot_nt(rows, w_key_t[...]).astype(BF16)
        values_t = dot_nt(rows, w_value_t[...]).astype(BF16).T
        bias[:, see] = mask_bias(code[at, :], low[:, see], high[:, see])
        for h in range(HEADS):
            p = h // 2
            if h % 2 == 0:
                both = pair_product(keys[:, p * PAIR : (p + 1) * PAIR], spread, p, see)
            scores = both[h % 2] * SCORE_SCALE + bias[:, see]
            before = top[h : h + 1, see]
            now = jnp.maximum(before, jnp.max(scores, axis=0, keepdims=True))
            weights = jnp.exp2(scores - now)
            shrink = jnp.exp2(before - now)
            top[h : h + 1, see] = now
            total[h : h + 1, see] = total[h : h + 1, see] * shrink + jnp.sum(weights, axis=0, keepdims=True)
            head = slice(h * HEAD_SIZE, (h + 1) * HEAD_SIZE)
            out[head, see] = out[head, see] * shrink + dot_nn(values_t[head, :], weights.astype(BF16))

    window.loops(out.shape[1], step)
    for h in range(HEADS):
        head = slice(h * HEAD_SIZE, (h + 1) * HEAD_SIZE)
        out[head, :] = out[head, :] / total[h : h + 1, :]


def attend_back(
    window, code, low, high, w_key_t, w_value_t, spread, grad_spread, pairs, grad_pairs, lse, delta, bias,
    query_grad, window_grad, w_key_grad, w_value_grad,
):
    count = spread.shape[1]
    query_grad[...] = jnp.zeros_like(query_grad)
    w_key_grad[...] = jnp.zeros_like(w_key_grad)
    w_value_grad[...] = jnp.zeros_like(w_value_grad)
    window_grad[...] = jnp.zeros_like(window_grad)

    def step(c, see):
        at = chunk_rows(window.start, c)
        seen = (see, pl.ds(count + see.start, see.size) if isinstance(see.start, int) else pl.ds(pl.multiple_of(count + see.start, LANES), see.size))
        rows = window.held[at, :]
        keys = dot_nt(rows, w_key_t[...]).astype(BF16)
        keys_t = keys.T
        values = dot_nt(rows, w_value_t[...]).astype(BF16)
        bias[:, see] = mask_bias(code[at, :], low[:, see], high[:, see])
        key_grads, value_grads = [], []
        for p in range(PAIRS):
            columns = slice(p * PAIR, (p + 1) * PAIR)
            probs, score_grads = [], []
            both_scores = pair_product(keys[:, columns], spread, p, see)
            both_dprobs = pair_product(values[:, columns], grad_spread, p, see)
            for h in (2 * p, 2 * p + 1):
                head = slice(h * HEAD_SIZE, (h + 1) * HEAD_SIZE)
                prob = jnp.exp2(both_scores[h % 2] * SCORE_SCALE + bias[:, see] - lse[h : h + 1, see])
                score_grad = (prob * (both_dprobs[h % 2] - delta[h : h + 1, see])).astype(BF16)
                query_grad[head, see] += dot_nn(keys_t[head, :], score_grad)
                probs.append(prob.astype(BF16))
                score_grads.append(score_grad)
            if count % LANES == 0:
                both = jnp.concatenate([pairs[p, r, :] for r in seen], axis=0)
                grad_both = jnp.concatenate([grad_pairs[p, r, :] for r in seen], axis=0)
                key_grads.append(dot_nn(jnp.concatenate(score_grads, axis=1), both))
                value_grads.append(dot_nn(jnp.concatenate(probs, axis=1), grad_both))
            else:
                key_grads.append(sum(dot_nn(x, pairs[p, r, :]) for x, r in zip(score_grads, seen)))
                value_grads.append(sum(dot_nn(x, grad_pairs[p, r, :]) for x, r in zip(probs, seen)))
        keys_low = (jnp.concatenate(key_grads, axis=1) * SCALE).astype(BF16)
        values_low = jnp.concatenate(value_grads, axis=1).astype(BF16)
        window_grad[at, :] = (dot_nn(keys_low, w_key_t[...]) + dot_nn(values_low, w_value_t[...])).astype(window_grad.dtype)
        w_key_grad[...] += dot_tn(rows, keys_low)
        w_value_grad[...] += dot_tn(rows, values_low)

    window.loops(count, step)


def forward_kernel(
    cols, bounds, own, content_window, encoded_window, gain, code, low, high_self, high_cross, pack_one, pack_two_in,
    self_t, lse_self, hidden, cross_t, lse_cross,
    spread, bias, top, total, low_t, content_held, encoded_held, pack_two, content_sems, encoded_sems, pack_sem,
):
    content = Window(bounds, content_window, content_held, content_sems)
    encoded = Window(bounds, encoded_window, encoded_held, encoded_sems)
    content.fetch()
    whole_pack = pltpu.make_async_copy(pack_two_in, pack_two, pack_sem.at[0])
    whole_pack.start()
    encoded.fetch()
    w_query_t, w_key_t, w_value_t = (Rows(pack_one, k, cols) for k in range(3))
    low_t[...] = dot_nt(w_query_t[...], own[...]).astype(BF16)
    spread_heads(low_t, spread)
    attend(content, code, low, high_self, w_key_t, w_value_t, spread, bias, top, total, self_t)
    lse_self[...] = top[...] + jnp.log2(total[...])
    whole_pack.wait()
    w_out, w_query_t, w_key_t, w_value_t = (Rows(pack_two, k, cols) for k in range(4))
    branch = dot_tn(self_t[...].astype(BF16), w_out[...])
    normed, _ = layer_norm(own[...].astype(F32) + branch)
    hidden[...] = normed * gain[...]
    low_t[...] = dot_nt(w_query_t[...], hidden[...].astype(BF16)).astype(BF16)
    spread_heads(low_t, spread)
    attend(encoded, code, low, high_cross, w_key_t, w_value_t, spread, bias, top, total, cross_t)
    lse_cross[...] = top[...] + jnp.log2(total[...])


def ffn_kernel(
    cols, hidden_one, cross_t, pack_two, gain_cross, pack_three_in, gain_final, out_grad,
    mixed, resid_grad, w_out_grad, grad_three_out, gain_cross_grad, gain_final_grad,
    normed_two, hidden_two_low, slope, active, sum_ffn, pack_out, pack_three, grad_three_pack, sems, out_sems,
):
    slices, units = pack_three.shape[0], active.shape[2]
    if grad_three_pack.shape[1] > 2 * units:
        grad_three_pack[:, 2 * units :, :] = jnp.zeros((slices, grad_three_pack.shape[1] - 2 * units, grad_three_pack.shape[2]), BF16)
    out_copy = pltpu.make_async_copy(pack_two.at[:, pl.ds(4 * cols, cols)], pack_out, sems.at[slices])
    out_copy.start()
    slice_copies = [pltpu.make_async_copy(pack_three_in.at[z], pack_three.at[z], sems.at[z]) for z in range(slices)]
    for copy in slice_copies:
        copy.start()
    out_copy.wait()
    w_out = Rows(pack_out, 0, cols)
    cross_low = cross_t[...].astype(BF16)
    normed, scale_two = layer_norm(hidden_one[...] + dot_tn(cross_low, w_out[...]))
    normed_two[...] = normed
    hidden_two = normed * gain_cross[...]
    hidden_two_low[...] = hidden_two.astype(BF16)
    sum_ffn[...] = hidden_two
    for z in range(slices):
        slice_copies[z].wait()
        inner = dot_nt(hidden_two_low[...], pack_three[z, 0:units, :])
        below = 0.5 * (1.0 + lax.erf(inner * math.sqrt(0.5)))
        slope[z] = below + inner * (jnp.exp2(inner * inner * (-0.5 * LOG2E)) * (1.0 / math.sqrt(2.0 * math.pi)))
        active[z] = (inner * below).astype(BF16)
        sum_ffn[...] += dot_nn(active[z], pack_three[z, units : 2 * units, :])
    normed_three, scale_three = layer_norm(sum_ffn[...])
    mixed[...] = (normed_three * gain_final[...]).astype(BF16)
    grad_three, gain_grad = norm_back(out_grad[...].astype(F32), normed_three, scale_three, gain_final[...])
    gain_final_grad[...] = gain_grad
    ffn_low = grad_three.astype(BF16)
    result_copies = [pltpu.make_async_copy(grad_three_pack.at[z], grad_three_out.at[z], out_sems.at[z]) for z in range(slices)]
    sum_ffn[...] = grad_three
    for z in range(slices):
        grad_three_pack[z, units : 2 * units, :] = dot_tn(active[z], ffn_low).astype(BF16)
        inner_low = (dot_nt(ffn_low, pack_three[z, units : 2 * units, :]) * slope[z]).astype(BF16)
        grad_three_pack[z, 0:units, :] = dot_tn(inner_low, hidden_two_low[...]).astype(BF16)
        sum_ffn[...] += dot_nn(inner_low, pack_three[z, 0:units, :])
        result_copies[z].start()
    grad, gain_grad = norm_back(sum_ffn[...], normed_two[...], scale_two, gain_cross[...])
    gain_cross_grad[...] = gain_grad
    resid_grad[...] = grad
    w_out_grad[...] = dot_nn(cross_low, grad.astype(BF16)).astype(BF16)
    for copy in result_copies:
        copy.wait()


def prepare_back(query, query_t, grad, grad_t, out, spread, grad_spread, pairs, grad_pairs, delta, low_t):
    low_t[...] = query_t.astype(BF16)
    spread_heads(low_t, spread)
    for p in range(PAIRS):
        pair_rows(query.astype(BF16), p, pairs)
        pair_rows(grad.astype(BF16), p, grad_pairs)
    low_t[...] = grad_t.astype(BF16)
    spread_heads(low_t, grad_spread)
    for h in range(HEADS):
        head = slice(h * HEAD_SIZE, (h + 1) * HEAD_SIZE)
        delta[h : h + 1, :] = jnp.sum(low_t[head, :].astype(F32) * out[head, :], axis=0, keepdims=True)


def cross_back_kernel(
    cols, bounds, own, self_t, gain, resid_two_grad, cross_t, lse, window_in, code, low, high, pack_two,
    w_cross_out_grad, gain_cross_grad, gain_final_grad, resid_one_grad, window_out, grad_two_pack,
    spread, grad_spread, pairs, grad_pairs, delta, bias, low_t, query_grad, key_sum, value_sum, held, window_grad, sems, out_sem,
    normed_one, scale_one,
):
    window = Window(bounds, window_in, held, sems)
    window.fetch()
    w_out, w_query_t, w_key_t, w_value_t, w_cross_out = (Rows(pack_two, k, cols) for k in range(5))
    self_low = self_t[...].astype(BF16)
    normed, scale = layer_norm(own[...].astype(F32) + dot_tn(self_low, w_out[...]))
    normed_one[...] = normed
    scale_one[...] = scale
    hidden_low = (normed * gain[...]).astype(BF16)
    branch_low = resid_two_grad[...].astype(BF16)
    prepare_back(
        dot_nt(hidden_low, w_query_t[...]), dot_nt(w_query_t[...], hidden_low),
        dot_nt(branch_low, w_cross_out[...]), dot_nt(w_cross_out[...], branch_low),
        cross_t, spread, grad_spread, pairs, grad_pairs, delta, low_t,
    )
    attend_back(
        window, code, low, high, w_key_t, w_value_t, spread, grad_spread, pairs, grad_pairs, lse, delta, bias,
        query_grad, window_grad, key_sum, value_sum,
    )
    result = pltpu.make_async_copy(window_grad, window_out, out_sem.at[0])
    result.start()
    query_low = (query_grad[...] * SCALE).astype(BF16)
    hidden_low = (normed_one[...] * gain[...]).astype(BF16)
    grad_one = resid_two_grad[...] + dot_tn(query_low, w_query_t[...])
    grad, gain_sum = norm_back(grad_one, normed_one[...], scale_one[...], gain[...])
    resid_one_grad[...] = grad
    write_rows(grad_two_pack, 0, cols, dot_nn(self_t[...].astype(BF16), grad.astype(BF16)))
    write_rows(grad_two_pack, 1, cols, dot_nn(query_low, hidden_low))
    write_rows(grad_two_pack, 2, cols, key_sum[...].T)
    write_rows(grad_two_pack, 3, cols, value_sum[...].T)
    write_rows(grad_two_pack, 4, cols, w_cross_out_grad[...])
    slices, rows, width = grad_two_pack.shape
    gains = jnp.concatenate([gain_sum, gain_cross_grad[...], gain_final_grad[...], jnp.zeros((13, width), F32)], axis=0)
    for z in range(slices):
        grad_two_pack[z, 5 * cols : 5 * cols + 16, :] = gains.astype(BF16)
        if rows > 5 * cols + 16:
            grad_two_pack[z, 5 * cols + 16 :, :] = jnp.zeros((rows - 5 * cols - 16, width), BF16)
    result.wait()


def self_back_kernel(
    cols, bounds, own, resid_one_grad, pack_two, self_t, lse, window_in, code, low, high, pack_one,
    own_grad, window_out, grad_one_pack,
    spread, grad_spread, pairs, grad_pairs, delta, bias, low_t, query_grad, key_sum, value_sum, held, window_grad, sems, out_sem,
    pack_out, pack_sem,
):
    out_copy = pltpu.make_async_copy(pack_two.at[:, pl.ds(0, cols)], pack_out, pack_sem.at[0])
    out_copy.start()
    window = Window(bounds, window_in, held, sems)
    window.fetch()
    out_copy.wait()
    w_query_t, w_key_t, w_value_t = (Rows(pack_one, k, cols) for k in range(3))
    w_out = Rows(pack_out, 0, cols)
    branch_low = resid_one_grad[...].astype(BF16)
    prepare_back(
        dot_nt(own[...], w_query_t[...]), dot_nt(w_query_t[...], own[...]),
        dot_nt(branch_low, w_out[...]), dot_nt(w_out[...], branch_low),
        self_t, spread, grad_spread, pairs, grad_pairs, delta, low_t,
    )
    attend_back(
        window, code, low, high, w_key_t, w_value_t, spread, grad_spread, pairs, grad_pairs, lse, delta, bias,
        query_grad, window_grad, key_sum, value_sum,
    )
    result = pltpu.make_async_copy(window_grad, window_out, out_sem.at[0])
    result.start()
    query_low = (query_grad[...] * SCALE).astype(BF16)
    write_rows(grad_one_pack, 0, cols, dot_nn(query_low, own[...]))
    write_rows(grad_one_pack, 1, cols, key_sum[...].T)
    write_rows(grad_one_pack, 2, cols, value_sum[...].T)
    slices, rows, width = grad_one_pack.shape
    if rows > 3 * cols:
        grad_one_pack[:, 3 * cols :, :] = jnp.zeros((slices, rows - 3 * cols, width), BF16)
    own_grad[...] = (resid_one_grad[...] + dot_tn(query_low, w_query_t[...])).astype(BF16)
    result.wait()


def finish_kernel(cols, units, slices, *refs):
    rows_in, (sum_one, sum_two, sum_three), outs = refs[:4], refs[4:7], refs[7:]
    step = pl.program_id(0)
    for source, target in zip(rows_in, outs[:4]):
        target[...] = source[...].astype(target.dtype)

    def weights(k):
        w_query, w_key, w_value, w_out, w_cross_query, w_cross_key, w_cross_value, w_cross_out, w_inner, w_outer = outs[4:14]
        width = sum_one.shape[1]
        wide, tall, unit_rows = width // slices, cols // slices, units // slices
        some = slice(k * wide, (k + 1) * wide)
        for n, target in enumerate((w_query, w_key, w_value)):
            target[...] = sum_one[n * cols : (n + 1) * cols, some].astype(F32).T
        for n, target in enumerate((w_cross_query, w_cross_key, w_cross_value)):
            target[...] = sum_two[(1 + n) * cols : (2 + n) * cols, some].astype(F32).T
        w_out[...] = sum_two[k * tall : (k + 1) * tall, :].astype(F32)
        w_cross_out[...] = sum_two[4 * cols + k * tall : 4 * cols + (k + 1) * tall, :].astype(F32)
        w_inner[...] = sum_three[0:units, some].astype(F32).T
        w_outer[...] = sum_three[units + k * unit_rows : units + (k + 1) * unit_rows, :].astype(F32)

    for k in range(slices):
        pl.when(step == k)(partial(weights, k))

    @pl.when(step == 0)
    def _():
        gains = sum_two[5 * cols : 5 * cols + 16, :].astype(F32)
        for k, target in enumerate(outs[14:17]):
            target[...] = gains[k : k + 1, :]


def call(kernel, outs, scratch, smem, *args, far=(), far_outs=(), micros=20):
    def space(k, left, scalars):
        return pl.ANY if k in left else pltpu.SMEM if k < scalars else pltpu.VMEM

    return pl.pallas_call(
        kernel,
        out_shape=[jax.ShapeDtypeStruct(shape, kind) for shape, kind in outs],
        in_specs=[pl.BlockSpec(memory_space=space(k, far, smem)) for k in range(len(args))],
        out_specs=[pl.BlockSpec(memory_space=space(k, far_outs, 0)) for k in range(len(outs))],
        scratch_shapes=[pltpu.SemaphoreType.DMA((shape,)) if kind is None else pltpu.VMEM(shape, kind) for shape, kind in scratch],
        compiler_params=pltpu.CompilerParams(vmem_limit_bytes=VMEM_LIMIT),
        cost_estimate=pl.CostEstimate(flops=micros * 10**9, bytes_accessed=micros * 10**6, transcendentals=0),
    )(*args)


def padded(size, unit):
    return -(-size // unit) * unit


def talk(kernel, outs, out_spaces, scratch, copies, number, spaces, *args):
    return pl.pallas_call(
        kernel,
        out_shape=[jax.ShapeDtypeStruct(shape, kind) for shape, kind in outs],
        in_specs=[pl.BlockSpec(memory_space=space) for space in spaces],
        out_specs=[pl.BlockSpec(memory_space=space) for space in out_spaces],
        scratch_shapes=[pltpu.SemaphoreType.DMA((n,)) for n in (copies[0], copies[0], copies[1])] + [pltpu.VMEM(shape, kind) for shape, kind in scratch],
        compiler_params=pltpu.CompilerParams(vmem_limit_bytes=VMEM_LIMIT, collective_id=number, has_side_effects=True),
        cost_estimate=pl.CostEstimate(flops=80 * 10**9, bytes_accessed=80 * 10**6, transcendentals=0),
    )(*args)


def body(
    query_state, content, encoded, sentence_lengths, key_score, query_cut, w_query, w_key, w_value, w_out, gain_self,
    w_cross_query, w_cross_key, w_cross_value, w_cross_out, gain_cross, w_inner, w_outer, gain_final, out_grad,
):
    rows, width = query_state.shape
    slices = lax.axis_size("head")
    count = rows // slices
    lanes = math.gcd(count, LANES)
    wide = padded(count + 2 * DOC_LEN + CHUNK, lanes)
    spare = wide - count - 2 * DOC_LEN
    seq, part = lax.axis_index("seq"), lax.axis_index("head")
    begin = seq * rows + part * count
    score, cut = key_score.reshape(-1, lanes), query_cut.reshape(-1, lanes)
    gain_self, gain_cross, gain_final = (g.reshape(1, width) for g in (gain_self, gain_cross, gain_final))

    peers = lax.axis_size("seq")
    chips = peers // 2
    cols, units = w_query.shape[1], w_inner.shape[1]
    unit = 16 * peers
    sizes = [padded(n, unit) for n in (3 * cols, 5 * cols, 2 * units)]
    grad_sizes = [sizes[0], padded(5 * cols + 16, unit), sizes[2]]

    share = sizes[2] // peers
    slice_three = jnp.concatenate([w_inner.T, w_outer, jnp.zeros((sizes[2] - 2 * units, width), BF16)], axis=0)
    share_three = lax.dynamic_slice_in_dim(slice_three, seq * share, share, 0)
    pack_three = lax.all_gather(share_three, ("head", "seq"), axis=0, tiled=True).reshape(slices, sizes[2], width)
    start_copies = 2 * (slices - 1) * (2 * chips) + 4 * slices
    hbm, vmem, smem = pl.ANY, pltpu.VMEM, pltpu.SMEM
    (
        content_window, encoded_window, pack_one, pack_two, own, own_out_grad, code, low, high_self, high_cross, bounds,
    ) = talk(
        partial(start_kernel, peers, slices, count),
        [((wide, width), BF16)] * 2 + [((slices, n, width), BF16) for n in sizes[:2]] + [((count, width), BF16)] * 2
        + [((wide, 1), F32)] + [((1, count), F32)] * 3 + [((1, 6), jnp.int32)],
        [vmem] * 10 + [smem],
        [((DOC_LEN, width), BF16), ((padded(wide // lanes, 8), lanes), F32)], (start_copies, 8 * slices + 16), 0,
        [hbm] * 4 + [vmem] * 8 + [smem] + [vmem] * 2,
        content, encoded, query_state, out_grad, w_query, w_key, w_value, w_out,
        w_cross_query, w_cross_key, w_cross_value, w_cross_out, sentence_lengths.reshape(1, -1), score, cut,
    )

    def split_refs(kernel, ins, outs):
        def run(*refs):
            return kernel(refs[:ins], refs[ins : ins + outs], refs[ins + outs :])
        return run

    touched = -(-wide // CHUNK)
    window_held = [((wide, width), BF16)]
    self_t, lse_self, hidden_one, cross_t, lse_cross = call(
        partial(forward_kernel, cols),
        [((width, count), F32), ((HEADS, count), F32), ((count, width), F32), ((width, count), F32), ((HEADS, count), F32)],
        [((HEADS * PAIR, count), BF16), ((CHUNK, count), F32), ((HEADS, count), F32), ((HEADS, count), F32), ((width, count), BF16)]
        + window_held * 2 + [((slices, sizes[1], width), BF16), (touched, None), (touched, None), (1, None)], 1,
        bounds, own, content_window, encoded_window, gain_self, code, low, high_self, high_cross, pack_one, pack_two, far=(2, 3, 10),
    )
    mixed, resid_two_grad, w_cross_out_grad, grads_three, gain_cross_grad, gain_final_grad = call(
        partial(ffn_kernel, cols),
        [
            ((count, width), BF16), ((count, width), F32), ((width, width), BF16), ((slices, grad_sizes[2], width), BF16),
            ((1, width), F32), ((1, width), F32),
        ],
        [
            ((count, width), F32), ((count, width), BF16), ((slices, count, units), F32),
            ((slices, count, units), BF16), ((count, width), F32), ((slices, cols, width), BF16), ((slices, sizes[2], width), BF16),
            ((slices, grad_sizes[2], width), BF16), (slices + 1, None), (slices, None),
        ], 0,
        hidden_one, cross_t, pack_two, gain_cross, pack_three, gain_final, own_out_grad, far=(2, 4), far_outs=(3,),
    )
    back = [
        ((HEADS * PAIR, count), BF16), ((HEADS * PAIR, count), BF16), ((PAIRS, 2 * count, PAIR), BF16),
        ((PAIRS, 2 * count, PAIR), BF16), ((HEADS, count), F32), ((CHUNK, count), F32), ((width, count), BF16),
        ((width, count), F32), ((width, width), F32), ((width, width), F32),
    ] + window_held * 2 + [(touched, None), (1, None)]
    resid_one_grad, encoded_part, grads_two = call(
        partial(cross_back_kernel, cols),
        [((count, width), F32), ((wide, width), BF16), ((slices, grad_sizes[1], width), BF16)],
        back + [((count, width), F32), ((count, 1), F32)], 1,
        bounds, own, self_t, gain_self, resid_two_grad, cross_t, lse_cross, encoded_window, code, low, high_cross, pack_two,
        w_cross_out_grad, gain_cross_grad, gain_final_grad, far=(7,), far_outs=(1,), micros=4,
    )
    mixed = lax.all_gather(mixed, "head", axis=0, tiled=True)
    own_grad, content_part, grads_one = call(
        partial(self_back_kernel, cols),
        [((count, width), BF16), ((wide, width), BF16), ((slices, grad_sizes[0], width), BF16)],
        back + [((slices, cols, width), BF16), (1, None)], 1,
        bounds, own, resid_one_grad, pack_two, self_t, lse_self, content_window, code, low, high_self, pack_one,
        far=(3, 6), far_outs=(1,), micros=4,
    )

    blocks, parts, grads, planes = [own_grad], [content_part, encoded_part], [grads_one, grads_two, grads_three], []
    weight_scratch = []
    for n in grad_sizes[: len(grads)]:
        half, size = n // 2, n // 2 // chips
        weight_scratch += [
            ((slices, half, width), BF16), ((slices, half, width), BF16), ((chips - 1, slices, size, width), BF16),
        ]
    halves = 2 if slices <= 4 else 1
    units_in = (slices - 1) * halves
    part_scratch = [
        ((rows, width), BF16), ((DOC_LEN, width), BF16), ((DOC_LEN, width), BF16),
        ((units_in, count // halves, width), BF16), ((units_in, count // halves, width), BF16),
    ] * len(parts)
    piece_rows = sum(grad_sizes) // peers
    plane_scratch = [((slices * piece_rows, width), BF16)] + [((slices - 1, piece_rows, width), BF16)] * 2
    ins, outs = (len(blocks), len(parts), len(grads), len(planes)), (len(blocks), len(parts), len(grad_sizes))

    def end(refs, out_refs, scratch):
        a, b, c = ins[0], ins[0] + ins[1], sum(ins[:3])
        end_kernel(
            peers, slices, count, refs[:a], refs[a:b], refs[b:c], refs[c:], out_refs[: outs[0]],
            out_refs[outs[0] : outs[0] + outs[1]], out_refs[outs[0] + outs[1] :], scratch,
        )

    end_copies = len(grad_sizes) * (1 + 3 * (chips - 1) + slices) + 2 * slices + len(parts) * 2 * slices + (len(blocks) + 2 * len(parts)) * 2 * slices * halves
    results = talk(
        split_refs(end, sum(ins), sum(outs)),
        [((rows, width), BF16)] * (len(blocks) + len(parts)) + [((n, width), BF16) for n in grad_sizes], [vmem] * sum(outs),
        weight_scratch + part_scratch + plane_scratch, (end_copies, 8 * slices + 8), 1, [hbm] * sum(ins), *blocks, *parts, *grads, *planes,
    )
    query_state_grad, content_grad, encoded_grad, sum_one, sum_two, sum_three = results

    square, tall = ((width, cols), F32), ((cols, width), F32)
    finals = [((rows, width), BF16)] + [((rows, width), F32)] * 3 + [square] * 3 + [tall, square, square, square, tall]
    finals += [((width, units), F32), ((units, width), F32)] + [((1, width), F32)] * 3
    by_rows = pl.BlockSpec((count, width), lambda i: (i, 0))

    def whole(shape):
        return pl.BlockSpec(shape, lambda i: (0,) * len(shape))

    def by_step(shape):
        return pl.BlockSpec((shape[0] // slices, shape[1]), lambda i: (i, 0))

    sums = [sum_one, sum_two, sum_three]
    results = pl.pallas_call(
        partial(finish_kernel, cols, units, slices),
        grid=(slices,),
        out_shape=[jax.ShapeDtypeStruct(shape, kind) for shape, kind in finals],
        in_specs=[by_rows] * 4 + [whole(x.shape) for x in sums],
        out_specs=[by_rows] * 4 + [by_step(shape) for shape, _ in finals[4:14]] + [whole(shape) for shape, _ in finals[14:]],
        compiler_params=pltpu.CompilerParams(vmem_limit_bytes=VMEM_LIMIT),
    )(mixed, query_state_grad, content_grad, encoded_grad, *sums)
    (
        mixed, query_state_grad, content_grad, encoded_grad, w_query_grad, w_key_grad, w_value_grad, w_out_grad,
        w_cross_query_grad, w_cross_key_grad, w_cross_value_grad, w_cross_out_grad, w_inner_grad, w_outer_grad, *gains,
    ) = results
    gains = [g.reshape(width) for g in gains]
    return (
        mixed, query_state_grad, content_grad, encoded_grad, w_query_grad, w_key_grad, w_value_grad, w_out_grad, gains[0],
        w_cross_query_grad, w_cross_key_grad, w_cross_value_grad, w_cross_out_grad, gains[1], w_inner_grad, w_outer_grad, gains[2],
    )


def solution(mesh):
    rows, whole, columns, split = P("seq", None), P(), P(None, "head"), P("head", None)
    in_specs = (
        rows, rows, rows, whole, whole, whole, columns, columns, columns, split, whole,
        columns, columns, columns, split, whole, columns, split, whole, rows,
    )
    out_specs = (
        rows, rows, rows, rows, columns, columns, columns, split, whole,
        columns, columns, columns, split, whole, columns, split, whole,
    )
    return jax.shard_map(body, mesh=mesh, in_specs=in_specs, out_specs=out_specs, check_vma=False)
```

```python
from functools import partial
import math

import jax
import jax.numpy as jnp
from jax import lax
from jax.experimental import pallas as pl
from jax.experimental.pallas import tpu as pltpu
from jax.sharding import PartitionSpec as P

HEADS = 8
HEAD_SIZE = 64
PAIR = 2 * HEAD_SIZE
PAIRS = HEADS // 2
DOC_LEN = 1024
CHUNK = 528
LANES = 128
IN_FLIGHT = 2
EPS = 1e-05
NEG_BIG = -1e30
LOG2E = 1.4426950408889634
SCALE = 1.0 / math.sqrt(HEAD_SIZE)
SCORE_SCALE = SCALE * LOG2E
CODES = 128
BF16 = jnp.bfloat16
F32 = jnp.float32
VMEM_LIMIT = 60 << 20


def dot_nn(left, right):
    return lax.dot_general(left, right, (((1,), (0,)), ((), ())), preferred_element_type=F32)


def dot_nt(left, right):
    return lax.dot_general(left, right, (((1,), (1,)), ((), ())), preferred_element_type=F32)


def dot_tn(left, right):
    return lax.dot_general(left, right, (((0,), (0,)), ((), ())), preferred_element_type=F32)


def chunk_range(bounds):
    start = bounds[0, 0] // 16 * 16
    return start, (bounds[0, 1] - start + CHUNK - 1) // CHUNK


def chunk_rows(start, c):
    return pl.ds(pl.multiple_of(start + c * CHUNK, 16), CHUNK)


class Window:
    def __init__(self, bounds, source, held, sems):
        self.bounds, self.source, self.held, self.sems = bounds, source, held, sems
        self.start, self.chunks = chunk_range(bounds)

    def copy(self, c):
        rows = chunk_rows(self.start, c)
        return pltpu.make_async_copy(self.source.at[rows], self.held.at[rows], self.sems.at[c])

    def fetch(self):
        def one(c, carry):
            self.copy(c).start()
            return carry

        lax.fori_loop(0, self.chunks, one, 0)

    def loops(self, count, step):
        bounds, start, chunks = self.bounds, self.start, self.chunks

        def loop(number, size, where):
            def one(i, carry):
                c, lane = where(i)
                self.copy(c).wait()
                step(c, pl.ds(lane, size) if isinstance(lane, int) else pl.ds(pl.multiple_of(lane, LANES), size))
                return carry

            lax.fori_loop(0, number, one, 0)

        if count != 3 * LANES:
            return loop(chunks, count, lambda i: (i, 0))
        thirds = [(bounds[0, k] - start) // CHUNK for k in (2, 3)] + [(bounds[0, k] - start + CHUNK - 1) // CHUNK for k in (4, 5)]
        edges = [chunks * 0]
        for edge in thirds:
            edges.append(jnp.clip(edge, edges[-1], chunks))
        edges.append(chunks)

        def two(first, second, second_lane):
            number = edges[first + 1] - edges[first]

            def where(i):
                early = i < number
                return jnp.where(early, edges[first] + i, edges[second] + i - number), jnp.where(early, 0, second_lane)

            return number + edges[second + 1] - edges[second], where

        loop(edges[3] - edges[2], count, lambda i: (edges[2] + i, 0))
        number, where = two(1, 3, LANES)
        loop(number, 2 * LANES, where)
        number, where = two(0, 4, 2 * LANES)
        loop(number, LANES, where)


def layer_norm(resid):
    mean_row = jnp.mean(resid, axis=1, keepdims=True)
    centred = resid - mean_row
    var_row = jnp.mean(centred * centred, axis=1, keepdims=True)
    scale_row = lax.rsqrt(var_row + EPS)
    return centred * scale_row, scale_row


def norm_back(grad, normed, scale_row, gain):
    gain_grad = jnp.sum(grad * normed, axis=0, keepdims=True)
    scaled = grad * gain
    centre = jnp.mean(scaled, axis=1, keepdims=True)
    along = jnp.mean(scaled * normed, axis=1, keepdims=True)
    return scale_row * (scaled - centre - normed * along), gain_grad


def spread_heads(source, target):
    target[...] = jnp.zeros_like(target)
    for h in range(HEADS):
        row = h * PAIR + (h % 2) * HEAD_SIZE
        target[row : row + HEAD_SIZE, :] = source[h * HEAD_SIZE : (h + 1) * HEAD_SIZE, :]


def pair_rows(source, p, target):
    rows = source.shape[0]
    both = source[:, p * PAIR : (p + 1) * PAIR]
    lane = lax.broadcasted_iota(jnp.int32, both.shape, 1)
    zero = jnp.zeros_like(both)
    target[p, 0:rows, :] = jnp.where(lane < HEAD_SIZE, both, zero)
    target[p, rows : 2 * rows, :] = jnp.where(lane < HEAD_SIZE, zero, both)


MESH = pl.DeviceIdType.MESH


class Copies:
    def __init__(self, send, recv, local):
        self.send, self.recv, self.local = send, recv, local
        self.remotes, self.locals = 0, 0

    def remote(self, source, target, seq, part):
        k = self.remotes
        self.remotes += 1
        return pltpu.make_async_remote_copy(
            src_ref=source, dst_ref=target, send_sem=self.send.at[k], recv_sem=self.recv.at[k],
            device_id=(seq, part), device_id_type=MESH,
        )

    def own(self, source, target):
        k = self.locals
        self.locals += 1
        return pltpu.make_async_copy(source, target, self.local.at[k])


def greet(seq, part, peers, slices):
    barrier = pltpu.get_barrier_semaphore()
    for d in range(1, peers):
        pl.semaphore_signal(barrier, inc=1, device_id=(lax.rem(seq + d, peers), part), device_id_type=MESH)
    for d in range(1, slices):
        pl.semaphore_signal(barrier, inc=1, device_id=(seq, lax.rem(part + d, slices)), device_id_type=MESH)
    pl.semaphore_wait(barrier, peers - 1 + slices - 1)


def halo_sizes(part, count, rows):
    return max(0, DOC_LEN - part * count), max(0, (part + 1) * count + DOC_LEN - rows)


def put_rows(whole, part, row, ref, flip):
    value = ref[...]
    if flip:
        value = value.astype(F32).T.astype(BF16)
    whole[part, row : row + value.shape[0], :] = value


def pad_rows(whole, part, row):
    if row < whole.shape[1]:
        whole[part, row:, :] = jnp.zeros((whole.shape[1] - row, whole.shape[2]), BF16)


def find_sentences(begin, count, total_rows, lengths, score, cut, code, low, high_self, high_cross, bounds, blocks_code):
    lanes, blocks = score.shape[1], code.shape[0] // score.shape[1]
    first_block = (begin - DOC_LEN) // lanes
    for j in range(blocks):
        at = jnp.clip(first_block + j, 0, score.shape[0] - 1)
        blocks_code[j : j + 1, :] = score[pl.ds(at, 1), :].astype(F32)
    pos = lax.broadcasted_iota(jnp.int32, (blocks, lanes), 0) * lanes + lax.broadcasted_iota(jnp.int32, (blocks, lanes), 1)
    pos = pos + (begin - DOC_LEN)
    own_pos = lax.broadcasted_iota(jnp.int32, (1, count), 1) + begin
    zero = jnp.zeros((blocks, lanes), jnp.int32)
    last_pos = begin + count - 1

    def one(s, carry):
        start, sentence, first, own_sentence, first_row, last_row, thirds = carry
        size = lengths[0, s]
        end = start + size
        passed = pos >= end
        sentence = sentence + jnp.where(passed, 1, 0)
        first = first + jnp.where(passed, size, 0)
        own_sentence = own_sentence + jnp.where(own_pos >= end, 1, 0)
        first_row = first_row + jnp.where(begin >= end, size, 0)
        last_row = last_row + jnp.where(last_pos >= start, size, 0)
        thirds = tuple(t + jnp.where(begin + LANES * (1 + k) >= end, size, 0) for k, t in enumerate(thirds[:2])) + tuple(
            t + jnp.where(begin + LANES * (1 + k) - 1 >= start, size, 0) for k, t in enumerate(thirds[2:])
        )
        return end, sentence, first, own_sentence, first_row, last_row, thirds

    none = lengths[0, 0] * 0
    carry = (none, zero, zero, jnp.zeros((1, count), jnp.int32), none, none, (none,) * 4)
    _, sentence, first, own_sentence, first_row, last_row, thirds = lax.fori_loop(0, lengths.shape[1], one, carry)
    shown = jnp.where(pos == first, -1.0, blocks_code[0:blocks, :])
    inside = jnp.logical_and(pos >= 0, pos < total_rows)
    blocks_code[0:blocks, :] = jnp.where(inside, (sentence * CODES).astype(F32) + shown, -float(CODES))
    for b in range(0, blocks, 8):
        turned = blocks_code[b : b + 8, :].T
        for j in range(min(8, blocks - b)):
            code[(b + j) * lanes : (b + j + 1) * lanes, :] = turned[:, j : j + 1]
    low[...] = (own_sentence * CODES - 1).astype(F32)
    for j in range(count // lanes):
        some = slice(j * lanes, (j + 1) * lanes)
        high_self[:, some] = (own_sentence[:, some] * CODES + cut[pl.ds(begin // lanes + j, 1), :]).astype(F32)
    high_cross[...] = (own_sentence * CODES + CODES // 2).astype(F32)
    origin = begin - DOC_LEN
    bounds[0, 0] = first_row - origin
    bounds[0, 1] = last_row - origin
    for k, row in enumerate(thirds):
        bounds[0, 2 + k] = row - origin


def start_kernel(
    peers, slices, count, content, encoded, query_state, out_grad, w_query, w_key, w_value, w_out,
    w_cross_query, w_cross_key, w_cross_value, w_cross_out, lengths, score, cut,
    content_window, encoded_window, all_one, all_two, own, own_out_grad, code, low, high_self, high_cross, bounds,
    send, recv, local, zeros, blocks_code,
):
    seq, part = lax.axis_index("seq"), lax.axis_index("head")
    chip, core = seq // 2, lax.rem(seq, 2)
    chips = peers // 2
    sibling = chip * 2 + 1 - core
    rows = content.shape[0]
    span = count + 2 * DOC_LEN
    spare = content_window.shape[0] - span
    copies = Copies(send, recv, local)
    cols = w_query.shape[1]
    for k, (ref, flip) in enumerate(((w_query, True), (w_key, True), (w_value, True))):
        put_rows(all_one, part, k * cols, ref, flip)
    pad_rows(all_one, part, 3 * cols)
    greet(seq, part, peers, slices)
    waits = []
    for source, target in ((query_state, own), (out_grad, own_out_grad)):
        mine = copies.own(source.at[pl.ds(pl.multiple_of(part * count, 16), count)], target)
        mine.start()
        waits.append(mine.wait)

    def halo(source, window):
        for k in range(slices):
            below, above = halo_sizes(k, count, rows)
            low = max(0, k * count - DOC_LEN)
            inner = span - below - above
            mine = copies.own(source.at[pl.ds(low, inner)], window.at[pl.ds(below, inner)])
            tail = copies.own(zeros.at[pl.ds(0, spare)], window.at[pl.ds(span, spare)])
            up = down = fill_low = fill_high = None
            if below:
                up = copies.remote(source.at[pl.ds(rows - below, below)], window.at[pl.ds(0, below)], seq + 1, part)
                fill_low = copies.own(zeros.at[pl.ds(0, below)], window.at[pl.ds(0, below)])
            if above:
                down = copies.remote(source.at[pl.ds(0, above)], window.at[pl.ds(span - above, above)], seq - 1, part)
                fill_high = copies.own(zeros.at[pl.ds(0, above)], window.at[pl.ds(span - above, above)])
            here, first, last = part == k, seq == 0, seq == peers - 1

            def start(mine=mine, tail=tail, up=up, down=down, fill_low=fill_low, fill_high=fill_high, here=here):
                @pl.when(here)
                def _():
                    if up is not None:
                        pl.when(jnp.logical_not(last))(up.start)
                        pl.when(first)(fill_low.start)
                    if down is not None:
                        pl.when(jnp.logical_not(first))(down.start)
                        pl.when(last)(fill_high.start)
                    mine.start()
                    tail.start()

            def finish(mine=mine, tail=tail, up=up, down=down, fill_low=fill_low, fill_high=fill_high, here=here):
                @pl.when(here)
                def _():
                    if up is not None:
                        pl.when(jnp.logical_not(last))(up.wait_send)
                        pl.when(jnp.logical_not(first))(up.wait_recv)
                        pl.when(first)(fill_low.wait)
                    if down is not None:
                        pl.when(jnp.logical_not(first))(down.wait_send)
                        pl.when(jnp.logical_not(last))(down.wait_recv)
                        pl.when(last)(fill_high.wait)
                    mine.wait()
                    tail.wait()

            start()
            waits.append(finish)

    packs = (all_one, all_two)

    def piece(ref, owner, index, size):
        return ref.at[owner, pl.ds(pl.multiple_of(index * size, 16), size)]

    across = {}
    for n, whole in enumerate(packs):
        size = whole.shape[1] // peers
        for d in range(1, slices):
            to = lax.rem(part + d, slices)
            across[n, d] = copies.remote(piece(whole, part, seq, size), piece(whole, part, seq, size), seq, to)
            across[n, d].start()
        if n == 0:
            zeros[...] = jnp.zeros_like(zeros)
            halo(content, content_window)
            put_rows(all_two, part, 0, w_out, False)
            for k, ref in enumerate((w_cross_query, w_cross_key, w_cross_value)):
                put_rows(all_two, part, (1 + k) * cols, ref, True)
            put_rows(all_two, part, 4 * cols, w_cross_out, False)
            pad_rows(all_two, part, 5 * cols)
    find_sentences(seq * rows + part * count, count, peers * rows, lengths, score, cut, code, low, high_self, high_cross, bounds, blocks_code)
    round_plane, to_sibling = {}, {}
    for n, whole in enumerate(packs):
        size = whole.shape[1] // peers
        for d in range(1, slices):
            across[n, d].wait_recv()
            owner = lax.rem(part + slices - d, slices)
            got = piece(whole, owner, seq, size)
            for e in range(1, chips):
                round_plane[n, d, e] = copies.remote(got, got, lax.rem(chip + e, chips) * 2 + core, part)
                round_plane[n, d, e].start()
            to_sibling[n, d, 0] = copies.remote(got, got, sibling, part)
            to_sibling[n, d, 0].start()
    halo(encoded, encoded_window)
    for n, whole in enumerate(packs):
        size = whole.shape[1] // peers
        for d in range(1, slices):
            owner = lax.rem(part + slices - d, slices)
            for e in range(1, chips):
                round_plane[n, d, e].wait_recv()
                got = piece(whole, owner, lax.rem(chip + chips - e, chips) * 2 + core, size)
                to_sibling[n, d, e] = copies.remote(got, got, sibling, part)
                to_sibling[n, d, e].start()
    for copy in to_sibling.values():
        copy.wait_recv()
    for copy in (*across.values(), *round_plane.values(), *to_sibling.values()):
        copy.wait_send()
    for wait in waits:
        wait()


def add_rows(target, source, target_at, source_at, size):
    step = 64 if size % 64 == 0 else 16

    def one(i, carry):
        to = pl.ds(pl.multiple_of(target_at + i * step, 16), step)
        by = pl.ds(pl.multiple_of(source_at + i * step, 16), step)
        target[to, :] = (target[to, :].astype(F32) + source[by, :].astype(F32)).astype(BF16)
        return carry

    lax.fori_loop(0, size // step, one, 0)


def end_kernel(
    peers, slices, count, blocks, parts, packs, plane_sums, outs, part_outs, pack_outs, scratch,
):
    seq, part = lax.axis_index("seq"), lax.axis_index("head")
    chip, core = seq // 2, lax.rem(seq, 2)
    chips = peers // 2
    sibling = chip * 2 + 1 - core
    rows = slices * count
    span = count + 2 * DOC_LEN
    send, recv, local = scratch[:3]
    copies = Copies(send, recv, local)
    first, last = seq == 0, seq == peers - 1
    start_line, end_line = part == 0, part == slices - 1
    greet(seq, part, peers, slices)
    sent = []

    def block(ref, index):
        return ref.at[pl.ds(pl.multiple_of(index * count, 16), count)]

    weight_scratch = scratch[3 : 3 + 3 * len(packs)]
    to_core, held = [], []
    for n, pack in enumerate(packs):
        half = pack.shape[1] // 2
        sibling_sum, mine = weight_scratch[3 * n : 3 * n + 2]
        copy = copies.remote(pack.at[:, pl.ds(pl.multiple_of((1 - core) * half, 16), half)], sibling_sum, sibling, part)
        copy.start()
        to_core.append(copy)
        keep = copies.own(pack.at[:, pl.ds(pl.multiple_of(core * half, 16), half)], mine)
        keep.start()
        held.append(keep)
        sent.append(copy)

    part_scratch = scratch[3 + 3 * len(packs) :]
    halos = []
    for n, grad in enumerate(parts):
        total, from_above, from_below = part_scratch[5 * n : 5 * n + 3]
        for k in range(slices):
            below, above = halo_sizes(k, count, rows)
            low = max(0, k * count - DOC_LEN)
            inner = span - below - above
            mine = copies.own(grad.at[pl.ds(below, inner)], total.at[pl.ds(low, inner)])
            down = up = None
            if below:
                down = copies.remote(grad.at[pl.ds(0, below)], from_above.at[pl.ds(0, below)], seq - 1, part)
            if above:
                up = copies.remote(grad.at[pl.ds(span - above, above)], from_below.at[pl.ds(0, above)], seq + 1, part)
            halos.append((n, k, below, above, low, inner, mine, down, up))

            @pl.when(part == k)
            def _(low=low, inner=inner, mine=mine, down=down, up=up, total=total):
                if down is not None:
                    pl.when(jnp.logical_not(first))(down.start)
                if up is not None:
                    pl.when(jnp.logical_not(last))(up.start)
                mine.start()
                if low:
                    total[0:low, :] = jnp.zeros((low, total.shape[1]), BF16)
                if low + inner < rows:
                    total[low + inner : rows, :] = jnp.zeros((rows - low - inner, total.shape[1]), BF16)

    def finish_halo(which):
        for n, k, below, above, low, inner, mine, down, up in halos:
            if n != which:
                continue
            total, from_above, from_below = part_scratch[5 * n : 5 * n + 3]

            @pl.when(part == k)
            def _(below=below, above=above, mine=mine, down=down, up=up, total=total, from_above=from_above, from_below=from_below):
                mine.wait()
                if down is not None:
                    pl.when(jnp.logical_not(first))(down.wait_send)

                    @pl.when(jnp.logical_not(last))
                    def _():
                        down.wait_recv()
                        add_rows(total, from_above, rows - below, 0, below)

                if up is not None:
                    pl.when(jnp.logical_not(last))(up.wait_send)

                    @pl.when(jnp.logical_not(first))
                    def _():
                        up.wait_recv()
                        add_rows(total, from_below, 0, 0, above)

    halves = 2 if slices <= 4 else 1
    sub = count // halves

    def unit_rows(ref, index, h, size=count, sub=sub):
        return ref.at[pl.ds(index * size + h * sub, sub)]

    def gather_rounds(out, me):
        rounds, flows = {}, ((1, slices - 1 - me), (-1, me))
        for sign, onward in flows:
            behind = me if sign > 0 else slices - 1 - me
            sends, waits = {}, {}
            for k in range(behind + 1):
                for h in range(halves):
                    ref = (me - sign * k, h)
                    if onward:
                        sends[k * halves + h] = ref
                    if k:
                        waits[k * halves + h] = ref
            rounds[sign] = (sends, waits)
        return rounds

    def line_gather(out, me, sems):
        steps, ends = [], []
        ring = gather_rounds(out, me)

        def onward(sign, i):
            ref = unit_rows(out, *ring[sign][0][i])
            return sems(sign, i, ref, ref, sign)

        def step(i):
            for sign in (1, -1):
                sends, waits = ring[sign]
                if i in waits:
                    sems(sign, i - halves, unit_rows(out, *waits[i]), unit_rows(out, *waits[i]), 0).wait_recv()
                if i in sends:
                    if i >= IN_FLIGHT:
                        onward(sign, i - IN_FLIGHT).wait_send()
                    onward(sign, i).start()

        def finish():
            for sign in (1, -1):
                sends, _ = ring[sign]
                for i in sorted(sends)[-IN_FLIGHT:]:
                    onward(sign, i).wait_send()

        return [partial(step, i) for i in range(slices * halves)], finish

    def line_sum(total, ins, out, me, sems, size=count, halves=halves):
        units, sub = (slices - 1) * halves, size // halves
        before = {1: [], -1: []}

        def place(sign, i):
            return slices - 1 - i // halves if sign > 0 else i // halves

        def slot(sign, i):
            return ins[0 if sign > 0 else 1].at[i]

        def onward(sign, i):
            return sems(sign, i, unit_rows(total, place(sign, i), i % halves, size, sub), slot(sign, i), sign)

        def step(r):
            for sign in (1, -1):
                depth = me if sign > 0 else slices - 1 - me
                i = r - depth
                if not 0 <= i < units:
                    continue
                b = place(sign, i)
                passes = b > me if sign > 0 else b < me
                if (passes or b == me) and depth:
                    sems(sign, i, slot(sign, i), slot(sign, i), 0).wait_recv()
                    add_rows(total, slot(sign, i), b * size + (i % halves) * sub, 0, sub)
                if passes:
                    if len(before[sign]) == IN_FLIGHT:
                        onward(sign, before[sign].pop(0)).wait_send()
                    before[sign].append(i)
                    onward(sign, i).start()

        def finish():
            for sign in (1, -1):
                for i in before[sign]:
                    onward(sign, i).wait_send()

        def place_own():
            if out is not None:
                out[pl.ds(me * size, size), :] = total[pl.ds(me * size, size), :]

        return [partial(step, r) for r in range(units + slices - 1)], place_own, finish

    def semaphores(units):
        base = copies.remotes
        copies.remotes += 2 * units

        def make(sign, i, source, target, to):
            k = base + i + (0 if sign > 0 else units)
            return pltpu.make_async_remote_copy(
                src_ref=source, dst_ref=target, send_sem=send.at[k], recv_sem=recv.at[k],
                device_id=(seq, part + to), device_id_type=MESH,
            )

        return make

    def interleave(*lists):
        for k in range(max((len(steps) for steps in lists), default=0)):
            for steps in lists:
                if k < len(steps):
                    steps[k]()

    def at_place(run):
        for me in range(slices):
            pl.when(part == me)(partial(run, me))

    own_copies = []
    for own, out in zip(blocks, outs):
        mine = copies.own(own, block(out, part))
        mine.start()
        own_copies.append(mine)
    plane_total, *plane_ins = part_scratch[5 * len(parts) :]
    pieces = [out.shape[0] // peers for out in pack_outs]
    piece_rows = sum(pieces)
    plane_sems = semaphores(slices)
    block_sems = [semaphores(slices * halves) for _ in outs]
    sum_sems = [semaphores(slices * halves) for _ in part_outs]
    after_sems = [semaphores(slices * halves) for _ in part_outs]

    to_chips = []

    def to_plane():
        for n, pack in enumerate(packs):
            half = pack.shape[1] // 2
            size = half // chips
            sibling_sum, mine, by_chip = weight_scratch[3 * n : 3 * n + 3]
            held[n].wait()
            to_core[n].wait_recv()

            def add_half(z, carry, sibling_sum=sibling_sum, mine=mine, half=half):
                add_rows(mine.at[z], sibling_sum.at[z], 0, 0, half)
                return carry

            lax.fori_loop(0, slices, add_half, 0)
            for e in range(1, chips):
                to = lax.rem(chip + e, chips)
                copy = copies.remote(mine.at[:, pl.ds(pl.multiple_of(to * size, 16), size)], by_chip.at[e - 1], to * 2 + core, part)
                copy.start()
                to_chips.append((n, e, copy))
                sent.append(copy)

    length = slices * halves
    plans = []
    for me in range(slices):
        gathers = [line_gather(out, me, sems) for out, sems in zip(outs, block_sems)]
        sums, afters = [], []
        for n, out in enumerate(part_outs):
            total, _, _, right_in, left_in = part_scratch[5 * n : 5 * n + 5]
            sums.append(line_sum(total, (right_in, left_in), out, me, sum_sems[n]))
            afters.append(line_gather(out, me, after_sems[n]))
        owned = [line_sum(plane_total, plane_ins, None, me, plane_sems, piece_rows, 1)]
        plans.append((gathers, sums, afters, owned))

    def rounds(me, *which):
        lists, ends = [], []
        for kind, n, low, high in which:
            entry = plans[me][kind][n]
            steps = entry[0]
            lists.append(steps[low:high])
            if low < len(steps) <= high:
                ends += list(entry[1:])
        interleave(*lists)
        for finish in ends:
            finish()

    def run(*which):
        at_place(lambda me: rounds(me, *which))

    def to_owners():
        for n, pack in enumerate(packs):
            half = pack.shape[1] // 2
            size, first_row = half // chips, sum(pieces[:n])
            mine, by_chip = weight_scratch[3 * n + 1 : 3 * n + 3]
            for m, e, copy in to_chips:
                if m == n:
                    copy.wait_recv()

            def add_plane(i, carry, mine=mine, by_chip=by_chip, size=size, first_row=first_row):
                z, r = i // (size // 16), lax.rem(i, size // 16)
                at = pl.ds(pl.multiple_of(r * 16, 16), 16)
                value = mine[z, pl.ds(pl.multiple_of(chip * size + r * 16, 16), 16), :].astype(F32)
                for e in range(chips - 1):
                    value = value + by_chip[e, z, at, :].astype(F32)
                plane_total[pl.ds(pl.multiple_of(z * piece_rows + first_row + r * 16, 16), 16), :] = value.astype(BF16)
                return carry

            lax.fori_loop(0, slices * (size // 16), add_plane, 0)

    def piece_at(n, of_chip, of_core):
        size = pack_outs[n].shape[0] // peers
        index = of_core * chips + of_chip if n < len(packs) else of_chip * 2 + of_core
        return pl.multiple_of(index * size, 16), size

    round_plane, to_sibling = [], []

    def back_to_plane():
        for n, out in enumerate(pack_outs):
            start, size = piece_at(n, chip, core)

            def keep(r, carry, out=out, start=start, first_row=sum(pieces[:n])):
                at = pl.ds(pl.multiple_of(part * piece_rows + first_row + r * 16, 16), 16)
                out[pl.ds(pl.multiple_of(start + r * 16, 16), 16), :] = plane_total[at, :]
                return carry

            lax.fori_loop(0, size // 16, keep, 0)
            piece = out.at[pl.ds(start, size)]
            for e in range(1, chips):
                copy = copies.remote(piece, piece, lax.rem(chip + e, chips) * 2 + core, part)
                copy.start()
                round_plane.append((n, e, copy))
                sent.append(copy)
            copy = copies.remote(piece, piece, sibling, part)
            copy.start()
            round_plane.append((n, 0, copy))
            sent.append(copy)

    sum_length = (slices - 1) * halves + slices - 1
    plane_copies = []
    for n, summed in enumerate(plane_sums):
        first_row, size = sum(pieces[: len(packs) + n]), pieces[len(packs) + n]
        for z in range(slices):
            plane_copies.append(copies.own(summed.at[z], plane_total.at[pl.ds(z * piece_rows + first_row, size)]))
    for keep in plane_copies:
        keep.start()
    for mine in own_copies:
        mine.wait()
    run((0, 0, 0, 2))
    finish_halo(0)
    run((0, 0, 2, 4), (1, 0, 0, 2))
    to_plane()
    run((0, 0, 4, length), (1, 0, 2, sum_length))
    for keep in plane_copies:
        keep.wait()
    if len(parts) > 1:
        finish_halo(1)
        run((1, 1, 0, 3), (2, 0, 0, 3))
        to_owners()
        run((1, 1, 3, sum_length), (2, 0, 3, length), (3, 0, 0, 5))
    else:
        to_owners()
        run((3, 0, 0, 4))
    last = len(parts) - 1
    run((3, 0, 5, 2 * (slices - 1)), (2, last, 0, 2))
    back_to_plane()
    run((2, last, 2, length))
    for n, e, copy in round_plane:
        copy.wait_recv()
        if e:
            start, size = piece_at(n, lax.rem(chip + chips - e, chips), core)
            piece = pack_outs[n].at[pl.ds(start, size)]
            copy = copies.remote(piece, piece, sibling, part)
            copy.start()
            to_sibling.append(copy)
            sent.append(copy)
    for copy in to_sibling:
        copy.wait_recv()
    for copy in sent:
        copy.wait_send()


class Rows:
    def __init__(self, pack, index, size):
        self.pack, self.at = pack, slice(index * size, (index + 1) * size)

    def __getitem__(self, _):
        value = self.pack[:, self.at, :]
        return value.reshape(value.shape[0] * value.shape[1], value.shape[2])


def write_rows(pack, index, size, value):
    slices = pack.shape[0]
    pack[:, index * size : (index + 1) * size, :] = value.astype(BF16).reshape(slices, size, value.shape[1])


def mask_bias(code, low, high):
    return jnp.where((code >= low) & (code < high), 0.0, NEG_BIG).astype(F32)


def pair_product(left, spread, p, see):
    count = see.size
    blocks = [spread[h * PAIR : (h + 1) * PAIR, see] for h in (2 * p, 2 * p + 1)]
    if count % LANES:
        return [dot_nn(left, block) for block in blocks]
    both = dot_nn(left, jnp.concatenate(blocks, axis=1))
    return both[:, :count], both[:, count:]


def attend(window, code, low, high, w_key_t, w_value_t, spread, bias, top, total, out):
    top[...] = jnp.full_like(top, NEG_BIG)
    total[...] = jnp.zeros_like(total)
    out[...] = jnp.zeros_like(out)

    def step(c, see):
        at = chunk_rows(window.start, c)
        rows = window.held[at, :]
        keys = dot_nt(rows, w_key_t[...]).astype(BF16)
        values_t = dot_nt(rows, w_value_t[...]).astype(BF16).T
        bias[:, see] = mask_bias(code[at, :], low[:, see], high[:, see])
        for h in range(HEADS):
            p = h // 2
            if h % 2 == 0:
                both = pair_product(keys[:, p * PAIR : (p + 1) * PAIR], spread, p, see)
            scores = both[h % 2] * SCORE_SCALE + bias[:, see]
            before = top[h : h + 1, see]
            now = jnp.maximum(before, jnp.max(scores, axis=0, keepdims=True))
            weights = jnp.exp2(scores - now)
            shrink = jnp.exp2(before - now)
            top[h : h + 1, see] = now
            total[h : h + 1, see] = total[h : h + 1, see] * shrink + jnp.sum(weights, axis=0, keepdims=True)
            head = slice(h * HEAD_SIZE, (h + 1) * HEAD_SIZE)
            out[head, see] = out[head, see] * shrink + dot_nn(values_t[head, :], weights.astype(BF16))

    window.loops(out.shape[1], step)
    for h in range(HEADS):
        head = slice(h * HEAD_SIZE, (h + 1) * HEAD_SIZE)
        out[head, :] = out[head, :] / total[h : h + 1, :]


def attend_back(
    window, code, low, high, w_key_t, w_value_t, spread, grad_spread, pairs, grad_pairs, lse, delta, bias,
    query_grad, window_grad, w_key_grad, w_value_grad,
):
    count = spread.shape[1]
    query_grad[...] = jnp.zeros_like(query_grad)
    w_key_grad[...] = jnp.zeros_like(w_key_grad)
    w_value_grad[...] = jnp.zeros_like(w_value_grad)
    window_grad[...] = jnp.zeros_like(window_grad)

    def step(c, see):
        at = chunk_rows(window.start, c)
        seen = (see, pl.ds(count + see.start, see.size) if isinstance(see.start, int) else pl.ds(pl.multiple_of(count + see.start, LANES), see.size))
        rows = window.held[at, :]
        keys = dot_nt(rows, w_key_t[...]).astype(BF16)
        keys_t = keys.T
        values = dot_nt(rows, w_value_t[...]).astype(BF16)
        bias[:, see] = mask_bias(code[at, :], low[:, see], high[:, see])
        key_grads, value_grads = [], []
        for p in range(PAIRS):
            columns = slice(p * PAIR, (p + 1) * PAIR)
            probs, score_grads = [], []
            both_scores = pair_product(keys[:, columns], spread, p, see)
            both_dprobs = pair_product(values[:, columns], grad_spread, p, see)
            for h in (2 * p, 2 * p + 1):
                head = slice(h * HEAD_SIZE, (h + 1) * HEAD_SIZE)
                prob = jnp.exp2(both_scores[h % 2] * SCORE_SCALE + bias[:, see] - lse[h : h + 1, see])
                score_grad = (prob * (both_dprobs[h % 2] - delta[h : h + 1, see])).astype(BF16)
                query_grad[head, see] += dot_nn(keys_t[head, :], score_grad)
                probs.append(prob.astype(BF16))
                score_grads.append(score_grad)
            if count % LANES == 0:
                both = jnp.concatenate([pairs[p, r, :] for r in seen], axis=0)
                grad_both = jnp.concatenate([grad_pairs[p, r, :] for r in seen], axis=0)
                key_grads.append(dot_nn(jnp.concatenate(score_grads, axis=1), both))
                value_grads.append(dot_nn(jnp.concatenate(probs, axis=1), grad_both))
            else:
                key_grads.append(sum(dot_nn(x, pairs[p, r, :]) for x, r in zip(score_grads, seen)))
                value_grads.append(sum(dot_nn(x, grad_pairs[p, r, :]) for x, r in zip(probs, seen)))
        keys_low = (jnp.concatenate(key_grads, axis=1) * SCALE).astype(BF16)
        values_low = jnp.concatenate(value_grads, axis=1).astype(BF16)
        window_grad[at, :] = (dot_nn(keys_low, w_key_t[...]) + dot_nn(values_low, w_value_t[...])).astype(window_grad.dtype)
        w_key_grad[...] += dot_tn(rows, keys_low)
        w_value_grad[...] += dot_tn(rows, values_low)

    window.loops(count, step)


def forward_kernel(
    cols, bounds, own, content_window, encoded_window, gain, code, low, high_self, high_cross, pack_one, pack_two_in,
    self_t, lse_self, hidden, cross_t, lse_cross,
    spread, bias, top, total, low_t, content_held, encoded_held, pack_two, content_sems, encoded_sems, pack_sem,
):
    content = Window(bounds, content_window, content_held, content_sems)
    encoded = Window(bounds, encoded_window, encoded_held, encoded_sems)
    content.fetch()
    whole_pack = pltpu.make_async_copy(pack_two_in, pack_two, pack_sem.at[0])
    whole_pack.start()
    encoded.fetch()
    w_query_t, w_key_t, w_value_t = (Rows(pack_one, k, cols) for k in range(3))
    low_t[...] = dot_nt(w_query_t[...], own[...]).astype(BF16)
    spread_heads(low_t, spread)
    attend(content, code, low, high_self, w_key_t, w_value_t, spread, bias, top, total, self_t)
    lse_self[...] = top[...] + jnp.log2(total[...])
    whole_pack.wait()
    w_out, w_query_t, w_key_t, w_value_t = (Rows(pack_two, k, cols) for k in range(4))
    branch = dot_tn(self_t[...].astype(BF16), w_out[...])
    normed, _ = layer_norm(own[...].astype(F32) + branch)
    hidden[...] = normed * gain[...]
    low_t[...] = dot_nt(w_query_t[...], hidden[...].astype(BF16)).astype(BF16)
    spread_heads(low_t, spread)
    attend(encoded, code, low, high_cross, w_key_t, w_value_t, spread, bias, top, total, cross_t)
    lse_cross[...] = top[...] + jnp.log2(total[...])


def ffn_kernel(
    cols, hidden_one, cross_t, pack_two, gain_cross, pack_three_in, gain_final, out_grad,
    mixed, resid_grad, w_out_grad, grad_three_out, gain_cross_grad, gain_final_grad,
    normed_two, hidden_two_low, slope, active, sum_ffn, pack_out, pack_three, grad_three_pack, sems, out_sems,
):
    slices, units = pack_three.shape[0], active.shape[2]
    if grad_three_pack.shape[1] > 2 * units:
        grad_three_pack[:, 2 * units :, :] = jnp.zeros((slices, grad_three_pack.shape[1] - 2 * units, grad_three_pack.shape[2]), BF16)
    out_copy = pltpu.make_async_copy(pack_two.at[:, pl.ds(4 * cols, cols)], pack_out, sems.at[slices])
    out_copy.start()
    slice_copies = [pltpu.make_async_copy(pack_three_in.at[z], pack_three.at[z], sems.at[z]) for z in range(slices)]
    for copy in slice_copies:
        copy.start()
    out_copy.wait()
    w_out = Rows(pack_out, 0, cols)
    cross_low = cross_t[...].astype(BF16)
    normed, scale_two = layer_norm(hidden_one[...] + dot_tn(cross_low, w_out[...]))
    normed_two[...] = normed
    hidden_two = normed * gain_cross[...]
    hidden_two_low[...] = hidden_two.astype(BF16)
    sum_ffn[...] = hidden_two
    for z in range(slices):
        slice_copies[z].wait()
        inner = dot_nt(hidden_two_low[...], pack_three[z, 0:units, :])
        below = 0.5 * (1.0 + lax.erf(inner * math.sqrt(0.5)))
        slope[z] = below + inner * (jnp.exp2(inner * inner * (-0.5 * LOG2E)) * (1.0 / math.sqrt(2.0 * math.pi)))
        active[z] = (inner * below).astype(BF16)
        sum_ffn[...] += dot_nn(active[z], pack_three[z, units : 2 * units, :])
    normed_three, scale_three = layer_norm(sum_ffn[...])
    mixed[...] = (normed_three * gain_final[...]).astype(BF16)
    grad_three, gain_grad = norm_back(out_grad[...].astype(F32), normed_three, scale_three, gain_final[...])
    gain_final_grad[...] = gain_grad
    ffn_low = grad_three.astype(BF16)
    result_copies = [pltpu.make_async_copy(grad_three_pack.at[z], grad_three_out.at[z], out_sems.at[z]) for z in range(slices)]
    sum_ffn[...] = grad_three
    for z in range(slices):
        grad_three_pack[z, units : 2 * units, :] = dot_tn(active[z], ffn_low).astype(BF16)
        inner_low = (dot_nt(ffn_low, pack_three[z, units : 2 * units, :]) * slope[z]).astype(BF16)
        grad_three_pack[z, 0:units, :] = dot_tn(inner_low, hidden_two_low[...]).astype(BF16)
        sum_ffn[...] += dot_nn(inner_low, pack_three[z, 0:units, :])
        result_copies[z].start()
    grad, gain_grad = norm_back(sum_ffn[...], normed_two[...], scale_two, gain_cross[...])
    gain_cross_grad[...] = gain_grad
    resid_grad[...] = grad
    w_out_grad[...] = dot_nn(cross_low, grad.astype(BF16)).astype(BF16)
    for copy in result_copies:
        copy.wait()


def prepare_back(query, query_t, grad, grad_t, out, spread, grad_spread, pairs, grad_pairs, delta, low_t):
    low_t[...] = query_t.astype(BF16)
    spread_heads(low_t, spread)
    for p in range(PAIRS):
        pair_rows(query.astype(BF16), p, pairs)
        pair_rows(grad.astype(BF16), p, grad_pairs)
    low_t[...] = grad_t.astype(BF16)
    spread_heads(low_t, grad_spread)
    for h in range(HEADS):
        head = slice(h * HEAD_SIZE, (h + 1) * HEAD_SIZE)
        delta[h : h + 1, :] = jnp.sum(low_t[head, :].astype(F32) * out[head, :], axis=0, keepdims=True)


def cross_back_kernel(
    cols, bounds, own, self_t, gain, resid_two_grad, cross_t, lse, window_in, code, low, high, pack_two,
    w_cross_out_grad, gain_cross_grad, gain_final_grad, resid_one_grad, window_out, grad_two_pack,
    spread, grad_spread, pairs, grad_pairs, delta, bias, low_t, query_grad, key_sum, value_sum, held, window_grad, sems, out_sem,
    normed_one, scale_one, after,
):
    window = Window(bounds, window_in, held, sems)
    window.fetch()
    after.fetch()
    w_out, w_query_t, w_key_t, w_value_t, w_cross_out = (Rows(pack_two, k, cols) for k in range(5))
    self_low = self_t[...].astype(BF16)
    normed, scale = layer_norm(own[...].astype(F32) + dot_tn(self_low, w_out[...]))
    normed_one[...] = normed
    scale_one[...] = scale
    hidden_low = (normed * gain[...]).astype(BF16)
    branch_low = resid_two_grad[...].astype(BF16)
    prepare_back(
        dot_nt(hidden_low, w_query_t[...]), dot_nt(w_query_t[...], hidden_low),
        dot_nt(branch_low, w_cross_out[...]), dot_nt(w_cross_out[...], branch_low),
        cross_t, spread, grad_spread, pairs, grad_pairs, delta, low_t,
    )
    attend_back(
        window, code, low, high, w_key_t, w_value_t, spread, grad_spread, pairs, grad_pairs, lse, delta, bias,
        query_grad, window_grad, key_sum, value_sum,
    )
    result = pltpu.make_async_copy(window_grad, window_out, out_sem.at[0])
    result.start()
    query_low = (query_grad[...] * SCALE).astype(BF16)
    hidden_low = (normed_one[...] * gain[...]).astype(BF16)
    grad_one = resid_two_grad[...] + dot_tn(query_low, w_query_t[...])
    grad, gain_sum = norm_back(grad_one, normed_one[...], scale_one[...], gain[...])
    resid_one_grad[...] = grad
    write_rows(grad_two_pack, 0, cols, dot_nn(self_t[...].astype(BF16), grad.astype(BF16)))
    write_rows(grad_two_pack, 1, cols, dot_nn(query_low, hidden_low))
    write_rows(grad_two_pack, 2, cols, key_sum[...].T)
    write_rows(grad_two_pack, 3, cols, value_sum[...].T)
    write_rows(grad_two_pack, 4, cols, w_cross_out_grad[...])
    slices, rows, width = grad_two_pack.shape
    gains = jnp.concatenate([gain_sum, gain_cross_grad[...], gain_final_grad[...], jnp.zeros((13, width), F32)], axis=0)
    for z in range(slices):
        grad_two_pack[z, 5 * cols : 5 * cols + 16, :] = gains.astype(BF16)
        if rows > 5 * cols + 16:
            grad_two_pack[z, 5 * cols + 16 :, :] = jnp.zeros((rows - 5 * cols - 16, width), BF16)
    result.wait()


def self_back_kernel(
    cols, own, resid_one_grad, pack_two, self_t, lse, window, code, low, high, pack_one,
    own_grad, window_out, grad_one_pack,
    spread, grad_spread, pairs, grad_pairs, delta, bias, low_t, query_grad, key_sum, value_sum, window_grad, out_sem,
):
    w_query_t, w_key_t, w_value_t = (Rows(pack_one, k, cols) for k in range(3))
    w_out = Rows(pack_two, 0, cols)
    branch_low = resid_one_grad[...].astype(BF16)
    prepare_back(
        dot_nt(own[...], w_query_t[...]), dot_nt(w_query_t[...], own[...]),
        dot_nt(branch_low, w_out[...]), dot_nt(w_out[...], branch_low),
        self_t, spread, grad_spread, pairs, grad_pairs, delta, low_t,
    )
    attend_back(
        window, code, low, high, w_key_t, w_value_t, spread, grad_spread, pairs, grad_pairs, lse, delta, bias,
        query_grad, window_grad, key_sum, value_sum,
    )
    result = pltpu.make_async_copy(window_grad, window_out, out_sem.at[0])
    result.start()
    query_low = (query_grad[...] * SCALE).astype(BF16)
    write_rows(grad_one_pack, 0, cols, dot_nn(query_low, own[...]))
    write_rows(grad_one_pack, 1, cols, key_sum[...].T)
    write_rows(grad_one_pack, 2, cols, value_sum[...].T)
    slices, rows, width = grad_one_pack.shape
    if rows > 3 * cols:
        grad_one_pack[:, 3 * cols :, :] = jnp.zeros((slices, rows - 3 * cols, width), BF16)
    own_grad[...] = (resid_one_grad[...] + dot_tn(query_low, w_query_t[...])).astype(BF16)
    result.wait()


def back_kernel(
    cols, bounds, own, self_t, gain, resid_two_grad, cross_t, lse_cross, encoded_window, code, low, high_cross, pack_two,
    w_cross_out_grad, gain_cross_grad, gain_final_grad, lse_self, content_window, high_self, pack_one,
    encoded_part, grad_two_pack, own_grad, content_part, grad_one_pack,
    spread, grad_spread, pairs, grad_pairs, delta, bias, low_t, query_grad, key_sum, value_sum,
    encoded_held, encoded_grad, content_held, content_grad, encoded_sems, content_sems, out_sems,
    normed_one, scale_one, resid_one_grad,
):
    shared = (spread, grad_spread, pairs, grad_pairs, delta, bias, low_t, query_grad, key_sum, value_sum)
    content = Window(bounds, content_window, content_held, content_sems)
    cross_back_kernel(
        cols, bounds, own, self_t, gain, resid_two_grad, cross_t, lse_cross, encoded_window, code, low, high_cross, pack_two,
        w_cross_out_grad, gain_cross_grad, gain_final_grad, resid_one_grad, encoded_part, grad_two_pack,
        *shared, encoded_held, encoded_grad, encoded_sems, out_sems.at[pl.ds(0, 1)], normed_one, scale_one, content,
    )
    self_back_kernel(
        cols, own, resid_one_grad, pack_two, self_t, lse_self, content, code, low, high_self, pack_one,
        own_grad, content_part, grad_one_pack, *shared, content_grad, out_sems.at[pl.ds(1, 1)],
    )


def finish_kernel(cols, units, slices, *refs):
    rows_in, (sum_one, sum_two, sum_three), outs = refs[:4], refs[4:7], refs[7:]
    step = pl.program_id(0)
    for source, target in zip(rows_in, outs[:4]):
        target[...] = source[...].astype(target.dtype)

    def weights(k):
        w_query, w_key, w_value, w_out, w_cross_query, w_cross_key, w_cross_value, w_cross_out, w_inner, w_outer = outs[4:14]
        width = sum_one.shape[1]
        wide, tall, unit_rows = width // slices, cols // slices, units // slices
        some = slice(k * wide, (k + 1) * wide)
        for n, target in enumerate((w_query, w_key, w_value)):
            target[...] = sum_one[n * cols : (n + 1) * cols, some].astype(F32).T
        for n, target in enumerate((w_cross_query, w_cross_key, w_cross_value)):
            target[...] = sum_two[(1 + n) * cols : (2 + n) * cols, some].astype(F32).T
        w_out[...] = sum_two[k * tall : (k + 1) * tall, :].astype(F32)
        w_cross_out[...] = sum_two[4 * cols + k * tall : 4 * cols + (k + 1) * tall, :].astype(F32)
        w_inner[...] = sum_three[0:units, some].astype(F32).T
        w_outer[...] = sum_three[units + k * unit_rows : units + (k + 1) * unit_rows, :].astype(F32)

    for k in range(slices):
        pl.when(step == k)(partial(weights, k))

    @pl.when(step == 0)
    def _():
        gains = sum_two[5 * cols : 5 * cols + 16, :].astype(F32)
        for k, target in enumerate(outs[14:17]):
            target[...] = gains[k : k + 1, :]


def call(kernel, outs, scratch, smem, *args, far=(), far_outs=(), micros=20):
    def space(k, left, scalars):
        return pl.ANY if k in left else pltpu.SMEM if k < scalars else pltpu.VMEM

    return pl.pallas_call(
        kernel,
        out_shape=[jax.ShapeDtypeStruct(shape, kind) for shape, kind in outs],
        in_specs=[pl.BlockSpec(memory_space=space(k, far, smem)) for k in range(len(args))],
        out_specs=[pl.BlockSpec(memory_space=space(k, far_outs, 0)) for k in range(len(outs))],
        scratch_shapes=[pltpu.SemaphoreType.DMA((shape,)) if kind is None else pltpu.VMEM(shape, kind) for shape, kind in scratch],
        compiler_params=pltpu.CompilerParams(vmem_limit_bytes=VMEM_LIMIT),
        cost_estimate=pl.CostEstimate(flops=micros * 10**9, bytes_accessed=micros * 10**6, transcendentals=0),
    )(*args)


def padded(size, unit):
    return -(-size // unit) * unit


def talk(kernel, outs, out_spaces, scratch, copies, number, spaces, *args):
    return pl.pallas_call(
        kernel,
        out_shape=[jax.ShapeDtypeStruct(shape, kind) for shape, kind in outs],
        in_specs=[pl.BlockSpec(memory_space=space) for space in spaces],
        out_specs=[pl.BlockSpec(memory_space=space) for space in out_spaces],
        scratch_shapes=[pltpu.SemaphoreType.DMA((n,)) for n in (copies[0], copies[0], copies[1])] + [pltpu.VMEM(shape, kind) for shape, kind in scratch],
        compiler_params=pltpu.CompilerParams(vmem_limit_bytes=VMEM_LIMIT, collective_id=number, has_side_effects=True),
        cost_estimate=pl.CostEstimate(flops=80 * 10**9, bytes_accessed=80 * 10**6, transcendentals=0),
    )(*args)


def body(
    query_state, content, encoded, sentence_lengths, key_score, query_cut, w_query, w_key, w_value, w_out, gain_self,
    w_cross_query, w_cross_key, w_cross_value, w_cross_out, gain_cross, w_inner, w_outer, gain_final, out_grad,
):
    rows, width = query_state.shape
    slices = lax.axis_size("head")
    count = rows // slices
    lanes = math.gcd(count, LANES)
    wide = padded(count + 2 * DOC_LEN + CHUNK, lanes)
    spare = wide - count - 2 * DOC_LEN
    seq, part = lax.axis_index("seq"), lax.axis_index("head")
    begin = seq * rows + part * count
    score, cut = key_score.reshape(-1, lanes), query_cut.reshape(-1, lanes)
    gain_self, gain_cross, gain_final = (g.reshape(1, width) for g in (gain_self, gain_cross, gain_final))

    peers = lax.axis_size("seq")
    chips = peers // 2
    cols, units = w_query.shape[1], w_inner.shape[1]
    unit = 16 * peers
    sizes = [padded(n, unit) for n in (3 * cols, 5 * cols, 2 * units)]
    grad_sizes = [sizes[0], padded(5 * cols + 16, unit), sizes[2]]

    share = sizes[2] // peers
    slice_three = jnp.concatenate([w_inner.T, w_outer, jnp.zeros((sizes[2] - 2 * units, width), BF16)], axis=0)
    share_three = lax.dynamic_slice_in_dim(slice_three, seq * share, share, 0)
    pack_three = lax.all_gather(share_three, ("head", "seq"), axis=0, tiled=True).reshape(slices, sizes[2], width)
    start_copies = 2 * (slices - 1) * (2 * chips) + 4 * slices
    hbm, vmem, smem = pl.ANY, pltpu.VMEM, pltpu.SMEM
    (
        content_window, encoded_window, pack_one, pack_two, own, own_out_grad, code, low, high_self, high_cross, bounds,
    ) = talk(
        partial(start_kernel, peers, slices, count),
        [((wide, width), BF16)] * 2 + [((slices, n, width), BF16) for n in sizes[:2]] + [((count, width), BF16)] * 2
        + [((wide, 1), F32)] + [((1, count), F32)] * 3 + [((1, 6), jnp.int32)],
        [vmem] * 10 + [smem],
        [((DOC_LEN, width), BF16), ((padded(wide // lanes, 8), lanes), F32)], (start_copies, 8 * slices + 16), 0,
        [hbm] * 4 + [vmem] * 8 + [smem] + [vmem] * 2,
        content, encoded, query_state, out_grad, w_query, w_key, w_value, w_out,
        w_cross_query, w_cross_key, w_cross_value, w_cross_out, sentence_lengths.reshape(1, -1), score, cut,
    )

    def split_refs(kernel, ins, outs):
        def run(*refs):
            return kernel(refs[:ins], refs[ins : ins + outs], refs[ins + outs :])
        return run

    touched = -(-wide // CHUNK)
    window_held = [((wide, width), BF16)]
    self_t, lse_self, hidden_one, cross_t, lse_cross = call(
        partial(forward_kernel, cols),
        [((width, count), F32), ((HEADS, count), F32), ((count, width), F32), ((width, count), F32), ((HEADS, count), F32)],
        [((HEADS * PAIR, count), BF16), ((CHUNK, count), F32), ((HEADS, count), F32), ((HEADS, count), F32), ((width, count), BF16)]
        + window_held * 2 + [((slices, sizes[1], width), BF16), (touched, None), (touched, None), (1, None)], 1,
        bounds, own, content_window, encoded_window, gain_self, code, low, high_self, high_cross, pack_one, pack_two, far=(2, 3, 10),
    )
    mixed, resid_two_grad, w_cross_out_grad, grads_three, gain_cross_grad, gain_final_grad = call(
        partial(ffn_kernel, cols),
        [
            ((count, width), BF16), ((count, width), F32), ((width, width), BF16), ((slices, grad_sizes[2], width), BF16),
            ((1, width), F32), ((1, width), F32),
        ],
        [
            ((count, width), F32), ((count, width), BF16), ((slices, count, units), F32),
            ((slices, count, units), BF16), ((count, width), F32), ((slices, cols, width), BF16), ((slices, sizes[2], width), BF16),
            ((slices, grad_sizes[2], width), BF16), (slices + 1, None), (slices, None),
        ], 0,
        hidden_one, cross_t, pack_two, gain_cross, pack_three, gain_final, own_out_grad, far=(2, 4), far_outs=(3,),
    )
    back = [
        ((HEADS * PAIR, count), BF16), ((HEADS * PAIR, count), BF16), ((PAIRS, 2 * count, PAIR), BF16),
        ((PAIRS, 2 * count, PAIR), BF16), ((HEADS, count), F32), ((CHUNK, count), F32), ((width, count), BF16),
        ((width, count), F32), ((width, width), F32), ((width, width), F32),
    ] + window_held * 4
    mixed = lax.all_gather(mixed, "head", axis=0, tiled=True)
    encoded_part, grads_two, own_grad, content_part, grads_one = call(
        partial(back_kernel, cols),
        [
            ((wide, width), BF16), ((slices, grad_sizes[1], width), BF16), ((count, width), BF16), ((wide, width), BF16),
            ((slices, grad_sizes[0], width), BF16),
        ],
        back + [(touched, None), (touched, None), (2, None), ((count, width), F32), ((count, 1), F32), ((count, width), F32)], 1,
        bounds, own, self_t, gain_self, resid_two_grad, cross_t, lse_cross, encoded_window, code, low, high_cross, pack_two,
        w_cross_out_grad, gain_cross_grad, gain_final_grad, lse_self, content_window, high_self, pack_one,
        far=(7, 16), far_outs=(0, 3), micros=8,
    )

    blocks, parts, grads, planes = [own_grad], [content_part, encoded_part], [grads_one, grads_two, grads_three], []
    weight_scratch = []
    for n in grad_sizes[: len(grads)]:
        half, size = n // 2, n // 2 // chips
        weight_scratch += [
            ((slices, half, width), BF16), ((slices, half, width), BF16), ((chips - 1, slices, size, width), BF16),
        ]
    halves = 2 if slices <= 4 else 1
    units_in = (slices - 1) * halves
    part_scratch = [
        ((rows, width), BF16), ((DOC_LEN, width), BF16), ((DOC_LEN, width), BF16),
        ((units_in, count // halves, width), BF16), ((units_in, count // halves, width), BF16),
    ] * len(parts)
    piece_rows = sum(grad_sizes) // peers
    plane_scratch = [((slices * piece_rows, width), BF16)] + [((slices - 1, piece_rows, width), BF16)] * 2
    ins, outs = (len(blocks), len(parts), len(grads), len(planes)), (len(blocks), len(parts), len(grad_sizes))

    def end(refs, out_refs, scratch):
        a, b, c = ins[0], ins[0] + ins[1], sum(ins[:3])
        end_kernel(
            peers, slices, count, refs[:a], refs[a:b], refs[b:c], refs[c:], out_refs[: outs[0]],
            out_refs[outs[0] : outs[0] + outs[1]], out_refs[outs[0] + outs[1] :], scratch,
        )

    end_copies = len(grad_sizes) * (1 + 3 * (chips - 1) + slices) + 2 * slices + len(parts) * 2 * slices + (len(blocks) + 2 * len(parts)) * 2 * slices * halves
    results = talk(
        split_refs(end, sum(ins), sum(outs)),
        [((rows, width), BF16)] * (len(blocks) + len(parts)) + [((n, width), BF16) for n in grad_sizes], [vmem] * sum(outs),
        weight_scratch + part_scratch + plane_scratch, (end_copies, 8 * slices + 8), 1, [hbm] * sum(ins), *blocks, *parts, *grads, *planes,
    )
    query_state_grad, content_grad, encoded_grad, sum_one, sum_two, sum_three = results

    square, tall = ((width, cols), F32), ((cols, width), F32)
    finals = [((rows, width), BF16)] + [((rows, width), F32)] * 3 + [square] * 3 + [tall, square, square, square, tall]
    finals += [((width, units), F32), ((units, width), F32)] + [((1, width), F32)] * 3
    by_rows = pl.BlockSpec((count, width), lambda i: (i, 0))

    def whole(shape):
        return pl.BlockSpec(shape, lambda i: (0,) * len(shape))

    def by_step(shape):
        return pl.BlockSpec((shape[0] // slices, shape[1]), lambda i: (i, 0))

    sums = [sum_one, sum_two, sum_three]
    results = pl.pallas_call(
        partial(finish_kernel, cols, units, slices),
        grid=(slices,),
        out_shape=[jax.ShapeDtypeStruct(shape, kind) for shape, kind in finals],
        in_specs=[by_rows] * 4 + [whole(x.shape) for x in sums],
        out_specs=[by_rows] * 4 + [by_step(shape) for shape, _ in finals[4:14]] + [whole(shape) for shape, _ in finals[14:]],
        compiler_params=pltpu.CompilerParams(vmem_limit_bytes=VMEM_LIMIT),
    )(mixed, query_state_grad, content_grad, encoded_grad, *sums)
    (
        mixed, query_state_grad, content_grad, encoded_grad, w_query_grad, w_key_grad, w_value_grad, w_out_grad,
        w_cross_query_grad, w_cross_key_grad, w_cross_value_grad, w_cross_out_grad, w_inner_grad, w_outer_grad, *gains,
    ) = results
    gains = [g.reshape(width) for g in gains]
    return (
        mixed, query_state_grad, content_grad, encoded_grad, w_query_grad, w_key_grad, w_value_grad, w_out_grad, gains[0],
        w_cross_query_grad, w_cross_key_grad, w_cross_value_grad, w_cross_out_grad, gains[1], w_inner_grad, w_outer_grad, gains[2],
    )


def solution(mesh):
    rows, whole, columns, split = P("seq", None), P(), P(None, "head"), P("head", None)
    in_specs = (
        rows, rows, rows, whole, whole, whole, columns, columns, columns, split, whole,
        columns, columns, columns, split, whole, columns, split, whole, rows,
    )
    out_specs = (
        rows, rows, rows, rows, columns, columns, columns, split, whole,
        columns, columns, columns, split, whole, columns, split, whole,
    )
    return jax.shard_map(body, mesh=mesh, in_specs=in_specs, out_specs=out_specs, check_vma=False)
```

```python
from functools import partial
import math

import jax
import jax.numpy as jnp
from jax import lax
from jax.experimental import pallas as pl
from jax.experimental.pallas import tpu as pltpu
from jax.sharding import PartitionSpec as P

HEADS = 8
HEAD_SIZE = 64
PAIR = 2 * HEAD_SIZE
PAIRS = HEADS // 2
DOC_LEN = 1024
CHUNK = 528
LANES = 128
IN_FLIGHT = 2
EPS = 1e-05
NEG_BIG = -1e30
LOG2E = 1.4426950408889634
SCALE = 1.0 / math.sqrt(HEAD_SIZE)
SCORE_SCALE = SCALE * LOG2E
CODES = 128
BF16 = jnp.bfloat16
F32 = jnp.float32
VMEM_LIMIT = 60 << 20


def dot_nn(left, right):
    return lax.dot_general(left, right, (((1,), (0,)), ((), ())), preferred_element_type=F32)


def dot_nt(left, right):
    return lax.dot_general(left, right, (((1,), (1,)), ((), ())), preferred_element_type=F32)


def dot_tn(left, right):
    return lax.dot_general(left, right, (((0,), (0,)), ((), ())), preferred_element_type=F32)


def chunk_range(bounds):
    start = bounds[0, 0] // 16 * 16
    return start, (bounds[0, 1] - start + CHUNK - 1) // CHUNK


def chunk_rows(start, c):
    return pl.ds(pl.multiple_of(start + c * CHUNK, 16), CHUNK)


class Window:
    def __init__(self, bounds, source, held, sems):
        self.bounds, self.source, self.held, self.sems = bounds, source, held, sems
        self.start, self.chunks = chunk_range(bounds)

    def copy(self, c):
        rows = chunk_rows(self.start, c)
        return pltpu.make_async_copy(self.source.at[rows], self.held.at[rows], self.sems.at[c])

    def fetch(self):
        def one(c, carry):
            self.copy(c).start()
            return carry

        lax.fori_loop(0, self.chunks, one, 0)

    def loops(self, count, step):
        bounds, start, chunks = self.bounds, self.start, self.chunks

        def loop(number, size, where):
            def one(i, carry):
                c, lane = where(i)
                self.copy(c).wait()
                step(c, pl.ds(lane, size) if isinstance(lane, int) else pl.ds(pl.multiple_of(lane, LANES), size))
                return carry

            lax.fori_loop(0, number, one, 0)

        if count != 3 * LANES:
            return loop(chunks, count, lambda i: (i, 0))
        thirds = [(bounds[0, k] - start) // CHUNK for k in (2, 3)] + [(bounds[0, k] - start + CHUNK - 1) // CHUNK for k in (4, 5)]
        edges = [chunks * 0]
        for edge in thirds:
            edges.append(jnp.clip(edge, edges[-1], chunks))
        edges.append(chunks)

        def two(first, second, second_lane):
            number = edges[first + 1] - edges[first]

            def where(i):
                early = i < number
                return jnp.where(early, edges[first] + i, edges[second] + i - number), jnp.where(early, 0, second_lane)

            return number + edges[second + 1] - edges[second], where

        loop(edges[3] - edges[2], count, lambda i: (edges[2] + i, 0))
        number, where = two(1, 3, LANES)
        loop(number, 2 * LANES, where)
        number, where = two(0, 4, 2 * LANES)
        loop(number, LANES, where)


def layer_norm(resid):
    mean_row = jnp.mean(resid, axis=1, keepdims=True)
    centred = resid - mean_row
    var_row = jnp.mean(centred * centred, axis=1, keepdims=True)
    scale_row = lax.rsqrt(var_row + EPS)
    return centred * scale_row, scale_row


def norm_back(grad, normed, scale_row, gain):
    gain_grad = jnp.sum(grad * normed, axis=0, keepdims=True)
    scaled = grad * gain
    centre = jnp.mean(scaled, axis=1, keepdims=True)
    along = jnp.mean(scaled * normed, axis=1, keepdims=True)
    return scale_row * (scaled - centre - normed * along), gain_grad


def spread_heads(source, target):
    target[...] = jnp.zeros_like(target)
    for h in range(HEADS):
        row = h * PAIR + (h % 2) * HEAD_SIZE
        target[row : row + HEAD_SIZE, :] = source[h * HEAD_SIZE : (h + 1) * HEAD_SIZE, :]


def pair_rows(source, p, target):
    rows = source.shape[0]
    both = source[:, p * PAIR : (p + 1) * PAIR]
    lane = lax.broadcasted_iota(jnp.int32, both.shape, 1)
    zero = jnp.zeros_like(both)
    target[p, 0:rows, :] = jnp.where(lane < HEAD_SIZE, both, zero)
    target[p, rows : 2 * rows, :] = jnp.where(lane < HEAD_SIZE, zero, both)


MESH = pl.DeviceIdType.MESH


class Copies:
    def __init__(self, send, recv, local):
        self.send, self.recv, self.local = send, recv, local
        self.remotes, self.locals = 0, 0

    def remote(self, source, target, seq, part):
        k = self.remotes
        self.remotes += 1
        return pltpu.make_async_remote_copy(
            src_ref=source, dst_ref=target, send_sem=self.send.at[k], recv_sem=self.recv.at[k],
            device_id=(seq, part), device_id_type=MESH,
        )

    def own(self, source, target):
        k = self.locals
        self.locals += 1
        return pltpu.make_async_copy(source, target, self.local.at[k])


def greet(seq, part, peers, slices):
    barrier = pltpu.get_barrier_semaphore()
    for d in range(1, peers):
        pl.semaphore_signal(barrier, inc=1, device_id=(lax.rem(seq + d, peers), part), device_id_type=MESH)
    for d in range(1, slices):
        pl.semaphore_signal(barrier, inc=1, device_id=(seq, lax.rem(part + d, slices)), device_id_type=MESH)
    pl.semaphore_wait(barrier, peers - 1 + slices - 1)


def halo_sizes(part, count, rows):
    return max(0, DOC_LEN - part * count), max(0, (part + 1) * count + DOC_LEN - rows)


def put_rows(whole, part, row, ref, flip):
    value = ref[...]
    if flip:
        value = value.astype(F32).T.astype(BF16)
    whole[part, row : row + value.shape[0], :] = value


def pad_rows(whole, part, row):
    if row < whole.shape[1]:
        whole[part, row:, :] = jnp.zeros((whole.shape[1] - row, whole.shape[2]), BF16)


def find_sentences(begin, count, total_rows, lengths, score, cut, code, low, high_self, high_cross, bounds, blocks_code):
    lanes, blocks = score.shape[1], code.shape[0] // score.shape[1]
    first_block = (begin - DOC_LEN) // lanes
    for j in range(blocks):
        at = jnp.clip(first_block + j, 0, score.shape[0] - 1)
        blocks_code[j : j + 1, :] = score[pl.ds(at, 1), :].astype(F32)
    pos = lax.broadcasted_iota(jnp.int32, (blocks, lanes), 0) * lanes + lax.broadcasted_iota(jnp.int32, (blocks, lanes), 1)
    pos = pos + (begin - DOC_LEN)
    own_pos = lax.broadcasted_iota(jnp.int32, (1, count), 1) + begin
    zero = jnp.zeros((blocks, lanes), jnp.int32)
    last_pos = begin + count - 1

    def one(s, carry):
        start, sentence, first, own_sentence, first_row, last_row, thirds = carry
        size = lengths[0, s]
        end = start + size
        passed = pos >= end
        sentence = sentence + jnp.where(passed, 1, 0)
        first = first + jnp.where(passed, size, 0)
        own_sentence = own_sentence + jnp.where(own_pos >= end, 1, 0)
        first_row = first_row + jnp.where(begin >= end, size, 0)
        last_row = last_row + jnp.where(last_pos >= start, size, 0)
        thirds = tuple(t + jnp.where(begin + LANES * (1 + k) >= end, size, 0) for k, t in enumerate(thirds[:2])) + tuple(
            t + jnp.where(begin + LANES * (1 + k) - 1 >= start, size, 0) for k, t in enumerate(thirds[2:])
        )
        return end, sentence, first, own_sentence, first_row, last_row, thirds

    none = lengths[0, 0] * 0
    carry = (none, zero, zero, jnp.zeros((1, count), jnp.int32), none, none, (none,) * 4)
    _, sentence, first, own_sentence, first_row, last_row, thirds = lax.fori_loop(0, lengths.shape[1], one, carry)
    shown = jnp.where(pos == first, -1.0, blocks_code[0:blocks, :])
    inside = jnp.logical_and(pos >= 0, pos < total_rows)
    blocks_code[0:blocks, :] = jnp.where(inside, (sentence * CODES).astype(F32) + shown, -float(CODES))
    for b in range(0, blocks, 8):
        turned = blocks_code[b : b + 8, :].T
        for j in range(min(8, blocks - b)):
            code[(b + j) * lanes : (b + j + 1) * lanes, :] = turned[:, j : j + 1]
    low[...] = (own_sentence * CODES - 1).astype(F32)
    for j in range(count // lanes):
        some = slice(j * lanes, (j + 1) * lanes)
        high_self[:, some] = (own_sentence[:, some] * CODES + cut[pl.ds(begin // lanes + j, 1), :]).astype(F32)
    high_cross[...] = (own_sentence * CODES + CODES // 2).astype(F32)
    origin = begin - DOC_LEN
    bounds[0, 0] = first_row - origin
    bounds[0, 1] = last_row - origin
    for k, row in enumerate(thirds):
        bounds[0, 2 + k] = row - origin


def start_kernel(
    peers, slices, count, content, encoded, query_state, out_grad, w_query, w_key, w_value, w_out,
    w_cross_query, w_cross_key, w_cross_value, w_cross_out, lengths, score, cut,
    content_window, encoded_window, all_one, all_two, own, own_out_grad, code, low, high_self, high_cross, bounds,
    send, recv, local, zeros, blocks_code,
):
    seq, part = lax.axis_index("seq"), lax.axis_index("head")
    chip, core = seq // 2, lax.rem(seq, 2)
    chips = peers // 2
    sibling = chip * 2 + 1 - core
    rows = content.shape[0]
    span = count + 2 * DOC_LEN
    spare = content_window.shape[0] - span
    copies = Copies(send, recv, local)
    cols = w_query.shape[1]
    for k, (ref, flip) in enumerate(((w_query, True), (w_key, True), (w_value, True))):
        put_rows(all_one, part, k * cols, ref, flip)
    pad_rows(all_one, part, 3 * cols)
    greet(seq, part, peers, slices)
    waits = []
    for source, target in ((query_state, own), (out_grad, own_out_grad)):
        mine = copies.own(source.at[pl.ds(pl.multiple_of(part * count, 16), count)], target)
        mine.start()
        waits.append(mine.wait)

    def halo(source, window):
        for k in range(slices):
            below, above = halo_sizes(k, count, rows)
            low = max(0, k * count - DOC_LEN)
            inner = span - below - above
            mine = copies.own(source.at[pl.ds(low, inner)], window.at[pl.ds(below, inner)])
            tail = copies.own(zeros.at[pl.ds(0, spare)], window.at[pl.ds(span, spare)])
            up = down = fill_low = fill_high = None
            if below:
                up = copies.remote(source.at[pl.ds(rows - below, below)], window.at[pl.ds(0, below)], seq + 1, part)
                fill_low = copies.own(zeros.at[pl.ds(0, below)], window.at[pl.ds(0, below)])
            if above:
                down = copies.remote(source.at[pl.ds(0, above)], window.at[pl.ds(span - above, above)], seq - 1, part)
                fill_high = copies.own(zeros.at[pl.ds(0, above)], window.at[pl.ds(span - above, above)])
            here, first, last = part == k, seq == 0, seq == peers - 1

            def start(mine=mine, tail=tail, up=up, down=down, fill_low=fill_low, fill_high=fill_high, here=here):
                @pl.when(here)
                def _():
                    if up is not None:
                        pl.when(jnp.logical_not(last))(up.start)
                        pl.when(first)(fill_low.start)
                    if down is not None:
                        pl.when(jnp.logical_not(first))(down.start)
                        pl.when(last)(fill_high.start)
                    mine.start()
                    tail.start()

            def finish(mine=mine, tail=tail, up=up, down=down, fill_low=fill_low, fill_high=fill_high, here=here):
                @pl.when(here)
                def _():
                    if up is not None:
                        pl.when(jnp.logical_not(last))(up.wait_send)
                        pl.when(jnp.logical_not(first))(up.wait_recv)
                        pl.when(first)(fill_low.wait)
                    if down is not None:
                        pl.when(jnp.logical_not(first))(down.wait_send)
                        pl.when(jnp.logical_not(last))(down.wait_recv)
                        pl.when(last)(fill_high.wait)
                    mine.wait()
                    tail.wait()

            start()
            waits.append(finish)

    packs = (all_one, all_two)

    def piece(ref, owner, index, size):
        return ref.at[owner, pl.ds(pl.multiple_of(index * size, 16), size)]

    across = {}
    for n, whole in enumerate(packs):
        size = whole.shape[1] // peers
        for d in range(1, slices):
            to = lax.rem(part + d, slices)
            across[n, d] = copies.remote(piece(whole, part, seq, size), piece(whole, part, seq, size), seq, to)
            across[n, d].start()
        if n == 0:
            zeros[...] = jnp.zeros_like(zeros)
            halo(content, content_window)
            put_rows(all_two, part, 0, w_out, False)
            for k, ref in enumerate((w_cross_query, w_cross_key, w_cross_value)):
                put_rows(all_two, part, (1 + k) * cols, ref, True)
            put_rows(all_two, part, 4 * cols, w_cross_out, False)
            pad_rows(all_two, part, 5 * cols)
    find_sentences(seq * rows + part * count, count, peers * rows, lengths, score, cut, code, low, high_self, high_cross, bounds, blocks_code)
    round_plane, to_sibling = {}, {}
    for n, whole in enumerate(packs):
        size = whole.shape[1] // peers
        for d in range(1, slices):
            across[n, d].wait_recv()
            owner = lax.rem(part + slices - d, slices)
            got = piece(whole, owner, seq, size)
            for e in range(1, chips):
                round_plane[n, d, e] = copies.remote(got, got, lax.rem(chip + e, chips) * 2 + core, part)
                round_plane[n, d, e].start()
            to_sibling[n, d, 0] = copies.remote(got, got, sibling, part)
            to_sibling[n, d, 0].start()
    halo(encoded, encoded_window)
    for n, whole in enumerate(packs):
        size = whole.shape[1] // peers
        for d in range(1, slices):
            owner = lax.rem(part + slices - d, slices)
            for e in range(1, chips):
                round_plane[n, d, e].wait_recv()
                got = piece(whole, owner, lax.rem(chip + chips - e, chips) * 2 + core, size)
                to_sibling[n, d, e] = copies.remote(got, got, sibling, part)
                to_sibling[n, d, e].start()
    for copy in to_sibling.values():
        copy.wait_recv()
    for copy in (*across.values(), *round_plane.values(), *to_sibling.values()):
        copy.wait_send()
    for wait in waits:
        wait()


def add_rows(target, source, target_at, source_at, size):
    step = 64 if size % 64 == 0 else 16

    def one(i, carry):
        to = pl.ds(pl.multiple_of(target_at + i * step, 16), step)
        by = pl.ds(pl.multiple_of(source_at + i * step, 16), step)
        target[to, :] = (target[to, :].astype(F32) + source[by, :].astype(F32)).astype(BF16)
        return carry

    lax.fori_loop(0, size // step, one, 0)


def end_kernel(
    peers, slices, count, blocks, parts, packs, plane_sums, outs, part_outs, pack_outs, scratch,
):
    seq, part = lax.axis_index("seq"), lax.axis_index("head")
    chip, core = seq // 2, lax.rem(seq, 2)
    chips = peers // 2
    sibling = chip * 2 + 1 - core
    rows = slices * count
    span = count + 2 * DOC_LEN
    send, recv, local = scratch[:3]
    copies = Copies(send, recv, local)
    first, last = seq == 0, seq == peers - 1
    start_line, end_line = part == 0, part == slices - 1
    greet(seq, part, peers, slices)
    sent = []

    def block(ref, index):
        return ref.at[pl.ds(pl.multiple_of(index * count, 16), count)]

    weight_scratch = scratch[3 : 3 + 3 * len(packs)]
    to_core, held = [], []
    for n, pack in enumerate(packs):
        half = pack.shape[1] // 2
        sibling_sum, mine = weight_scratch[3 * n : 3 * n + 2]
        copy = copies.remote(pack.at[:, pl.ds(pl.multiple_of((1 - core) * half, 16), half)], sibling_sum, sibling, part)
        copy.start()
        to_core.append(copy)
        keep = copies.own(pack.at[:, pl.ds(pl.multiple_of(core * half, 16), half)], mine)
        keep.start()
        held.append(keep)
        sent.append(copy)

    part_scratch = scratch[3 + 3 * len(packs) :]
    halos = []
    for n, grad in enumerate(parts):
        total, from_above, from_below = part_scratch[5 * n : 5 * n + 3]
        for k in range(slices):
            below, above = halo_sizes(k, count, rows)
            low = max(0, k * count - DOC_LEN)
            inner = span - below - above
            mine = copies.own(grad.at[pl.ds(below, inner)], total.at[pl.ds(low, inner)])
            down = up = None
            if below:
                down = copies.remote(grad.at[pl.ds(0, below)], from_above.at[pl.ds(0, below)], seq - 1, part)
            if above:
                up = copies.remote(grad.at[pl.ds(span - above, above)], from_below.at[pl.ds(0, above)], seq + 1, part)
            halos.append((n, k, below, above, low, inner, mine, down, up))

            @pl.when(part == k)
            def _(low=low, inner=inner, mine=mine, down=down, up=up, total=total):
                if down is not None:
                    pl.when(jnp.logical_not(first))(down.start)
                if up is not None:
                    pl.when(jnp.logical_not(last))(up.start)
                mine.start()
                if low:
                    total[0:low, :] = jnp.zeros((low, total.shape[1]), BF16)
                if low + inner < rows:
                    total[low + inner : rows, :] = jnp.zeros((rows - low - inner, total.shape[1]), BF16)

    def finish_halo(which):
        for n, k, below, above, low, inner, mine, down, up in halos:
            if n != which:
                continue
            total, from_above, from_below = part_scratch[5 * n : 5 * n + 3]

            @pl.when(part == k)
            def _(below=below, above=above, mine=mine, down=down, up=up, total=total, from_above=from_above, from_below=from_below):
                mine.wait()
                if down is not None:
                    pl.when(jnp.logical_not(first))(down.wait_send)

                    @pl.when(jnp.logical_not(last))
                    def _():
                        down.wait_recv()
                        add_rows(total, from_above, rows - below, 0, below)

                if up is not None:
                    pl.when(jnp.logical_not(last))(up.wait_send)

                    @pl.when(jnp.logical_not(first))
                    def _():
                        up.wait_recv()
                        add_rows(total, from_below, 0, 0, above)

    halves = 2 if slices <= 4 else 1
    sub = count // halves

    def unit_rows(ref, index, h, size=count, sub=sub):
        return ref.at[pl.ds(index * size + h * sub, sub)]

    def gather_rounds(out, me):
        rounds, flows = {}, ((1, slices - 1 - me), (-1, me))
        for sign, onward in flows:
            behind = me if sign > 0 else slices - 1 - me
            sends, waits = {}, {}
            for k in range(behind + 1):
                for h in range(halves):
                    ref = (me - sign * k, h)
                    if onward:
                        sends[k * halves + h] = ref
                    if k:
                        waits[k * halves + h] = ref
            rounds[sign] = (sends, waits)
        return rounds

    def line_gather(out, me, sems):
        steps, ends = [], []
        ring = gather_rounds(out, me)

        def onward(sign, i):
            ref = unit_rows(out, *ring[sign][0][i])
            return sems(sign, i, ref, ref, sign)

        def step(i):
            for sign in (1, -1):
                sends, waits = ring[sign]
                if i in waits:
                    sems(sign, i - halves, unit_rows(out, *waits[i]), unit_rows(out, *waits[i]), 0).wait_recv()
                if i in sends:
                    if i >= IN_FLIGHT:
                        onward(sign, i - IN_FLIGHT).wait_send()
                    onward(sign, i).start()

        def finish():
            for sign in (1, -1):
                sends, _ = ring[sign]
                for i in sorted(sends)[-IN_FLIGHT:]:
                    onward(sign, i).wait_send()

        return [partial(step, i) for i in range(slices * halves)], finish

    def line_sum(total, ins, out, me, sems, size=count, halves=halves):
        units, sub = (slices - 1) * halves, size // halves
        before = {1: [], -1: []}

        def place(sign, i):
            return slices - 1 - i // halves if sign > 0 else i // halves

        def slot(sign, i):
            return ins[0 if sign > 0 else 1].at[i]

        def onward(sign, i):
            return sems(sign, i, unit_rows(total, place(sign, i), i % halves, size, sub), slot(sign, i), sign)

        def step(r):
            for sign in (1, -1):
                depth = me if sign > 0 else slices - 1 - me
                i = r - depth
                if not 0 <= i < units:
                    continue
                b = place(sign, i)
                passes = b > me if sign > 0 else b < me
                if (passes or b == me) and depth:
                    sems(sign, i, slot(sign, i), slot(sign, i), 0).wait_recv()
                    add_rows(total, slot(sign, i), b * size + (i % halves) * sub, 0, sub)
                if passes:
                    if len(before[sign]) == IN_FLIGHT:
                        onward(sign, before[sign].pop(0)).wait_send()
                    before[sign].append(i)
                    onward(sign, i).start()

        def finish():
            for sign in (1, -1):
                for i in before[sign]:
                    onward(sign, i).wait_send()

        def place_own():
            if out is not None:
                out[pl.ds(me * size, size), :] = total[pl.ds(me * size, size), :]

        return [partial(step, r) for r in range(units + slices - 1)], place_own, finish

    def semaphores(units):
        base = copies.remotes
        copies.remotes += 2 * units

        def make(sign, i, source, target, to):
            k = base + i + (0 if sign > 0 else units)
            return pltpu.make_async_remote_copy(
                src_ref=source, dst_ref=target, send_sem=send.at[k], recv_sem=recv.at[k],
                device_id=(seq, part + to), device_id_type=MESH,
            )

        return make

    def interleave(*lists):
        for k in range(max((len(steps) for steps in lists), default=0)):
            for steps in lists:
                if k < len(steps):
                    steps[k]()

    def at_place(run):
        for me in range(slices):
            pl.when(part == me)(partial(run, me))

    own_copies = []
    for own, out in zip(blocks, outs):
        mine = copies.own(own, block(out, part))
        mine.start()
        own_copies.append(mine)
    plane_total, *plane_ins = part_scratch[5 * len(parts) :]
    pieces = [out.shape[0] // peers for out in pack_outs]
    piece_rows = sum(pieces)
    plane_sems = semaphores(slices)
    block_sems = [semaphores(slices * halves) for _ in outs]
    sum_sems = [semaphores(slices * halves) for _ in part_outs]
    after_sems = [semaphores(slices * halves) for _ in part_outs]

    to_chips = []

    def to_plane():
        for n, pack in enumerate(packs):
            half = pack.shape[1] // 2
            size = half // chips
            sibling_sum, mine, by_chip = weight_scratch[3 * n : 3 * n + 3]
            held[n].wait()
            to_core[n].wait_recv()

            def add_half(z, carry, sibling_sum=sibling_sum, mine=mine, half=half):
                add_rows(mine.at[z], sibling_sum.at[z], 0, 0, half)
                return carry

            lax.fori_loop(0, slices, add_half, 0)
            for e in range(1, chips):
                to = lax.rem(chip + e, chips)
                copy = copies.remote(mine.at[:, pl.ds(pl.multiple_of(to * size, 16), size)], by_chip.at[e - 1], to * 2 + core, part)
                copy.start()
                to_chips.append((n, e, copy))
                sent.append(copy)

    length = slices * halves
    plans = []
    for me in range(slices):
        gathers = [line_gather(out, me, sems) for out, sems in zip(outs, block_sems)]
        sums, afters = [], []
        for n, out in enumerate(part_outs):
            total, _, _, right_in, left_in = part_scratch[5 * n : 5 * n + 5]
            sums.append(line_sum(total, (right_in, left_in), out, me, sum_sems[n]))
            afters.append(line_gather(out, me, after_sems[n]))
        owned = [line_sum(plane_total, plane_ins, None, me, plane_sems, piece_rows, 1)]
        plans.append((gathers, sums, afters, owned))

    def rounds(me, *which):
        lists, ends = [], []
        for kind, n, low, high in which:
            entry = plans[me][kind][n]
            steps = entry[0]
            lists.append(steps[low:high])
            if low < len(steps) <= high:
                ends += list(entry[1:])
        interleave(*lists)
        for finish in ends:
            finish()

    def run(*which):
        at_place(lambda me: rounds(me, *which))

    def to_owners():
        for n, pack in enumerate(packs):
            half = pack.shape[1] // 2
            size, first_row = half // chips, sum(pieces[:n])
            mine, by_chip = weight_scratch[3 * n + 1 : 3 * n + 3]
            for m, e, copy in to_chips:
                if m == n:
                    copy.wait_recv()

            def add_plane(i, carry, mine=mine, by_chip=by_chip, size=size, first_row=first_row):
                z, r = i // (size // 16), lax.rem(i, size // 16)
                at = pl.ds(pl.multiple_of(r * 16, 16), 16)
                value = mine[z, pl.ds(pl.multiple_of(chip * size + r * 16, 16), 16), :].astype(F32)
                for e in range(chips - 1):
                    value = value + by_chip[e, z, at, :].astype(F32)
                plane_total[pl.ds(pl.multiple_of(z * piece_rows + first_row + r * 16, 16), 16), :] = value.astype(BF16)
                return carry

            lax.fori_loop(0, slices * (size // 16), add_plane, 0)

    def piece_at(n, of_chip, of_core):
        size = pack_outs[n].shape[0] // peers
        index = of_core * chips + of_chip if n < len(packs) else of_chip * 2 + of_core
        return pl.multiple_of(index * size, 16), size

    round_plane, to_sibling = [], []

    def back_to_plane():
        for n, out in enumerate(pack_outs):
            start, size = piece_at(n, chip, core)

            def keep(r, carry, out=out, start=start, first_row=sum(pieces[:n])):
                at = pl.ds(pl.multiple_of(part * piece_rows + first_row + r * 16, 16), 16)
                out[pl.ds(pl.multiple_of(start + r * 16, 16), 16), :] = plane_total[at, :]
                return carry

            lax.fori_loop(0, size // 16, keep, 0)
            piece = out.at[pl.ds(start, size)]
            for e in range(1, chips):
                copy = copies.remote(piece, piece, lax.rem(chip + e, chips) * 2 + core, part)
                copy.start()
                round_plane.append((n, e, copy))
                sent.append(copy)
            copy = copies.remote(piece, piece, sibling, part)
            copy.start()
            round_plane.append((n, 0, copy))
            sent.append(copy)

    sum_length = (slices - 1) * halves + slices - 1
    plane_copies = []
    for n, summed in enumerate(plane_sums):
        first_row, size = sum(pieces[: len(packs) + n]), pieces[len(packs) + n]
        for z in range(slices):
            plane_copies.append(copies.own(summed.at[z], plane_total.at[pl.ds(z * piece_rows + first_row, size)]))
    for keep in plane_copies:
        keep.start()
    for mine in own_copies:
        mine.wait()
    run((0, 0, 0, 2))
    finish_halo(0)
    run((0, 0, 2, 4), (1, 0, 0, 2))
    to_plane()
    run((0, 0, 4, length), (1, 0, 2, sum_length))
    for keep in plane_copies:
        keep.wait()
    if len(parts) > 1:
        finish_halo(1)
        run((1, 1, 0, 3), (2, 0, 0, 3))
        to_owners()
        run((1, 1, 3, sum_length), (2, 0, 3, length), (3, 0, 0, 5))
    else:
        to_owners()
        run((3, 0, 0, 4))
    last = len(parts) - 1
    run((3, 0, 5, 2 * (slices - 1)), (2, last, 0, 2))
    back_to_plane()
    run((2, last, 2, length))
    for n, e, copy in round_plane:
        copy.wait_recv()
        if e:
            start, size = piece_at(n, lax.rem(chip + chips - e, chips), core)
            piece = pack_outs[n].at[pl.ds(start, size)]
            copy = copies.remote(piece, piece, sibling, part)
            copy.start()
            to_sibling.append(copy)
            sent.append(copy)
    for copy in to_sibling:
        copy.wait_recv()
    for copy in sent:
        copy.wait_send()


class Rows:
    def __init__(self, pack, index, size):
        self.pack, self.at = pack, slice(index * size, (index + 1) * size)

    def __getitem__(self, _):
        value = self.pack[:, self.at, :]
        return value.reshape(value.shape[0] * value.shape[1], value.shape[2])


def write_rows(pack, index, size, value):
    slices = pack.shape[0]
    pack[:, index * size : (index + 1) * size, :] = value.astype(BF16).reshape(slices, size, value.shape[1])


def mask_bias(code, low, high):
    return jnp.where((code >= low) & (code < high), 0.0, NEG_BIG).astype(F32)


def pair_product(left, spread, p, see):
    count = see.size
    blocks = [spread[h * PAIR : (h + 1) * PAIR, see] for h in (2 * p, 2 * p + 1)]
    if count % LANES:
        return [dot_nn(left, block) for block in blocks]
    both = dot_nn(left, jnp.concatenate(blocks, axis=1))
    return both[:, :count], both[:, count:]


def attend(window, code, low, high, w_key_t, w_value_t, spread, bias, top, total, out):
    top[...] = jnp.full_like(top, NEG_BIG)
    total[...] = jnp.zeros_like(total)
    out[...] = jnp.zeros_like(out)

    def step(c, see):
        at = chunk_rows(window.start, c)
        rows = window.held[at, :]
        keys = dot_nt(rows, w_key_t[...]).astype(BF16)
        values_t = dot_nt(rows, w_value_t[...]).astype(BF16).T
        bias[:, see] = mask_bias(code[at, :], low[:, see], high[:, see])
        for h in range(HEADS):
            p = h // 2
            if h % 2 == 0:
                both = pair_product(keys[:, p * PAIR : (p + 1) * PAIR], spread, p, see)
            scores = both[h % 2] * SCORE_SCALE + bias[:, see]
            before = top[h : h + 1, see]
            now = jnp.maximum(before, jnp.max(scores, axis=0, keepdims=True))
            weights = jnp.exp2(scores - now)
            shrink = jnp.exp2(before - now)
            top[h : h + 1, see] = now
            total[h : h + 1, see] = total[h : h + 1, see] * shrink + jnp.sum(weights, axis=0, keepdims=True)
            head = slice(h * HEAD_SIZE, (h + 1) * HEAD_SIZE)
            out[head, see] = out[head, see] * shrink + dot_nn(values_t[head, :], weights.astype(BF16))

    window.loops(out.shape[1], step)
    for h in range(HEADS):
        head = slice(h * HEAD_SIZE, (h + 1) * HEAD_SIZE)
        out[head, :] = out[head, :] / total[h : h + 1, :]


def attend_back(
    window, code, low, high, w_key_t, w_value_t, spread, grad_spread, pairs, grad_pairs, lse, delta, bias,
    query_grad, window_grad, w_key_grad, w_value_grad,
):
    count = spread.shape[1]
    query_grad[...] = jnp.zeros_like(query_grad)
    w_key_grad[...] = jnp.zeros_like(w_key_grad)
    w_value_grad[...] = jnp.zeros_like(w_value_grad)
    window_grad[...] = jnp.zeros_like(window_grad)

    def step(c, see):
        at = chunk_rows(window.start, c)
        seen = (see, pl.ds(count + see.start, see.size) if isinstance(see.start, int) else pl.ds(pl.multiple_of(count + see.start, LANES), see.size))
        rows = window.held[at, :]
        keys = dot_nt(rows, w_key_t[...]).astype(BF16)
        keys_t = keys.T
        values = dot_nt(rows, w_value_t[...]).astype(BF16)
        bias[:, see] = mask_bias(code[at, :], low[:, see], high[:, see])
        key_grads, value_grads = [], []
        for p in range(PAIRS):
            columns = slice(p * PAIR, (p + 1) * PAIR)
            probs, score_grads = [], []
            both_scores = pair_product(keys[:, columns], spread, p, see)
            both_dprobs = pair_product(values[:, columns], grad_spread, p, see)
            for h in (2 * p, 2 * p + 1):
                head = slice(h * HEAD_SIZE, (h + 1) * HEAD_SIZE)
                prob = jnp.exp2(both_scores[h % 2] * SCORE_SCALE + bias[:, see] - lse[h : h + 1, see])
                score_grad = (prob * (both_dprobs[h % 2] - delta[h : h + 1, see])).astype(BF16)
                query_grad[head, see] += dot_nn(keys_t[head, :], score_grad)
                probs.append(prob.astype(BF16))
                score_grads.append(score_grad)
            if count % LANES == 0:
                both = jnp.concatenate([pairs[p, r, :] for r in seen], axis=0)
                grad_both = jnp.concatenate([grad_pairs[p, r, :] for r in seen], axis=0)
                key_grads.append(dot_nn(jnp.concatenate(score_grads, axis=1), both))
                value_grads.append(dot_nn(jnp.concatenate(probs, axis=1), grad_both))
            else:
                key_grads.append(sum(dot_nn(x, pairs[p, r, :]) for x, r in zip(score_grads, seen)))
                value_grads.append(sum(dot_nn(x, grad_pairs[p, r, :]) for x, r in zip(probs, seen)))
        keys_low = (jnp.concatenate(key_grads, axis=1) * SCALE).astype(BF16)
        values_low = jnp.concatenate(value_grads, axis=1).astype(BF16)
        window_grad[at, :] = (dot_nn(keys_low, w_key_t[...]) + dot_nn(values_low, w_value_t[...])).astype(window_grad.dtype)
        w_key_grad[...] += dot_tn(rows, keys_low)
        w_value_grad[...] += dot_tn(rows, values_low)

    window.loops(count, step)


def forward_kernel(
    cols, bounds, own, content_window, encoded_window, gain, code, low, high_self, high_cross, pack_one, pack_two_in,
    self_t, lse_self, hidden, cross_t, lse_cross,
    spread, bias, top, total, low_t, content_held, encoded_held, pack_two, content_sems, encoded_sems, pack_sem,
):
    content = Window(bounds, content_window, content_held, content_sems)
    encoded = Window(bounds, encoded_window, encoded_held, encoded_sems)
    content.fetch()
    whole_pack = pltpu.make_async_copy(pack_two_in, pack_two, pack_sem.at[0])
    whole_pack.start()
    encoded.fetch()
    w_query_t, w_key_t, w_value_t = (Rows(pack_one, k, cols) for k in range(3))
    low_t[...] = dot_nt(w_query_t[...], own[...]).astype(BF16)
    spread_heads(low_t, spread)
    attend(content, code, low, high_self, w_key_t, w_value_t, spread, bias, top, total, self_t)
    lse_self[...] = top[...] + jnp.log2(total[...])
    whole_pack.wait()
    w_out, w_query_t, w_key_t, w_value_t = (Rows(pack_two, k, cols) for k in range(4))
    branch = dot_tn(self_t[...].astype(BF16), w_out[...])
    normed, _ = layer_norm(own[...].astype(F32) + branch)
    hidden[...] = normed * gain[...]
    low_t[...] = dot_nt(w_query_t[...], hidden[...].astype(BF16)).astype(BF16)
    spread_heads(low_t, spread)
    attend(encoded, code, low, high_cross, w_key_t, w_value_t, spread, bias, top, total, cross_t)
    lse_cross[...] = top[...] + jnp.log2(total[...])


def ffn_kernel(
    cols, hidden_one, cross_t, pack_two, gain_cross, pack_three_in, gain_final, out_grad,
    mixed, resid_grad, w_out_grad, grad_three_out, gain_cross_grad, gain_final_grad,
    normed_two, hidden_two_low, slope, active, sum_ffn, pack_out, pack_three, grad_three_pack, sems, out_sems,
):
    slices, units = pack_three.shape[0], active.shape[2]
    if grad_three_pack.shape[1] > 2 * units:
        grad_three_pack[:, 2 * units :, :] = jnp.zeros((slices, grad_three_pack.shape[1] - 2 * units, grad_three_pack.shape[2]), BF16)
    out_copy = pltpu.make_async_copy(pack_two.at[:, pl.ds(4 * cols, cols)], pack_out, sems.at[slices])
    out_copy.start()
    slice_copies = [pltpu.make_async_copy(pack_three_in.at[z], pack_three.at[z], sems.at[z]) for z in range(slices)]
    for copy in slice_copies:
        copy.start()
    out_copy.wait()
    w_out = Rows(pack_out, 0, cols)
    cross_low = cross_t[...].astype(BF16)
    normed, scale_two = layer_norm(hidden_one[...] + dot_tn(cross_low, w_out[...]))
    normed_two[...] = normed
    hidden_two = normed * gain_cross[...]
    hidden_two_low[...] = hidden_two.astype(BF16)
    sum_ffn[...] = hidden_two
    for z in range(slices):
        slice_copies[z].wait()
        inner = dot_nt(hidden_two_low[...], pack_three[z, 0:units, :])
        below = 0.5 * (1.0 + lax.erf(inner * math.sqrt(0.5)))
        slope[z] = below + inner * (jnp.exp2(inner * inner * (-0.5 * LOG2E)) * (1.0 / math.sqrt(2.0 * math.pi)))
        active[z] = (inner * below).astype(BF16)
        sum_ffn[...] += dot_nn(active[z], pack_three[z, units : 2 * units, :])
    normed_three, scale_three = layer_norm(sum_ffn[...])
    mixed[...] = (normed_three * gain_final[...]).astype(BF16)
    grad_three, gain_grad = norm_back(out_grad[...].astype(F32), normed_three, scale_three, gain_final[...])
    gain_final_grad[...] = gain_grad
    ffn_low = grad_three.astype(BF16)
    result_copies = [pltpu.make_async_copy(grad_three_pack.at[z], grad_three_out.at[z], out_sems.at[z]) for z in range(slices)]
    sum_ffn[...] = grad_three
    for z in range(slices):
        grad_three_pack[z, units : 2 * units, :] = dot_tn(active[z], ffn_low).astype(BF16)
        inner_low = (dot_nt(ffn_low, pack_three[z, units : 2 * units, :]) * slope[z]).astype(BF16)
        grad_three_pack[z, 0:units, :] = dot_tn(inner_low, hidden_two_low[...]).astype(BF16)
        sum_ffn[...] += dot_nn(inner_low, pack_three[z, 0:units, :])
        result_copies[z].start()
    grad, gain_grad = norm_back(sum_ffn[...], normed_two[...], scale_two, gain_cross[...])
    gain_cross_grad[...] = gain_grad
    resid_grad[...] = grad
    w_out_grad[...] = dot_nn(cross_low, grad.astype(BF16)).astype(BF16)
    for copy in result_copies:
        copy.wait()


def prepare_back(query, query_t, grad, grad_t, out, spread, grad_spread, pairs, grad_pairs, delta, low_t):
    low_t[...] = query_t.astype(BF16)
    spread_heads(low_t, spread)
    for p in range(PAIRS):
        pair_rows(query.astype(BF16), p, pairs)
        pair_rows(grad.astype(BF16), p, grad_pairs)
    low_t[...] = grad_t.astype(BF16)
    spread_heads(low_t, grad_spread)
    for h in range(HEADS):
        head = slice(h * HEAD_SIZE, (h + 1) * HEAD_SIZE)
        delta[h : h + 1, :] = jnp.sum(low_t[head, :].astype(F32) * out[head, :], axis=0, keepdims=True)


def cross_back_kernel(
    cols, bounds, own, self_t, gain, resid_two_grad, cross_t, lse, window_in, code, low, high, pack_two,
    w_cross_out_grad, gain_cross_grad, gain_final_grad, resid_one_grad, window_out, grad_two_pack,
    spread, grad_spread, pairs, grad_pairs, delta, bias, low_t, query_grad, key_sum, value_sum, held, window_grad, sems, out_sem,
    normed_one, scale_one, after,
):
    window = Window(bounds, window_in, held, sems)
    window.fetch()
    after.fetch()
    w_out, w_query_t, w_key_t, w_value_t, w_cross_out = (Rows(pack_two, k, cols) for k in range(5))
    self_low = self_t[...].astype(BF16)
    normed, scale = layer_norm(own[...].astype(F32) + dot_tn(self_low, w_out[...]))
    normed_one[...] = normed
    scale_one[...] = scale
    hidden_low = (normed * gain[...]).astype(BF16)
    branch_low = resid_two_grad[...].astype(BF16)
    prepare_back(
        dot_nt(hidden_low, w_query_t[...]), dot_nt(w_query_t[...], hidden_low),
        dot_nt(branch_low, w_cross_out[...]), dot_nt(w_cross_out[...], branch_low),
        cross_t, spread, grad_spread, pairs, grad_pairs, delta, low_t,
    )
    attend_back(
        window, code, low, high, w_key_t, w_value_t, spread, grad_spread, pairs, grad_pairs, lse, delta, bias,
        query_grad, window_grad, key_sum, value_sum,
    )
    result = pltpu.make_async_copy(window_grad, window_out, out_sem.at[0])
    result.start()
    query_low = (query_grad[...] * SCALE).astype(BF16)
    hidden_low = (normed_one[...] * gain[...]).astype(BF16)
    grad_one = resid_two_grad[...] + dot_tn(query_low, w_query_t[...])
    grad, gain_sum = norm_back(grad_one, normed_one[...], scale_one[...], gain[...])
    resid_one_grad[...] = grad
    write_rows(grad_two_pack, 0, cols, dot_nn(self_t[...].astype(BF16), grad.astype(BF16)))
    write_rows(grad_two_pack, 1, cols, dot_nn(query_low, hidden_low))
    write_rows(grad_two_pack, 2, cols, key_sum[...].T)
    write_rows(grad_two_pack, 3, cols, value_sum[...].T)
    write_rows(grad_two_pack, 4, cols, w_cross_out_grad[...])
    slices, rows, width = grad_two_pack.shape
    gains = jnp.concatenate([gain_sum, gain_cross_grad[...], gain_final_grad[...], jnp.zeros((13, width), F32)], axis=0)
    for z in range(slices):
        grad_two_pack[z, 5 * cols : 5 * cols + 16, :] = gains.astype(BF16)
        if rows > 5 * cols + 16:
            grad_two_pack[z, 5 * cols + 16 :, :] = jnp.zeros((rows - 5 * cols - 16, width), BF16)
    result.wait()


def self_back_kernel(
    cols, own, resid_one_grad, pack_two, self_t, lse, window, code, low, high, pack_one,
    own_grad, window_out, grad_one_pack,
    spread, grad_spread, pairs, grad_pairs, delta, bias, low_t, query_grad, key_sum, value_sum, window_grad, out_sem,
):
    w_query_t, w_key_t, w_value_t = (Rows(pack_one, k, cols) for k in range(3))
    w_out = Rows(pack_two, 0, cols)
    branch_low = resid_one_grad[...].astype(BF16)
    prepare_back(
        dot_nt(own[...], w_query_t[...]), dot_nt(w_query_t[...], own[...]),
        dot_nt(branch_low, w_out[...]), dot_nt(w_out[...], branch_low),
        self_t, spread, grad_spread, pairs, grad_pairs, delta, low_t,
    )
    attend_back(
        window, code, low, high, w_key_t, w_value_t, spread, grad_spread, pairs, grad_pairs, lse, delta, bias,
        query_grad, window_grad, key_sum, value_sum,
    )
    result = pltpu.make_async_copy(window_grad, window_out, out_sem.at[0])
    result.start()
    query_low = (query_grad[...] * SCALE).astype(BF16)
    write_rows(grad_one_pack, 0, cols, dot_nn(query_low, own[...]))
    write_rows(grad_one_pack, 1, cols, key_sum[...].T)
    write_rows(grad_one_pack, 2, cols, value_sum[...].T)
    slices, rows, width = grad_one_pack.shape
    if rows > 3 * cols:
        grad_one_pack[:, 3 * cols :, :] = jnp.zeros((slices, rows - 3 * cols, width), BF16)
    own_grad[...] = (resid_one_grad[...] + dot_tn(query_low, w_query_t[...])).astype(BF16)
    result.wait()


def back_kernel(
    cols, bounds, own, self_t, gain, resid_two_grad, cross_t, lse_cross, encoded_window, code, low, high_cross, pack_two,
    w_cross_out_grad, gain_cross_grad, gain_final_grad, lse_self, content_window, high_self, pack_one_in,
    encoded_part, grad_two_out, own_grad, content_part, grad_one_pack,
    spread, grad_spread, pairs, grad_pairs, delta, bias, low_t, query_grad, key_sum, value_sum,
    encoded_held, encoded_grad, content_held, content_grad, encoded_sems, content_sems, out_sems,
    normed_one, scale_one, resid_one_grad, pack_one, grad_two_pack, pack_sems,
):
    pack_copy = pltpu.make_async_copy(pack_one_in, pack_one, pack_sems.at[0])
    pack_copy.start()
    shared = (spread, grad_spread, pairs, grad_pairs, delta, bias, low_t, query_grad, key_sum, value_sum)
    content = Window(bounds, content_window, content_held, content_sems)
    cross_back_kernel(
        cols, bounds, own, self_t, gain, resid_two_grad, cross_t, lse_cross, encoded_window, code, low, high_cross, pack_two,
        w_cross_out_grad, gain_cross_grad, gain_final_grad, resid_one_grad, encoded_part, grad_two_pack,
        *shared, encoded_held, encoded_grad, encoded_sems, out_sems.at[pl.ds(0, 1)], normed_one, scale_one, content,
    )
    grad_copy = pltpu.make_async_copy(grad_two_pack, grad_two_out, pack_sems.at[1])
    grad_copy.start()
    pack_copy.wait()
    self_back_kernel(
        cols, own, resid_one_grad, pack_two, self_t, lse_self, content, code, low, high_self, pack_one,
        own_grad, content_part, grad_one_pack, *shared, content_grad, out_sems.at[pl.ds(1, 1)],
    )
    grad_copy.wait()


def finish_kernel(cols, units, slices, *refs):
    rows_in, (sum_one, sum_two, sum_three), outs = refs[:4], refs[4:7], refs[7:]
    step = pl.program_id(0)
    for source, target in zip(rows_in, outs[:4]):
        target[...] = source[...].astype(target.dtype)

    def weights(k):
        w_query, w_key, w_value, w_out, w_cross_query, w_cross_key, w_cross_value, w_cross_out, w_inner, w_outer = outs[4:14]
        width = sum_one.shape[1]
        wide, tall, unit_rows = width // slices, cols // slices, units // slices
        some = slice(k * wide, (k + 1) * wide)
        for n, target in enumerate((w_query, w_key, w_value)):
            target[...] = sum_one[n * cols : (n + 1) * cols, some].astype(F32).T
        for n, target in enumerate((w_cross_query, w_cross_key, w_cross_value)):
            target[...] = sum_two[(1 + n) * cols : (2 + n) * cols, some].astype(F32).T
        w_out[...] = sum_two[k * tall : (k + 1) * tall, :].astype(F32)
        w_cross_out[...] = sum_two[4 * cols + k * tall : 4 * cols + (k + 1) * tall, :].astype(F32)
        w_inner[...] = sum_three[0:units, some].astype(F32).T
        w_outer[...] = sum_three[units + k * unit_rows : units + (k + 1) * unit_rows, :].astype(F32)

    for k in range(slices):
        pl.when(step == k)(partial(weights, k))

    @pl.when(step == 0)
    def _():
        gains = sum_two[5 * cols : 5 * cols + 16, :].astype(F32)
        for k, target in enumerate(outs[14:17]):
            target[...] = gains[k : k + 1, :]


def call(kernel, outs, scratch, smem, *args, far=(), far_outs=(), micros=20):
    def space(k, left, scalars):
        return pl.ANY if k in left else pltpu.SMEM if k < scalars else pltpu.VMEM

    return pl.pallas_call(
        kernel,
        out_shape=[jax.ShapeDtypeStruct(shape, kind) for shape, kind in outs],
        in_specs=[pl.BlockSpec(memory_space=space(k, far, smem)) for k in range(len(args))],
        out_specs=[pl.BlockSpec(memory_space=space(k, far_outs, 0)) for k in range(len(outs))],
        scratch_shapes=[pltpu.SemaphoreType.DMA((shape,)) if kind is None else pltpu.VMEM(shape, kind) for shape, kind in scratch],
        compiler_params=pltpu.CompilerParams(vmem_limit_bytes=VMEM_LIMIT),
        cost_estimate=pl.CostEstimate(flops=micros * 10**9, bytes_accessed=micros * 10**6, transcendentals=0),
    )(*args)


def padded(size, unit):
    return -(-size // unit) * unit


def talk(kernel, outs, out_spaces, scratch, copies, number, spaces, *args):
    return pl.pallas_call(
        kernel,
        out_shape=[jax.ShapeDtypeStruct(shape, kind) for shape, kind in outs],
        in_specs=[pl.BlockSpec(memory_space=space) for space in spaces],
        out_specs=[pl.BlockSpec(memory_space=space) for space in out_spaces],
        scratch_shapes=[pltpu.SemaphoreType.DMA((n,)) for n in (copies[0], copies[0], copies[1])] + [pltpu.VMEM(shape, kind) for shape, kind in scratch],
        compiler_params=pltpu.CompilerParams(vmem_limit_bytes=VMEM_LIMIT, collective_id=number, has_side_effects=True),
        cost_estimate=pl.CostEstimate(flops=80 * 10**9, bytes_accessed=80 * 10**6, transcendentals=0),
    )(*args)


def body(
    query_state, content, encoded, sentence_lengths, key_score, query_cut, w_query, w_key, w_value, w_out, gain_self,
    w_cross_query, w_cross_key, w_cross_value, w_cross_out, gain_cross, w_inner, w_outer, gain_final, out_grad,
):
    rows, width = query_state.shape
    slices = lax.axis_size("head")
    count = rows // slices
    lanes = math.gcd(count, LANES)
    wide = padded(count + 2 * DOC_LEN + CHUNK, lanes)
    spare = wide - count - 2 * DOC_LEN
    seq, part = lax.axis_index("seq"), lax.axis_index("head")
    begin = seq * rows + part * count
    score, cut = key_score.reshape(-1, lanes), query_cut.reshape(-1, lanes)
    gain_self, gain_cross, gain_final = (g.reshape(1, width) for g in (gain_self, gain_cross, gain_final))

    peers = lax.axis_size("seq")
    chips = peers // 2
    cols, units = w_query.shape[1], w_inner.shape[1]
    unit = 16 * peers
    sizes = [padded(n, unit) for n in (3 * cols, 5 * cols, 2 * units)]
    grad_sizes = [sizes[0], padded(5 * cols + 16, unit), sizes[2]]

    share = sizes[2] // peers
    slice_three = jnp.concatenate([w_inner.T, w_outer, jnp.zeros((sizes[2] - 2 * units, width), BF16)], axis=0)
    share_three = lax.dynamic_slice_in_dim(slice_three, seq * share, share, 0)
    pack_three = lax.all_gather(share_three, ("head", "seq"), axis=0, tiled=True).reshape(slices, sizes[2], width)
    start_copies = 2 * (slices - 1) * (2 * chips) + 4 * slices
    hbm, vmem, smem = pl.ANY, pltpu.VMEM, pltpu.SMEM
    (
        content_window, encoded_window, pack_one, pack_two, own, own_out_grad, code, low, high_self, high_cross, bounds,
    ) = talk(
        partial(start_kernel, peers, slices, count),
        [((wide, width), BF16)] * 2 + [((slices, n, width), BF16) for n in sizes[:2]] + [((count, width), BF16)] * 2
        + [((wide, 1), F32)] + [((1, count), F32)] * 3 + [((1, 6), jnp.int32)],
        [vmem] * 10 + [smem],
        [((DOC_LEN, width), BF16), ((padded(wide // lanes, 8), lanes), F32)], (start_copies, 8 * slices + 16), 0,
        [hbm] * 4 + [vmem] * 8 + [smem] + [vmem] * 2,
        content, encoded, query_state, out_grad, w_query, w_key, w_value, w_out,
        w_cross_query, w_cross_key, w_cross_value, w_cross_out, sentence_lengths.reshape(1, -1), score, cut,
    )

    def split_refs(kernel, ins, outs):
        def run(*refs):
            return kernel(refs[:ins], refs[ins : ins + outs], refs[ins + outs :])
        return run

    touched = -(-wide // CHUNK)
    window_held = [((wide, width), BF16)]
    self_t, lse_self, hidden_one, cross_t, lse_cross = call(
        partial(forward_kernel, cols),
        [((width, count), F32), ((HEADS, count), F32), ((count, width), F32), ((width, count), F32), ((HEADS, count), F32)],
        [((HEADS * PAIR, count), BF16), ((CHUNK, count), F32), ((HEADS, count), F32), ((HEADS, count), F32), ((width, count), BF16)]
        + window_held * 2 + [((slices, sizes[1], width), BF16), (touched, None), (touched, None), (1, None)], 1,
        bounds, own, content_window, encoded_window, gain_self, code, low, high_self, high_cross, pack_one, pack_two, far=(2, 3, 10),
    )
    mixed, resid_two_grad, w_cross_out_grad, grads_three, gain_cross_grad, gain_final_grad = call(
        partial(ffn_kernel, cols),
        [
            ((count, width), BF16), ((count, width), F32), ((width, width), BF16), ((slices, grad_sizes[2], width), BF16),
            ((1, width), F32), ((1, width), F32),
        ],
        [
            ((count, width), F32), ((count, width), BF16), ((slices, count, units), F32),
            ((slices, count, units), BF16), ((count, width), F32), ((slices, cols, width), BF16), ((slices, sizes[2], width), BF16),
            ((slices, grad_sizes[2], width), BF16), (slices + 1, None), (slices, None),
        ], 0,
        hidden_one, cross_t, pack_two, gain_cross, pack_three, gain_final, own_out_grad, far=(2, 4), far_outs=(3,),
    )
    back = [
        ((HEADS * PAIR, count), BF16), ((HEADS * PAIR, count), BF16), ((PAIRS, 2 * count, PAIR), BF16),
        ((PAIRS, 2 * count, PAIR), BF16), ((HEADS, count), F32), ((CHUNK, count), F32), ((width, count), BF16),
        ((width, count), F32), ((width, width), F32), ((width, width), F32),
    ] + window_held * 4
    mixed = lax.all_gather(mixed, "head", axis=0, tiled=True)
    encoded_part, grads_two, own_grad, content_part, grads_one = call(
        partial(back_kernel, cols),
        [
            ((wide, width), BF16), ((slices, grad_sizes[1], width), BF16), ((count, width), BF16), ((wide, width), BF16),
            ((slices, grad_sizes[0], width), BF16),
        ],
        back + [(touched, None), (touched, None), (2, None), ((count, width), F32), ((count, 1), F32), ((count, width), F32)]
        + [((slices, sizes[0], width), BF16), ((slices, grad_sizes[1], width), BF16), (2, None)], 1,
        bounds, own, self_t, gain_self, resid_two_grad, cross_t, lse_cross, encoded_window, code, low, high_cross, pack_two,
        w_cross_out_grad, gain_cross_grad, gain_final_grad, lse_self, content_window, high_self, pack_one,
        far=(7, 16, 18), far_outs=(0, 1, 3), micros=8,
    )

    blocks, parts, grads, planes = [own_grad], [content_part, encoded_part], [grads_one, grads_two, grads_three], []
    weight_scratch = []
    for n in grad_sizes[: len(grads)]:
        half, size = n // 2, n // 2 // chips
        weight_scratch += [
            ((slices, half, width), BF16), ((slices, half, width), BF16), ((chips - 1, slices, size, width), BF16),
        ]
    halves = 2 if slices <= 4 else 1
    units_in = (slices - 1) * halves
    part_scratch = [
        ((rows, width), BF16), ((DOC_LEN, width), BF16), ((DOC_LEN, width), BF16),
        ((units_in, count // halves, width), BF16), ((units_in, count // halves, width), BF16),
    ] * len(parts)
    piece_rows = sum(grad_sizes) // peers
    plane_scratch = [((slices * piece_rows, width), BF16)] + [((slices - 1, piece_rows, width), BF16)] * 2
    ins, outs = (len(blocks), len(parts), len(grads), len(planes)), (len(blocks), len(parts), len(grad_sizes))

    def end(refs, out_refs, scratch):
        a, b, c = ins[0], ins[0] + ins[1], sum(ins[:3])
        end_kernel(
            peers, slices, count, refs[:a], refs[a:b], refs[b:c], refs[c:], out_refs[: outs[0]],
            out_refs[outs[0] : outs[0] + outs[1]], out_refs[outs[0] + outs[1] :], scratch,
        )

    end_copies = len(grad_sizes) * (1 + 3 * (chips - 1) + slices) + 2 * slices + len(parts) * 2 * slices + (len(blocks) + 2 * len(parts)) * 2 * slices * halves
    results = talk(
        split_refs(end, sum(ins), sum(outs)),
        [((rows, width), BF16)] * (len(blocks) + len(parts)) + [((n, width), BF16) for n in grad_sizes], [vmem] * sum(outs),
        weight_scratch + part_scratch + plane_scratch, (end_copies, 8 * slices + 8), 1, [hbm] * sum(ins), *blocks, *parts, *grads, *planes,
    )
    query_state_grad, content_grad, encoded_grad, sum_one, sum_two, sum_three = results

    square, tall = ((width, cols), F32), ((cols, width), F32)
    finals = [((rows, width), BF16)] + [((rows, width), F32)] * 3 + [square] * 3 + [tall, square, square, square, tall]
    finals += [((width, units), F32), ((units, width), F32)] + [((1, width), F32)] * 3
    by_rows = pl.BlockSpec((count, width), lambda i: (i, 0))

    def whole(shape):
        return pl.BlockSpec(shape, lambda i: (0,) * len(shape))

    def by_step(shape):
        return pl.BlockSpec((shape[0] // slices, shape[1]), lambda i: (i, 0))

    sums = [sum_one, sum_two, sum_three]
    results = pl.pallas_call(
        partial(finish_kernel, cols, units, slices),
        grid=(slices,),
        out_shape=[jax.ShapeDtypeStruct(shape, kind) for shape, kind in finals],
        in_specs=[by_rows] * 4 + [whole(x.shape) for x in sums],
        out_specs=[by_rows] * 4 + [by_step(shape) for shape, _ in finals[4:14]] + [whole(shape) for shape, _ in finals[14:]],
        compiler_params=pltpu.CompilerParams(vmem_limit_bytes=VMEM_LIMIT),
    )(mixed, query_state_grad, content_grad, encoded_grad, *sums)
    (
        mixed, query_state_grad, content_grad, encoded_grad, w_query_grad, w_key_grad, w_value_grad, w_out_grad,
        w_cross_query_grad, w_cross_key_grad, w_cross_value_grad, w_cross_out_grad, w_inner_grad, w_outer_grad, *gains,
    ) = results
    gains = [g.reshape(width) for g in gains]
    return (
        mixed, query_state_grad, content_grad, encoded_grad, w_query_grad, w_key_grad, w_value_grad, w_out_grad, gains[0],
        w_cross_query_grad, w_cross_key_grad, w_cross_value_grad, w_cross_out_grad, gains[1], w_inner_grad, w_outer_grad, gains[2],
    )


def solution(mesh):
    rows, whole, columns, split = P("seq", None), P(), P(None, "head"), P("head", None)
    in_specs = (
        rows, rows, rows, whole, whole, whole, columns, columns, columns, split, whole,
        columns, columns, columns, split, whole, columns, split, whole, rows,
    )
    out_specs = (
        rows, rows, rows, rows, columns, columns, columns, split, whole,
        columns, columns, columns, split, whole, columns, split, whole,
    )
    return jax.shard_map(body, mesh=mesh, in_specs=in_specs, out_specs=out_specs, check_vma=False)
```
